32 devices in a mesh: rows: 8 (over y, x, core), kv: 4 (over z).
Axes of the slice: x: 2, y: 2, z: 4, core: 2. Of those that a mesh axis runs over, the one named last changes fastest.
Arguments:
- tokens: bfloat16 [8, 1024, 768], P('rows', 'kv'), may hold values from -6 to 6
- lengths: int32 [8, 4], P('rows'), may hold values from 0 to 1024, as said below
- w_qkv: bfloat16 [2, 768, 2304], P(None, ('rows', 'kv')), may hold values from -0.21875 to 0.21875
- w_out: bfloat16 [2, 768, 768], P(None, ('rows', 'kv')), may hold values from -1.75 to 1.75
- w_up: bfloat16 [2, 768, 3072], P(None, ('rows', 'kv')), may hold values from -0.21875 to 0.21875
- w_down: bfloat16 [2, 3072, 768], P(None, ('rows', 'kv')), may hold values from -0.109375 to 0.109375
- gains: bfloat16 [2, 2, 768], P(None, None, ('rows', 'kv')), may hold values from 0.5 to 1.5
- biases: bfloat16 [2, 2, 768], P(None, None, ('rows', 'kv')), may hold values from -3 to 3
- cotangent: bfloat16 [8, 1024, 768], P('rows', 'kv'), may hold values from -6 to 6
Outputs:
- result: bfloat16 [8, 1024, 768], P('rows', 'kv')
- input_grad: float32 [8, 1024, 768], P('rows', 'kv')
- grad_qkv: float32 [2, 768, 2304], P(None, ('rows', 'kv'))
- grad_out: float32 [2, 768, 768], P(None, ('rows', 'kv'))
- grad_up: float32 [2, 768, 3072], P(None, ('rows', 'kv'))
- grad_down: float32 [2, 3072, 768], P(None, ('rows', 'kv'))
- grad_gains: float32 [2, 2, 768], P(None, None, ('rows', 'kv'))
- grad_biases: float32 [2, 768], P(None, ('rows', 'kv'))
- grad_mid_biases: float32 [2, 768], P(None, ('rows', 'kv'))
The draws below stay inside these ranges and needn't reach their ends.
Inputs may be any that keep to these rules, and one draw needn't show every extreme that they name: Zero entries are unused; every other length is 64 or more; a row's lengths sum to at most 1024 and the rest of the row is padding. In every row the document of the second length entry starts in the row's first eighth and ends in its last eighth; some row is one document of 1024.
All inputs are finite; a program needn't handle non-finite values.
Results may differ from the reference program's by a relative error of at most 0.019.
Values may be sent and summed in bfloat16 or wider, within the bound.
A program may use at most 256 MiB of HBM per device.

```python
import math
import jax
import jax.numpy as jnp
from jax import lax

D = 768
HEADS = 12
HEAD = 64
FF = 3072
LAYERS = 2
SLOTS = 1024
MINLEN = 64
ROWS = 8


def draw_lengths(key, part):
    key = jax.random.fold_in(key, 7)
    streams = jax.random.split(key, 5)
    margin = SLOTS // 8
    leading = jax.random.randint(streams[0], (ROWS,), 0, margin)
    leading = jnp.where(leading >= MINLEN, leading, 0)
    trailing = jax.random.randint(streams[1], (ROWS,), 0, margin)
    chosen = jax.random.randint(streams[2], (), 0, ROWS)
    forced = jnp.arange(ROWS) == chosen
    leading = jnp.where(forced, 0, leading)
    trailing = jnp.where(forced, 0, trailing)
    spanning = SLOTS - leading - trailing
    padding = jax.random.randint(streams[3], (ROWS,), 0, trailing + 1)
    remains = trailing - padding
    cut_point = jax.random.randint(streams[4], (ROWS,), MINLEN, jnp.maximum(remains - MINLEN + 1, MINLEN + 1))
    paired = remains >= 2 * MINLEN
    first_doc = jnp.where(paired, cut_point, jnp.where(remains >= MINLEN, remains, 0))
    second_doc = jnp.where(paired, remains - cut_point, 0)
    return jnp.stack([leading, spanning, first_doc, second_doc], -1).astype(jnp.int32)


def level_of(stream_key, dims, cuts, smallest, top_value):
    level, own = 1.0, jax.random.fold_in(stream_key, 6)
    for axis_at, parts in cuts:
        steps = jnp.exp(jax.random.uniform(jax.random.fold_in(own, axis_at), (parts,), jnp.float32, smallest / len(cuts), top_value / len(cuts)))
        level = level * jnp.repeat(steps, dims[axis_at] // parts).reshape([-1 if axis == axis_at else 1 for axis in range(len(dims))])
    return level


def centred(stream_key, shape, width, bound, shards=(), kind=jnp.bfloat16):
    factor_of = level_of(stream_key, shape, shards, -0.22, 0.18) if shards else 1.0
    values = jax.random.normal(stream_key, shape, jnp.float32) * width * factor_of
    return jnp.minimum(jnp.maximum(values, -bound), bound).astype(kind)


def setup_inputs(seed: int = 0) -> dict:
    key_list = jax.random.split(jax.random.key(seed), 10)
    tokens = centred(key_list[0], (ROWS, SLOTS, D), 1.0, 6.0, ((0, 8), (1, 4)))
    lengths = draw_lengths(jax.random.fold_in(key_list[9], 71), 0)
    w_qkv = centred(key_list[2], (LAYERS, D, 3 * D), D ** -0.5, 0.21875, ((1, 32),))
    w_out = centred(key_list[3], (LAYERS, D, D), (D // 64) ** -0.5, 1.75, ((1, 32),))
    w_up = centred(key_list[4], (LAYERS, D, FF), D ** -0.5, 0.21875, ((1, 32),))
    w_down = centred(key_list[5], (LAYERS, FF, D), FF ** -0.5, 0.109375, ((1, 32),))
    gains = jnp.clip(1.0 + 0.1 * jax.random.normal(key_list[6], (LAYERS, 2, D), jnp.float32), 0.5, 1.5).astype(jnp.bfloat16)
    biases = centred(key_list[7], (LAYERS, 2, D), 0.3, 3.0, ((2, 32),))
    cotangent = centred(key_list[8], (ROWS, SLOTS, D), 1.0, 6.0, ((0, 8), (1, 4)))
    return {"tokens": tokens, "lengths": lengths, "w_qkv": w_qkv, "w_out": w_out, "w_up": w_up, "w_down": w_down, "gains": gains, "biases": biases, "cotangent": cotangent}


@jax.custom_vjp
def low(v):
    return lax.optimization_barrier(v.astype(jnp.bfloat16)).astype(jnp.float32)

@jax.custom_vjp
def low_back(v):
    return v

def low_keep(v):
    return (low(v), None)

def low_pass(kept, grad):
    return (grad,)

def back_keep(v):
    return (v, None)

def back_low(kept, grad):
    return (low(grad),)
low.defvjp(low_keep, low_pass)
low_back.defvjp(back_keep, back_low)
EPSILON = 1e-05

def layer_norm(stream, gain, bias):
    center = stream - lax.optimization_barrier(jnp.mean(stream, -1, keepdims=True))
    spread = lax.optimization_barrier(jnp.mean(center * center, -1, keepdims=True))
    return center * lax.rsqrt(spread + EPSILON) * gain + bias

def normalise(scores, allowed, query_live, signed):
    if signed:
        magnitude = jnp.sqrt(scores * scores + 1.0)
        ceiling = lax.optimization_barrier(jnp.max(jnp.where(allowed > 0, magnitude, 0.0), -1, keepdims=True))
        shifted = jnp.where(allowed > 0, magnitude - ceiling, -60.0)
    else:
        ceiling = lax.optimization_barrier(jnp.max(jnp.where(allowed > 0, scores, -10000.0), -1, keepdims=True))
        shifted = jnp.where(allowed > 0, scores - ceiling, -60.0)
    raised = jnp.exp(shifted) * allowed
    normaliser = lax.optimization_barrier(jnp.sum(raised, -1, keepdims=True)) + (1.0 - query_live)[None, :, None]
    unsigned_w = raised / normaliser
    if signed:
        return (jnp.tanh(scores) * unsigned_w, unsigned_w)
    return (unsigned_w, unsigned_w)

def attend_row(query, keys, values, docs, live, signed):
    span = min(512, SLOTS)
    scaling = 1.0 / math.sqrt(HEAD)
    places = jnp.arange(SLOTS, dtype=jnp.int32)

    def block(items):
        query_block, block_places, block_docs, block_live = items
        allowed = ((block_docs[:, None] == docs[None, :]) & (places[None, :] <= block_places[:, None])).astype(jnp.float32)
        allowed = allowed * block_live[:, None] * live[None, :]
        scores = low_back(jnp.einsum('qhd,khd->hqk', query_block, keys, precision=lax.Precision.HIGHEST) * scaling)
        weights, unused = normalise(scores, allowed, block_live, signed)
        return jnp.einsum('hqk,khd->qhd', low(weights), values, precision=lax.Precision.HIGHEST)
    blocks = (query.reshape(SLOTS // span, span, HEADS, HEAD), places.reshape(SLOTS // span, span), docs.reshape(SLOTS // span, span), live.reshape(SLOTS // span, span))
    outcome = lax.map(jax.checkpoint(block), blocks)
    return outcome.reshape(SLOTS, HEADS * HEAD)

def block_forward(stream, params, docs, live, signed):
    full_qkv, full_out, full_up, full_down, gain_pair, bias_pair = params
    normed_in = low(layer_norm(stream, gain_pair[0], bias_pair[0]))
    projected = low(low_back(jnp.dot(normed_in, full_qkv, precision=lax.Precision.HIGHEST)))
    query = projected[..., :D].reshape(ROWS, SLOTS, HEADS, HEAD)
    keys = projected[..., D:2 * D].reshape(ROWS, SLOTS, HEADS, HEAD)
    values = projected[..., 2 * D:].reshape(ROWS, SLOTS, HEADS, HEAD)

    def row_function(items):
        return attend_row(items[0], items[1], items[2], items[3], items[4], signed)
    attended = lax.map(jax.checkpoint(row_function), (query, keys, values, docs, live))
    attended = low(low_back(attended))
    middle = stream + low_back(jnp.dot(attended, full_out, precision=lax.Precision.HIGHEST))
    normed_mid = low(layer_norm(middle, gain_pair[1], bias_pair[1]))
    pre_act = low_back(jnp.dot(normed_mid, full_up, precision=lax.Precision.HIGHEST))
    activated = low(jax.nn.gelu(pre_act))
    return middle + low_back(jnp.dot(activated, full_down, precision=lax.Precision.HIGHEST))

def reference(tokens, lengths, w_qkv, w_out, w_up, w_down, gains, biases, cotangent):
    doc_ends = jnp.cumsum(lengths, -1).astype(jnp.int32)
    places = jnp.arange(SLOTS, dtype=jnp.int32)
    docs = lax.optimization_barrier(jnp.sum((doc_ends[:, None, :] <= places[None, :, None]).astype(jnp.int32), -1)).astype(jnp.int32)
    live = (places[None, :] < doc_ends[:, -1:]).astype(jnp.float32)

    def forward(stream, all_qkv, all_out, all_up, all_down, all_gains, all_biases):
        for number in range(LAYERS):
            params = (all_qkv[number], all_out[number], all_up[number], all_down[number], all_gains[number], all_biases[number])
            stream = block_forward(stream, params, docs, live, number == 0)
        return stream * live[..., None]
    outcome, pull = jax.vjp(forward, tokens.astype(jnp.float32), w_qkv.astype(jnp.float32), w_out.astype(jnp.float32), w_up.astype(jnp.float32), w_down.astype(jnp.float32), gains.astype(jnp.float32), biases.astype(jnp.float32))
    grads = pull(cotangent.astype(jnp.float32))
    return (outcome.astype(jnp.bfloat16), grads[0], grads[1], grads[2], grads[3], grads[4], grads[5], grads[6][:, 0], grads[6][:, 1])
```

```python
import math

import jax
import jax.numpy as jnp
from jax import lax
from jax.experimental import pallas as pl
from jax.experimental.pallas import tpu as pltpu
from jax.sharding import PartitionSpec as P

HEADS = 12
HEAD = 64
LAYERS = 2


EPSILON = 1e-05


def norm_rows(stream, gain, bias):
    center = stream - jnp.mean(stream, -1, keepdims=True)
    spread = jnp.mean(center * center, -1, keepdims=True)
    return center * lax.rsqrt(spread + EPSILON) * gain + bias


def normalise(scores, allowed, query_live, signed):
    if signed:
        magnitude = jnp.sqrt(scores * scores + 1.0)
        ceiling = jnp.max(jnp.where(allowed > 0, magnitude, 0.0), -1, keepdims=True)
        shifted = jnp.where(allowed > 0, magnitude - ceiling, -60.0)
    else:
        ceiling = jnp.max(jnp.where(allowed > 0, scores, -10000.0), -1, keepdims=True)
        shifted = jnp.where(allowed > 0, scores - ceiling, -60.0)
    raised = jnp.exp(shifted) * allowed
    normaliser = jnp.sum(raised, -1, keepdims=True) + (1.0 - query_live)[None, :, None]
    unsigned_w = raised / normaliser
    if signed:
        return (jnp.tanh(scores) * unsigned_w, unsigned_w)
    return (unsigned_w, unsigned_w)


def make_mask(query_places, query_docs, query_live, key_places, key_docs, key_live):
    allowed = (
        (query_docs[:, None] == key_docs[None, :]) & (key_places[None, :] <= query_places[:, None])
    ).astype(jnp.float32)
    return allowed * query_live[:, None] * key_live[None, :]


def split_heads(query, keys_vals):
    model_width = query.shape[-1]
    slot_count = keys_vals.shape[0]
    query_heads = query.reshape(-1, HEADS, HEAD)
    key_heads = keys_vals[:, :model_width].reshape(slot_count, HEADS, HEAD)
    value_heads = keys_vals[:, model_width:].reshape(slot_count, HEADS, HEAD)
    return (query_heads, key_heads, value_heads)


def score_grads(scores, unsigned_w, weight_grad, inner_sum, signed):
    if signed:
        tanh_s = jnp.tanh(scores)
        magnitude = jnp.sqrt(scores * scores + 1.0)
        return unsigned_w * (
            (tanh_s * weight_grad - inner_sum) * scores / magnitude
            + weight_grad * (1.0 - tanh_s * tanh_s)
        )
    return unsigned_w * (weight_grad - inner_sum)


def attend_row(query, keys_vals, allowed, query_live, signed, scaling):
    query_heads, key_heads, value_heads = split_heads(query, keys_vals)
    scores = (
        jnp.einsum("qhd,khd->hqk", query_heads, key_heads, preferred_element_type=jnp.float32)
        * scaling
    )
    weights, unsigned_w = normalise(scores, allowed, query_live, signed)
    outcome = jnp.einsum(
        "hqk,khd->qhd",
        weights.astype(jnp.bfloat16),
        value_heads,
        preferred_element_type=jnp.float32,
    )
    return outcome.reshape(query.shape[0], query.shape[1]).astype(jnp.bfloat16)


def attend_back(query, keys_vals, grad_att, allowed, query_live, signed, scaling):
    query_heads, key_heads, value_heads = split_heads(query, keys_vals)
    slot_count = keys_vals.shape[0]
    model_width = query.shape[-1]
    scores = (
        jnp.einsum("qhd,khd->hqk", query_heads, key_heads, preferred_element_type=jnp.float32)
        * scaling
    )
    weights, unsigned_w = normalise(scores, allowed, query_live, signed)
    weights_low = weights.astype(jnp.bfloat16)
    grad_heads = grad_att.reshape(-1, HEADS, HEAD)
    weight_grad = jnp.einsum(
        "qhd,khd->hqk", grad_heads, value_heads, preferred_element_type=jnp.float32
    )
    inner_sum = jnp.sum(weight_grad * weights, -1, keepdims=True)
    score_low = score_grads(scores, unsigned_w, weight_grad, inner_sum, signed).astype(jnp.bfloat16)
    query_grad = (
        jnp.einsum("hqk,khd->qhd", score_low, key_heads, preferred_element_type=jnp.float32)
        * scaling
    )
    key_grad = (
        jnp.einsum("hqk,qhd->khd", score_low, query_heads, preferred_element_type=jnp.float32)
        * scaling
    )
    value_grad = jnp.einsum(
        "hqk,qhd->khd", weights_low, grad_heads, preferred_element_type=jnp.float32
    )
    kv_grad = jnp.concatenate(
        [key_grad.reshape(slot_count, model_width), value_grad.reshape(slot_count, model_width)], -1
    )
    return (query_grad.reshape(query.shape[0], model_width), kv_grad)


def reduce_grads(pairs, g_gain, g_bias):
    n_rows = lax.axis_size("rows")
    n_kv = lax.axis_size("kv")
    lefts = []
    rights = []
    for left_side, right_side in pairs:
        tok_count = left_side.shape[0] * left_side.shape[1]
        in_width = left_side.shape[-1]
        lefts.append(left_side.reshape(tok_count, n_rows, n_kv, in_width // (n_rows * n_kv)))
        rights.append(right_side.reshape(tok_count, right_side.shape[-1]))
    moved = (
        lax.all_to_all(lefts[0], "kv", split_axis=2, concat_axis=0, tiled=True),
        lax.all_to_all(lefts[1], "kv", split_axis=2, concat_axis=0, tiled=True),
        lax.all_to_all(lefts[2], "kv", split_axis=2, concat_axis=0, tiled=True),
        lax.all_to_all(lefts[3], "kv", split_axis=2, concat_axis=0, tiled=True),
    )
    whole = (
        lax.all_gather(rights[0], "kv", axis=0, tiled=True),
        lax.all_gather(rights[1], "kv", axis=0, tiled=True),
        lax.all_gather(rights[2], "kv", axis=0, tiled=True),
        lax.all_gather(rights[3], "kv", axis=0, tiled=True),
    )
    partial_sums = []
    for number in range(4):
        left_block = moved[number].reshape(moved[number].shape[0], -1)
        product = jnp.einsum(
            "ti,to->io", left_block, whole[number], preferred_element_type=jnp.float32
        )
        partial_sums.append(product.reshape(n_rows, -1, product.shape[-1]))
    reduced = (
        lax.psum_scatter(
            partial_sums[0].astype(jnp.bfloat16), "rows", scatter_dimension=0, tiled=True
        ).astype(jnp.float32),
        lax.psum_scatter(
            partial_sums[1].astype(jnp.bfloat16), "rows", scatter_dimension=0, tiled=True
        ).astype(jnp.float32),
        lax.psum_scatter(
            partial_sums[2].astype(jnp.bfloat16), "rows", scatter_dimension=0, tiled=True
        ).astype(jnp.float32),
        lax.psum_scatter(
            partial_sums[3].astype(jnp.bfloat16), "rows", scatter_dimension=0, tiled=True
        ).astype(jnp.float32),
    )
    norm_parts = (
        lax.psum_scatter(g_gain, ("rows", "kv"), scatter_dimension=1, tiled=True),
        lax.psum_scatter(g_bias, ("rows", "kv"), scatter_dimension=1, tiled=True),
    )
    results = tuple((piece.reshape(piece.shape[1], piece.shape[2]) for piece in reduced))
    return results + (norm_parts[0], norm_parts[1])


def local_generic(tokens, lengths, w_qkv, w_out, w_up, w_down, gains, biases, cotangent):
    rows_here, slot_dev, model_width = tokens.shape
    slot_count = slot_dev * lax.axis_size("kv")
    first_slot = lax.axis_index("kv") * slot_dev
    scaling = 1.0 / math.sqrt(HEAD)
    doc_ends = jnp.cumsum(lengths, -1)
    places = jnp.arange(slot_count, dtype=jnp.int32)
    docs_all = jnp.sum((doc_ends[:, None, :] <= places[None, :, None]).astype(jnp.int32), -1)
    live_all = (places[None, :] < doc_ends[:, -1:]).astype(jnp.float32)
    docs_here = lax.dynamic_slice_in_dim(docs_all, first_slot, slot_dev, 1)
    live_here = lax.dynamic_slice_in_dim(live_all, first_slot, slot_dev, 1)
    local_places = first_slot + jnp.arange(slot_dev, dtype=jnp.int32)
    masks = make_mask(local_places, docs_here[0], live_here[0], places, docs_all[0], live_all[0])
    stream = tokens.astype(jnp.float32)
    stored = []
    for number in range(LAYERS):
        signed = number == 0
        pieces = (
            lax.all_gather(w_qkv[number], ("rows", "kv"), axis=0, tiled=True),
            lax.all_gather(w_out[number], ("rows", "kv"), axis=0, tiled=True),
            lax.all_gather(w_up[number], ("rows", "kv"), axis=0, tiled=True),
            lax.all_gather(w_down[number], ("rows", "kv"), axis=0, tiled=True),
            lax.all_gather(gains[number], ("rows", "kv"), axis=1, tiled=True),
            lax.all_gather(biases[number], ("rows", "kv"), axis=1, tiled=True),
        )
        full_qkv, full_out, full_up, full_down, gain_pair, bias_pair = pieces
        gain_pair = gain_pair.astype(jnp.float32)
        bias_pair = bias_pair.astype(jnp.float32)
        normed_in = norm_rows(stream, gain_pair[0], bias_pair[0]).astype(jnp.bfloat16)
        projected = jnp.dot(normed_in, full_qkv, preferred_element_type=jnp.float32).astype(
            jnp.bfloat16
        )
        kv_all = lax.all_gather(projected[:, :, model_width:], "kv", axis=1, tiled=True)
        attended = jnp.stack(
            [
                attend_row(
                    projected[0, :, :model_width], kv_all[0], masks, live_here[0], signed, scaling
                )
            ]
        )
        shared = kv_all
        middle = stream + jnp.dot(attended, full_out, preferred_element_type=jnp.float32)
        normed_mid = norm_rows(middle, gain_pair[1], bias_pair[1]).astype(jnp.bfloat16)
        pre_act = jnp.dot(normed_mid, full_up, preferred_element_type=jnp.float32)
        activated = jax.nn.gelu(pre_act).astype(jnp.bfloat16)
        stored.append(
            (
                stream,
                normed_in,
                projected,
                shared,
                attended,
                middle,
                normed_mid,
                pre_act,
                activated,
                pieces,
            )
        )
        stream = middle + jnp.dot(activated, full_down, preferred_element_type=jnp.float32)
    result = (stream * live_here[..., None]).astype(jnp.bfloat16)
    residual_grad = cotangent.astype(jnp.float32) * live_here[..., None]
    collected = [None] * LAYERS
    for number in reversed(range(LAYERS)):
        signed = number == 0
        (
            stream_in,
            normed_in,
            projected,
            shared,
            attended,
            middle,
            normed_mid,
            pre_act,
            activated,
            kept,
        ) = stored[number]
        pieces = (
            lax.all_gather(w_qkv[number], ("rows", "kv"), axis=0, tiled=True),
            lax.all_gather(w_out[number], ("rows", "kv"), axis=0, tiled=True),
            lax.all_gather(w_up[number], ("rows", "kv"), axis=0, tiled=True),
            lax.all_gather(w_down[number], ("rows", "kv"), axis=0, tiled=True),
            lax.all_gather(gains[number], ("rows", "kv"), axis=1, tiled=True),
            lax.all_gather(biases[number], ("rows", "kv"), axis=1, tiled=True),
        )
        full_qkv, full_out, full_up, full_down, gain_pair, bias_pair = pieces
        gain_pair = gain_pair.astype(jnp.float32)
        bias_pair = bias_pair.astype(jnp.float32)
        down_in = residual_grad.astype(jnp.bfloat16)
        act_grad = jnp.einsum("rtd,fd->rtf", down_in, full_down, preferred_element_type=jnp.float32)
        unused, gelu_pull = jax.vjp(jax.nn.gelu, pre_act)
        pre_grad = gelu_pull(act_grad)[0].astype(jnp.bfloat16)
        mid_normed_grad = jnp.einsum(
            "rtf,df->rtd", pre_grad, full_up, preferred_element_type=jnp.float32
        )
        unused, norm_pull = jax.vjp(norm_rows, middle, gain_pair[1], bias_pair[1])
        middle_part, gain_late, bias_late = norm_pull(mid_normed_grad)
        middle_grad = residual_grad + middle_part
        branch_grad = middle_grad.astype(jnp.bfloat16)
        att_grad = jnp.einsum(
            "rte,de->rtd", branch_grad, full_out, preferred_element_type=jnp.float32
        ).astype(jnp.bfloat16)
        kv_all = shared
        query_grad, kv_grad = attend_back(
            projected[0, :, :model_width],
            kv_all[0],
            att_grad[0],
            masks,
            live_here[0],
            signed,
            scaling,
        )
        query_grads = [query_grad]
        kv_grads = [kv_grad]
        kv_here = lax.psum_scatter(
            jnp.stack(kv_grads).astype(jnp.bfloat16), "kv", scatter_dimension=1, tiled=True
        ).astype(jnp.float32)
        qkv_grad = jnp.concatenate([jnp.stack(query_grads), kv_here], -1).astype(jnp.bfloat16)
        in_normed_grad = jnp.einsum(
            "rte,de->rtd", qkv_grad, full_qkv, preferred_element_type=jnp.float32
        )
        unused, first_pull = jax.vjp(norm_rows, stream_in, gain_pair[0], bias_pair[0])
        stream_part, gain_early, bias_early = first_pull(in_normed_grad)
        residual_grad = middle_grad + stream_part
        g_gain = jnp.stack([gain_early, gain_late])
        g_bias = jnp.stack([bias_early, bias_late])
        pairs = [
            (normed_in, qkv_grad),
            (attended, branch_grad),
            (normed_mid, pre_grad),
            (activated, down_in),
        ]
        collected[number] = reduce_grads(pairs, g_gain, g_bias)
    grad_qkv = jnp.stack([collected[number][0] for number in range(LAYERS)])
    grad_out = jnp.stack([collected[number][1] for number in range(LAYERS)])
    grad_up = jnp.stack([collected[number][2] for number in range(LAYERS)])
    grad_down = jnp.stack([collected[number][3] for number in range(LAYERS)])
    grad_gains = jnp.stack([collected[number][4] for number in range(LAYERS)])
    grad_biases = jnp.stack([collected[number][5][0] for number in range(LAYERS)])
    grad_mid_biases = jnp.stack([collected[number][5][1] for number in range(LAYERS)])
    return (
        result,
        residual_grad,
        grad_qkv,
        grad_out,
        grad_up,
        grad_down,
        grad_gains,
        grad_biases,
        grad_mid_biases,
    )


F32 = jnp.float32
BF16 = jnp.bfloat16
MESH = pl.DeviceIdType.MESH
ZN = 4


def flip(value, unit):
    bit = lax.rem(lax.div(value, unit), 2)
    return value + unit - 2 * unit * bit


def places_of():
    r = lax.axis_index("rows")
    z = lax.axis_index("kv")
    return r, z, flip(r, 2), flip(r, 4), flip(flip(r, 2), 4), flip(r, 1)


def turn(z, k):
    return lax.rem(z + k, ZN)


def rcopy(src, dst, ssem, rsem, device):
    return pltpu.make_async_remote_copy(
        src_ref=src, dst_ref=dst, send_sem=ssem, recv_sem=rsem, device_id=device, device_id_type=MESH
    )


def band(start, size):
    return pl.ds(pl.multiple_of(start, 16), size)


def greet(peers):
    barrier = pltpu.get_barrier_semaphore()
    for peer in peers:
        pl.semaphore_signal(barrier, inc=1, device_id=peer, device_id_type=MESH)
    pl.semaphore_wait(barrier, len(peers))


def comm_peers():
    r, z, rx, ry, rd, rc = places_of()
    return [(r, turn(z, 1)), (r, turn(z, 2)), (r, turn(z, 3)), (rx, z), (ry, z), (rc, z)]


def col_step(width):
    return 256 if width % 256 == 0 else 128


class Gather:
    SEMS = 14

    def __init__(self, own, whole, zm, zt, ssem, rsem, base):
        self.own, self.whole, self.zm, self.zt = own, whole, zm, zt
        self.ssem, self.rsem, self.base = ssem, rsem, base
        self.split = zm is not None
        self.rows = whole.shape[0] // 8
        self.width = whole.shape[1]
        self.sent = []

    def _copy(self, src, dst, at, device):
        return rcopy(src, dst, self.ssem.at[self.base + at], self.rsem.at[self.base + at], device)

    def _block(self, r, half=None):
        if half is None:
            return self.whole.at[band(r * self.rows, self.rows), :]
        part = self.rows // 2
        return self.whole.at[band(r * self.rows + half * part, part), :]

    def _send(self, src, dst, at, device):
        copy = self._copy(src, dst, at, device)
        copy.start()
        self.sent.append(copy)

    def prepare(self):
        r, z = places_of()[:2]
        if self.split:
            half = self.width // 2
            own = self.own[...].astype(F32)
            self.zm[pl.ds(z, 1)] = own[:16].astype(BF16)[None]
            self.zt[pl.ds(z, 1)] = jnp.concatenate([own[16:, :half], own[16:, half:]], 0).astype(BF16)[None]
        else:
            part = self.rows // ZN
            self.whole[band(r * self.rows + z * part, part), :] = self.own[...]

    def _zrefs(self, z):
        if self.split:
            return [self.zm.at[z], self.zt.at[z]]
        part = self.rows // ZN
        return [self.whole.at[band(places_of()[0] * self.rows + z * part, part), :]]

    def send_z(self):
        r, z = places_of()[:2]
        for k in (1, 2, 3):
            for i, ref in enumerate(self._zrefs(z)):
                self._send(ref, ref, 2 * (k - 1) + i, (r, turn(z, k)))

    def wait_z(self):
        r, z = places_of()[:2]
        for k in (1, 2, 3):
            for i, ref in enumerate(self._zrefs(turn(z, ZN - k))):
                self._copy(ref, ref, 2 * (k - 1) + i, (r, turn(z, ZN - k))).wait_recv()
        if self.split:
            half = self.width // 2
            step = col_step(half)
            for side in (0, 1):
                def assemble(i, carry, side=side):
                    at = pl.multiple_of(i * step, step)
                    here = pl.ds(pl.multiple_of(side * half + i * step, 128), step)
                    parts = []
                    for piece in range(ZN):
                        parts.append(self.zm[piece, :, here].astype(F32))
                        parts.append(self.zt[piece, :, pl.ds(at, step)].astype(F32)[8 * side : 8 * side + 8])
                    self.whole[band(r * self.rows, self.rows), here] = jnp.concatenate(parts, 0).astype(BF16)
                    return carry
                lax.fori_loop(0, half // step, assemble, 0)

    def send_plane(self):
        r, z, rx, ry, rd, rc = places_of()
        own = self._block(r)
        self._send(own, own, 6, (rx, z))
        self._send(own, own, 7, (ry, z))
        self._send(own, own, 10, (rc, z))

    def forward(self):
        r, z, rx, ry, rd, rc = places_of()
        first, second = self._block(rx), self._block(ry)
        self._copy(first, first, 6, (rx, z)).wait_recv()
        part = self._block(rx, 0)
        self._send(part, part, 8, (ry, z))
        self._send(first, first, 11, (rc, z))
        self._copy(second, second, 7, (ry, z)).wait_recv()
        part = self._block(ry, 1)
        self._send(part, part, 9, (rx, z))
        self._send(second, second, 12, (rc, z))

    def forward_last(self):
        r, z, rx, ry, rd, rc = places_of()
        part = self._block(rd, 0)
        self._copy(part, part, 8, (ry, z)).wait_recv()
        part = self._block(rd, 1)
        self._copy(part, part, 9, (rx, z)).wait_recv()
        diagonal = self._block(rd)
        self._send(diagonal, diagonal, 13, (rc, z))

    def finish(self):
        r, z, rx, ry, rd, rc = places_of()
        for at, block in ((10, r), (11, rx), (12, ry), (13, rd)):
            ref = self._block(flip(block, 1))
            self._copy(ref, ref, at, (rc, z)).wait_recv()

    def drain(self):
        for copy in self.sent:
            copy.wait_send()


def add_rows(dst, src, rows):
    def step(i, carry):
        here = band(i * 16, 16)
        dst[here, :] = (dst[here, :].astype(F32) + src[here, :].astype(F32)).astype(BF16)
        return carry
    lax.fori_loop(0, rows // 16, step, 0)


class Scatter:
    SEMS = 14

    def __init__(self, mine, got, half, near, zs, zr, out, ssem, rsem, base):
        self.mine, self.got, self.half, self.near = mine, got, half, near
        self.zs, self.zr, self.out = zs, zr, out
        self.ssem, self.rsem, self.base = ssem, rsem, base
        self.rows, self.width = mine.shape[1], mine.shape[2]
        self.split = len(zs) == 2
        self.sent = []

    def _copy(self, src, dst, at, device):
        return rcopy(src, dst, self.ssem.at[self.base + at], self.rsem.at[self.base + at], device)

    def _send(self, src, dst, at, device):
        copy = self._copy(src, dst, at, device)
        copy.start()
        self.sent.append(copy)

    def send_core(self, b, src):
        r, z, rx, ry, rd, rc = places_of()
        self._send(src, self.got.at[b], b, (rc, z))

    def add_core(self, b):
        r, z, rx, ry, rd, rc = places_of()
        self._copy(self.got.at[b], self.got.at[b], b, (rc, z)).wait_recv()
        add_rows(self.mine.at[b], self.got.at[b], self.rows)

    def add_core_block(self, block):
        r, z, rx, ry, rd, rc = places_of()
        return block

    def send_diagonal(self):
        r, z, rx, ry, rd, rc = places_of()
        part = self.rows // 2
        diagonal = lax.div(rd, 2)
        self._send(self.mine.at[diagonal, pl.ds(0, part)], self.half.at[0], 4, (ry, z))
        self._send(self.mine.at[diagonal, pl.ds(part, part)], self.half.at[1], 5, (rx, z))

    def send_near(self):
        r, z, rx, ry, rd, rc = places_of()
        part = self.rows // 2
        for at, side, other in ((4, ry, rx), (5, rx, ry)):
            i = at - 4
            self._copy(self.half.at[i], self.half.at[i], at, (side, z)).wait_recv()
            block = self.mine.at[lax.div(other, 2)]
            add_rows(block.at[pl.ds(i * part, part)], self.half.at[i], part)
            self._send(block, self.near.at[i], 6 + i, (other, z))

    def send_z(self):
        r, z, rx, ry, rd, rc = places_of()
        for i, side in ((0, rx), (1, ry)):
            self._copy(self.near.at[i], self.near.at[i], 6 + i, (side, z)).wait_recv()
        own = self.mine.at[lax.div(r, 2)]
        if self.split:
            half = self.width // 2
            step = col_step(half)
            def cut(i, carry):
                sums = []
                for side in (0, 1):
                    here = pl.ds(pl.multiple_of(side * half + i * step, 128), step)
                    sums.append(
                        own[:, here].astype(F32) + self.near[0, :, here].astype(F32) + self.near[1, :, here].astype(F32)
                    )
                at = pl.ds(pl.multiple_of(i * step, 128), step)
                for piece in range(ZN):
                    for side in (0, 1):
                        here = pl.ds(pl.multiple_of(side * half + i * step, 128), step)
                        self.zs[0][piece, :, here] = sums[side][24 * piece : 24 * piece + 16].astype(BF16)
                    self.zs[1][piece, :, at] = jnp.concatenate(
                        [sums[side][24 * piece + 16 : 24 * piece + 24] for side in (0, 1)], 0
                    ).astype(BF16)
                return carry
            lax.fori_loop(0, half // step, cut, 0)
        else:
            part = self.rows // ZN
            for piece in range(ZN):
                def cut_rows(i, carry, piece=piece):
                    here = band(piece * part + i * 16, 16)
                    self.zs[0][piece, band(i * 16, 16), :] = (
                        own[here, :].astype(F32) + self.near[0, here, :].astype(F32) + self.near[1, here, :].astype(F32)
                    ).astype(BF16)
                    return carry
                lax.fori_loop(0, part // 16, cut_rows, 0)
        for k in (1, 2, 3):
            for i in range(len(self.zs)):
                self._send(self.zs[i].at[turn(z, k)], self.zr[i].at[k - 1], 8 + 2 * (k - 1) + i, (r, turn(z, k)))

    def finish(self):
        r, z = places_of()[:2]
        for k in (1, 2, 3):
            for i in range(len(self.zs)):
                ref = self.zr[i].at[k - 1]
                self._copy(ref, ref, 8 + 2 * (k - 1) + i, (r, turn(z, ZN - k))).wait_recv()
        if self.split:
            half = self.width // 2
            main = self.zs[0][z].astype(F32)
            tail = self.zs[1][z].astype(F32)
            for k in range(3):
                main = main + self.zr[0][k].astype(F32)
                tail = tail + self.zr[1][k].astype(F32)
            self.out[pl.ds(0, 16), :] = main
            self.out[pl.ds(16, 8), pl.ds(0, half)] = tail[:8]
            self.out[pl.ds(16, 8), pl.ds(half, half)] = tail[8:]
        else:
            def total(i, carry):
                here = band(i * 16, 16)
                value = self.zs[0][z, here, :].astype(F32)
                for k in range(3):
                    value = value + self.zr[0][k, here, :].astype(F32)
                self.out[here, :] = value
                return carry
            lax.fori_loop(0, self.out.shape[0] // 16, total, 0)

    def drain(self):
        for copy in self.sent:
            copy.wait_send()


def gather_kernel(*refs):
    owns, outs, rest = refs[:8], refs[8:16], list(refs[16:])
    wholes = [rest.pop(0) for _ in range(8)]
    zbuf = [(None, None) if n % 4 == 3 else (rest.pop(0), rest.pop(0)) for n in range(8)]
    ssem, rsem, osem = rest
    greet(comm_peers())
    jobs = [
        Gather(owns[n], wholes[n], zbuf[n][0], zbuf[n][1], ssem, rsem, n * Gather.SEMS) for n in range(8)
    ]
    for job in jobs:
        job.prepare()
        job.send_z()
    stores = []
    for n in range(8 + 3):
        if n < 8:
            jobs[n].wait_z()
            jobs[n].send_plane()
        if 0 <= n - 1 < 8:
            jobs[n - 1].forward()
        if 0 <= n - 2 < 8:
            jobs[n - 2].forward_last()
        if 0 <= n - 3 < 8:
            jobs[n - 3].finish()
            store = pltpu.make_async_copy(wholes[n - 3], outs[n - 3], osem.at[n - 3])
            store.start()
            stores.append(store)
    for job in jobs:
        job.drain()
    for store in stores:
        store.wait()


def gather_weights(owns):
    shapes = [((own.shape[0] * 32), own.shape[1]) for own in owns]
    zshapes = []
    for n, own in enumerate(owns):
        if n % 4 != 3:
            zshapes += [
                pltpu.VMEM((ZN, 16, own.shape[1]), BF16),
                pltpu.VMEM((ZN, 16, own.shape[1] // 2), BF16),
            ]
    return pl.pallas_call(
        gather_kernel,
        out_shape=[jax.ShapeDtypeStruct(shape, BF16) for shape in shapes],
        in_specs=[pl.BlockSpec(memory_space=pltpu.VMEM)] * 8,
        out_specs=[pl.BlockSpec(memory_space=pl.ANY)] * 8,
        scratch_shapes=[pltpu.VMEM(shape, BF16) for shape in shapes]
        + zshapes
        + [
            pltpu.SemaphoreType.DMA((8 * Gather.SEMS,)),
            pltpu.SemaphoreType.DMA((8 * Gather.SEMS,)),
            pltpu.SemaphoreType.DMA((8,)),
        ],
        compiler_params=pltpu.CompilerParams(collective_id=0, has_side_effects=True, vmem_limit_bytes=58 * 2**20),
    )(*owns)


def scatter_kernel(*refs):
    terms, outs, rest = refs[:4], refs[4:8], list(refs[8:])
    jobs = []
    sems = rest[-3:]
    ssem, rsem, lsem = sems
    greet(comm_peers())
    r, z, rx, ry, rd, rc = places_of()
    for n in range(4):
        mine, got, half, near = [rest.pop(0) for _ in range(4)]
        count = 1 if n == 3 else 2
        zs = [rest.pop(0) for _ in range(count)]
        zr = [rest.pop(0) for _ in range(count)]
        jobs.append(Scatter(mine, got, half, near, zs, zr, outs[n], ssem, rsem, n * Scatter.SEMS))
    loads = []
    for n, job in enumerate(jobs):
        rows = job.rows
        for b in range(4):
            theirs = terms[n].at[band((2 * b + lax.rem(rc, 2)) * rows, rows), :]
            job.send_core(b, theirs)
            ours = terms[n].at[band((2 * b + lax.rem(r, 2)) * rows, rows), :]
            load = pltpu.make_async_copy(ours, job.mine.at[b], lsem.at[4 * n + b])
            load.start()
            loads.append(load)
    for n in range(4 + 3):
        if n < 4:
            for b in range(4):
                loads[4 * n + b].wait()
                jobs[n].add_core(b)
            jobs[n].send_diagonal()
        if 0 <= n - 1 < 4:
            jobs[n - 1].send_near()
        if 0 <= n - 2 < 4:
            jobs[n - 2].send_z()
        if 0 <= n - 3 < 4:
            jobs[n - 3].finish()
    for job in jobs:
        job.drain()


def scatter_grads(terms):
    scratch = []
    outs = []
    for n, term in enumerate(terms):
        rows, width = term.shape[0] // 8, term.shape[1]
        scratch += [
            pltpu.VMEM((4, rows, width), BF16),
            pltpu.VMEM((4, rows, width), BF16),
            pltpu.VMEM((2, rows // 2, width), BF16),
            pltpu.VMEM((2, rows, width), BF16),
        ]
        if n == 3:
            cuts = [(rows // 4, width)]
        else:
            cuts = [(16, width), (16, width // 2)]
        scratch += [pltpu.VMEM((4,) + cut, BF16) for cut in cuts]
        scratch += [pltpu.VMEM((3,) + cut, BF16) for cut in cuts]
        outs.append(jax.ShapeDtypeStruct((rows // 4, width), F32))
    return pl.pallas_call(
        scatter_kernel,
        out_shape=outs,
        in_specs=[pl.BlockSpec(memory_space=pl.ANY)] * 4,
        out_specs=[pl.BlockSpec(memory_space=pltpu.VMEM)] * 4,
        scratch_shapes=scratch
        + [
            pltpu.SemaphoreType.DMA((4 * Scatter.SEMS,)),
            pltpu.SemaphoreType.DMA((4 * Scatter.SEMS,)),
            pltpu.SemaphoreType.DMA((16,)),
        ],
        compiler_params=pltpu.CompilerParams(collective_id=1, has_side_effects=True, vmem_limit_bytes=58 * 2**20),
    )(*terms)


def local_fast(tokens, lengths, w_qkv, w_out, w_up, w_down, gains, biases, cotangent):
    rows_here, slot_dev, model_width = tokens.shape
    slot_count = slot_dev * lax.axis_size("kv")
    first_slot = lax.axis_index("kv") * slot_dev
    scaling = 1.0 / math.sqrt(HEAD)
    doc_ends = jnp.cumsum(lengths, -1)
    places = jnp.arange(slot_count, dtype=jnp.int32)
    docs_all = jnp.sum((doc_ends[:, None, :] <= places[None, :, None]).astype(jnp.int32), -1)
    live_all = (places[None, :] < doc_ends[:, -1:]).astype(jnp.float32)
    docs_here = lax.dynamic_slice_in_dim(docs_all, first_slot, slot_dev, 1)
    live_here = lax.dynamic_slice_in_dim(live_all, first_slot, slot_dev, 1)
    local_places = first_slot + jnp.arange(slot_dev, dtype=jnp.int32)
    masks = make_mask(local_places, docs_here[0], live_here[0], places, docs_all[0], live_all[0])
    stream = tokens.astype(jnp.float32)
    norms = lax.all_gather(
        jnp.concatenate([gains.reshape(4, -1), biases.reshape(4, -1)], 0), ("rows", "kv"), axis=1, tiled=True
    )
    weights = gather_weights([w[number] for number in range(LAYERS) for w in (w_qkv, w_out, w_up, w_down)])
    gathered = [
        tuple(weights[4 * number : 4 * number + 4]) + (norms[2 * number : 2 * number + 2], norms[4 + 2 * number : 6 + 2 * number])
        for number in range(LAYERS)
    ]
    stored = []
    for number in range(LAYERS):
        signed = number == 0
        pieces = gathered[number]
        full_qkv, full_out, full_up, full_down, gain_pair, bias_pair = pieces
        gain_pair = gain_pair.astype(jnp.float32)
        bias_pair = bias_pair.astype(jnp.float32)
        normed_in = norm_rows(stream, gain_pair[0], bias_pair[0]).astype(jnp.bfloat16)
        projected = jnp.dot(normed_in, full_qkv, preferred_element_type=jnp.float32).astype(
            jnp.bfloat16
        )
        kv_all = lax.all_gather(projected[:, :, model_width:], "kv", axis=1, tiled=True)
        attended = jnp.stack(
            [
                attend_row(
                    projected[0, :, :model_width], kv_all[0], masks, live_here[0], signed, scaling
                )
            ]
        )
        shared = kv_all
        middle = stream + jnp.dot(attended, full_out, preferred_element_type=jnp.float32)
        normed_mid = norm_rows(middle, gain_pair[1], bias_pair[1]).astype(jnp.bfloat16)
        pre_act = jnp.dot(normed_mid, full_up, preferred_element_type=jnp.float32)
        activated = jax.nn.gelu(pre_act).astype(jnp.bfloat16)
        stored.append(
            (
                stream,
                normed_in,
                projected,
                shared,
                attended,
                middle,
                normed_mid,
                pre_act,
                activated,
                pieces,
            )
        )
        stream = middle + jnp.dot(activated, full_down, preferred_element_type=jnp.float32)
    result = (stream * live_here[..., None]).astype(jnp.bfloat16)
    residual_grad = cotangent.astype(jnp.float32) * live_here[..., None]
    collected = [None] * LAYERS
    norm_grads = [None] * LAYERS
    for number in reversed(range(LAYERS)):
        signed = number == 0
        (
            stream_in,
            normed_in,
            projected,
            shared,
            attended,
            middle,
            normed_mid,
            pre_act,
            activated,
            kept,
        ) = stored[number]
        pieces = gathered[number]
        full_qkv, full_out, full_up, full_down, gain_pair, bias_pair = pieces
        gain_pair = gain_pair.astype(jnp.float32)
        bias_pair = bias_pair.astype(jnp.float32)
        down_in = residual_grad.astype(jnp.bfloat16)
        act_grad = jnp.einsum("rtd,fd->rtf", down_in, full_down, preferred_element_type=jnp.float32)
        unused, gelu_pull = jax.vjp(jax.nn.gelu, pre_act)
        pre_grad = gelu_pull(act_grad)[0].astype(jnp.bfloat16)
        mid_normed_grad = jnp.einsum(
            "rtf,df->rtd", pre_grad, full_up, preferred_element_type=jnp.float32
        )
        unused, norm_pull = jax.vjp(norm_rows, middle, gain_pair[1], bias_pair[1])
        middle_part, gain_late, bias_late = norm_pull(mid_normed_grad)
        middle_grad = residual_grad + middle_part
        branch_grad = middle_grad.astype(jnp.bfloat16)
        att_grad = jnp.einsum(
            "rte,de->rtd", branch_grad, full_out, preferred_element_type=jnp.float32
        ).astype(jnp.bfloat16)
        kv_all = shared
        query_grad, kv_grad = attend_back(
            projected[0, :, :model_width],
            kv_all[0],
            att_grad[0],
            masks,
            live_here[0],
            signed,
            scaling,
        )
        query_grads = [query_grad]
        kv_grads = [kv_grad]
        kv_here = lax.psum_scatter(
            jnp.stack(kv_grads).astype(jnp.bfloat16), "kv", scatter_dimension=1, tiled=True
        ).astype(jnp.float32)
        qkv_grad = jnp.concatenate([jnp.stack(query_grads), kv_here], -1).astype(jnp.bfloat16)
        in_normed_grad = jnp.einsum(
            "rte,de->rtd", qkv_grad, full_qkv, preferred_element_type=jnp.float32
        )
        unused, first_pull = jax.vjp(norm_rows, stream_in, gain_pair[0], bias_pair[0])
        stream_part, gain_early, bias_early = first_pull(in_normed_grad)
        residual_grad = middle_grad + stream_part
        pairs = [
            (normed_in, qkv_grad),
            (attended, branch_grad),
            (normed_mid, pre_grad),
            (activated, down_in),
        ]
        terms = [
            jnp.einsum("ti,to->io", left[0], right[0], preferred_element_type=F32).astype(BF16)
            for left, right in pairs
        ]
        collected[number] = scatter_grads(terms)
        norm_grads[number] = [gain_early, gain_late, bias_early, bias_late]
    norm_sums = lax.psum_scatter(
        jnp.stack([norm_grads[n][i] for n in range(LAYERS) for i in range(4)]), ("rows", "kv"), scatter_dimension=1, tiled=True
    ).reshape(LAYERS, 4, -1)
    return (
        result,
        residual_grad,
    ) + tuple(jnp.stack([collected[number][i] for number in range(LAYERS)]) for i in range(4)) + (
        norm_sums[:, :2], norm_sums[:, 2], norm_sums[:, 3]
    )


def solution(mesh):
    in_specs = (
        P("rows", "kv", None),
        P("rows", None),
        P(None, ("rows", "kv"), None),
        P(None, ("rows", "kv"), None),
        P(None, ("rows", "kv"), None),
        P(None, ("rows", "kv"), None),
        P(None, None, ("rows", "kv")),
        P(None, None, ("rows", "kv")),
        P("rows", "kv", None),
    )
    out_specs = (
        P("rows", "kv", None),
        P("rows", "kv", None),
        P(None, ("rows", "kv"), None),
        P(None, ("rows", "kv"), None),
        P(None, ("rows", "kv"), None),
        P(None, ("rows", "kv"), None),
        P(None, None, ("rows", "kv")),
        P(None, ("rows", "kv")),
        P(None, ("rows", "kv")),
    )
    fast = dict(mesh.shape) == {"rows": 8, "kv": 4}
    return jax.shard_map(local_fast if fast else local_generic, mesh=mesh, in_specs=in_specs, out_specs=out_specs, check_vma=False)
```

```python
import math

import jax
import jax.numpy as jnp
from jax import lax
from jax.experimental import pallas as pl
from jax.experimental.pallas import tpu as pltpu
from jax.sharding import PartitionSpec as P

HEADS = 12
HEAD = 64
LAYERS = 2


EPSILON = 1e-05


def norm_rows(stream, gain, bias):
    center = stream - jnp.mean(stream, -1, keepdims=True)
    spread = jnp.mean(center * center, -1, keepdims=True)
    return center * lax.rsqrt(spread + EPSILON) * gain + bias


def normalise(scores, allowed, query_live, signed):
    if signed:
        magnitude = jnp.sqrt(scores * scores + 1.0)
        ceiling = jnp.max(jnp.where(allowed > 0, magnitude, 0.0), -1, keepdims=True)
        shifted = jnp.where(allowed > 0, magnitude - ceiling, -60.0)
    else:
        ceiling = jnp.max(jnp.where(allowed > 0, scores, -10000.0), -1, keepdims=True)
        shifted = jnp.where(allowed > 0, scores - ceiling, -60.0)
    raised = jnp.exp(shifted) * allowed
    normaliser = jnp.sum(raised, -1, keepdims=True) + (1.0 - query_live)[None, :, None]
    unsigned_w = raised / normaliser
    if signed:
        return (jnp.tanh(scores) * unsigned_w, unsigned_w)
    return (unsigned_w, unsigned_w)


def make_mask(query_places, query_docs, query_live, key_places, key_docs, key_live):
    allowed = (
        (query_docs[:, None] == key_docs[None, :]) & (key_places[None, :] <= query_places[:, None])
    ).astype(jnp.float32)
    return allowed * query_live[:, None] * key_live[None, :]


def split_heads(query, keys_vals):
    model_width = query.shape[-1]
    slot_count = keys_vals.shape[0]
    query_heads = query.reshape(-1, HEADS, HEAD)
    key_heads = keys_vals[:, :model_width].reshape(slot_count, HEADS, HEAD)
    value_heads = keys_vals[:, model_width:].reshape(slot_count, HEADS, HEAD)
    return (query_heads, key_heads, value_heads)


def score_grads(scores, unsigned_w, weight_grad, inner_sum, signed):
    if signed:
        tanh_s = jnp.tanh(scores)
        magnitude = jnp.sqrt(scores * scores + 1.0)
        return unsigned_w * (
            (tanh_s * weight_grad - inner_sum) * scores / magnitude
            + weight_grad * (1.0 - tanh_s * tanh_s)
        )
    return unsigned_w * (weight_grad - inner_sum)


def attend_row(query, keys_vals, allowed, query_live, signed, scaling):
    query_heads, key_heads, value_heads = split_heads(query, keys_vals)
    scores = (
        jnp.einsum("qhd,khd->hqk", query_heads, key_heads, preferred_element_type=jnp.float32)
        * scaling
    )
    weights, unsigned_w = normalise(scores, allowed, query_live, signed)
    outcome = jnp.einsum(
        "hqk,khd->qhd",
        weights.astype(jnp.bfloat16),
        value_heads,
        preferred_element_type=jnp.float32,
    )
    return outcome.reshape(query.shape[0], query.shape[1]).astype(jnp.bfloat16)


def attend_back(query, keys_vals, grad_att, allowed, query_live, signed, scaling):
    query_heads, key_heads, value_heads = split_heads(query, keys_vals)
    slot_count = keys_vals.shape[0]
    model_width = query.shape[-1]
    scores = (
        jnp.einsum("qhd,khd->hqk", query_heads, key_heads, preferred_element_type=jnp.float32)
        * scaling
    )
    weights, unsigned_w = normalise(scores, allowed, query_live, signed)
    weights_low = weights.astype(jnp.bfloat16)
    grad_heads = grad_att.reshape(-1, HEADS, HEAD)
    weight_grad = jnp.einsum(
        "qhd,khd->hqk", grad_heads, value_heads, preferred_element_type=jnp.float32
    )
    inner_sum = jnp.sum(weight_grad * weights, -1, keepdims=True)
    score_low = score_grads(scores, unsigned_w, weight_grad, inner_sum, signed).astype(jnp.bfloat16)
    query_grad = (
        jnp.einsum("hqk,khd->qhd", score_low, key_heads, preferred_element_type=jnp.float32)
        * scaling
    )
    key_grad = (
        jnp.einsum("hqk,qhd->khd", score_low, query_heads, preferred_element_type=jnp.float32)
        * scaling
    )
    value_grad = jnp.einsum(
        "hqk,qhd->khd", weights_low, grad_heads, preferred_element_type=jnp.float32
    )
    kv_grad = jnp.concatenate(
        [key_grad.reshape(slot_count, model_width), value_grad.reshape(slot_count, model_width)], -1
    )
    return (query_grad.reshape(query.shape[0], model_width), kv_grad)


def reduce_grads(pairs, g_gain, g_bias):
    n_rows = lax.axis_size("rows")
    n_kv = lax.axis_size("kv")
    lefts = []
    rights = []
    for left_side, right_side in pairs:
        tok_count = left_side.shape[0] * left_side.shape[1]
        in_width = left_side.shape[-1]
        lefts.append(left_side.reshape(tok_count, n_rows, n_kv, in_width // (n_rows * n_kv)))
        rights.append(right_side.reshape(tok_count, right_side.shape[-1]))
    moved = (
        lax.all_to_all(lefts[0], "kv", split_axis=2, concat_axis=0, tiled=True),
        lax.all_to_all(lefts[1], "kv", split_axis=2, concat_axis=0, tiled=True),
        lax.all_to_all(lefts[2], "kv", split_axis=2, concat_axis=0, tiled=True),
        lax.all_to_all(lefts[3], "kv", split_axis=2, concat_axis=0, tiled=True),
    )
    whole = (
        lax.all_gather(rights[0], "kv", axis=0, tiled=True),
        lax.all_gather(rights[1], "kv", axis=0, tiled=True),
        lax.all_gather(rights[2], "kv", axis=0, tiled=True),
        lax.all_gather(rights[3], "kv", axis=0, tiled=True),
    )
    partial_sums = []
    for number in range(4):
        left_block = moved[number].reshape(moved[number].shape[0], -1)
        product = jnp.einsum(
            "ti,to->io", left_block, whole[number], preferred_element_type=jnp.float32
        )
        partial_sums.append(product.reshape(n_rows, -1, product.shape[-1]))
    reduced = (
        lax.psum_scatter(
            partial_sums[0].astype(jnp.bfloat16), "rows", scatter_dimension=0, tiled=True
        ).astype(jnp.float32),
        lax.psum_scatter(
            partial_sums[1].astype(jnp.bfloat16), "rows", scatter_dimension=0, tiled=True
        ).astype(jnp.float32),
        lax.psum_scatter(
            partial_sums[2].astype(jnp.bfloat16), "rows", scatter_dimension=0, tiled=True
        ).astype(jnp.float32),
        lax.psum_scatter(
            partial_sums[3].astype(jnp.bfloat16), "rows", scatter_dimension=0, tiled=True
        ).astype(jnp.float32),
    )
    norm_parts = (
        lax.psum_scatter(g_gain, ("rows", "kv"), scatter_dimension=1, tiled=True),
        lax.psum_scatter(g_bias, ("rows", "kv"), scatter_dimension=1, tiled=True),
    )
    results = tuple((piece.reshape(piece.shape[1], piece.shape[2]) for piece in reduced))
    return results + (norm_parts[0], norm_parts[1])


def local_generic(tokens, lengths, w_qkv, w_out, w_up, w_down, gains, biases, cotangent):
    rows_here, slot_dev, model_width = tokens.shape
    slot_count = slot_dev * lax.axis_size("kv")
    first_slot = lax.axis_index("kv") * slot_dev
    scaling = 1.0 / math.sqrt(HEAD)
    doc_ends = jnp.cumsum(lengths, -1)
    places = jnp.arange(slot_count, dtype=jnp.int32)
    docs_all = jnp.sum((doc_ends[:, None, :] <= places[None, :, None]).astype(jnp.int32), -1)
    live_all = (places[None, :] < doc_ends[:, -1:]).astype(jnp.float32)
    docs_here = lax.dynamic_slice_in_dim(docs_all, first_slot, slot_dev, 1)
    live_here = lax.dynamic_slice_in_dim(live_all, first_slot, slot_dev, 1)
    local_places = first_slot + jnp.arange(slot_dev, dtype=jnp.int32)
    masks = make_mask(local_places, docs_here[0], live_here[0], places, docs_all[0], live_all[0])
    stream = tokens.astype(jnp.float32)
    stored = []
    for number in range(LAYERS):
        signed = number == 0
        pieces = (
            lax.all_gather(w_qkv[number], ("rows", "kv"), axis=0, tiled=True),
            lax.all_gather(w_out[number], ("rows", "kv"), axis=0, tiled=True),
            lax.all_gather(w_up[number], ("rows", "kv"), axis=0, tiled=True),
            lax.all_gather(w_down[number], ("rows", "kv"), axis=0, tiled=True),
            lax.all_gather(gains[number], ("rows", "kv"), axis=1, tiled=True),
            lax.all_gather(biases[number], ("rows", "kv"), axis=1, tiled=True),
        )
        full_qkv, full_out, full_up, full_down, gain_pair, bias_pair = pieces
        gain_pair = gain_pair.astype(jnp.float32)
        bias_pair = bias_pair.astype(jnp.float32)
        normed_in = norm_rows(stream, gain_pair[0], bias_pair[0]).astype(jnp.bfloat16)
        projected = jnp.dot(normed_in, full_qkv, preferred_element_type=jnp.float32).astype(
            jnp.bfloat16
        )
        kv_all = lax.all_gather(projected[:, :, model_width:], "kv", axis=1, tiled=True)
        attended = jnp.stack(
            [
                attend_row(
                    projected[0, :, :model_width], kv_all[0], masks, live_here[0], signed, scaling
                )
            ]
        )
        shared = kv_all
        middle = stream + jnp.dot(attended, full_out, preferred_element_type=jnp.float32)
        normed_mid = norm_rows(middle, gain_pair[1], bias_pair[1]).astype(jnp.bfloat16)
        pre_act = jnp.dot(normed_mid, full_up, preferred_element_type=jnp.float32)
        activated = jax.nn.gelu(pre_act).astype(jnp.bfloat16)
        stored.append(
            (
                stream,
                normed_in,
                projected,
                shared,
                attended,
                middle,
                normed_mid,
                pre_act,
                activated,
                pieces,
            )
        )
        stream = middle + jnp.dot(activated, full_down, preferred_element_type=jnp.float32)
    result = (stream * live_here[..., None]).astype(jnp.bfloat16)
    residual_grad = cotangent.astype(jnp.float32) * live_here[..., None]
    collected = [None] * LAYERS
    for number in reversed(range(LAYERS)):
        signed = number == 0
        (
            stream_in,
            normed_in,
            projected,
            shared,
            attended,
            middle,
            normed_mid,
            pre_act,
            activated,
            kept,
        ) = stored[number]
        pieces = (
            lax.all_gather(w_qkv[number], ("rows", "kv"), axis=0, tiled=True),
            lax.all_gather(w_out[number], ("rows", "kv"), axis=0, tiled=True),
            lax.all_gather(w_up[number], ("rows", "kv"), axis=0, tiled=True),
            lax.all_gather(w_down[number], ("rows", "kv"), axis=0, tiled=True),
            lax.all_gather(gains[number], ("rows", "kv"), axis=1, tiled=True),
            lax.all_gather(biases[number], ("rows", "kv"), axis=1, tiled=True),
        )
        full_qkv, full_out, full_up, full_down, gain_pair, bias_pair = pieces
        gain_pair = gain_pair.astype(jnp.float32)
        bias_pair = bias_pair.astype(jnp.float32)
        down_in = residual_grad.astype(jnp.bfloat16)
        act_grad = jnp.einsum("rtd,fd->rtf", down_in, full_down, preferred_element_type=jnp.float32)
        unused, gelu_pull = jax.vjp(jax.nn.gelu, pre_act)
        pre_grad = gelu_pull(act_grad)[0].astype(jnp.bfloat16)
        mid_normed_grad = jnp.einsum(
            "rtf,df->rtd", pre_grad, full_up, preferred_element_type=jnp.float32
        )
        unused, norm_pull = jax.vjp(norm_rows, middle, gain_pair[1], bias_pair[1])
        middle_part, gain_late, bias_late = norm_pull(mid_normed_grad)
        middle_grad = residual_grad + middle_part
        branch_grad = middle_grad.astype(jnp.bfloat16)
        att_grad = jnp.einsum(
            "rte,de->rtd", branch_grad, full_out, preferred_element_type=jnp.float32
        ).astype(jnp.bfloat16)
        kv_all = shared
        query_grad, kv_grad = attend_back(
            projected[0, :, :model_width],
            kv_all[0],
            att_grad[0],
            masks,
            live_here[0],
            signed,
            scaling,
        )
        query_grads = [query_grad]
        kv_grads = [kv_grad]
        kv_here = lax.psum_scatter(
            jnp.stack(kv_grads).astype(jnp.bfloat16), "kv", scatter_dimension=1, tiled=True
        ).astype(jnp.float32)
        qkv_grad = jnp.concatenate([jnp.stack(query_grads), kv_here], -1).astype(jnp.bfloat16)
        in_normed_grad = jnp.einsum(
            "rte,de->rtd", qkv_grad, full_qkv, preferred_element_type=jnp.float32
        )
        unused, first_pull = jax.vjp(norm_rows, stream_in, gain_pair[0], bias_pair[0])
        stream_part, gain_early, bias_early = first_pull(in_normed_grad)
        residual_grad = middle_grad + stream_part
        g_gain = jnp.stack([gain_early, gain_late])
        g_bias = jnp.stack([bias_early, bias_late])
        pairs = [
            (normed_in, qkv_grad),
            (attended, branch_grad),
            (normed_mid, pre_grad),
            (activated, down_in),
        ]
        collected[number] = reduce_grads(pairs, g_gain, g_bias)
    grad_qkv = jnp.stack([collected[number][0] for number in range(LAYERS)])
    grad_out = jnp.stack([collected[number][1] for number in range(LAYERS)])
    grad_up = jnp.stack([collected[number][2] for number in range(LAYERS)])
    grad_down = jnp.stack([collected[number][3] for number in range(LAYERS)])
    grad_gains = jnp.stack([collected[number][4] for number in range(LAYERS)])
    grad_biases = jnp.stack([collected[number][5][0] for number in range(LAYERS)])
    grad_mid_biases = jnp.stack([collected[number][5][1] for number in range(LAYERS)])
    return (
        result,
        residual_grad,
        grad_qkv,
        grad_out,
        grad_up,
        grad_down,
        grad_gains,
        grad_biases,
        grad_mid_biases,
    )


F32 = jnp.float32
BF16 = jnp.bfloat16
MESH = pl.DeviceIdType.MESH
ZN = 4


def flip(value, unit):
    bit = lax.rem(lax.div(value, unit), 2)
    return value + unit - 2 * unit * bit


def places_of():
    r = lax.axis_index("rows")
    z = lax.axis_index("kv")
    return r, z, flip(r, 2), flip(r, 4), flip(flip(r, 2), 4), flip(r, 1)


def turn(z, k):
    return lax.rem(z + k, ZN)


def rcopy(src, dst, ssem, rsem, device):
    return pltpu.make_async_remote_copy(
        src_ref=src, dst_ref=dst, send_sem=ssem, recv_sem=rsem, device_id=device, device_id_type=MESH
    )


def band(start, size):
    return pl.ds(pl.multiple_of(start, 16), size)


def greet(peers):
    barrier = pltpu.get_barrier_semaphore()
    for peer in peers:
        pl.semaphore_signal(barrier, inc=1, device_id=peer, device_id_type=MESH)
    pl.semaphore_wait(barrier, len(peers))


def comm_peers():
    r, z, rx, ry, rd, rc = places_of()
    return [(r, turn(z, 1)), (r, turn(z, 2)), (r, turn(z, 3)), (rx, z), (ry, z), (rc, z)]


def col_step(width):
    return 256 if width % 256 == 0 else 128


class Gather:
    SEMS = 14

    def __init__(self, own, whole, zm, zt, ssem, rsem, base):
        self.own, self.whole, self.zm, self.zt = own, whole, zm, zt
        self.ssem, self.rsem, self.base = ssem, rsem, base
        self.split = zm is not None
        self.rows = whole.shape[0] // 8
        self.width = whole.shape[1]
        self.sent = []

    def _copy(self, src, dst, at, device):
        return rcopy(src, dst, self.ssem.at[self.base + at], self.rsem.at[self.base + at], device)

    def _block(self, r, half=None):
        if half is None:
            return self.whole.at[band(r * self.rows, self.rows), :]
        part = self.rows // 2
        return self.whole.at[band(r * self.rows + half * part, part), :]

    def _send(self, src, dst, at, device):
        copy = self._copy(src, dst, at, device)
        copy.start()
        self.sent.append(copy)

    def prepare(self):
        r, z = places_of()[:2]
        if self.split:
            half = self.width // 2
            own = self.own[...].astype(F32)
            self.zm[pl.ds(z, 1)] = own[:16].astype(BF16)[None]
            self.zt[pl.ds(z, 1)] = jnp.concatenate([own[16:, :half], own[16:, half:]], 0).astype(BF16)[None]
        else:
            part = self.rows // ZN
            self.whole[band(r * self.rows + z * part, part), :] = self.own[...]

    def _zrefs(self, z):
        if self.split:
            return [self.zm.at[z], self.zt.at[z]]
        part = self.rows // ZN
        return [self.whole.at[band(places_of()[0] * self.rows + z * part, part), :]]

    def send_z(self):
        r, z = places_of()[:2]
        for k in (1, 2, 3):
            for i, ref in enumerate(self._zrefs(z)):
                self._send(ref, ref, 2 * (k - 1) + i, (r, turn(z, k)))

    def wait_z(self):
        r, z = places_of()[:2]
        for k in (1, 2, 3):
            for i, ref in enumerate(self._zrefs(turn(z, ZN - k))):
                self._copy(ref, ref, 2 * (k - 1) + i, (r, turn(z, ZN - k))).wait_recv()
        if self.split:
            half = self.width // 2
            step = col_step(half)
            for side in (0, 1):
                def assemble(i, carry, side=side):
                    at = pl.multiple_of(i * step, step)
                    here = pl.ds(pl.multiple_of(side * half + i * step, 128), step)
                    parts = []
                    for piece in range(ZN):
                        parts.append(self.zm[piece, :, here].astype(F32))
                        parts.append(self.zt[piece, :, pl.ds(at, step)].astype(F32)[8 * side : 8 * side + 8])
                    self.whole[band(r * self.rows, self.rows), here] = jnp.concatenate(parts, 0).astype(BF16)
                    return carry
                lax.fori_loop(0, half // step, assemble, 0)

    def send_plane(self):
        r, z, rx, ry, rd, rc = places_of()
        own = self._block(r)
        self._send(own, own, 6, (rx, z))
        self._send(own, own, 7, (ry, z))
        self._send(own, own, 10, (rc, z))

    def forward(self):
        r, z, rx, ry, rd, rc = places_of()
        first, second = self._block(rx), self._block(ry)
        self._copy(first, first, 6, (rx, z)).wait_recv()
        part = self._block(rx, 0)
        self._send(part, part, 8, (ry, z))
        self._send(first, first, 11, (rc, z))
        self._copy(second, second, 7, (ry, z)).wait_recv()
        part = self._block(ry, 1)
        self._send(part, part, 9, (rx, z))
        self._send(second, second, 12, (rc, z))

    def forward_last(self):
        r, z, rx, ry, rd, rc = places_of()
        part = self._block(rd, 0)
        self._copy(part, part, 8, (ry, z)).wait_recv()
        part = self._block(rd, 1)
        self._copy(part, part, 9, (rx, z)).wait_recv()
        diagonal = self._block(rd)
        self._send(diagonal, diagonal, 13, (rc, z))

    def finish(self):
        r, z, rx, ry, rd, rc = places_of()
        for at, block in ((10, r), (11, rx), (12, ry), (13, rd)):
            ref = self._block(flip(block, 1))
            self._copy(ref, ref, at, (rc, z)).wait_recv()

    def drain(self):
        for copy in self.sent:
            copy.wait_send()


def add_rows(dst, src, rows):
    def step(i, carry):
        here = band(i * 16, 16)
        dst[here, :] = (dst[here, :].astype(F32) + src[here, :].astype(F32)).astype(BF16)
        return carry
    lax.fori_loop(0, rows // 16, step, 0)


GROUP = 640
TOK = 256
WIDE = 256


def dot(a, b):
    return jnp.dot(a, b, preferred_element_type=F32)


def dot_nt(a, b):
    return lax.dot_general(a, b, (((1,), (1,)), ((), ())), preferred_element_type=F32)


def dot_tn(a, b):
    return lax.dot_general(a, b, (((0,), (0,)), ((), ())), preferred_element_type=F32)


def loop(count, body):
    def step(i, carry):
        body(i)
        return carry
    lax.fori_loop(0, count, step, 0)


def cols(i, size):
    return pl.ds(pl.multiple_of(i * size, 128), size)


class Spot:
    def __init__(self):
        self.r, self.z, self.rx, self.ry, self.rd, self.rc = places_of()
        self.c = lax.rem(self.r, 2)
        self.member = 2 * self.c + lax.rem(self.z, 2)
        self.swaps = (self.c + lax.div(self.z, 2)) == 1
        self.partner = (self.rc, flip(self.z, 2))

    def mate(self, k):
        r = self.rc if k >= 2 else self.r
        z = flip(self.z, 1) if k % 2 else self.z
        return (r, z), 2 * lax.rem(r, 2) + lax.rem(z, 2)

    def device(self, member):
        return (self.r - self.c + lax.div(member, 2), self.z - lax.rem(self.z, 2) + lax.rem(member, 2))

    def peers(self):
        return comm_peers() + [(self.rc, flip(self.z, 1)), self.partner]


def swap(spot, src, dst, ssem, rsem):
    @pl.when(spot.swaps)
    def _():
        rcopy(src, dst, ssem, rsem, spot.partner).start()

    @pl.when(jnp.logical_not(spot.swaps))
    def _():
        pltpu.make_async_copy(src, dst, rsem).start()


def swap_wait(spot, src, dst, ssem, rsem):
    @pl.when(spot.swaps)
    def _():
        rcopy(src, dst, ssem, rsem, spot.partner).wait()

    @pl.when(jnp.logical_not(spot.swaps))
    def _():
        pltpu.make_async_copy(src, dst, rsem).wait()


def starts_of(lens, i):
    places = lax.broadcasted_iota(jnp.int32, (1, TOK), 1) + i * TOK
    end = jnp.zeros((1, 1), jnp.int32)
    start = jnp.zeros((1, TOK), jnp.int32)
    for n in range(4):
        end = end + lens[0:1, n : n + 1]
        start = jnp.maximum(start, jnp.where(end <= places, end, 0))
    live = places < end
    return places, jnp.where(live, start, 1 << 20), live


def live_column(lens, spot, rows, first):
    places = lax.broadcasted_iota(jnp.int32, (rows, 1), 0) + spot.member * TOK + first
    end = lens[0:1, 0:1] + lens[0:1, 1:2] + lens[0:1, 2:3] + lens[0:1, 3:4]
    return (places < end).astype(F32)


def centred(value):
    center = value - jnp.mean(value, -1, keepdims=True)
    spread = jnp.mean(center * center, -1, keepdims=True)
    return center * lax.rsqrt(spread + EPSILON)


CHUNK = 64


def allowed_rows(first, rows, places, start):
    keys = lax.broadcasted_iota(jnp.int32, (rows, TOK), 0) + first
    return (keys >= start) & (keys <= places)


def fold_rows(value, op):
    rows = value.shape[0]
    parts = [value[8 * n : 8 * n + 8] for n in range(rows // 8)]
    while len(parts) > 1:
        parts = [op(parts[n], parts[n + 1]) if n + 1 < len(parts) else parts[n] for n in range(0, len(parts), 2)]
    return parts[0]


def head_lanes(shape, h, offset):
    lanes = lax.broadcasted_iota(jnp.int32, shape, 1)
    return lax.div(lanes, HEAD) == h + offset


def ceiling_of(s_ref, count, places, start, signed):
    def step(n, top):
        here = pl.ds(pl.multiple_of(n * CHUNK, CHUNK), CHUNK)
        s = s_ref[here, :]
        value = s * s if signed else s
        value = jnp.where(allowed_rows(n * CHUNK, CHUNK, places, start), value, 0.0 if signed else -10000.0)
        return jnp.maximum(top, fold_rows(value, jnp.maximum))
    first = -1.0 if signed else -10000.0
    top = lax.fori_loop(0, count, step, jnp.full((8, TOK), first, F32))
    return jnp.max(top, 0, keepdims=True)


def attend_quarter(i, lens, qkv, vt, s_ref, p_ref, o_ref, signed):
    places, start, live = starts_of(lens, i)
    queries = qkv[i, :, 0:WIDE].astype(F32)
    keys_len = TOK * (i + 1)

    def head(h):
        mine = jnp.where(head_lanes((TOK, WIDE), h, 0), queries * 0.125, 0.0).astype(BF16)

        def score(j):
            s_ref[pl.ds(pl.multiple_of(j * TOK, TOK), TOK), :] = dot_nt(qkv[j, :, 384:640], mine)
        loop(i + 1, score)
        top = ceiling_of(s_ref, keys_len // CHUNK, places, start, signed)
        if signed:
            top = jnp.where(top < 0.0, 0.0, jnp.sqrt(jnp.maximum(top, 0.0) + 1.0))

        def weigh(n, total):
            here = pl.ds(pl.multiple_of(n * CHUNK, CHUNK), CHUNK)
            s = s_ref[here, :]
            okay = allowed_rows(n * CHUNK, CHUNK, places, start)
            if signed:
                shifted = jnp.sqrt(s * s + 1.0) - top
            else:
                shifted = s - top
            raised = jnp.where(okay, jnp.exp(jnp.where(okay, shifted, -60.0)), 0.0)
            weights = jnp.tanh(s) * raised if signed else raised
            p_ref[here, :] = weights.astype(BF16)
            return total + fold_rows(raised, jnp.add)
        total = lax.fori_loop(0, keys_len // CHUNK, weigh, jnp.zeros((8, TOK), F32))
        normaliser = jnp.sum(total, 0, keepdims=True) + (1.0 - live.astype(F32))
        outcome = dot(vt[pl.ds(pl.multiple_of(HEAD + HEAD * h, HEAD), HEAD), 0:keys_len], p_ref[0:keys_len, :])
        o_ref[i, pl.ds(pl.multiple_of(HEAD * h, HEAD), HEAD), :] = (outcome / normaliser).astype(BF16)
    loop(HEADS // 4, head)


class Keep:
    def __init__(self, src, dst, sem):
        self.copy = pltpu.make_async_copy(src, dst, sem)
        self.copy.start()
        self.open = True

    def wait(self):
        if self.open:
            self.copy.wait()
        self.open = False


class Pump:
    def __init__(self, jobs):
        self.steps = []
        self.done = set()
        count = len(jobs)
        ahead = 2

        def zstep(n):
            def run():
                jobs[n].wait_z()
                jobs[n].send_plane()
                if n + ahead < count:
                    jobs[n + ahead].send_z()
            return run
        for n in range(count + 2):
            if n < count:
                self.steps.append((("z", n), zstep(n)))
            if 0 <= n - 1 < count:
                self.steps.append((("f", n - 1), jobs[n - 1].forward))
            if 0 <= n - 2 < count:
                self.steps.append((("l", n - 2), jobs[n - 2].forward_last))
        self.jobs = jobs

    def __call__(self, n=1):
        for _ in range(n):
            if self.steps:
                name, run = self.steps.pop(0)
                run()
                self.done.add(name)

    def need(self, n):
        while ("l", n) not in self.done:
            self()
        self.jobs[n].finish()


STASH = ("stream", "qkv", "middle", "nin_t", "att_t", "nmid_t", "pre", "act_t")


def stash_shapes(d, ff):
    return [
        ((TOK, d), F32),
        ((4, TOK, GROUP), BF16),
        ((TOK, d), F32),
        ((d, TOK), BF16),
        ((d, TOK), BF16),
        ((d, TOK), BF16),
        ((TOK, ff), F32),
        ((ff, TOK), BF16),
    ]


def forward_kernel(*refs):
    refs = list(refs)
    take = lambda n: [refs.pop(0) for _ in range(n)]
    tok, cot, lens_in = take(3)
    owns = take(8)
    result_o, cot_o, lens_o, norms_o = take(4)
    whole_o = take(8)
    stash_o = [take(8), take(8)]
    wholes = take(8)
    zbuf = [(None, None) if n % 4 == 3 else tuple(take(2)) for n in range(8)]
    tok_v, lens_v, stream, normed, qkv_s, qkv0, qkv1, vt, s_ref, p_ref, o_ref, att0, att1, pre, act, act_t, nt_in, nt_mid, middle, res = take(20)
    ssem, rsem, osem, stsem, qs, qr, os_, or_, ms, mr = take(10)
    spot = Spot()
    greet(spot.peers())
    jobs = [Gather(owns[n], wholes[n], zbuf[n][0], zbuf[n][1], ssem, rsem, n * Gather.SEMS) for n in range(8)]
    jobs[0].prepare()
    jobs[0].send_z()
    swap(spot, tok, tok_v, ms.at[0], mr.at[0])
    swap(spot, lens_in, lens_v, ms.at[1], mr.at[1])
    for job in jobs[1:]:
        job.prepare()
    jobs[1].send_z()
    swap(spot, cot, cot_o, ms.at[2], mr.at[2])
    pump = Pump(jobs)
    stores = []

    def keep(src, dst, sem):
        stores.append(Keep(src, dst, sem))
        return stores[-1]

    swap_wait(spot, tok, tok_v, ms.at[0], mr.at[0])
    swap_wait(spot, lens_in, lens_v, ms.at[1], mr.at[1])
    lens_o[...] = lens_v[...]
    pump(2)

    def widen(n):
        here = band(n * CHUNK, CHUNK)
        stream[here, :] = tok_v[here, :].astype(F32)
    loop(TOK // CHUNK, widen)

    stream_store = keep(stream, stash_o[0][0], stsem.at[0])
    previous = None
    for layer in range(LAYERS):
        w_qkv, w_out, w_up, w_down = wholes[4 * layer : 4 * layer + 4]
        qkv = (qkv0, qkv1)[layer]
        att = (att0, att1)[layer]
        out = stash_o[layer]
        base = 8 * layer
        signed = layer == 0
        pump.need(4 * layer)
        keep(w_qkv, whole_o[4 * layer], osem.at[4 * layer])
        edge = w_qkv[:, 512:640].astype(F32).T
        norms_o[layer] = edge[HEAD : HEAD + 8]
        if previous:
            previous[3].wait()

        def first_norm(n):
            here = band(n * CHUNK, CHUNK)
            value = centred(stream[here, :]) * norms_o[layer, 0:1, :] + norms_o[layer, 1:2, :]
            normed[here, :] = value.astype(BF16)
        loop(TOK // CHUNK, first_norm)
        for k in (1, 3, 2, 0):
            mate, member = spot.mate(k)
            group = dot(normed[...], w_qkv[:, pl.ds(pl.multiple_of(member * GROUP, 128), GROUP)]).astype(BF16)
            if k:
                qkv_s[layer, k - 1] = group
                rcopy(qkv_s.at[layer, k - 1], qkv.at[spot.member], qs.at[4 * layer + k], qr.at[4 * layer + k], mate).start()
            else:
                qkv[pl.ds(spot.member, 1)] = group[None]
        nt_in[...] = normed[...].astype(F32).T.astype(BF16)
        kept = [None] * 8
        kept[3] = keep(nt_in, out[3], stsem.at[base + 3])
        pump(2)
        for k in (1, 3, 2):
            mate, member = spot.mate(k)
            rcopy(qkv_s.at[layer, k - 1], qkv.at[member], qs.at[4 * layer + k], qr.at[4 * layer + k], mate).wait_recv()
        kept[1] = keep(qkv, out[1], stsem.at[base + 1])

        def turn_values(j):
            vt[:, cols(j, TOK)] = qkv[j, :, 128:384].astype(F32).T.astype(BF16)
        loop(4, turn_values)
        for i in range(4):
            attend_quarter(i, lens_v, qkv, vt, s_ref, p_ref, o_ref.at[layer], signed)

            @pl.when(spot.member != i)
            def _():
                rcopy(
                    o_ref.at[layer, i],
                    att.at[band(spot.member * 192, 192), :],
                    os_.at[4 * layer + i],
                    or_.at[4 * layer + spot.member],
                    spot.device(i),
                ).start()

            @pl.when(spot.member == i)
            def _():
                att[i * 192 : (i + 1) * 192, :] = o_ref[layer, i]
            pump(1)
        pump.need(4 * layer + 1)
        keep(w_out, whole_o[4 * layer + 1], osem.at[4 * layer + 1])
        for i in range(4):
            @pl.when(spot.member != i)
            def _():
                ref = att.at[i * 192 : (i + 1) * 192, :]
                rcopy(ref, ref, os_.at[4 * layer + i], or_.at[4 * layer + i], spot.device(i)).wait_recv()
        kept[4] = keep(att, out[4], stsem.at[base + 4])
        if previous:
            previous[2].wait()
        middle[...] = stream[...] + dot_tn(att[...], w_out[...])
        kept[2] = keep(middle, out[2], stsem.at[base + 2])
        if previous:
            previous[5].wait()

        def second_norm(n):
            here = band(n * CHUNK, CHUNK)
            value = centred(middle[here, :]) * norms_o[layer, 2:3, :] + norms_o[layer, 3:4, :]
            normed[here, :] = value.astype(BF16)
        loop(TOK // CHUNK, second_norm)
        nt_mid[...] = normed[...].astype(F32).T.astype(BF16)
        kept[5] = keep(nt_mid, out[5], stsem.at[base + 5])
        pump.need(4 * layer + 2)
        keep(w_up, whole_o[4 * layer + 2], osem.at[4 * layer + 2])
        if previous:
            previous[6].wait()
            previous[7].wait()
        tile = 512

        def up(n):
            value = dot(normed[...], w_up[:, cols(n, tile)])
            pre[:, cols(n, tile)] = value
            active = jax.nn.gelu(value)
            act[:, cols(n, tile)] = active.astype(BF16)
            act_t[pl.ds(pl.multiple_of(n * tile, tile), tile), :] = active.T.astype(BF16)
        loop(w_up.shape[1] // tile, up)
        kept[6] = keep(pre, out[6], stsem.at[base + 6])
        kept[7] = keep(act_t, out[7], stsem.at[base + 7])
        pump(1)
        pump.need(4 * layer + 3)
        keep(w_down, whole_o[4 * layer + 3], osem.at[4 * layer + 3])
        if previous:
            previous[0].wait()
        else:
            stream_store.wait()

        def down(n):
            here = cols(n, 256)
            stream[:, here] = middle[:, here] + dot(act[...], w_down[:, here])
        loop(3, down)
        if layer == 0:
            kept[0] = keep(stream, stash_o[1][0], stsem.at[8])
        previous = kept

    def last(n):
        here = band(n * CHUNK, CHUNK)
        res[here, :] = (stream[here, :] * live_column(lens_v, spot, CHUNK, n * CHUNK)).astype(BF16)
    loop(TOK // CHUNK, last)
    swap(spot, res, result_o, ms.at[3], mr.at[3])
    for job in jobs:
        job.drain()
    for layer in range(LAYERS):
        qkv = (qkv0, qkv1)[layer]
        att = (att0, att1)[layer]
        for k in (1, 3, 2):
            mate, member = spot.mate(k)
            rcopy(qkv_s.at[layer, k - 1], qkv.at[spot.member], qs.at[4 * layer + k], qr.at[4 * layer + k], mate).wait_send()
        for i in range(4):
            @pl.when(spot.member != i)
            def _():
                rcopy(
                    o_ref.at[layer, i],
                    att.at[band(spot.member * 192, 192), :],
                    os_.at[4 * layer + i],
                    or_.at[4 * layer + spot.member],
                    spot.device(i),
                ).wait_send()
    for store in stores:
        store.wait()
    swap_wait(spot, cot, cot_o, ms.at[2], mr.at[2])
    swap_wait(spot, res, result_o, ms.at[3], mr.at[3])


def forward_call(tok, cot, lens, owns):
    d, ff = tok.shape[1], owns[2].shape[1]
    shapes = [(own.shape[0] * 32, own.shape[1]) for own in owns]
    zshapes = []
    for n, own in enumerate(owns):
        if n % 4 != 3:
            zshapes += [pltpu.VMEM((ZN, 16, own.shape[1]), BF16), pltpu.VMEM((ZN, 16, own.shape[1] // 2), BF16)]
    any_space = pl.BlockSpec(memory_space=pl.ANY)
    vmem = pl.BlockSpec(memory_space=pltpu.VMEM)
    stash = [jax.ShapeDtypeStruct(shape, kind) for shape, kind in stash_shapes(d, ff)]
    dma = lambda n: pltpu.SemaphoreType.DMA((n,))
    outs = pl.pallas_call(
        forward_kernel,
        out_shape=[
            jax.ShapeDtypeStruct((TOK, d), BF16),
            jax.ShapeDtypeStruct((TOK, d), BF16),
            jax.ShapeDtypeStruct((8, 128), jnp.int32),
            jax.ShapeDtypeStruct((LAYERS, 8, d), F32),
        ]
        + [jax.ShapeDtypeStruct(shape, BF16) for shape in shapes]
        + stash
        + stash,
        in_specs=[any_space, any_space] + [vmem] * 9,
        out_specs=[any_space, any_space, vmem, vmem] + [any_space] * 24,
        scratch_shapes=[pltpu.VMEM(shape, BF16) for shape in shapes]
        + zshapes
        + [
            pltpu.VMEM((TOK, d), BF16),
            pltpu.VMEM((8, 128), jnp.int32),
            pltpu.VMEM((TOK, d), F32),
            pltpu.VMEM((TOK, d), BF16),
            pltpu.VMEM((LAYERS, 3, TOK, GROUP), BF16),
            pltpu.VMEM((4, TOK, GROUP), BF16),
            pltpu.VMEM((4, TOK, GROUP), BF16),
            pltpu.VMEM((WIDE, 4 * TOK), BF16),
            pltpu.VMEM((4 * TOK, TOK), F32),
            pltpu.VMEM((4 * TOK, TOK), BF16),
            pltpu.VMEM((LAYERS, 4, 192, TOK), BF16),
            pltpu.VMEM((d, TOK), BF16),
            pltpu.VMEM((d, TOK), BF16),
            pltpu.VMEM((TOK, ff), F32),
            pltpu.VMEM((TOK, ff), BF16),
            pltpu.VMEM((ff, TOK), BF16),
            pltpu.VMEM((d, TOK), BF16),
            pltpu.VMEM((d, TOK), BF16),
            pltpu.VMEM((TOK, d), F32),
            pltpu.VMEM((TOK, d), BF16),
        ]
        + [dma(8 * Gather.SEMS), dma(8 * Gather.SEMS), dma(8), dma(16), dma(8), dma(8), dma(8), dma(8), dma(4), dma(4)],
        compiler_params=pltpu.CompilerParams(collective_id=0, has_side_effects=True, vmem_limit_bytes=62 * 2**20),
    )(tok, cot, lens, *owns)
    return outs[:4], outs[4:12], (outs[12:20], outs[20:28])


class Reduce:
    SEMS = 14

    def __init__(self, send, got, half, near, zs, zr, out, ssem, rsem, base):
        self.send, self.got, self.half, self.near = send, got, half, near
        self.zs, self.zr, self.out = zs, zr, out
        self.ssem, self.rsem, self.base = ssem, rsem, base
        self.rows, self.width = got.shape[1], got.shape[2]
        self.split = len(zs) == 2
        self.sent = []
        self.core_sent = []

    def _copy(self, src, dst, at, device):
        return rcopy(src, dst, self.ssem.at[self.base + at], self.rsem.at[self.base + at], device)

    def _send(self, src, dst, at, device):
        copy = self._copy(src, dst, at, device)
        copy.start()
        self.sent.append(copy)

    def send_core(self):
        r, z, rx, ry, rd, rc = places_of()
        for b in range(4):
            copy = self._copy(self.send.at[b, :, pl.ds(0, self.width)], self.got.at[b], b, (rc, z))
            copy.start()
            self.core_sent.append(copy)

    def free_send(self):
        for copy in self.core_sent:
            copy.wait_send()
        self.core_sent = []

    def wait_core(self):
        r, z, rx, ry, rd, rc = places_of()
        for b in range(4):
            self._copy(self.got.at[b], self.got.at[b], b, (rc, z)).wait_recv()

    def send_diagonal(self):
        r, z, rx, ry, rd, rc = places_of()
        part = self.rows // 2
        diagonal = lax.div(rd, 2)
        self._send(self.got.at[diagonal, pl.ds(0, part)], self.half.at[0], 4, (ry, z))
        self._send(self.got.at[diagonal, pl.ds(part, part)], self.half.at[1], 5, (rx, z))

    def send_near(self):
        r, z, rx, ry, rd, rc = places_of()
        part = self.rows // 2
        for at, side, other in ((4, ry, rx), (5, rx, ry)):
            i = at - 4
            self._copy(self.half.at[i], self.half.at[i], at, (side, z)).wait_recv()
            block = self.got.at[lax.div(other, 2)]
            add_rows(block.at[pl.ds(i * part, part)], self.half.at[i], part)
            self._send(block, self.near.at[i], 6 + i, (other, z))

    def send_z(self):
        r, z, rx, ry, rd, rc = places_of()
        for i, side in ((0, rx), (1, ry)):
            self._copy(self.near.at[i], self.near.at[i], 6 + i, (side, z)).wait_recv()
        own = self.got.at[lax.div(r, 2)]
        near = self.near

        def total(rows, here):
            return own[rows, here].astype(F32) + near[0, rows, here].astype(F32) + near[1, rows, here].astype(F32)

        if self.split:
            half = self.width // 2
            step = col_step(half)

            def cut(i):
                at = pl.ds(pl.multiple_of(i * step, 128), step)
                sums = [
                    total(slice(None), pl.ds(pl.multiple_of(side * half + i * step, 128), step)) for side in (0, 1)
                ]
                for piece in range(ZN):
                    for side in (0, 1):
                        here = pl.ds(pl.multiple_of(side * half + i * step, 128), step)
                        self.zs[0][piece, :, here] = sums[side][24 * piece : 24 * piece + 16].astype(BF16)
                    self.zs[1][piece, :, at] = jnp.concatenate(
                        [sums[side][24 * piece + 16 : 24 * piece + 24] for side in (0, 1)], 0
                    ).astype(BF16)
            loop(half // step, cut)
        else:
            part = self.rows // ZN
            for piece in range(ZN):
                def cut_rows(i, piece=piece):
                    self.zs[0][piece, band(i * 16, 16), :] = total(band(piece * part + i * 16, 16), slice(None)).astype(BF16)
                loop(part // 16, cut_rows)
        for k in (1, 2, 3):
            for i in range(len(self.zs)):
                self._send(self.zs[i].at[turn(z, k)], self.zr[i].at[k - 1], 8 + 2 * (k - 1) + i, (r, turn(z, k)))

    def finish(self):
        r, z = places_of()[:2]
        for k in (1, 2, 3):
            for i in range(len(self.zs)):
                ref = self.zr[i].at[k - 1]
                self._copy(ref, ref, 8 + 2 * (k - 1) + i, (r, turn(z, ZN - k))).wait_recv()
        if self.split:
            half = self.width // 2
            main = self.zs[0][z].astype(F32)
            tail = self.zs[1][z].astype(F32)
            for k in range(3):
                main = main + self.zr[0][k].astype(F32)
                tail = tail + self.zr[1][k].astype(F32)
            self.out[pl.ds(0, 16), :] = main
            self.out[pl.ds(16, 8), pl.ds(0, half)] = tail[:8]
            self.out[pl.ds(16, 8), pl.ds(half, half)] = tail[8:]
        else:
            def total(i):
                here = band(i * 16, 16)
                value = self.zs[0][z, here, :].astype(F32)
                for k in range(3):
                    value = value + self.zr[0][k, here, :].astype(F32)
                self.out[here, :] = value
            loop(self.out.shape[0] // 16, total)

    def drain(self):
        self.free_send()
        for copy in self.sent:
            copy.wait_send()
        self.sent = []


class Line:
    def __init__(self):
        self.queue = []

    def add(self, steps):
        self.queue.append(list(steps))

    def __call__(self, n=1):
        for _ in range(n):
            if self.queue:
                steps = self.queue.pop(0)
                steps.pop(0)()
                if steps:
                    self.queue.append(steps)

    def flush(self):
        while self.queue:
            self()


def left_rows(left, c):
    return jnp.concatenate([left[band((2 * b + c) * 96, 96), :] for b in range(4)], 0)


def norm_back(source, upstream, gain, add, out, low, sums):
    sums[...] = jnp.zeros_like(sums)

    def step(n):
        here = band(n * CHUNK, CHUNK)
        value = source[here, :]
        center = value - jnp.mean(value, -1, keepdims=True)
        scale = lax.rsqrt(jnp.mean(center * center, -1, keepdims=True) + EPSILON)
        normal = center * scale
        up = upstream[here, :]
        sums[0:8, :] += fold_rows(up * normal, jnp.add)
        sums[8:16, :] += fold_rows(up, jnp.add)
        up = up * gain
        inner = up - jnp.mean(up, -1, keepdims=True) - normal * jnp.mean(up * normal, -1, keepdims=True)
        total = add[here, :] + inner * scale
        out[here, :] = total
        low[here, :] = total.astype(BF16)
    loop(TOK // CHUNK, step)
    gain_grad = jnp.sum(sums[0:8, :], 0, keepdims=True)
    bias_grad = jnp.sum(sums[8:16, :], 0, keepdims=True)
    return gain_grad, bias_grad


def gelu_slope(x):
    root = 0.7978845608028654
    square = x * x
    bend = jnp.tanh(root * (x + 0.044715 * x * square))
    return 0.5 * (1.0 + bend) + 0.5 * x * (1.0 - bend * bend) * root * (1.0 + 3 * 0.044715 * square)


def attend_quarter_back(i, lens, qkv, kt, datt, scratch, signed):
    s_ref, dp_ref, e_ref, t_ref, p_ref, ds_ref, dk, dv, dq = scratch
    places, start, live = starts_of(lens, i)
    queries = qkv[i, :, 0:WIDE].astype(F32)
    keys_len = TOK * (i + 1)
    grads_t = jnp.concatenate([jnp.zeros((HEAD, TOK), F32), datt[i].astype(F32)], 0)
    grads = grads_t.T
    rows = lax.div(lax.broadcasted_iota(jnp.int32, (WIDE, TOK), 0), HEAD)

    def head(h):
        mine = jnp.where(head_lanes((TOK, WIDE), h, 0), queries * 0.125, 0.0).astype(BF16)
        out_t = jnp.where(rows == h + 1, grads_t, 0.0).astype(BF16)
        out = jnp.where(head_lanes((TOK, WIDE), h, 1), grads, 0.0).astype(BF16)

        def score(j):
            here = pl.ds(pl.multiple_of(j * TOK, TOK), TOK)
            s_ref[here, :] = dot_nt(qkv[j, :, 384:640], mine)
            dp_ref[here, :] = dot(qkv[j, :, 128:384], out_t)
        loop(i + 1, score)
        top = ceiling_of(s_ref, keys_len // CHUNK, places, start, signed)
        if signed:
            top = jnp.where(top < 0.0, 0.0, jnp.sqrt(jnp.maximum(top, 0.0) + 1.0))

        def weigh(n, sums):
            here = pl.ds(pl.multiple_of(n * CHUNK, CHUNK), CHUNK)
            s = s_ref[here, :]
            dp = dp_ref[here, :]
            okay = allowed_rows(n * CHUNK, CHUNK, places, start)
            if signed:
                square = s * s + 1.0
                back = lax.rsqrt(square)
                shifted = square * back - top
            else:
                shifted = s - top
            raised = jnp.where(okay, jnp.exp(jnp.where(okay, shifted, -60.0)), 0.0)
            e_ref[here, :] = raised
            weights = raised
            if signed:
                bend = jnp.tanh(s)
                t_ref[here, :] = bend
                s_ref[here, :] = s * back
                weights = bend * raised
            return sums[0] + fold_rows(raised, jnp.add), sums[1] + fold_rows(dp * weights, jnp.add)
        zero = jnp.zeros((8, TOK), F32)
        sums = lax.fori_loop(0, keys_len // CHUNK, weigh, (zero, zero))
        inverse = 1.0 / (jnp.sum(sums[0], 0, keepdims=True) + (1.0 - live.astype(F32)))
        inner = jnp.sum(sums[1], 0, keepdims=True) * inverse

        def slope(n):
            here = pl.ds(pl.multiple_of(n * CHUNK, CHUNK), CHUNK)
            dp = dp_ref[here, :]
            unsigned = e_ref[here, :] * inverse
            if signed:
                bend = t_ref[here, :]
                p_ref[here, :] = (unsigned * bend).astype(BF16)
                grad = unsigned * ((bend * dp - inner) * s_ref[here, :] + dp * (1.0 - bend * bend))
            else:
                p_ref[here, :] = unsigned.astype(BF16)
                grad = unsigned * (dp - inner)
            ds_ref[here, :] = grad.astype(BF16)
        loop(keys_len // CHUNK, slope)

        def spread(j):
            here = pl.ds(pl.multiple_of(j * TOK, TOK), TOK)
            dv[here, :] += dot(p_ref[here, :], out)
            dk[here, :] += dot(ds_ref[here, :], mine)
        loop(i + 1, spread)
        dq[pl.ds(pl.multiple_of(HEAD * h, HEAD), HEAD), :] = 0.125 * dot(
            kt[pl.ds(pl.multiple_of(HEAD * h, HEAD), HEAD), 0:keys_len], ds_ref[0:keys_len, :]
        )
    loop(HEADS // 4, head)
    query_grad = jnp.concatenate([dq[...], jnp.zeros((HEAD, TOK), F32)], 0).T
    value_grad = dv[i * TOK : (i + 1) * TOK, :]
    key_grad = dk[i * TOK : (i + 1) * TOK, :]
    lanes = lax.broadcasted_iota(jnp.int32, (TOK, 128), 1)
    return jnp.concatenate(
        [
            query_grad[:, :128],
            jnp.where(lanes < HEAD, query_grad[:, 128:], value_grad[:, :128]),
            value_grad[:, 128:],
            key_grad,
        ],
        1,
    ).astype(BF16)


def backward_kernel(*refs):
    refs = list(refs)
    take = lambda n: [refs.pop(0) for _ in range(n)]
    cot, lens, norms = take(3)
    wholes = take(8)
    stash = [take(8), take(8)]
    (input_o,) = take(1)
    grads_o = take(8)
    w_qkv, w_out, w_up, w_down = take(4)
    stream, qkv, middle, nin_t, att_t, nmid_t, pre, act_t = take(8)
    cot_v, grad, low, branch, dpre, dmid, sums, edge, datt_s, datt_r, kt = take(11)
    scratch = take(9)
    dk, dv = scratch[6], scratch[7]
    dq_s, dq_r, big, small, tall, final_r = take(6)
    buffers = []
    for n in range(4):
        got, half, near = take(3)
        count = 1 if n == 3 else 2
        buffers.append((got, half, near, take(count), take(count)))
    ssem, rsem, lsem, csem, as_, ar, ds_, dr, ms, mr = take(10)
    spot = Spot()
    r, z, rx, ry, rd, rc = spot.r, spot.z, spot.rx, spot.ry, spot.rd, spot.rc
    sources = dict(zip(STASH, range(8)))
    homes = dict(zip(STASH, (stream, qkv, middle, nin_t, att_t, nmid_t, pre, act_t)))
    loads = {}

    def load(layer, *names):
        for name in names:
            if name in homes:
                src, dst, at = stash[layer][sources[name]], homes[name], sources[name]
            else:
                at = ("w_qkv", "w_out", "w_up", "w_down").index(name)
                src, dst = wholes[4 * layer + at], (w_qkv, w_out, w_up, w_down)[at]
                at = 8 + at
            loads[(layer, name)] = Keep(src, dst, lsem.at[12 * layer + at])

    def ready(layer, *names):
        for name in names:
            loads[(layer, name)].wait()

    start = Keep(cot, cot_v, lsem.at[24])
    load(1, "act_t", "w_down", "pre", "nmid_t", "w_up", "middle", "w_out", "att_t", "qkv", "nin_t", "w_qkv", "stream")
    greet(spot.peers())
    jobs = []
    for layer in range(LAYERS):
        row = []
        for n in range(4):
            got, half, near, zs, zr = buffers[n]
            send = (big, small, big, tall)[n]
            row.append(Reduce(send, got, half, near, zs, zr, grads_o[4 * layer + n], ssem, rsem, (4 * layer + n) * Reduce.SEMS))
        jobs.append(row)
    line = Line()
    closed = set()
    peers = comm_peers()

    def steps_of(layer, n):
        job = jobs[layer][n]

        def close():
            job.finish()
            closed.add((layer, n))
            if layer == 1:
                job.drain()
                for peer in peers:
                    pl.semaphore_signal(csem.at[n], inc=1, device_id=peer, device_id_type=MESH)
        return [job.send_near, job.send_z, close]

    def credit(layer, n):
        if layer == 0:
            assert (1, n) in closed
            pl.semaphore_wait(csem.at[n], len(peers))

    def begin(n):
        here = band(n * CHUNK, CHUNK)
        value = cot_v[here, :].astype(F32) * live_column(lens, spot, CHUNK, n * CHUNK)
        grad[here, :] = value
        low[here, :] = value.astype(BF16)
    start.wait()
    loop(TOK // CHUNK, begin)

    def terms(job, left, width, tile, right, other, extra=None):
        c = lax.rem(rc, 2) if other else spot.c
        rows = left_rows(left, c)

        def step(n):
            here = cols(n, tile)
            value = dot(rows, right(n))
            for b in range(4):
                part = value[96 * b : 96 * b + 96]
                if other:
                    job.send[b, :, here] = part.astype(BF16)
                else:
                    job.got[b, :, here] = (job.got[b, :, here].astype(F32) + part).astype(BF16)
        loop(width // tile, step)
        if extra is not None:
            target = job.send if other else job.got
            for b in range(4):
                target[b, :, 512:640] = (
                    target[b, :, 512:640].astype(F32) + extra[pl.ds(pl.multiple_of((2 * b + c) * 96, 8), 96), :]
                ).astype(BF16)

    def down_terms(job, other):
        c = lax.rem(rc, 2) if other else spot.c

        def step(b):
            value = dot(act_t[band((2 * b + c) * 384, 384), :], low[...])
            if other:
                job.send[b] = value.astype(BF16)
            else:
                job.got[b] = (job.got[b].astype(F32) + value).astype(BF16)
        loop(4, step)

    def att_sent(layer, g):
        @pl.when(spot.member != g)
        def _():
            rcopy(
                datt_s.at[g], datt_r.at[spot.member], as_.at[4 * layer + g], ar.at[4 * layer + spot.member], spot.device(g)
            ).wait_send()

    for layer in (1, 0):
        signed = layer == 0
        j_qkv, j_out, j_up, j_down = jobs[layer]
        prior = jobs[1] if layer == 0 else None
        gains = norms[layer]
        ready(layer, "act_t")
        credit(layer, 3)
        down_terms(j_down, True)
        j_down.send_core()
        ready(layer, "w_down", "pre")
        line(1)

        def slope(n):
            here = cols(n, 512)
            value = dot_nt(low[...], w_down[pl.ds(pl.multiple_of(n * 512, 512), 512), :])
            dpre[:, here] = (gelu_slope(pre[:, here]) * value).astype(BF16)
        loop(6, slope)
        if layer:
            load(0, "w_down", "pre")
        ready(layer, "nmid_t")
        credit(layer, 2)
        if prior:
            prior[0].free_send()
        terms(j_up, nmid_t, 3072, 512, lambda n: dpre[:, cols(n, 512)], True)
        j_up.send_core()
        j_down.wait_core()
        down_terms(j_down, False)
        if layer:
            load(0, "act_t")
        line(1)
        j_down.send_diagonal()
        ready(layer, "w_up")
        dmid[...] = jnp.zeros_like(dmid)

        def through_up(n):
            here = cols(n, 512)
            dmid[...] += dot_nt(dpre[:, here], w_up[:, here])
        loop(6, through_up)
        if layer:
            load(0, "w_up")
        ready(layer, "middle")
        gain_late, bias_late = norm_back(middle, dmid, gains[2:3, :], grad, grad, branch, sums)
        if layer:
            load(0, "middle")
        ready(layer, "w_out")
        for g in range(4):
            value = dot_nt(w_out[192 * g : 192 * g + 192, :], branch[...]).astype(BF16)
            if layer == 0:
                att_sent(1, g)
            datt_s[g] = value

            @pl.when(spot.member != g)
            def _():
                rcopy(
                    datt_s.at[g], datt_r.at[spot.member], as_.at[4 * layer + g], ar.at[4 * layer + spot.member], spot.device(g)
                ).start()

            @pl.when(spot.member == g)
            def _():
                datt_r[g] = datt_s[g]
        if layer:
            load(0, "w_out")
        line.add(steps_of(layer, 3))
        line(1)
        ready(layer, "att_t")
        credit(layer, 1)
        terms(j_out, att_t, 768, 256, lambda n: branch[:, cols(n, 256)], True)
        j_out.send_core()
        j_up.wait_core()
        terms(j_up, nmid_t, 3072, 512, lambda n: dpre[:, cols(n, 512)], False)
        j_up.send_diagonal()
        if layer:
            load(0, "nmid_t")
        j_out.wait_core()
        terms(j_out, att_t, 768, 256, lambda n: branch[:, cols(n, 256)], False)
        if layer:
            load(0, "att_t")
        line(1)
        j_out.send_diagonal()
        ready(layer, "qkv")

        def turn_keys(j):
            kt[:, cols(j, TOK)] = qkv[j, :, 384:640].astype(F32).T.astype(BF16)
        loop(4, turn_keys)
        dk[...] = jnp.zeros_like(dk)
        dv[...] = jnp.zeros_like(dv)
        line.add(steps_of(layer, 2))
        line.add(steps_of(layer, 1))
        for g in range(4):
            @pl.when(spot.member != g)
            def _():
                rcopy(
                    datt_r.at[g], datt_r.at[g], as_.at[4 * layer + g], ar.at[4 * layer + g], spot.device(g)
                ).wait_recv()
        if layer == 0:
            for g in range(4):
                @pl.when(spot.member != g)
                def _():
                    rcopy(dq_s.at[g], dq_r.at[spot.member], ds_.at[4 + g], dr.at[4 + spot.member], spot.device(g)).wait_send()
        for i in (3, 2, 1, 0):
            block = attend_quarter_back(i, lens, qkv, kt, datt_r, scratch, signed)
            dq_s[i] = block

            @pl.when(spot.member != i)
            def _():
                rcopy(
                    dq_s.at[i], dq_r.at[spot.member], ds_.at[4 * layer + i], dr.at[4 * layer + spot.member], spot.device(i)
                ).start()

            @pl.when(spot.member == i)
            def _():
                dq_r[i] = dq_s[i]
            line(2)
        if layer:
            load(0, "qkv")
        ready(layer, "w_qkv", "stream", "nin_t")
        for g in range(4):
            @pl.when(spot.member != g)
            def _():
                rcopy(dq_r.at[g], dq_r.at[g], ds_.at[4 * layer + g], dr.at[4 * layer + g], spot.device(g)).wait_recv()
        dmid[...] = jnp.zeros_like(dmid)

        def through_qkv(g):
            dmid[...] += dot_nt(dq_r[g], w_qkv[:, cols(g, GROUP)])
        loop(4, through_qkv)
        if layer:
            load(0, "w_qkv")
        gain_early, bias_early = norm_back(stream, dmid, gains[0:1, :], grad, grad, low, sums)
        if layer:
            load(0, "stream")
        rows = [jnp.zeros((HEAD, 768), F32), gain_early, bias_early, gain_late, bias_late, jnp.zeros((HEAD - 4, 768), F32)]
        edge[...] = jnp.concatenate(rows, 0).T
        if layer == 0:
            swap(spot, low, final_r, ms.at[0], mr.at[0])
        credit(layer, 0)
        j_up.free_send()
        terms(j_qkv, nin_t, 4 * GROUP, GROUP, lambda g: dq_r[g], True, edge)
        j_qkv.send_core()
        line(1)
        j_qkv.wait_core()
        terms(j_qkv, nin_t, 4 * GROUP, GROUP, lambda g: dq_r[g], False, edge)
        if layer:
            load(0, "nin_t")
        j_qkv.send_diagonal()
        line.add(steps_of(layer, 0))
    line.flush()
    for job in jobs[0]:
        job.drain()
    for g in range(4):
        att_sent(0, g)
    for g in range(4):
        @pl.when(spot.member != g)
        def _():
            rcopy(dq_s.at[g], dq_r.at[spot.member], ds_.at[g], dr.at[spot.member], spot.device(g)).wait_send()
    swap_wait(spot, low, final_r, ms.at[0], mr.at[0])

    def widen(n):
        here = band(n * CHUNK, CHUNK)
        input_o[here, :] = final_r[here, :].astype(F32)
    loop(TOK // CHUNK, widen)


def backward_call(cot, lens, norms, wholes, stash):
    d = cot.shape[1]
    ff = wholes[2].shape[1]
    any_space = pl.BlockSpec(memory_space=pl.ANY)
    vmem = pl.BlockSpec(memory_space=pltpu.VMEM)
    dma = lambda n: pltpu.SemaphoreType.DMA((n,))
    shapes = [(whole.shape[0] // 32, whole.shape[1]) for whole in wholes]
    buffers = []
    for n in range(4):
        rows, width = wholes[n].shape[0] // 8, wholes[n].shape[1]
        cuts = [(rows // 4, width)] if n == 3 else [(16, width), (16, width // 2)]
        buffers += [
            pltpu.VMEM((4, rows, width), BF16),
            pltpu.VMEM((2, rows // 2, width), BF16),
            pltpu.VMEM((2, rows, width), BF16),
        ]
        buffers += [pltpu.VMEM((4,) + cut, BF16) for cut in cuts]
        buffers += [pltpu.VMEM((3,) + cut, BF16) for cut in cuts]
    outs = pl.pallas_call(
        backward_kernel,
        out_shape=[jax.ShapeDtypeStruct((TOK, d), F32)] + [jax.ShapeDtypeStruct(shape, F32) for shape in shapes],
        in_specs=[any_space, vmem, vmem] + [any_space] * 24,
        out_specs=[vmem] * 9,
        scratch_shapes=[pltpu.VMEM(whole.shape, BF16) for whole in wholes[:4]]
        + [pltpu.VMEM(shape, kind) for shape, kind in stash_shapes(d, ff)]
        + [
            pltpu.VMEM((TOK, d), BF16),
            pltpu.VMEM((TOK, d), F32),
            pltpu.VMEM((TOK, d), BF16),
            pltpu.VMEM((TOK, d), BF16),
            pltpu.VMEM((TOK, ff), BF16),
            pltpu.VMEM((TOK, d), F32),
            pltpu.VMEM((16, d), F32),
            pltpu.VMEM((d, 128), F32),
            pltpu.VMEM((4, 192, TOK), BF16),
            pltpu.VMEM((4, 192, TOK), BF16),
            pltpu.VMEM((WIDE, 4 * TOK), BF16),
        ]
        + [pltpu.VMEM((4 * TOK, TOK), F32)] * 4
        + [pltpu.VMEM((4 * TOK, TOK), BF16)] * 2
        + [pltpu.VMEM((4 * TOK, WIDE), F32)] * 2
        + [
            pltpu.VMEM((192, TOK), F32),
            pltpu.VMEM((4, TOK, GROUP), BF16),
            pltpu.VMEM((4, TOK, GROUP), BF16),
            pltpu.VMEM((4, 96, ff), BF16),
            pltpu.VMEM((4, 96, d), BF16),
            pltpu.VMEM((4, ff // 8, d), BF16),
            pltpu.VMEM((TOK, d), BF16),
        ]
        + buffers
        + [
            dma(8 * Reduce.SEMS),
            dma(8 * Reduce.SEMS),
            dma(25),
            pltpu.SemaphoreType.REGULAR((4,)),
            dma(8),
            dma(8),
            dma(8),
            dma(8),
            dma(1),
            dma(1),
        ],
        compiler_params=pltpu.CompilerParams(collective_id=1, has_side_effects=True, vmem_limit_bytes=63 * 2**20),
    )(cot, lens, norms, *wholes, *stash[0], *stash[1])
    return outs[0], outs[1:]


def backward_part(result, cot, lens, norms, wholes, stash):
    input_grad, grads = backward_call(cot, lens, norms, wholes, stash)
    both = [jnp.stack([grads[n], grads[4 + n]]) for n in range(4)]
    own = both[0].shape[1]
    groups = both[0].reshape(LAYERS, own, 4, GROUP)
    parts = [groups[..., at : at + 192].reshape(LAYERS, own, -1) for at in (0, 384, 192)]
    edge = groups[:, :, 0, 3 * 192 : 3 * 192 + 4]
    return (
        result[None],
        input_grad[None],
        jnp.concatenate(parts, -1),
        both[1],
        both[2],
        both[3],
        jnp.stack([edge[..., 0], edge[..., 2]], 1),
        edge[..., 1],
        edge[..., 3],
    )


def local_fast(tokens, lengths, w_qkv, w_out, w_up, w_down, gains, biases, cotangent):
    own = w_qkv.shape[1]
    parts = [w_qkv[:, :, n * 768 : (n + 1) * 768].reshape(LAYERS, own, 4, 192) for n in range(3)]
    edge = jnp.stack([gains[:, 0], biases[:, 0], gains[:, 1], biases[:, 1]], -1)
    edge = jnp.pad(edge[:, :, None, :], ((0, 0), (0, 0), (0, 3), (0, HEAD - 4)))
    grouped = jnp.concatenate([parts[0], parts[2], parts[1], edge], -1).reshape(LAYERS, own, 4 * GROUP)
    lens = jnp.pad(lengths, ((0, 7), (0, 124)))
    owns = []
    for number in range(LAYERS):
        owns += [grouped[number], w_out[number], w_up[number], w_down[number]]
    (result, cot, lens, norms), wholes, stash = forward_call(tokens[0], cotangent[0], lens, owns)
    return backward_part(result, cot, lens, norms, wholes, stash)


def solution(mesh):
    in_specs = (
        P("rows", "kv", None),
        P("rows", None),
        P(None, ("rows", "kv"), None),
        P(None, ("rows", "kv"), None),
        P(None, ("rows", "kv"), None),
        P(None, ("rows", "kv"), None),
        P(None, None, ("rows", "kv")),
        P(None, None, ("rows", "kv")),
        P("rows", "kv", None),
    )
    out_specs = (
        P("rows", "kv", None),
        P("rows", "kv", None),
        P(None, ("rows", "kv"), None),
        P(None, ("rows", "kv"), None),
        P(None, ("rows", "kv"), None),
        P(None, ("rows", "kv"), None),
        P(None, None, ("rows", "kv")),
        P(None, ("rows", "kv")),
        P(None, ("rows", "kv")),
    )
    fast = dict(mesh.shape) == {"rows": 8, "kv": 4}
    return jax.shard_map(local_fast if fast else local_generic, mesh=mesh, in_specs=in_specs, out_specs=out_specs, check_vma=False)
```

```python
import math

import jax
import jax.numpy as jnp
from jax import lax
from jax.experimental import pallas as pl
from jax.experimental.pallas import tpu as pltpu
from jax.sharding import PartitionSpec as P

HEADS = 12
HEAD = 64
LAYERS = 2


EPSILON = 1e-05


def norm_rows(stream, gain, bias):
    center = stream - jnp.mean(stream, -1, keepdims=True)
    spread = jnp.mean(center * center, -1, keepdims=True)
    return center * lax.rsqrt(spread + EPSILON) * gain + bias


def normalise(scores, allowed, query_live, signed):
    if signed:
        magnitude = jnp.sqrt(scores * scores + 1.0)
        ceiling = jnp.max(jnp.where(allowed > 0, magnitude, 0.0), -1, keepdims=True)
        shifted = jnp.where(allowed > 0, magnitude - ceiling, -60.0)
    else:
        ceiling = jnp.max(jnp.where(allowed > 0, scores, -10000.0), -1, keepdims=True)
        shifted = jnp.where(allowed > 0, scores - ceiling, -60.0)
    raised = jnp.exp(shifted) * allowed
    normaliser = jnp.sum(raised, -1, keepdims=True) + (1.0 - query_live)[None, :, None]
    unsigned_w = raised / normaliser
    if signed:
        return (jnp.tanh(scores) * unsigned_w, unsigned_w)
    return (unsigned_w, unsigned_w)


def make_mask(query_places, query_docs, query_live, key_places, key_docs, key_live):
    allowed = (
        (query_docs[:, None] == key_docs[None, :]) & (key_places[None, :] <= query_places[:, None])
    ).astype(jnp.float32)
    return allowed * query_live[:, None] * key_live[None, :]


def split_heads(query, keys_vals):
    model_width = query.shape[-1]
    slot_count = keys_vals.shape[0]
    query_heads = query.reshape(-1, HEADS, HEAD)
    key_heads = keys_vals[:, :model_width].reshape(slot_count, HEADS, HEAD)
    value_heads = keys_vals[:, model_width:].reshape(slot_count, HEADS, HEAD)
    return (query_heads, key_heads, value_heads)


def score_grads(scores, unsigned_w, weight_grad, inner_sum, signed):
    if signed:
        tanh_s = jnp.tanh(scores)
        magnitude = jnp.sqrt(scores * scores + 1.0)
        return unsigned_w * (
            (tanh_s * weight_grad - inner_sum) * scores / magnitude
            + weight_grad * (1.0 - tanh_s * tanh_s)
        )
    return unsigned_w * (weight_grad - inner_sum)


def attend_row(query, keys_vals, allowed, query_live, signed, scaling):
    query_heads, key_heads, value_heads = split_heads(query, keys_vals)
    scores = (
        jnp.einsum("qhd,khd->hqk", query_heads, key_heads, preferred_element_type=jnp.float32)
        * scaling
    )
    weights, unsigned_w = normalise(scores, allowed, query_live, signed)
    outcome = jnp.einsum(
        "hqk,khd->qhd",
        weights.astype(jnp.bfloat16),
        value_heads,
        preferred_element_type=jnp.float32,
    )
    return outcome.reshape(query.shape[0], query.shape[1]).astype(jnp.bfloat16)


def attend_back(query, keys_vals, grad_att, allowed, query_live, signed, scaling):
    query_heads, key_heads, value_heads = split_heads(query, keys_vals)
    slot_count = keys_vals.shape[0]
    model_width = query.shape[-1]
    scores = (
        jnp.einsum("qhd,khd->hqk", query_heads, key_heads, preferred_element_type=jnp.float32)
        * scaling
    )
    weights, unsigned_w = normalise(scores, allowed, query_live, signed)
    weights_low = weights.astype(jnp.bfloat16)
    grad_heads = grad_att.reshape(-1, HEADS, HEAD)
    weight_grad = jnp.einsum(
        "qhd,khd->hqk", grad_heads, value_heads, preferred_element_type=jnp.float32
    )
    inner_sum = jnp.sum(weight_grad * weights, -1, keepdims=True)
    score_low = score_grads(scores, unsigned_w, weight_grad, inner_sum, signed).astype(jnp.bfloat16)
    query_grad = (
        jnp.einsum("hqk,khd->qhd", score_low, key_heads, preferred_element_type=jnp.float32)
        * scaling
    )
    key_grad = (
        jnp.einsum("hqk,qhd->khd", score_low, query_heads, preferred_element_type=jnp.float32)
        * scaling
    )
    value_grad = jnp.einsum(
        "hqk,qhd->khd", weights_low, grad_heads, preferred_element_type=jnp.float32
    )
    kv_grad = jnp.concatenate(
        [key_grad.reshape(slot_count, model_width), value_grad.reshape(slot_count, model_width)], -1
    )
    return (query_grad.reshape(query.shape[0], model_width), kv_grad)


def reduce_grads(pairs, g_gain, g_bias):
    n_rows = lax.axis_size("rows")
    n_kv = lax.axis_size("kv")
    lefts = []
    rights = []
    for left_side, right_side in pairs:
        tok_count = left_side.shape[0] * left_side.shape[1]
        in_width = left_side.shape[-1]
        lefts.append(left_side.reshape(tok_count, n_rows, n_kv, in_width // (n_rows * n_kv)))
        rights.append(right_side.reshape(tok_count, right_side.shape[-1]))
    moved = (
        lax.all_to_all(lefts[0], "kv", split_axis=2, concat_axis=0, tiled=True),
        lax.all_to_all(lefts[1], "kv", split_axis=2, concat_axis=0, tiled=True),
        lax.all_to_all(lefts[2], "kv", split_axis=2, concat_axis=0, tiled=True),
        lax.all_to_all(lefts[3], "kv", split_axis=2, concat_axis=0, tiled=True),
    )
    whole = (
        lax.all_gather(rights[0], "kv", axis=0, tiled=True),
        lax.all_gather(rights[1], "kv", axis=0, tiled=True),
        lax.all_gather(rights[2], "kv", axis=0, tiled=True),
        lax.all_gather(rights[3], "kv", axis=0, tiled=True),
    )
    partial_sums = []
    for number in range(4):
        left_block = moved[number].reshape(moved[number].shape[0], -1)
        product = jnp.einsum(
            "ti,to->io", left_block, whole[number], preferred_element_type=jnp.float32
        )
        partial_sums.append(product.reshape(n_rows, -1, product.shape[-1]))
    reduced = (
        lax.psum_scatter(
            partial_sums[0].astype(jnp.bfloat16), "rows", scatter_dimension=0, tiled=True
        ).astype(jnp.float32),
        lax.psum_scatter(
            partial_sums[1].astype(jnp.bfloat16), "rows", scatter_dimension=0, tiled=True
        ).astype(jnp.float32),
        lax.psum_scatter(
            partial_sums[2].astype(jnp.bfloat16), "rows", scatter_dimension=0, tiled=True
        ).astype(jnp.float32),
        lax.psum_scatter(
            partial_sums[3].astype(jnp.bfloat16), "rows", scatter_dimension=0, tiled=True
        ).astype(jnp.float32),
    )
    norm_parts = (
        lax.psum_scatter(g_gain, ("rows", "kv"), scatter_dimension=1, tiled=True),
        lax.psum_scatter(g_bias, ("rows", "kv"), scatter_dimension=1, tiled=True),
    )
    results = tuple((piece.reshape(piece.shape[1], piece.shape[2]) for piece in reduced))
    return results + (norm_parts[0], norm_parts[1])


def local_generic(tokens, lengths, w_qkv, w_out, w_up, w_down, gains, biases, cotangent):
    rows_here, slot_dev, model_width = tokens.shape
    slot_count = slot_dev * lax.axis_size("kv")
    first_slot = lax.axis_index("kv") * slot_dev
    scaling = 1.0 / math.sqrt(HEAD)
    doc_ends = jnp.cumsum(lengths, -1)
    places = jnp.arange(slot_count, dtype=jnp.int32)
    docs_all = jnp.sum((doc_ends[:, None, :] <= places[None, :, None]).astype(jnp.int32), -1)
    live_all = (places[None, :] < doc_ends[:, -1:]).astype(jnp.float32)
    docs_here = lax.dynamic_slice_in_dim(docs_all, first_slot, slot_dev, 1)
    live_here = lax.dynamic_slice_in_dim(live_all, first_slot, slot_dev, 1)
    local_places = first_slot + jnp.arange(slot_dev, dtype=jnp.int32)
    masks = make_mask(local_places, docs_here[0], live_here[0], places, docs_all[0], live_all[0])
    stream = tokens.astype(jnp.float32)
    stored = []
    for number in range(LAYERS):
        signed = number == 0
        pieces = (
            lax.all_gather(w_qkv[number], ("rows", "kv"), axis=0, tiled=True),
            lax.all_gather(w_out[number], ("rows", "kv"), axis=0, tiled=True),
            lax.all_gather(w_up[number], ("rows", "kv"), axis=0, tiled=True),
            lax.all_gather(w_down[number], ("rows", "kv"), axis=0, tiled=True),
            lax.all_gather(gains[number], ("rows", "kv"), axis=1, tiled=True),
            lax.all_gather(biases[number], ("rows", "kv"), axis=1, tiled=True),
        )
        full_qkv, full_out, full_up, full_down, gain_pair, bias_pair = pieces
        gain_pair = gain_pair.astype(jnp.float32)
        bias_pair = bias_pair.astype(jnp.float32)
        normed_in = norm_rows(stream, gain_pair[0], bias_pair[0]).astype(jnp.bfloat16)
        projected = jnp.dot(normed_in, full_qkv, preferred_element_type=jnp.float32).astype(
            jnp.bfloat16
        )
        kv_all = lax.all_gather(projected[:, :, model_width:], "kv", axis=1, tiled=True)
        attended = jnp.stack(
            [
                attend_row(
                    projected[0, :, :model_width], kv_all[0], masks, live_here[0], signed, scaling
                )
            ]
        )
        shared = kv_all
        middle = stream + jnp.dot(attended, full_out, preferred_element_type=jnp.float32)
        normed_mid = norm_rows(middle, gain_pair[1], bias_pair[1]).astype(jnp.bfloat16)
        pre_act = jnp.dot(normed_mid, full_up, preferred_element_type=jnp.float32)
        activated = jax.nn.gelu(pre_act).astype(jnp.bfloat16)
        stored.append(
            (
                stream,
                normed_in,
                projected,
                shared,
                attended,
                middle,
                normed_mid,
                pre_act,
                activated,
                pieces,
            )
        )
        stream = middle + jnp.dot(activated, full_down, preferred_element_type=jnp.float32)
    result = (stream * live_here[..., None]).astype(jnp.bfloat16)
    residual_grad = cotangent.astype(jnp.float32) * live_here[..., None]
    collected = [None] * LAYERS
    for number in reversed(range(LAYERS)):
        signed = number == 0
        (
            stream_in,
            normed_in,
            projected,
            shared,
            attended,
            middle,
            normed_mid,
            pre_act,
            activated,
            kept,
        ) = stored[number]
        pieces = (
            lax.all_gather(w_qkv[number], ("rows", "kv"), axis=0, tiled=True),
            lax.all_gather(w_out[number], ("rows", "kv"), axis=0, tiled=True),
            lax.all_gather(w_up[number], ("rows", "kv"), axis=0, tiled=True),
            lax.all_gather(w_down[number], ("rows", "kv"), axis=0, tiled=True),
            lax.all_gather(gains[number], ("rows", "kv"), axis=1, tiled=True),
            lax.all_gather(biases[number], ("rows", "kv"), axis=1, tiled=True),
        )
        full_qkv, full_out, full_up, full_down, gain_pair, bias_pair = pieces
        gain_pair = gain_pair.astype(jnp.float32)
        bias_pair = bias_pair.astype(jnp.float32)
        down_in = residual_grad.astype(jnp.bfloat16)
        act_grad = jnp.einsum("rtd,fd->rtf", down_in, full_down, preferred_element_type=jnp.float32)
        unused, gelu_pull = jax.vjp(jax.nn.gelu, pre_act)
        pre_grad = gelu_pull(act_grad)[0].astype(jnp.bfloat16)
        mid_normed_grad = jnp.einsum(
            "rtf,df->rtd", pre_grad, full_up, preferred_element_type=jnp.float32
        )
        unused, norm_pull = jax.vjp(norm_rows, middle, gain_pair[1], bias_pair[1])
        middle_part, gain_late, bias_late = norm_pull(mid_normed_grad)
        middle_grad = residual_grad + middle_part
        branch_grad = middle_grad.astype(jnp.bfloat16)
        att_grad = jnp.einsum(
            "rte,de->rtd", branch_grad, full_out, preferred_element_type=jnp.float32
        ).astype(jnp.bfloat16)
        kv_all = shared
        query_grad, kv_grad = attend_back(
            projected[0, :, :model_width],
            kv_all[0],
            att_grad[0],
            masks,
            live_here[0],
            signed,
            scaling,
        )
        query_grads = [query_grad]
        kv_grads = [kv_grad]
        kv_here = lax.psum_scatter(
            jnp.stack(kv_grads).astype(jnp.bfloat16), "kv", scatter_dimension=1, tiled=True
        ).astype(jnp.float32)
        qkv_grad = jnp.concatenate([jnp.stack(query_grads), kv_here], -1).astype(jnp.bfloat16)
        in_normed_grad = jnp.einsum(
            "rte,de->rtd", qkv_grad, full_qkv, preferred_element_type=jnp.float32
        )
        unused, first_pull = jax.vjp(norm_rows, stream_in, gain_pair[0], bias_pair[0])
        stream_part, gain_early, bias_early = first_pull(in_normed_grad)
        residual_grad = middle_grad + stream_part
        g_gain = jnp.stack([gain_early, gain_late])
        g_bias = jnp.stack([bias_early, bias_late])
        pairs = [
            (normed_in, qkv_grad),
            (attended, branch_grad),
            (normed_mid, pre_grad),
            (activated, down_in),
        ]
        collected[number] = reduce_grads(pairs, g_gain, g_bias)
    grad_qkv = jnp.stack([collected[number][0] for number in range(LAYERS)])
    grad_out = jnp.stack([collected[number][1] for number in range(LAYERS)])
    grad_up = jnp.stack([collected[number][2] for number in range(LAYERS)])
    grad_down = jnp.stack([collected[number][3] for number in range(LAYERS)])
    grad_gains = jnp.stack([collected[number][4] for number in range(LAYERS)])
    grad_biases = jnp.stack([collected[number][5][0] for number in range(LAYERS)])
    grad_mid_biases = jnp.stack([collected[number][5][1] for number in range(LAYERS)])
    return (
        result,
        residual_grad,
        grad_qkv,
        grad_out,
        grad_up,
        grad_down,
        grad_gains,
        grad_biases,
        grad_mid_biases,
    )


F32 = jnp.float32
BF16 = jnp.bfloat16
MESH = pl.DeviceIdType.MESH
ZN = 4


def flip(value, unit):
    bit = lax.rem(lax.div(value, unit), 2)
    return value + unit - 2 * unit * bit


def places_of():
    r = lax.axis_index("rows")
    z = lax.axis_index("kv")
    return r, z, flip(r, 2), flip(r, 4), flip(flip(r, 2), 4), flip(r, 1)


def turn(z, k):
    return lax.rem(z + k, ZN)


def rcopy(src, dst, ssem, rsem, device):
    return pltpu.make_async_remote_copy(
        src_ref=src, dst_ref=dst, send_sem=ssem, recv_sem=rsem, device_id=device, device_id_type=MESH
    )


def band(start, size):
    return pl.ds(pl.multiple_of(start, 16), size)


def greet(peers):
    barrier = pltpu.get_barrier_semaphore()
    for peer in peers:
        pl.semaphore_signal(barrier, inc=1, device_id=peer, device_id_type=MESH)
    pl.semaphore_wait(barrier, len(peers))


def comm_peers():
    r, z, rx, ry, rd, rc = places_of()
    return [(r, turn(z, 1)), (r, turn(z, 2)), (r, turn(z, 3)), (rx, z), (ry, z), (rc, z)]


def col_step(width):
    return 256 if width % 256 == 0 else 128


def add_rows(dst, src, rows):
    def step(i, carry):
        here = band(i * 16, 16)
        dst[here, :] = (dst[here, :].astype(F32) + src[here, :].astype(F32)).astype(BF16)
        return carry
    lax.fori_loop(0, rows // 16, step, 0)


SEND = 0
PLANE = 100
PASS = 200
LAST = 300
WHOLE = 400
NORM = 600
SHARE = 700
PROJECT = 800
ATTEND = 900
OUTPUT = 1000
UP = 1100
DOWN = 1200
TOKENS = 500
COTANGENT = 510
WIDEN = 520
RESULT = 530
SECOND = 0
NEAR = 100
OVER_Z = 200
CLOSE = 300
THEIRS = 400
OURS = 500
SLOPE = 600
THROUGH = 700
NORM_BACK = 800
ASK = 900
KEYS = 1000
ASKED = 1100
ATTEND_BACK = 1200
PARTIAL = 1300
FIRST_BACK = 1400
BEGIN = 1500
SWAP_BACK = 1510

FORWARD_ORDER = [
    0, 100, 1, 2, 200, 500, 3, 300, 101, 400, 102, 201, 301, 4, 401, 103, 202, 520, 600, 5, 800, 802, 104,
    302, 203, 402, 105, 6, 303, 204, 700, 403, 7, 801, 803, 106, 8, 9, 900, 901, 304, 205, 107, 902, 903, 404,
    206, 305, 207, 10, 1000, 108, 405, 1100, 306, 307, 109, 11, 1101, 406, 407, 1200, 1201, 110, 601, 810,
    812, 208, 111, 701, 811, 209, 813, 910, 911, 912, 308, 913, 210, 408, 510, 309, 211, 1001, 1110, 409, 310,
    1111, 311, 410, 1210, 411, 1211, 530,
]
BACKWARD_ORDER = [
    1500, 410, 610, 710, 408, 611, 510, 10, 411, 711, 801, 1001, 901, 407, 508, 409, 511, 110, 11, 1101, 1213,
    1212, 108, 1211, 1210, 111, 509, 210, 9, 507, 1312, 406, 8, 1313, 1311, 506, 6, 310, 211, 1401, 109, 404,
    600, 208, 106, 311, 504, 209, 4, 700, 601, 405, 107, 701, 308, 104, 800, 900, 402, 505, 5, 309, 7, 1000,
    204, 206, 403, 1100, 502, 207, 2, 1203, 105, 1202, 102, 306, 307, 205, 503, 3, 401, 1201, 202, 1200, 501,
    1, 1302, 400, 1303, 305, 103, 1301, 304, 101, 500, 302, 0, 203, 201, 100, 200, 301, 1400, 1510, 412, 303,
    512, 12, 112, 212, 300, 312,
]


GROUP = 640
TOK = 256
WIDE = 256
PARTS = HEADS // 4
CHUNK = 64
FAR = -1e30
KB = 256
JOBS = 6


def dot(a, b):
    return jnp.dot(a, b, preferred_element_type=F32)


def dot_nt(a, b):
    return lax.dot_general(a, b, (((1,), (1,)), ((), ())), preferred_element_type=F32)


def dot_tn(a, b):
    return lax.dot_general(a, b, (((0,), (0,)), ((), ())), preferred_element_type=F32)


def loop(count, body):
    def step(i, carry):
        body(i)
        return carry
    lax.fori_loop(0, count, step, 0)


def cols(i, size):
    return pl.ds(pl.multiple_of(i * size, 128), size)


class Spot:
    def __init__(self):
        self.r, self.z, self.rx, self.ry, self.rd, self.rc = places_of()
        self.c = lax.rem(self.r, 2)
        self.parity = lax.rem(self.z, 2)
        self.member = 2 * self.c + self.parity
        self.swaps = (self.c + lax.div(self.z, 2)) == 1
        self.partner = (self.rc, flip(self.z, 2))

    def mate(self, k):
        r = self.rc if k >= 2 else self.r
        z = flip(self.z, 1) if k % 2 else self.z
        return (r, z), 2 * lax.rem(r, 2) + lax.rem(z, 2)

    def device(self, member):
        return (self.r - self.c + lax.div(member, 2), self.z - self.parity + lax.rem(member, 2))

    def peers(self):
        return comm_peers() + [(self.rc, flip(self.z, 1)), self.partner]


class Gather:
    SEMS = 11

    def __init__(self, own, whole, bufs, ssem, rsem, base, paired=False):
        self.own, self.whole, self.bufs = own, whole, bufs
        self.ssem, self.rsem, self.base = ssem, rsem, base
        self.split, self.paired = len(bufs) > 0, paired
        self.rows, self.width = whole.shape[0] // 8, whole.shape[1]
        self.sent = []

    def _copy(self, src, dst, at, device):
        return rcopy(src, dst, self.ssem.at[self.base + at], self.rsem.at[self.base + at], device)

    def _block(self, r, half=None):
        if half is None:
            return self.whole.at[band(r * self.rows, self.rows), :]
        part = self.rows // 2
        return self.whole.at[band(r * self.rows + half * part, part), :]

    def _cored(self, r, column):
        if not self.paired:
            return self._block(r)
        return self.whole.at[band(r * self.rows, self.rows), cols(column, self.width // 2)]

    def _send(self, src, dst, at, device):
        copy = self._copy(src, dst, at, device)
        copy.start()
        self.sent.append(copy)

    def prepare(self):
        r, z = places_of()[:2]
        if self.split:
            zbuf = self.bufs[0]
            half = self.width // 2
            values = [self.own(place) for place in (0, 1)] if self.paired else [self.own[...].astype(F32)]
            for place, own in enumerate(values):
                packed = jnp.concatenate(
                    [own[:16], jnp.concatenate([own[16:, :half], own[16:, half:]], 0)], 1
                ).astype(BF16)
                if self.paired:
                    self.bufs[1][place] = packed
                else:
                    zbuf[pl.ds(z, 1)] = packed[None]
            if self.paired:
                zbuf[pl.ds(z, 1)] = self.bufs[1][pl.ds(lax.rem(z, 2), 1)]
        else:
            part = self.rows // ZN
            self.whole[band(r * self.rows + z * part, part), :] = self.own[...]

    def _zref(self, z):
        if self.split:
            return self.bufs[0].at[z]
        part = self.rows // ZN
        return self.whole.at[band(places_of()[0] * self.rows + z * part, part), :]

    def send_z(self):
        r, z = places_of()[:2]
        for k in (1, 2, 3):
            there = turn(z, k)
            src = self.bufs[1].at[lax.rem(there, 2)] if self.paired else self._zref(z)
            self._send(src, self._zref(z), k - 1, (r, there))

    def wait_z(self):
        r, z = places_of()[:2]
        for k in (1, 2, 3):
            ref = self._zref(turn(z, ZN - k))
            self._copy(ref, ref, k - 1, (r, turn(z, ZN - k))).wait_recv()
        if self.split:
            zbuf = self.bufs[0]
            half = self.width // 2
            step = col_step(half)
            for side in (0, 1):
                def assemble(i, side=side):
                    at = pl.multiple_of(self.width + i * step, 128)
                    here = pl.ds(pl.multiple_of(side * half + i * step, 128), step)
                    parts = []
                    for piece in range(ZN):
                        parts.append(zbuf[piece, :, here].astype(F32))
                        parts.append(zbuf[piece, :, pl.ds(at, step)].astype(F32)[8 * side : 8 * side + 8])
                    self.whole[band(r * self.rows, self.rows), here] = jnp.concatenate(parts, 0).astype(BF16)
                loop(half // step, assemble)

    def send_plane(self):
        r, z, rx, ry, rd, rc = places_of()
        own = self._block(r)
        self._send(own, own, 3, (rx, z))
        self._send(own, own, 4, (ry, z))
        self._core(r, 7)

    def _core(self, block, at):
        r, z, rx, ry, rd, rc = places_of()
        ref = self._cored(block, lax.rem(rc, 2))
        self._send(ref, ref, at, (rc, z))

    def forward(self):
        r, z, rx, ry, rd, rc = places_of()
        first, second = self._block(rx), self._block(ry)
        self._copy(first, first, 3, (rx, z)).wait_recv()
        part = self._block(rx, 0)
        self._send(part, part, 5, (ry, z))
        self._copy(second, second, 4, (ry, z)).wait_recv()
        part = self._block(ry, 1)
        self._send(part, part, 6, (rx, z))
        self._core(rx, 8)
        self._core(ry, 9)

    def forward_last(self):
        r, z, rx, ry, rd, rc = places_of()
        part = self._block(rd, 0)
        self._copy(part, part, 5, (ry, z)).wait_recv()
        part = self._block(rd, 1)
        self._copy(part, part, 6, (rx, z)).wait_recv()
        self._core(rd, 10)

    def finish(self):
        r, z, rx, ry, rd, rc = places_of()
        for at, block in ((7, r), (8, rx), (9, ry), (10, rd)):
            ref = self._cored(flip(block, 1), lax.rem(r, 2))
            self._copy(ref, ref, at, (rc, z)).wait_recv()

    def drain(self):
        for copy in self.sent:
            copy.wait_send()


def swap(spot, src, dst, ssem, rsem):
    @pl.when(spot.swaps)
    def _():
        rcopy(src, dst, ssem, rsem, spot.partner).start()

    @pl.when(jnp.logical_not(spot.swaps))
    def _():
        pltpu.make_async_copy(src, dst, rsem).start()


def swap_wait(spot, src, dst, ssem, rsem):
    @pl.when(spot.swaps)
    def _():
        rcopy(src, dst, ssem, rsem, spot.partner).wait()

    @pl.when(jnp.logical_not(spot.swaps))
    def _():
        pltpu.make_async_copy(src, dst, rsem).wait()


def starts_of(lens, i):
    places = lax.broadcasted_iota(jnp.int32, (1, TOK), 1) + i * TOK
    end = jnp.zeros((1, 1), jnp.int32)
    start = jnp.zeros((1, TOK), jnp.int32)
    for n in range(4):
        end = end + lens[0:1, n : n + 1]
        start = jnp.maximum(start, jnp.where(end <= places, end, 0))
    live = places < end
    return places, jnp.where(live, start, 1 << 20), live


def live_column(lens, spot, rows, first):
    places = lax.broadcasted_iota(jnp.int32, (rows, 1), 0) + spot.member * TOK + first
    end = lens[0:1, 0:1] + lens[0:1, 1:2] + lens[0:1, 2:3] + lens[0:1, 3:4]
    return (places < end).astype(F32)


def centred(value):
    center = value - jnp.mean(value, -1, keepdims=True)
    spread = jnp.mean(center * center, -1, keepdims=True)
    return center * lax.rsqrt(spread + EPSILON)


def fold_rows(value, op):
    rows = value.shape[0]
    parts = [value[8 * n : 8 * n + 8] for n in range(rows // 8)]
    while len(parts) > 1:
        parts = [op(parts[n], parts[n + 1]) if n + 1 < len(parts) else parts[n] for n in range(0, len(parts), 2)]
    return parts[0]


def head_lanes(shape, h, offset):
    lanes = lax.broadcasted_iota(jnp.int32, shape, 1)
    return lax.div(lanes, HEAD) == h + offset


def masked_rows(first, rows, places, start, diagonal):
    keys = lax.broadcasted_iota(jnp.int32, (rows, TOK), 0) + first
    okay = keys >= start
    return okay & (keys <= places) if diagonal else okay


def over_blocks(i, body, carry):
    per = TOK // KB if KB <= TOK else 1
    if i:
        carry = lax.fori_loop(0, i * per, lambda n, c: body(n * KB, c, False), carry)
    for n in range(per):
        carry = body(i * TOK + n * KB, carry, True)
    return carry


def key_rows(qkv, first, at):
    quarter = lax.div(first, TOK)
    here = pl.ds(pl.multiple_of(lax.rem(first, TOK), KB), KB)
    return qkv[quarter, here, at : at + WIDE]


def masked_heads(value_t, offset):
    rows = lax.div(lax.broadcasted_iota(jnp.int32, value_t.shape, 0), HEAD)
    return jnp.concatenate([jnp.where(rows == h + offset, value_t, 0.0) for h in range(PARTS)], 1).astype(BF16)


def magnitude_of(s):
    square = s * s + 1.0
    back = lax.rsqrt(square)
    return square * back, back


def attend_quarter(i, lens, qkv, vt, acc, o_ref, stats, signed):
    places, start, live = starts_of(lens, i)
    mine = masked_heads(qkv[i, :, 0:WIDE].astype(F32).T * 0.125, 0)
    acc[...] = jnp.zeros_like(acc)

    def block(first, carry, diagonal):
        keys = key_rows(qkv, first, 384)
        okay = masked_rows(first, KB, places, start, diagonal)
        here = pl.ds(pl.multiple_of(first, KB), KB)
        out, lows, shrinks = [], [], []
        scores = [dot(keys, mine[:, h * TOK : (h + 1) * TOK]) for h in range(PARTS)]
        for h in range(PARTS):
            old, total = carry[2 * h], carry[2 * h + 1]
            s = scores[h]
            value = jnp.where(okay, magnitude_of(s)[0] if signed else s, FAR)
            new = jnp.maximum(old, jnp.max(fold_rows(value, jnp.maximum), 0, keepdims=True))
            raised = jnp.exp(value - new)
            shrink = jnp.exp(old - new)
            lows.append((jnp.tanh(s) * raised if signed else raised).astype(BF16))
            shrinks.append(shrink)
            out += [new, total * shrink + jnp.sum(fold_rows(raised, jnp.add), 0, keepdims=True)]
        terms = [dot(vt[HEAD * (h + 1) : HEAD * (h + 2), here], lows[h]) for h in range(PARTS)]
        for h in range(PARTS):
            rows = slice(HEAD * h, HEAD * (h + 1))
            acc[rows, :] = acc[rows, :] * shrinks[h] + terms[h]
        return tuple(out)
    lowest = jnp.full((1, TOK), 0.0 if signed else -10000.0, F32)
    carry = over_blocks(i, block, (lowest, jnp.zeros((1, TOK), F32)) * PARTS)
    for h in range(PARTS):
        inverse = 1.0 / (carry[2 * h + 1] + (1.0 - live.astype(F32)))
        stats[i, h : h + 1, :] = carry[2 * h]
        stats[i, PARTS + h : PARTS + h + 1, :] = inverse
        acc[HEAD * h : HEAD * (h + 1), :] = acc[HEAD * h : HEAD * (h + 1), :] * inverse
    o_ref[i] = acc[...].astype(BF16)


class Keep:
    def __init__(self, src, dst, sem):
        self.copy = pltpu.make_async_copy(src, dst, sem)
        self.copy.start()
        self.open = True

    def wait(self):
        if self.open:
            self.copy.wait()
        self.open = False


STASH = ("stream", "qkv", "middle", "nin_t", "att_t", "nmid_t", "pre", "act_t", "out", "stats")


def stash_shapes(d, ff):
    return [
        ((TOK, d), F32),
        ((4, TOK, GROUP), BF16),
        ((TOK, d), F32),
        ((d, 4 * TOK), BF16),
        ((d, TOK), BF16),
        ((d, TOK), BF16),
        ((TOK, ff), F32),
        ((ff, TOK), BF16),
        ((4, 192, TOK), F32),
        ((4, 8, TOK), F32),
    ]


def forward_kernel(*refs):
    refs = list(refs)
    take = lambda n: [refs.pop(0) for _ in range(n)]
    tok, cot, lengths = take(3)
    sources = take(4)
    gains, biases = take(2)
    result_o, cot_o, lens_o, norms_o = take(4)
    whole_o = take(2 * JOBS)
    stash_o = [take(10), take(10)]
    wholes = take(2 * JOBS)
    zbuf = [take((2, 1, 1, 1, 0, 0)[n % JOBS]) for n in range(2 * JOBS)]
    tok_v, lens_in, lens_v, stream, nin0, nin1, qkv, vt, outs, stats, o_ref, att0, att1, pre, act, act_t, nin_t, nt_mid, normed, middle, res = take(21)
    ssem, rsem, osem, stsem, ns, nr, os_, or_, ms, mr = take(10)
    spot = Spot()
    lens_in[...] = jnp.zeros_like(lens_in)
    lens_in[0:1, 0:4] = lengths[...]
    greet(spot.peers())
    jobs = []

    def grouped(layer):
        def pair(place):
            vectors = [ref[layer, which : which + 1, :].astype(F32) for which in (0, 1) for ref in (gains, biases)]
            own = vectors[0].shape[1]
            top = jnp.concatenate([jnp.concatenate(vectors, 0), jnp.zeros((4, 128 - own), F32)], 1)
            edge = jnp.concatenate([top, jnp.zeros((124, 128), F32)], 0).T[:own, :HEAD]
            parts = []
            for g in (place, place + 2):
                for at in (0, 2, 1):
                    parts.append(sources[0][layer, :, 768 * at + 192 * g : 768 * at + 192 * g + 192].astype(F32))
                parts.append(edge)
            return jnp.concatenate(parts, 1)
        return pair

    for layer in range(LAYERS):
        out_in, up_in, down_in = [source.at[layer] for source in sources[1:]]
        ff, d = up_in.shape[1] // 2, down_in.shape[1] // 2
        owns = [grouped(layer), out_in] + [up_in.at[:, h * ff : (h + 1) * ff] for h in (0, 1)] + [down_in.at[:, h * d : (h + 1) * d] for h in (0, 1)]
        for n, own in enumerate(owns):
            at = layer * JOBS + n
            jobs.append(Gather(own, wholes[at], zbuf[at], ssem, rsem, at * Gather.SEMS, n == 0))
    kept = {}

    def keep(name, src, dst, sem):
        kept[name] = Keep(src, dst, sem)

    def settle(name):
        if name in kept:
            kept[name].wait()

    def stash(layer, name, src):
        at = STASH.index(name)
        keep((layer, name), src, stash_o[layer][at], stsem.at[10 * layer + at])

    steps = {}

    def step(name):
        def note(run):
            steps[name] = run
        return note

    for n, job in enumerate(jobs):
        def first(job=job):
            job.prepare()
            job.send_z()

        def plane(job=job):
            job.wait_z()
            job.send_plane()

        def done(job=job, n=n):
            job.finish()
            src = wholes[n]
            if n % JOBS == 0:
                src = src.at[:, cols(spot.c, GROUP)]
            keep(("whole", n), src, whole_o[n], osem.at[n])
        steps.update({SEND + n: first, PLANE + n: plane, PASS + n: job.forward, LAST + n: job.forward_last, WHOLE + n: done})

    @step(TOKENS)
    def _():
        swap(spot, tok, tok_v, ms.at[0], mr.at[0])
        swap(spot, lens_in, lens_v, ms.at[1], mr.at[1])

    @step(COTANGENT)
    def _():
        swap(spot, cot, cot_o, ms.at[2], mr.at[2])

    @step(WIDEN)
    def _():
        swap_wait(spot, tok, tok_v, ms.at[0], mr.at[0])
        swap_wait(spot, lens_in, lens_v, ms.at[1], mr.at[1])
        lens_o[...] = lens_v[...]

        def widen(n):
            here = band(n * CHUNK, CHUNK)
            stream[here, :] = tok_v[here, :].astype(F32)
        loop(TOK // CHUNK, widen)
        stash(0, "stream", stream)

    def layer_steps(layer):
        base = layer * JOBS
        w_qkv, w_out, w_up0, w_up1, w_down0, w_down1 = wholes[base : base + JOBS]
        nin = (nin0, nin1)[layer]
        att = (att0, att1)[layer]
        signed = layer == 0

        def gathered(k):
            mate, member = spot.mate(k)
            return rcopy(nin.at[member], nin.at[member], ns.at[4 * layer + k], nr.at[4 * layer + k], mate)

        def give(k, member):
            mate = spot.mate(1 if k == 1 else 2)[0]
            return rcopy(nin.at[member], nin.at[member], ns.at[4 * layer + k], nr.at[4 * layer + k], mate)

        @step(NORM + layer)
        def _():
            edge = w_qkv[:, pl.ds(pl.multiple_of(spot.c * GROUP + 512, 128), 128)].astype(F32).T
            norms_o[layer] = edge[HEAD : HEAD + 8]

            def first_norm(n):
                here = band(n * CHUNK, CHUNK)
                value = centred(stream[here, :]) * norms_o[layer, 0:1, :] + norms_o[layer, 1:2, :]
                nin[spot.member, here, :] = value.astype(BF16)
            loop(TOK // CHUNK, first_norm)
            give(1, spot.member).start()
            give(2, spot.member).start()

        @step(SHARE + layer)
        def _():
            gathered(1).wait_recv()
            give(3, spot.mate(1)[1]).start()

        def project(k):
            def run():
                member = spot.member
                if k:
                    member = spot.mate(k)[1]
                    if k != 1:
                        gathered(k).wait_recv()
                group = dot(nin[member], w_qkv[:, cols(spot.c, GROUP)]).astype(BF16)
                if (layer, k) == (1, 0):
                    settle((0, "qkv"))
                    settle((0, "nin_t"))
                qkv[pl.ds(member, 1)] = group[None]
                at = pl.multiple_of(member * TOK, TOK)
                vt[:, pl.ds(at, TOK)] = group[:, 128:384].astype(F32).T.astype(BF16)
                nin_t[:, pl.ds(at, TOK)] = nin[member].astype(F32).T.astype(BF16)
                if k == 3:
                    stash(layer, "qkv", qkv)
                    stash(layer, "nin_t", nin_t)
            return run
        for k in range(4):
            steps[PROJECT + 10 * layer + k] = project(k)

        def returned(i):
            return rcopy(
                o_ref.at[layer, i], att.at[band(spot.member * 192, 192), :], os_.at[4 * layer + i], or_.at[4 * layer + spot.member], spot.device(i)
            )

        def attend(i):
            def run():
                attend_quarter(i, lens_v, qkv, vt, outs.at[layer, i], o_ref.at[layer], stats.at[layer], signed)

                @pl.when(spot.member != i)
                def _():
                    returned(i).start()

                @pl.when(spot.member == i)
                def _():
                    att[i * 192 : (i + 1) * 192, :] = o_ref[layer, i]
                if i == 3:
                    stash(layer, "out", outs.at[layer])
                    stash(layer, "stats", stats.at[layer])
            return run
        for i in range(4):
            steps[ATTEND + 10 * layer + i] = attend(i)

        @step(OUTPUT + layer)
        def _():
            for i in range(4):
                @pl.when(spot.member != i)
                def _():
                    ref = att.at[i * 192 : (i + 1) * 192, :]
                    rcopy(ref, ref, os_.at[4 * layer + i], or_.at[4 * layer + i], spot.device(i)).wait_recv()
            stash(layer, "att_t", att)
            settle((0, "middle"))
            middle[...] = stream[...] + dot_tn(att[...], w_out[...])
            stash(layer, "middle", middle)

            def second_norm(n):
                here = band(n * CHUNK, CHUNK)
                value = centred(middle[here, :]) * norms_o[layer, 2:3, :] + norms_o[layer, 3:4, :]
                normed[here, :] = value.astype(BF16)
            loop(TOK // CHUNK, second_norm)
            settle((0, "nmid_t"))
            nt_mid[...] = normed[...].astype(F32).T.astype(BF16)
            stash(layer, "nmid_t", nt_mid)
            settle((0, "pre"))
            settle((0, "act_t"))

        def up(h):
            w_up = (w_up0, w_up1)[h]
            tile = 512
            count = w_up.shape[1] // tile

            def run():
                def part(n):
                    value = dot(normed[...], w_up[:, cols(n, tile)])
                    here = cols(h * count + n, tile)
                    pre[:, here] = value
                    active = jax.nn.gelu(value)
                    act[:, here] = active.astype(BF16)
                    act_t[pl.ds(pl.multiple_of((h * count + n) * tile, tile), tile), :] = active.T.astype(BF16)
                loop(count, part)
                if h:
                    stash(layer, "pre", pre)
                    stash(layer, "act_t", act_t)
            return run

        def down(h):
            w_down = (w_down0, w_down1)[h]
            width = w_down.shape[1]

            def run():
                settle((layer, "stream"))

                def part(n):
                    here = cols(n + h * (width // 128), 128)
                    stream[:, here] = middle[:, here] + dot(act[...], w_down[:, cols(n, 128)])
                if width % 384 == 0:
                    here = slice(h * width, (h + 1) * width)
                    stream[:, here] = middle[:, here] + dot(act[...], w_down[...])
                else:
                    loop(width // 128, part)
                if h and layer == 0:
                    stash(1, "stream", stream)
            return run
        for h in (0, 1):
            steps[UP + 10 * layer + h] = up(h)
            steps[DOWN + 10 * layer + h] = down(h)

        def close():
            for k in (1, 2):
                give(k, spot.member).wait_send()
            give(3, spot.mate(1)[1]).wait_send()
            for i in range(4):
                @pl.when(spot.member != i)
                def _():
                    returned(i).wait_send()
        return close

    closes = [layer_steps(layer) for layer in range(LAYERS)]

    @step(RESULT)
    def _():
        def last(n):
            here = band(n * CHUNK, CHUNK)
            res[here, :] = (stream[here, :] * live_column(lens_v, spot, CHUNK, n * CHUNK)).astype(BF16)
        loop(TOK // CHUNK, last)
        swap(spot, res, result_o, ms.at[3], mr.at[3])

    for name in FORWARD_ORDER:
        steps.pop(name)()
    assert not steps
    for job in jobs:
        job.drain()
    for close in closes:
        close()
    for copy in kept.values():
        copy.wait()
    swap_wait(spot, cot, cot_o, ms.at[2], mr.at[2])
    swap_wait(spot, res, result_o, ms.at[3], mr.at[3])


def forward_call(tok, cot, lengths, w_qkv, w_out, w_up, w_down, gains, biases):
    d, ff = tok.shape[1], w_up.shape[2]
    shapes = [(d, 2 * GROUP), (d, d), (d, ff // 2), (d, ff // 2), (ff, d // 2), (ff, d // 2)] * LAYERS
    zshapes = []
    for n, (rows, width) in enumerate(shapes):
        if n % JOBS < 4:
            zshapes.append(pltpu.VMEM((ZN, 16, width * 3 // 2), BF16))
        if n % JOBS == 0:
            zshapes.append(pltpu.VMEM((2, 16, width * 3 // 2), BF16))
    any_space = pl.BlockSpec(memory_space=pl.ANY)
    vmem = pl.BlockSpec(memory_space=pltpu.VMEM)
    stash = [jax.ShapeDtypeStruct(shape, kind) for shape, kind in stash_shapes(d, ff)]
    dma = lambda n: pltpu.SemaphoreType.DMA((n,))
    kept_shapes = [(rows, GROUP if n % JOBS == 0 else width) for n, (rows, width) in enumerate(shapes)]
    outs = pl.pallas_call(
        forward_kernel,
        out_shape=[
            jax.ShapeDtypeStruct((TOK, d), BF16),
            jax.ShapeDtypeStruct((TOK, d), BF16),
            jax.ShapeDtypeStruct((8, 128), jnp.int32),
            jax.ShapeDtypeStruct((LAYERS, 8, d), F32),
        ]
        + [jax.ShapeDtypeStruct(shape, BF16) for shape in kept_shapes]
        + stash
        + stash,
        in_specs=[any_space, any_space] + [vmem] * 7,
        out_specs=[any_space, any_space, vmem, vmem] + [any_space] * (2 * JOBS + 20),
        scratch_shapes=[pltpu.VMEM(shape, BF16) for shape in shapes]
        + zshapes
        + [
            pltpu.VMEM((TOK, d), BF16),
            pltpu.VMEM((8, 128), jnp.int32),
            pltpu.VMEM((8, 128), jnp.int32),
            pltpu.VMEM((TOK, d), F32),
            pltpu.VMEM((4, TOK, d), BF16),
            pltpu.VMEM((4, TOK, d), BF16),
            pltpu.VMEM((4, TOK, GROUP), BF16),
            pltpu.VMEM((WIDE, 4 * TOK), BF16),
            pltpu.VMEM((LAYERS, 4, 192, TOK), F32),
            pltpu.VMEM((LAYERS, 4, 8, TOK), F32),
            pltpu.VMEM((LAYERS, 4, 192, TOK), BF16),
            pltpu.VMEM((d, TOK), BF16),
            pltpu.VMEM((d, TOK), BF16),
            pltpu.VMEM((TOK, ff), F32),
            pltpu.VMEM((TOK, ff), BF16),
            pltpu.VMEM((ff, TOK), BF16),
            pltpu.VMEM((d, 4 * TOK), BF16),
            pltpu.VMEM((d, TOK), BF16),
            pltpu.VMEM((TOK, d), BF16),
            pltpu.VMEM((TOK, d), F32),
            pltpu.VMEM((TOK, d), BF16),
        ]
        + [dma(2 * JOBS * Gather.SEMS), dma(2 * JOBS * Gather.SEMS), dma(2 * JOBS), dma(20), dma(8), dma(8), dma(8), dma(8), dma(4), dma(4)],
        compiler_params=pltpu.CompilerParams(collective_id=0, has_side_effects=True, vmem_limit_bytes=62 * 2**20),
    )(tok, cot, lengths, w_qkv, w_out, w_up, w_down, gains, biases)
    at = 4 + 2 * JOBS
    return outs[:4], outs[4:at], (outs[at : at + 10], outs[at + 10 : at + 20])


class Reduce:
    SEMS = 10

    def __init__(self, send, bufs, out, ssem, rsem, base, paired=False):
        self.send = send
        self.got, self.half, self.near = bufs[:3]
        self.zs, self.zr = bufs[3:5]
        self.out = out
        self.ssem, self.rsem, self.base = ssem, rsem, base
        self.rows, self.width = self.got.shape[1], self.got.shape[2]
        self.split, self.paired = self.zs.shape[1] == 16, paired
        self.sent = []

    def _copy(self, src, dst, at, device):
        return rcopy(src, dst, self.ssem.at[self.base + at], self.rsem.at[self.base + at], device)

    def _send(self, src, dst, at, device):
        copy = self._copy(src, dst, at, device)
        copy.start()
        self.sent.append(copy)

    def _got(self, core):
        if self.paired:
            return self.got.at[:, :, cols(core, self.width // 2)]
        return self.got

    def send_core(self):
        r, z, rx, ry, rd, rc = places_of()
        self._send(self.send, self._got(lax.rem(r, 2)), 0, (rc, z))

    def wait_core(self):
        r, z, rx, ry, rd, rc = places_of()
        ref = self._got(lax.rem(rc, 2))
        self._copy(ref, ref, 0, (rc, z)).wait_recv()

    def _part(self, other, i):
        part = self.rows // 2
        return self.got.at[lax.div(other, 2), pl.ds(i * part, part)]

    def send_first(self):
        r, z, rx, ry, rd, rc = places_of()
        part = self.rows // 2
        self._send(self._part(rd, 0), self.half.at[0], 1, (ry, z))
        self._send(self._part(rd, 1), self.half.at[1], 2, (rx, z))

    def send_second(self):
        r, z, rx, ry, rd, rc = places_of()
        part = self.rows // 2
        self._send(self._part(rx, 1), self.near.at[0, pl.ds(part, part)], 3, (rx, z))
        self._send(self._part(ry, 0), self.near.at[1, pl.ds(0, part)], 4, (ry, z))

    def send_near(self):
        r, z, rx, ry, rd, rc = places_of()
        part = self.rows // 2
        for i, side, other in ((0, ry, rx), (1, rx, ry)):
            self._copy(self.half.at[i], self.half.at[i], 1 + i, (side, z)).wait_recv()
            block = self._part(other, i)
            add_rows(block, self.half.at[i], part)
            self._send(block, self.near.at[i, pl.ds(i * part, part)], 5 + i, (other, z))

    def send_z(self):
        r, z, rx, ry, rd, rc = places_of()
        part = self.rows // 2
        for at, i, h, side in ((3, 0, 1, rx), (4, 1, 0, ry), (5, 0, 0, rx), (6, 1, 1, ry)):
            ref = self.near.at[i, pl.ds(h * part, part)]
            self._copy(ref, ref, at, (side, z)).wait_recv()
        own = self.got.at[lax.div(r, 2)]
        near = self.near

        def total(rows, here):
            return own[rows, here].astype(F32) + near[0, rows, here].astype(F32) + near[1, rows, here].astype(F32)

        if self.split:
            half = self.width // 2
            step = col_step(half)

            def cut(i):
                at = pl.ds(pl.multiple_of(self.width + i * step, 128), step)
                sums = [
                    total(slice(None), pl.ds(pl.multiple_of(side * half + i * step, 128), step)) for side in (0, 1)
                ]
                for piece in range(ZN):
                    for side in (0, 1):
                        here = pl.ds(pl.multiple_of(side * half + i * step, 128), step)
                        self.zs[piece, :, here] = sums[side][24 * piece : 24 * piece + 16].astype(BF16)
                    self.zs[piece, :, at] = jnp.concatenate(
                        [sums[side][24 * piece + 16 : 24 * piece + 24] for side in (0, 1)], 0
                    ).astype(BF16)
            loop(half // step, cut)
        else:
            size = self.rows // ZN
            for piece in range(ZN):
                def cut_rows(i, piece=piece):
                    self.zs[piece, band(i * 16, 16), :] = total(band(piece * size + i * 16, 16), slice(None)).astype(BF16)
                loop(size // 16, cut_rows)
        for k in (1, 2, 3):
            self._send(self.zs.at[turn(z, k)], self.zr.at[k - 1], 6 + k, (r, turn(z, k)))

    def finish(self):
        r, z = places_of()[:2]
        for k in (1, 2, 3):
            ref = self.zr.at[k - 1]
            self._copy(ref, ref, 6 + k, (r, turn(z, ZN - k))).wait_recv()
        half, width = self.width // 2, self.width
        if self.paired:
            for place, value in (
                (lax.rem(z, 2), self.zs[z].astype(F32) + self.zr[1].astype(F32)),
                (lax.rem(z + 1, 2), self.zr[0].astype(F32) + self.zr[2].astype(F32)),
            ):
                for side in (0, 1):
                    here = cols(place + 2 * side, GROUP)
                    self.out[pl.ds(0, 16), here] = value[:, side * GROUP : (side + 1) * GROUP]
                    self.out[pl.ds(16, 8), here] = value[8 * side : 8 * side + 8, width:]
        elif self.split:
            value = self.zs[z].astype(F32)
            for k in range(3):
                value = value + self.zr[k].astype(F32)
            self.out[pl.ds(0, 16), :] = value[:, :width]
            self.out[pl.ds(16, 8), pl.ds(0, half)] = value[:8, width:]
            self.out[pl.ds(16, 8), pl.ds(half, half)] = value[8:, width:]
        else:
            def total(i):
                here = band(i * 16, 16)
                value = self.zs[z, here, :].astype(F32)
                for k in range(3):
                    value = value + self.zr[k, here, :].astype(F32)
                self.out[here, :] = value
            loop(self.out.shape[0] // 16, total)

    def drain(self):
        for copy in self.sent:
            copy.wait_send()
        self.sent = []


def left_rows(left, c):
    return jnp.concatenate([left[band((2 * b + c) * 96, 96), :] for b in range(4)], 0)


def norm_back(source, upstream, gain, add, out, low, sums):
    sums[...] = jnp.zeros_like(sums)

    def step(n):
        here = band(n * CHUNK, CHUNK)
        value = source[here, :]
        center = value - jnp.mean(value, -1, keepdims=True)
        scale = lax.rsqrt(jnp.mean(center * center, -1, keepdims=True) + EPSILON)
        normal = center * scale
        up = upstream(here)
        sums[0:8, :] += fold_rows(up * normal, jnp.add)
        sums[8:16, :] += fold_rows(up, jnp.add)
        up = up * gain
        inner = up - jnp.mean(up, -1, keepdims=True) - normal * jnp.mean(up * normal, -1, keepdims=True)
        total = add[here, :] + inner * scale
        out[here, :] = total
        low[here, :] = total.astype(BF16)
    loop(TOK // CHUNK, step)
    gain_grad = jnp.sum(sums[0:8, :], 0, keepdims=True)
    bias_grad = jnp.sum(sums[8:16, :], 0, keepdims=True)
    return gain_grad, bias_grad


def gelu_slope(x):
    root = 0.7978845608028654
    square = x * x
    bend = jnp.tanh(root * (x + 0.044715 * x * square))
    return 0.5 * (1.0 + bend) + 0.5 * x * (1.0 - bend * bend) * root * (1.0 + 3 * 0.044715 * square)


def attend_quarter_back(i, lens, qkv, kt, datt, out, stats, scratch, signed):
    dk, dv, dq = scratch
    places, start, live = starts_of(lens, i)
    queries = qkv[i, :, 0:WIDE].astype(F32) * 0.125
    mine = masked_heads(queries.T, 0)
    mine_rows = jnp.concatenate(
        [jnp.where(head_lanes((TOK, WIDE), h, 0), queries, 0.0).astype(BF16) for h in range(PARTS)], 0
    )
    upstream = datt[i].astype(F32)
    grads_t = jnp.concatenate([jnp.zeros((HEAD, TOK), F32), upstream], 0)
    out_t = masked_heads(grads_t, 1)
    grads = grads_t.T
    out_rows = jnp.concatenate(
        [jnp.where(head_lanes((TOK, WIDE), h, 1), grads, 0.0).astype(BF16) for h in range(PARTS)], 0
    )
    product = upstream * out[i].astype(F32)
    inner = [
        jnp.sum(fold_rows(product[HEAD * h : HEAD * (h + 1)], jnp.add), 0, keepdims=True) for h in range(PARTS)
    ]
    top = [stats[i, h : h + 1, :] for h in range(PARTS)]
    inverse = [stats[i, PARTS + h : PARTS + h + 1, :] for h in range(PARTS)]
    dq[...] = jnp.zeros_like(dq)

    def block(first, carry, diagonal):
        keys = key_rows(qkv, first, 384)
        values = key_rows(qkv, first, 128)
        okay = masked_rows(first, KB, places, start, diagonal)
        here = pl.ds(pl.multiple_of(first, KB), KB)
        lows, slopes = [], []
        scores = [dot(keys, mine[:, h * TOK : (h + 1) * TOK]) for h in range(PARTS)]
        gains = [dot(values, out_t[:, h * TOK : (h + 1) * TOK]) for h in range(PARTS)]
        for h in range(PARTS):
            s, dp = scores[h], gains[h]
            if signed:
                size, back = magnitude_of(s)
                unsigned = jnp.exp(jnp.where(okay, size - top[h], FAR)) * inverse[h]
                bend = jnp.tanh(s)
                lows.append((unsigned * bend).astype(BF16))
                slope = unsigned * ((bend * dp - inner[h]) * (s * back) + dp * (1.0 - bend * bend))
            else:
                unsigned = jnp.exp(jnp.where(okay, s - top[h], FAR)) * inverse[h]
                lows.append(unsigned.astype(BF16))
                slope = unsigned * (dp - inner[h])
            slopes.append(slope.astype(BF16))
        value_terms = dot(jnp.concatenate(lows, 1), out_rows)
        key_terms = dot(jnp.concatenate(slopes, 1), mine_rows)
        query_terms = [dot(kt[HEAD * h : HEAD * (h + 1), here], slopes[h]) for h in range(PARTS)]
        dv[here, :] += value_terms
        dk[here, :] += key_terms
        for h in range(PARTS):
            dq[HEAD * h : HEAD * (h + 1), :] += query_terms[h]
        return carry
    over_blocks(i, block, 0)
    query_grad = jnp.concatenate([dq[...] * 0.125, jnp.zeros((HEAD, TOK), F32)], 0).T
    value_grad = dv[i * TOK : (i + 1) * TOK, :]
    key_grad = dk[i * TOK : (i + 1) * TOK, :]
    lanes = lax.broadcasted_iota(jnp.int32, (TOK, 128), 1)
    return jnp.concatenate(
        [
            query_grad[:, :128],
            jnp.where(lanes < HEAD, query_grad[:, 128:], value_grad[:, :128]),
            value_grad[:, 128:],
            key_grad,
        ],
        1,
    ).astype(BF16)


EDGE = 256


def reduce_shapes(d, ff):
    return [(96, 2 * GROUP), (96, d), (96, ff // 2), (96, ff // 2), (ff // 8, d // 2), (ff // 8, d // 2), (96, EDGE)]


def backward_kernel(*refs):
    refs = list(refs)
    take = lambda n: [refs.pop(0) for _ in range(n)]
    cot, lens, norms = take(3)
    wholes = take(2 * JOBS)
    stash = [take(10), take(10)]
    (input_o,) = take(1)
    grads_o = take(4)
    (edge_o,) = take(1)
    weights = take(JOBS)
    homes = take(10)
    stream, qkv, middle, nin_t, att_t, nmid_t, pre, act_t, att_out, stats = homes
    w_qkv, w_out, w_up0, w_up1, w_down0, w_down1 = weights
    cot_v, grad, low, branch, dpre, dmid, sums, edges, datt_s, datt_r, kt, dk, dv, dq, dqkv, pn_s, pn_r = take(17)
    sends = take(JOBS + 1)
    buffers = [take(5) for n in range(JOBS + 1)]
    ssem, rsem, lsem, csem, as_, ar, ps, pr, ms, mr = take(10)
    spot = Spot()
    r, z, rx, ry, rd, rc = spot.r, spot.z, spot.rx, spot.ry, spot.rd, spot.rc
    loads = {}

    def load(layer, *names):
        for name in names:
            if name in STASH:
                at = STASH.index(name)
                src, dst = stash[layer][at], homes[at]
            else:
                src, dst = wholes[JOBS * layer + name], weights[name]
                at = 10 + name
            loads[(layer, name)] = Keep(src, dst, lsem.at[(10 + JOBS) * layer + at])

    def ready(layer, *names):
        for name in names:
            loads[(layer, name)].wait()

    def free(layer, *names):
        if layer:
            load(0, *names)

    start = Keep(cot, cot_v, lsem.at[2 * (10 + JOBS)])
    load(1, "act_t", 4, 5, "pre", "nmid_t", 2, 3, "middle", 1, "att_t", "qkv", "out", "stats", "nin_t", 0, "stream")
    greet(spot.peers())
    peers = comm_peers()
    jobs = []
    for layer in range(LAYERS):
        qkv_g, out_g, up_g, down_g = [ref.at[layer] for ref in grads_o]
        ff, d = up_g.shape[1] // 2, down_g.shape[1] // 2
        outs = [qkv_g, out_g] + [up_g.at[:, h * ff : (h + 1) * ff] for h in (0, 1)] + [down_g.at[:, h * d : (h + 1) * d] for h in (0, 1)]
        for n, out in enumerate(outs):
            jobs.append(Reduce(sends[n], buffers[n], out, ssem, rsem, (JOBS * layer + n) * Reduce.SEMS, n == 0))
    jobs.append(Reduce(sends[JOBS], buffers[JOBS], edge_o, ssem, rsem, 2 * JOBS * Reduce.SEMS))
    steps = {}

    def step(name):
        def note(run):
            steps[name] = run
        return note

    for at, job in enumerate(jobs):
        def close(job=job, at=at):
            job.finish()
            if JOBS <= at < 2 * JOBS:
                job.drain()
                for peer in peers:
                    pl.semaphore_signal(csem.at[at - JOBS], inc=1, device_id=peer, device_id_type=MESH)
        steps.update({SECOND + at: job.send_second, NEAR + at: job.send_near, OVER_Z + at: job.send_z, CLOSE + at: close})

    def credit(at):
        if at < JOBS:
            pl.semaphore_wait(csem.at[at], len(peers))

    @step(BEGIN)
    def _():
        def begin(n):
            here = band(n * CHUNK, CHUNK)
            value = cot_v[here, :].astype(F32) * live_column(lens, spot, CHUNK, n * CHUNK)
            grad[here, :] = value
            low[here, :] = value.astype(BF16)
        start.wait()
        loop(TOK // CHUNK, begin)

    def terms(job, left, tile, right, other):
        c = lax.rem(rc, 2) if other else spot.c
        rows = left_rows(left, c)
        width = job.width // 2 if job.paired else job.width

        def part(n):
            here = cols(n, tile)
            value = dot(rows, right(n))
            for b in range(4):
                piece = value[96 * b : 96 * b + 96]
                if other:
                    job.send[b, :, here] = piece.astype(BF16)
                elif job.paired:
                    job.got[b, :, cols(spot.c, GROUP)] = piece.astype(BF16)
                else:
                    job.got[b, :, here] = (job.got[b, :, here].astype(F32) + piece).astype(BF16)
        if width == tile:
            part(0)
        else:
            loop(width // tile, part)

    def down_terms(job, right, other):
        c = lax.rem(rc, 2) if other else spot.c

        def part(b):
            value = dot(act_t[band((2 * b + c) * 384, 384), :], right())
            if other:
                job.send[b] = value.astype(BF16)
            else:
                job.got[b] = (job.got[b].astype(F32) + value).astype(BF16)
        loop(4, part)

    late = {}

    def layer_steps(layer):
        base = JOBS * layer
        signed = layer == 0
        gains = norms.at[layer]

        def both(at, needs, compute, after=()):
            job = jobs[at]

            def theirs():
                ready(layer, *needs)
                credit(at)
                compute(job, True)
                job.send_core()

            def ours():
                job.wait_core()
                compute(job, False)
                free(layer, *after)
                job.send_first()
            steps[THEIRS + at] = theirs
            steps[OURS + at] = ours

        for h in (0, 1):
            half = w_down0.shape[1]
            both(
                base + 4 + h,
                ["act_t"],
                lambda job, other, h=h: down_terms(job, lambda: low[:, h * half : (h + 1) * half], other),
                ["act_t"] if h else [],
            )
            ff = w_up0.shape[1]
            both(
                base + 2 + h,
                ["nmid_t"],
                lambda job, other, h=h: terms(job, nmid_t, 512, lambda n: dpre[:, cols(n + h * (ff // 512), 512)], other),
                ["nmid_t"] if h else [],
            )
        both(base + 1, ["att_t"], lambda job, other: terms(job, att_t, 256, lambda n: branch[:, cols(n, 256)], other), ["att_t"])
        both(
            base,
            ["nin_t"],
            lambda job, other: terms(job, nin_t, GROUP, lambda n: dqkv[...].reshape(4 * TOK, GROUP), other),
            ["nin_t"],
        )

        def slope(h):
            def run():
                ready(layer, 4, 5, "pre")
                half = w_down0.shape[1]

                def part(n):
                    here = cols(n, 512)
                    rows = pl.ds(pl.multiple_of(n * 512, 512), 512)
                    value = dot_nt(low[:, :half], w_down0[rows, :]) + dot_nt(low[:, half:], w_down1[rows, :])
                    dpre[:, here] = (gelu_slope(pre[:, here]) * value).astype(BF16)
                lax.fori_loop(3 * h, 3 * h + 3, lambda n, carry: (part(n), carry)[1], 0)
                if h:
                    free(layer, 4, 5, "pre")
            return run
        steps[SLOPE + 10 * layer + 0] = slope(0)
        steps[SLOPE + 10 * layer + 1] = slope(1)

        def through(h):
            w_up = (w_up0, w_up1)[h]

            def run():
                ready(layer, 2 + h)
                if h == 0:
                    dmid[...] = jnp.zeros_like(dmid)
                count = w_up.shape[1] // 512

                def part(n):
                    dmid[...] += dot_nt(dpre[:, cols(n + h * count, 512)], w_up[:, cols(n, 512)])
                loop(count, part)
                free(layer, 2 + h)
            return run
        steps[THROUGH + 10 * layer + 0] = through(0)
        steps[THROUGH + 10 * layer + 1] = through(1)

        @step(NORM_BACK + layer)
        def _():
            ready(layer, "middle")
            late[layer] = norm_back(middle, lambda here: dmid[here, :], gains[2:3, :], grad, grad, branch, sums)
            free(layer, "middle")

        def asked(g, which=layer):
            return rcopy(
                datt_s.at[g], datt_r.at[spot.member], as_.at[4 * which + g], ar.at[4 * which + spot.member], spot.device(g)
            )

        @step(ASK + layer)
        def _():
            ready(layer, 1)
            for g in range(4):
                value = dot_nt(w_out[192 * g : 192 * g + 192, :], branch[...]).astype(BF16)
                if layer == 0:
                    @pl.when(spot.member != g)
                    def _():
                        asked(g, 1).wait_send()
                datt_s[g] = value

                @pl.when(spot.member != g)
                def _():
                    asked(g).start()

                @pl.when(spot.member == g)
                def _():
                    datt_r[g] = datt_s[g]
            free(layer, 1)

        @step(KEYS + layer)
        def _():
            ready(layer, "qkv", "out", "stats")

            def turn_keys(j):
                kt[:, cols(j, TOK)] = qkv[j, :, 384:640].astype(F32).T.astype(BF16)
            loop(4, turn_keys)
            dk[...] = jnp.zeros_like(dk)
            dv[...] = jnp.zeros_like(dv)

        @step(ASKED + layer)
        def _():
            for g in range(4):
                @pl.when(spot.member != g)
                def _():
                    rcopy(datt_r.at[g], datt_r.at[g], as_.at[4 * layer + g], ar.at[4 * layer + g], spot.device(g)).wait_recv()

        def back(i):
            def run():
                dqkv[i] = attend_quarter_back(i, lens, qkv, kt, datt_r, att_out, stats, (dk, dv, dq), signed)
                if i == 0:
                    free(layer, "qkv", "out", "stats")
            return run
        for i in range(4):
            steps[ATTEND_BACK + 10 * layer + i] = back(i)

        def given(which, k):
            mate = spot.mate(1 if k == 1 else 2)[0]
            src = pn_s.at[k - 1]
            return rcopy(src, pn_r.at[k - 1], ps.at[4 * which + k], pr.at[4 * which + k], mate)

        def partial(member):
            return dot_nt(dqkv[member], w_qkv[...])

        @step(PARTIAL + 10 * layer + 2)
        def _():
            ready(layer, 0)
            if layer == 0:
                given(1, 2).wait_send()
            pn_s[1] = partial(spot.mate(3)[1]).astype(BF16)
            given(layer, 2).start()

        @step(PARTIAL + 10 * layer + 3)
        def _():
            if layer == 0:
                given(1, 3).wait_send()
            pn_s[2] = partial(spot.mate(2)[1]).astype(BF16)
            given(layer, 3).start()

        @step(PARTIAL + 10 * layer + 1)
        def _():
            value = partial(spot.mate(1)[1])
            if layer == 0:
                given(1, 1).wait_send()
            given(layer, 2).wait_recv()
            pn_s[0] = (value + pn_r[1].astype(F32)).astype(BF16)
            given(layer, 1).start()
            dmid[...] = partial(spot.member)
            free(layer, 0)

        @step(FIRST_BACK + layer)
        def _():
            ready(layer, "stream")
            given(layer, 3).wait_recv()
            given(layer, 1).wait_recv()

            def upstream(here):
                return dmid[here, :] + pn_r[2, here, :].astype(F32) + pn_r[0, here, :].astype(F32)
            early = norm_back(stream, upstream, gains[0:1, :], grad, grad, low, sums)
            free(layer, "stream")
            for n, value in enumerate(early + late[layer]):
                edges[4 * layer + n : 4 * layer + n + 1, :] = value

    for layer in (1, 0):
        layer_steps(layer)

    @step(SWAP_BACK)
    def _():
        swap(spot, low, input_o, ms.at[0], mr.at[0])

    last = 2 * JOBS

    def edge_rows(c):
        turned = jnp.concatenate([edges[...], jnp.zeros((128 - 8, edges.shape[1]), F32)], 0).T
        return [
            jnp.where(c == 0, turned[192 * b : 192 * b + 96], turned[192 * b + 96 : 192 * b + 192]) for b in range(4)
        ]

    @step(THEIRS + last)
    def _():
        job = jobs[last]
        for b, rows in enumerate(edge_rows(lax.rem(rc, 2))):
            job.send[b, :, 0:128] = rows.astype(BF16)
            job.send[b, :, 128:256] = jnp.zeros((96, 128), BF16)
        job.send_core()

    @step(OURS + last)
    def _():
        job = jobs[last]
        job.wait_core()
        for b, rows in enumerate(edge_rows(spot.c)):
            job.got[b, :, 0:128] = (job.got[b, :, 0:128].astype(F32) + rows).astype(BF16)
        job.send_first()

    for name in BACKWARD_ORDER:
        steps.pop(name)()
    assert not steps
    for job in jobs:
        job.drain()
    for g in range(4):
        @pl.when(spot.member != g)
        def _():
            rcopy(
                datt_s.at[g], datt_r.at[spot.member], as_.at[g], ar.at[spot.member], spot.device(g)
            ).wait_send()
    for k in (1, 2, 3):
        mate = spot.mate(1 if k == 1 else 2)[0]
        rcopy(pn_s.at[k - 1], pn_r.at[k - 1], ps.at[k], pr.at[k], mate).wait_send()
    swap_wait(spot, low, input_o, ms.at[0], mr.at[0])


def backward_call(cot, lens, norms, wholes, stash):
    d, ff = cot.shape[1], stash[0][6].shape[1]
    any_space = pl.BlockSpec(memory_space=pl.ANY)
    vmem = pl.BlockSpec(memory_space=pltpu.VMEM)
    dma = lambda n: pltpu.SemaphoreType.DMA((n,))
    shapes = reduce_shapes(d, ff)
    sends, buffers = [], []
    for n, (rows, width) in enumerate(shapes):
        sends.append(pltpu.VMEM((4, rows, width // 2 if n == 0 else width), BF16))
        cut = (rows // 4, width) if n in (4, 5) else (16, width * 3 // 2)
        buffers += [
            pltpu.VMEM((4, rows, width), BF16),
            pltpu.VMEM((2, rows // 2, width), BF16),
            pltpu.VMEM((2, rows, width), BF16),
        ]
        buffers += [pltpu.VMEM((4,) + cut, BF16), pltpu.VMEM((3,) + cut, BF16)]
    count = 2 * JOBS + 1
    outs = pl.pallas_call(
        backward_kernel,
        out_shape=[
            jax.ShapeDtypeStruct((TOK, d), BF16),
            jax.ShapeDtypeStruct((LAYERS, 24, 4 * GROUP), F32),
            jax.ShapeDtypeStruct((LAYERS, 24, d), F32),
            jax.ShapeDtypeStruct((LAYERS, 24, ff), F32),
            jax.ShapeDtypeStruct((LAYERS, ff // 32, d), F32),
            jax.ShapeDtypeStruct((24, EDGE), F32),
        ],
        in_specs=[any_space, vmem, vmem] + [any_space] * (2 * JOBS + 20),
        out_specs=[any_space] + [vmem] * 5,
        scratch_shapes=[pltpu.VMEM(whole.shape, BF16) for whole in wholes[:JOBS]]
        + [pltpu.VMEM(shape, kind) for shape, kind in stash_shapes(d, ff)]
        + [
            pltpu.VMEM((TOK, d), BF16),
            pltpu.VMEM((TOK, d), F32),
            pltpu.VMEM((TOK, d), BF16),
            pltpu.VMEM((TOK, d), BF16),
            pltpu.VMEM((TOK, ff), BF16),
            pltpu.VMEM((TOK, d), F32),
            pltpu.VMEM((16, d), F32),
            pltpu.VMEM((8, d), F32),
            pltpu.VMEM((4, 192, TOK), BF16),
            pltpu.VMEM((4, 192, TOK), BF16),
            pltpu.VMEM((WIDE, 4 * TOK), BF16),
            pltpu.VMEM((4 * TOK, WIDE), F32),
            pltpu.VMEM((4 * TOK, WIDE), F32),
            pltpu.VMEM((192, TOK), F32),
            pltpu.VMEM((4, TOK, GROUP), BF16),
            pltpu.VMEM((3, TOK, d), BF16),
            pltpu.VMEM((3, TOK, d), BF16),
        ]
        + sends
        + buffers
        + [
            dma(count * Reduce.SEMS),
            dma(count * Reduce.SEMS),
            dma(2 * (10 + JOBS) + 1),
            pltpu.SemaphoreType.REGULAR((JOBS,)),
            dma(8),
            dma(8),
            dma(8),
            dma(8),
            dma(1),
            dma(1),
        ],
        compiler_params=pltpu.CompilerParams(collective_id=1, has_side_effects=True, vmem_limit_bytes=62 * 2**20),
    )(cot, lens, norms, *wholes, *stash[0], *stash[1])
    return outs


def finish_kernel(result, grad_in, qkv, out, up, down, edge, result_o, input_o, qkv_o, out_o, up_o, down_o, gains_o, biases_o, mids_o):
    result_o[0] = result[...]
    input_o[0] = grad_in[...].astype(F32)
    out_o[...] = out[...]
    up_o[...] = up[...]
    down_o[...] = down[...]
    own = edge.shape[0]
    turned = jnp.concatenate([edge[:, 0:128], jnp.zeros((128 - own, 128), F32)], 0).T
    for layer in range(LAYERS):
        parts = [
            qkv[layer, :, GROUP * g + at : GROUP * g + at + 192] for at in (0, 384, 192) for g in range(4)
        ]
        qkv_o[layer] = jnp.concatenate(parts, 1)
        for n, ref in enumerate((gains_o.at[layer, 0:1], biases_o.at[layer : layer + 1], gains_o.at[layer, 1:2], mids_o.at[layer : layer + 1])):
            ref[...] = turned[4 * layer + n : 4 * layer + n + 1, 0:own]


def backward_part(result, cot, lens, norms, wholes, stash):
    grads = backward_call(cot, lens, norms, wholes, stash)
    d, own = cot.shape[1], grads[1].shape[1]
    shape = lambda *sizes: jax.ShapeDtypeStruct(sizes, F32)
    return pl.pallas_call(
        finish_kernel,
        out_shape=[
            jax.ShapeDtypeStruct((1, TOK, d), BF16),
            shape(1, TOK, d),
            shape(LAYERS, own, 3 * d),
            shape(*grads[2].shape),
            shape(*grads[3].shape),
            shape(*grads[4].shape),
            shape(LAYERS, 2, own),
            shape(LAYERS, own),
            shape(LAYERS, own),
        ],
        in_specs=[pl.BlockSpec(memory_space=pltpu.VMEM)] * 7,
        out_specs=[pl.BlockSpec(memory_space=pltpu.VMEM)] * 9,
        compiler_params=pltpu.CompilerParams(vmem_limit_bytes=62 * 2**20),
    )(result, *grads)


def local_fast(tokens, lengths, w_qkv, w_out, w_up, w_down, gains, biases, cotangent):
    (result, cot, lens, norms), wholes, stash = forward_call(
        tokens[0], cotangent[0], lengths, w_qkv, w_out, w_up, w_down, gains, biases
    )
    return tuple(backward_part(result, cot, lens, norms, wholes, stash))


def solution(mesh):
    in_specs = (
        P("rows", "kv", None),
        P("rows", None),
        P(None, ("rows", "kv"), None),
        P(None, ("rows", "kv"), None),
        P(None, ("rows", "kv"), None),
        P(None, ("rows", "kv"), None),
        P(None, None, ("rows", "kv")),
        P(None, None, ("rows", "kv")),
        P("rows", "kv", None),
    )
    out_specs = (
        P("rows", "kv", None),
        P("rows", "kv", None),
        P(None, ("rows", "kv"), None),
        P(None, ("rows", "kv"), None),
        P(None, ("rows", "kv"), None),
        P(None, ("rows", "kv"), None),
        P(None, None, ("rows", "kv")),
        P(None, ("rows", "kv")),
        P(None, ("rows", "kv")),
    )
    fast = dict(mesh.shape) == {"rows": 8, "kv": 4}
    return jax.shard_map(local_fast if fast else local_generic, mesh=mesh, in_specs=in_specs, out_specs=out_specs, check_vma=False)
```

```python
import math

import jax
import jax.numpy as jnp
from jax import lax
from jax.experimental import pallas as pl
from jax.experimental.pallas import tpu as pltpu
from jax.sharding import PartitionSpec as P

HEADS = 12
HEAD = 64
LAYERS = 2


EPSILON = 1e-05


def norm_rows(stream, gain, bias):
    center = stream - jnp.mean(stream, -1, keepdims=True)
    spread = jnp.mean(center * center, -1, keepdims=True)
    return center * lax.rsqrt(spread + EPSILON) * gain + bias


def normalise(scores, allowed, query_live, signed):
    if signed:
        magnitude = jnp.sqrt(scores * scores + 1.0)
        ceiling = jnp.max(jnp.where(allowed > 0, magnitude, 0.0), -1, keepdims=True)
        shifted = jnp.where(allowed > 0, magnitude - ceiling, -60.0)
    else:
        ceiling = jnp.max(jnp.where(allowed > 0, scores, -10000.0), -1, keepdims=True)
        shifted = jnp.where(allowed > 0, scores - ceiling, -60.0)
    raised = jnp.exp(shifted) * allowed
    normaliser = jnp.sum(raised, -1, keepdims=True) + (1.0 - query_live)[None, :, None]
    unsigned_w = raised / normaliser
    if signed:
        return (jnp.tanh(scores) * unsigned_w, unsigned_w)
    return (unsigned_w, unsigned_w)


def make_mask(query_places, query_docs, query_live, key_places, key_docs, key_live):
    allowed = (
        (query_docs[:, None] == key_docs[None, :]) & (key_places[None, :] <= query_places[:, None])
    ).astype(jnp.float32)
    return allowed * query_live[:, None] * key_live[None, :]


def split_heads(query, keys_vals):
    model_width = query.shape[-1]
    slot_count = keys_vals.shape[0]
    query_heads = query.reshape(-1, HEADS, HEAD)
    key_heads = keys_vals[:, :model_width].reshape(slot_count, HEADS, HEAD)
    value_heads = keys_vals[:, model_width:].reshape(slot_count, HEADS, HEAD)
    return (query_heads, key_heads, value_heads)


def score_grads(scores, unsigned_w, weight_grad, inner_sum, signed):
    if signed:
        tanh_s = jnp.tanh(scores)
        magnitude = jnp.sqrt(scores * scores + 1.0)
        return unsigned_w * (
            (tanh_s * weight_grad - inner_sum) * scores / magnitude
            + weight_grad * (1.0 - tanh_s * tanh_s)
        )
    return unsigned_w * (weight_grad - inner_sum)


def attend_row(query, keys_vals, allowed, query_live, signed, scaling):
    query_heads, key_heads, value_heads = split_heads(query, keys_vals)
    scores = (
        jnp.einsum("qhd,khd->hqk", query_heads, key_heads, preferred_element_type=jnp.float32)
        * scaling
    )
    weights, unsigned_w = normalise(scores, allowed, query_live, signed)
    outcome = jnp.einsum(
        "hqk,khd->qhd",
        weights.astype(jnp.bfloat16),
        value_heads,
        preferred_element_type=jnp.float32,
    )
    return outcome.reshape(query.shape[0], query.shape[1]).astype(jnp.bfloat16)


def attend_back(query, keys_vals, grad_att, allowed, query_live, signed, scaling):
    query_heads, key_heads, value_heads = split_heads(query, keys_vals)
    slot_count = keys_vals.shape[0]
    model_width = query.shape[-1]
    scores = (
        jnp.einsum("qhd,khd->hqk", query_heads, key_heads, preferred_element_type=jnp.float32)
        * scaling
    )
    weights, unsigned_w = normalise(scores, allowed, query_live, signed)
    weights_low = weights.astype(jnp.bfloat16)
    grad_heads = grad_att.reshape(-1, HEADS, HEAD)
    weight_grad = jnp.einsum(
        "qhd,khd->hqk", grad_heads, value_heads, preferred_element_type=jnp.float32
    )
    inner_sum = jnp.sum(weight_grad * weights, -1, keepdims=True)
    score_low = score_grads(scores, unsigned_w, weight_grad, inner_sum, signed).astype(jnp.bfloat16)
    query_grad = (
        jnp.einsum("hqk,khd->qhd", score_low, key_heads, preferred_element_type=jnp.float32)
        * scaling
    )
    key_grad = (
        jnp.einsum("hqk,qhd->khd", score_low, query_heads, preferred_element_type=jnp.float32)
        * scaling
    )
    value_grad = jnp.einsum(
        "hqk,qhd->khd", weights_low, grad_heads, preferred_element_type=jnp.float32
    )
    kv_grad = jnp.concatenate(
        [key_grad.reshape(slot_count, model_width), value_grad.reshape(slot_count, model_width)], -1
    )
    return (query_grad.reshape(query.shape[0], model_width), kv_grad)


def reduce_grads(pairs, g_gain, g_bias):
    n_rows = lax.axis_size("rows")
    n_kv = lax.axis_size("kv")
    lefts = []
    rights = []
    for left_side, right_side in pairs:
        tok_count = left_side.shape[0] * left_side.shape[1]
        in_width = left_side.shape[-1]
        lefts.append(left_side.reshape(tok_count, n_rows, n_kv, in_width // (n_rows * n_kv)))
        rights.append(right_side.reshape(tok_count, right_side.shape[-1]))
    moved = (
        lax.all_to_all(lefts[0], "kv", split_axis=2, concat_axis=0, tiled=True),
        lax.all_to_all(lefts[1], "kv", split_axis=2, concat_axis=0, tiled=True),
        lax.all_to_all(lefts[2], "kv", split_axis=2, concat_axis=0, tiled=True),
        lax.all_to_all(lefts[3], "kv", split_axis=2, concat_axis=0, tiled=True),
    )
    whole = (
        lax.all_gather(rights[0], "kv", axis=0, tiled=True),
        lax.all_gather(rights[1], "kv", axis=0, tiled=True),
        lax.all_gather(rights[2], "kv", axis=0, tiled=True),
        lax.all_gather(rights[3], "kv", axis=0, tiled=True),
    )
    partial_sums = []
    for number in range(4):
        left_block = moved[number].reshape(moved[number].shape[0], -1)
        product = jnp.einsum(
            "ti,to->io", left_block, whole[number], preferred_element_type=jnp.float32
        )
        partial_sums.append(product.reshape(n_rows, -1, product.shape[-1]))
    reduced = (
        lax.psum_scatter(
            partial_sums[0].astype(jnp.bfloat16), "rows", scatter_dimension=0, tiled=True
        ).astype(jnp.float32),
        lax.psum_scatter(
            partial_sums[1].astype(jnp.bfloat16), "rows", scatter_dimension=0, tiled=True
        ).astype(jnp.float32),
        lax.psum_scatter(
            partial_sums[2].astype(jnp.bfloat16), "rows", scatter_dimension=0, tiled=True
        ).astype(jnp.float32),
        lax.psum_scatter(
            partial_sums[3].astype(jnp.bfloat16), "rows", scatter_dimension=0, tiled=True
        ).astype(jnp.float32),
    )
    norm_parts = (
        lax.psum_scatter(g_gain, ("rows", "kv"), scatter_dimension=1, tiled=True),
        lax.psum_scatter(g_bias, ("rows", "kv"), scatter_dimension=1, tiled=True),
    )
    results = tuple((piece.reshape(piece.shape[1], piece.shape[2]) for piece in reduced))
    return results + (norm_parts[0], norm_parts[1])


def local_generic(tokens, lengths, w_qkv, w_out, w_up, w_down, gains, biases, cotangent):
    rows_here, slot_dev, model_width = tokens.shape
    slot_count = slot_dev * lax.axis_size("kv")
    first_slot = lax.axis_index("kv") * slot_dev
    scaling = 1.0 / math.sqrt(HEAD)
    doc_ends = jnp.cumsum(lengths, -1)
    places = jnp.arange(slot_count, dtype=jnp.int32)
    docs_all = jnp.sum((doc_ends[:, None, :] <= places[None, :, None]).astype(jnp.int32), -1)
    live_all = (places[None, :] < doc_ends[:, -1:]).astype(jnp.float32)
    docs_here = lax.dynamic_slice_in_dim(docs_all, first_slot, slot_dev, 1)
    live_here = lax.dynamic_slice_in_dim(live_all, first_slot, slot_dev, 1)
    local_places = first_slot + jnp.arange(slot_dev, dtype=jnp.int32)
    masks = make_mask(local_places, docs_here[0], live_here[0], places, docs_all[0], live_all[0])
    stream = tokens.astype(jnp.float32)
    stored = []
    for number in range(LAYERS):
        signed = number == 0
        pieces = (
            lax.all_gather(w_qkv[number], ("rows", "kv"), axis=0, tiled=True),
            lax.all_gather(w_out[number], ("rows", "kv"), axis=0, tiled=True),
            lax.all_gather(w_up[number], ("rows", "kv"), axis=0, tiled=True),
            lax.all_gather(w_down[number], ("rows", "kv"), axis=0, tiled=True),
            lax.all_gather(gains[number], ("rows", "kv"), axis=1, tiled=True),
            lax.all_gather(biases[number], ("rows", "kv"), axis=1, tiled=True),
        )
        full_qkv, full_out, full_up, full_down, gain_pair, bias_pair = pieces
        gain_pair = gain_pair.astype(jnp.float32)
        bias_pair = bias_pair.astype(jnp.float32)
        normed_in = norm_rows(stream, gain_pair[0], bias_pair[0]).astype(jnp.bfloat16)
        projected = jnp.dot(normed_in, full_qkv, preferred_element_type=jnp.float32).astype(
            jnp.bfloat16
        )
        kv_all = lax.all_gather(projected[:, :, model_width:], "kv", axis=1, tiled=True)
        attended = jnp.stack(
            [
                attend_row(
                    projected[0, :, :model_width], kv_all[0], masks, live_here[0], signed, scaling
                )
            ]
        )
        shared = kv_all
        middle = stream + jnp.dot(attended, full_out, preferred_element_type=jnp.float32)
        normed_mid = norm_rows(middle, gain_pair[1], bias_pair[1]).astype(jnp.bfloat16)
        pre_act = jnp.dot(normed_mid, full_up, preferred_element_type=jnp.float32)
        activated = jax.nn.gelu(pre_act).astype(jnp.bfloat16)
        stored.append(
            (
                stream,
                normed_in,
                projected,
                shared,
                attended,
                middle,
                normed_mid,
                pre_act,
                activated,
                pieces,
            )
        )
        stream = middle + jnp.dot(activated, full_down, preferred_element_type=jnp.float32)
    result = (stream * live_here[..., None]).astype(jnp.bfloat16)
    residual_grad = cotangent.astype(jnp.float32) * live_here[..., None]
    collected = [None] * LAYERS
    for number in reversed(range(LAYERS)):
        signed = number == 0
        (
            stream_in,
            normed_in,
            projected,
            shared,
            attended,
            middle,
            normed_mid,
            pre_act,
            activated,
            kept,
        ) = stored[number]
        pieces = (
            lax.all_gather(w_qkv[number], ("rows", "kv"), axis=0, tiled=True),
            lax.all_gather(w_out[number], ("rows", "kv"), axis=0, tiled=True),
            lax.all_gather(w_up[number], ("rows", "kv"), axis=0, tiled=True),
            lax.all_gather(w_down[number], ("rows", "kv"), axis=0, tiled=True),
            lax.all_gather(gains[number], ("rows", "kv"), axis=1, tiled=True),
            lax.all_gather(biases[number], ("rows", "kv"), axis=1, tiled=True),
        )
        full_qkv, full_out, full_up, full_down, gain_pair, bias_pair = pieces
        gain_pair = gain_pair.astype(jnp.float32)
        bias_pair = bias_pair.astype(jnp.float32)
        down_in = residual_grad.astype(jnp.bfloat16)
        act_grad = jnp.einsum("rtd,fd->rtf", down_in, full_down, preferred_element_type=jnp.float32)
        unused, gelu_pull = jax.vjp(jax.nn.gelu, pre_act)
        pre_grad = gelu_pull(act_grad)[0].astype(jnp.bfloat16)
        mid_normed_grad = jnp.einsum(
            "rtf,df->rtd", pre_grad, full_up, preferred_element_type=jnp.float32
        )
        unused, norm_pull = jax.vjp(norm_rows, middle, gain_pair[1], bias_pair[1])
        middle_part, gain_late, bias_late = norm_pull(mid_normed_grad)
        middle_grad = residual_grad + middle_part
        branch_grad = middle_grad.astype(jnp.bfloat16)
        att_grad = jnp.einsum(
            "rte,de->rtd", branch_grad, full_out, preferred_element_type=jnp.float32
        ).astype(jnp.bfloat16)
        kv_all = shared
        query_grad, kv_grad = attend_back(
            projected[0, :, :model_width],
            kv_all[0],
            att_grad[0],
            masks,
            live_here[0],
            signed,
            scaling,
        )
        query_grads = [query_grad]
        kv_grads = [kv_grad]
        kv_here = lax.psum_scatter(
            jnp.stack(kv_grads).astype(jnp.bfloat16), "kv", scatter_dimension=1, tiled=True
        ).astype(jnp.float32)
        qkv_grad = jnp.concatenate([jnp.stack(query_grads), kv_here], -1).astype(jnp.bfloat16)
        in_normed_grad = jnp.einsum(
            "rte,de->rtd", qkv_grad, full_qkv, preferred_element_type=jnp.float32
        )
        unused, first_pull = jax.vjp(norm_rows, stream_in, gain_pair[0], bias_pair[0])
        stream_part, gain_early, bias_early = first_pull(in_normed_grad)
        residual_grad = middle_grad + stream_part
        g_gain = jnp.stack([gain_early, gain_late])
        g_bias = jnp.stack([bias_early, bias_late])
        pairs = [
            (normed_in, qkv_grad),
            (attended, branch_grad),
            (normed_mid, pre_grad),
            (activated, down_in),
        ]
        collected[number] = reduce_grads(pairs, g_gain, g_bias)
    grad_qkv = jnp.stack([collected[number][0] for number in range(LAYERS)])
    grad_out = jnp.stack([collected[number][1] for number in range(LAYERS)])
    grad_up = jnp.stack([collected[number][2] for number in range(LAYERS)])
    grad_down = jnp.stack([collected[number][3] for number in range(LAYERS)])
    grad_gains = jnp.stack([collected[number][4] for number in range(LAYERS)])
    grad_biases = jnp.stack([collected[number][5][0] for number in range(LAYERS)])
    grad_mid_biases = jnp.stack([collected[number][5][1] for number in range(LAYERS)])
    return (
        result,
        residual_grad,
        grad_qkv,
        grad_out,
        grad_up,
        grad_down,
        grad_gains,
        grad_biases,
        grad_mid_biases,
    )


F32 = jnp.float32
BF16 = jnp.bfloat16
MESH = pl.DeviceIdType.MESH
ZN = 4


def flip(value, unit):
    bit = lax.rem(lax.div(value, unit), 2)
    return value + unit - 2 * unit * bit


def places_of():
    r = lax.axis_index("rows")
    z = lax.axis_index("kv")
    return r, z, flip(r, 2), flip(r, 4), flip(flip(r, 2), 4), flip(r, 1)


def turn(z, k):
    return lax.rem(z + k, ZN)


def rcopy(src, dst, ssem, rsem, device):
    return pltpu.make_async_remote_copy(
        src_ref=src, dst_ref=dst, send_sem=ssem, recv_sem=rsem, device_id=device, device_id_type=MESH
    )


def band(start, size):
    return pl.ds(pl.multiple_of(start, 16), size)


def greet(peers):
    barrier = pltpu.get_barrier_semaphore()
    for peer in peers:
        pl.semaphore_signal(barrier, inc=1, device_id=peer, device_id_type=MESH)
    pl.semaphore_wait(barrier, len(peers))


def comm_peers():
    r, z, rx, ry, rd, rc = places_of()
    return [(r, turn(z, 1)), (r, turn(z, 2)), (r, turn(z, 3)), (rx, z), (ry, z), (rc, z)]


def col_step(width):
    return 256 if width % 256 == 0 else 128


def add_rows(dst, src, rows):
    def step(i, carry):
        here = band(i * 16, 16)
        dst[here, :] = (dst[here, :].astype(F32) + src[here, :].astype(F32)).astype(BF16)
        return carry
    lax.fori_loop(0, rows // 16, step, 0)


SEND = 0
PLANE = 100
PASS = 200
LAST = 300
WHOLE = 400
NORM = 600
SHARE = 700
PROJECT = 800
ATTEND = 900
OUTPUT = 1000
UP = 1100
DOWN = 1200
TOKENS = 500
COTANGENT = 510
WIDEN = 520
RESULT = 530
SECOND = 0
NEAR = 100
OVER_Z = 200
CLOSE = 300
THEIRS = 400
OURS = 500
SLOPE = 600
THROUGH = 700
NORM_BACK = 800
ASK = 900
KEYS = 1000
ASKED = 1100
ATTEND_BACK = 1200
PARTIAL = 1300
FIRST_BACK = 1400
RELAY = 1600
BEGIN = 1500
SWAP_BACK = 1510
RESULT_BACK = 1520

FORWARD_ORDER = [
    2, 1, 101, 0, 102, 201, 500, 3, 100, 301, 401, 4, 202, 200, 103, 300, 400, 5, 520, 600, 800, 104, 802,
    203, 6, 105, 303, 403, 8, 9, 106, 302, 700, 801, 7, 204, 803, 205, 900, 402, 901, 902, 206, 903, 304, 107,
    11, 10, 306, 305, 108, 109, 404, 406, 1000, 405, 1100, 1101, 1200, 1201, 601, 207, 810, 110, 812, 208,
    209, 307, 111, 407, 701, 811, 813, 910, 911, 912, 913, 510, 308, 309, 210, 211, 1001, 409, 408, 1110, 310,
    1111, 311, 410, 1210, 411, 1211, 530,
]
BACKWARD_ORDER = [
    1500, 410, 610, 408, 710, 611, 711, 801, 901, 510, 10, 409, 1001, 407, 508, 8, 411, 1520, 1101, 1213,
    1313, 1212, 1312, 110, 509, 1613, 1211, 1612, 1311, 108, 1210, 1310, 1611, 1610, 406, 9, 511, 210, 109,
    11, 208, 506, 1401, 600, 507, 601, 700, 701, 800, 900, 1000, 111, 310, 308, 404, 6, 209, 107, 106, 402,
    1100, 1203, 211, 1303, 7, 502, 2, 1202, 1603, 1302, 206, 207, 504, 311, 1602, 1201, 102, 405, 1301, 1200,
    104, 1300, 4, 307, 202, 1601, 306, 309, 1600, 403, 505, 5, 204, 503, 105, 1400, 1510, 401, 400, 103, 3,
    412, 304, 205, 501, 500, 0, 512, 112, 203, 101, 1, 305, 302, 100, 201, 303, 200, 301, 12, 212, 300, 312,
]


GROUP = 640
TOK = 256
WIDE = 256
PARTS = HEADS // 4
CHUNK = 64
FAR = -1e30
KB = 256
JOBS = 6


def dot(a, b):
    return jnp.dot(a, b, preferred_element_type=F32)


def dot_nt(a, b):
    return lax.dot_general(a, b, (((1,), (1,)), ((), ())), preferred_element_type=F32)


def dot_tn(a, b):
    return lax.dot_general(a, b, (((0,), (0,)), ((), ())), preferred_element_type=F32)


def loop(count, body):
    def step(i, carry):
        body(i)
        return carry
    lax.fori_loop(0, count, step, 0)


def cols(i, size):
    return pl.ds(pl.multiple_of(i * size, 128), size)


class Spot:
    def __init__(self):
        self.r, self.z, self.rx, self.ry, self.rd, self.rc = places_of()
        self.c = lax.rem(self.r, 2)
        self.parity = lax.rem(self.z, 2)
        self.member = 2 * self.c + self.parity
        self.swaps = (self.c + lax.div(self.z, 2)) == 1
        self.partner = (self.rc, flip(self.z, 2))

    def mate(self, k):
        r = self.rc if k >= 2 else self.r
        z = flip(self.z, 1) if k % 2 else self.z
        return (r, z), 2 * lax.rem(r, 2) + lax.rem(z, 2)

    def device(self, member):
        return (self.r - self.c + lax.div(member, 2), self.z - self.parity + lax.rem(member, 2))

    def peers(self):
        return comm_peers() + [(self.rc, flip(self.z, 1)), self.partner]


class Gather:
    SEMS = 11

    def __init__(self, own, whole, bufs, ssem, rsem, base, paired=False):
        self.own, self.whole, self.bufs = own, whole, bufs
        self.ssem, self.rsem, self.base = ssem, rsem, base
        self.split, self.paired = len(bufs) > 0, paired
        self.rows, self.width = whole.shape[0] // 8, whole.shape[1]
        self.sent = []

    def _copy(self, src, dst, at, device):
        return rcopy(src, dst, self.ssem.at[self.base + at], self.rsem.at[self.base + at], device)

    def _block(self, r, half=None):
        if half is None:
            return self.whole.at[band(r * self.rows, self.rows), :]
        part = self.rows // 2
        return self.whole.at[band(r * self.rows + half * part, part), :]

    def _cored(self, r, column):
        if not self.paired:
            return self._block(r)
        return self.whole.at[band(r * self.rows, self.rows), cols(column, self.width // 2)]

    def _send(self, src, dst, at, device):
        copy = self._copy(src, dst, at, device)
        copy.start()
        self.sent.append(copy)

    def prepare(self):
        r, z = places_of()[:2]
        if self.split:
            zbuf = self.bufs[0]
            half = self.width // 2
            values = [self.own(place) for place in (0, 1)] if self.paired else [self.own[...].astype(F32)]
            for place, own in enumerate(values):
                packed = jnp.concatenate(
                    [own[:16], jnp.concatenate([own[16:, :half], own[16:, half:]], 0)], 1
                ).astype(BF16)
                if self.paired:
                    self.bufs[1][place] = packed
                else:
                    zbuf[pl.ds(z, 1)] = packed[None]
            if self.paired:
                zbuf[pl.ds(z, 1)] = self.bufs[1][pl.ds(lax.rem(z, 2), 1)]
        else:
            part = self.rows // ZN
            self.whole[band(r * self.rows + z * part, part), :] = self.own[...]

    def _zref(self, z):
        if self.split:
            return self.bufs[0].at[z]
        part = self.rows // ZN
        return self.whole.at[band(places_of()[0] * self.rows + z * part, part), :]

    def send_z(self):
        r, z = places_of()[:2]
        for k in (1, 2, 3):
            there = turn(z, k)
            src = self.bufs[1].at[lax.rem(there, 2)] if self.paired else self._zref(z)
            self._send(src, self._zref(z), k - 1, (r, there))

    def wait_z(self):
        r, z = places_of()[:2]
        for k in (1, 2, 3):
            ref = self._zref(turn(z, ZN - k))
            self._copy(ref, ref, k - 1, (r, turn(z, ZN - k))).wait_recv()
        if self.split:
            zbuf = self.bufs[0]
            half = self.width // 2
            step = col_step(half)
            for side in (0, 1):
                def assemble(i, side=side):
                    at = pl.multiple_of(self.width + i * step, 128)
                    here = pl.ds(pl.multiple_of(side * half + i * step, 128), step)
                    parts = []
                    for piece in range(ZN):
                        parts.append(zbuf[piece, :, here].astype(F32))
                        parts.append(zbuf[piece, :, pl.ds(at, step)].astype(F32)[8 * side : 8 * side + 8])
                    self.whole[band(r * self.rows, self.rows), here] = jnp.concatenate(parts, 0).astype(BF16)
                loop(half // step, assemble)

    def send_plane(self):
        r, z, rx, ry, rd, rc = places_of()
        own = self._block(r)
        self._send(own, own, 3, (rx, z))
        self._send(own, own, 4, (ry, z))
        self._core(r, 7)

    def _core(self, block, at):
        r, z, rx, ry, rd, rc = places_of()
        ref = self._cored(block, lax.rem(rc, 2))
        self._send(ref, ref, at, (rc, z))

    def forward(self):
        r, z, rx, ry, rd, rc = places_of()
        first, second = self._block(rx), self._block(ry)
        self._copy(first, first, 3, (rx, z)).wait_recv()
        part = self._block(rx, 0)
        self._send(part, part, 5, (ry, z))
        self._copy(second, second, 4, (ry, z)).wait_recv()
        part = self._block(ry, 1)
        self._send(part, part, 6, (rx, z))
        self._core(rx, 8)
        self._core(ry, 9)

    def forward_last(self):
        r, z, rx, ry, rd, rc = places_of()
        part = self._block(rd, 0)
        self._copy(part, part, 5, (ry, z)).wait_recv()
        part = self._block(rd, 1)
        self._copy(part, part, 6, (rx, z)).wait_recv()
        self._core(rd, 10)

    def finish(self):
        r, z, rx, ry, rd, rc = places_of()
        for at, block in ((7, r), (8, rx), (9, ry), (10, rd)):
            ref = self._cored(flip(block, 1), lax.rem(r, 2))
            self._copy(ref, ref, at, (rc, z)).wait_recv()

    def drain(self):
        for copy in self.sent:
            copy.wait_send()


def swap(spot, src, dst, ssem, rsem):
    @pl.when(spot.swaps)
    def _():
        rcopy(src, dst, ssem, rsem, spot.partner).start()

    @pl.when(jnp.logical_not(spot.swaps))
    def _():
        pltpu.make_async_copy(src, dst, rsem).start()


def swap_wait(spot, src, dst, ssem, rsem):
    @pl.when(spot.swaps)
    def _():
        rcopy(src, dst, ssem, rsem, spot.partner).wait()

    @pl.when(jnp.logical_not(spot.swaps))
    def _():
        pltpu.make_async_copy(src, dst, rsem).wait()


def starts_of(lens, i):
    places = lax.broadcasted_iota(jnp.int32, (1, TOK), 1) + i * TOK
    end = jnp.zeros((1, 1), jnp.int32)
    start = jnp.zeros((1, TOK), jnp.int32)
    for n in range(4):
        end = end + lens[0:1, n : n + 1]
        start = jnp.maximum(start, jnp.where(end <= places, end, 0))
    live = places < end
    return places, jnp.where(live, start, 1 << 20), live


def live_column(lens, spot, rows, first):
    places = lax.broadcasted_iota(jnp.int32, (rows, 1), 0) + spot.member * TOK + first
    end = lens[0:1, 0:1] + lens[0:1, 1:2] + lens[0:1, 2:3] + lens[0:1, 3:4]
    return (places < end).astype(F32)


def centred(value):
    center = value - jnp.mean(value, -1, keepdims=True)
    spread = jnp.mean(center * center, -1, keepdims=True)
    return center * lax.rsqrt(spread + EPSILON)


def fold_rows(value, op):
    rows = value.shape[0]
    parts = [value[8 * n : 8 * n + 8] for n in range(rows // 8)]
    while len(parts) > 1:
        parts = [op(parts[n], parts[n + 1]) if n + 1 < len(parts) else parts[n] for n in range(0, len(parts), 2)]
    return parts[0]


def head_lanes(shape, h, offset):
    lanes = lax.broadcasted_iota(jnp.int32, shape, 1)
    return lax.div(lanes, HEAD) == h + offset


def masked_rows(first, rows, places, start, diagonal):
    keys = lax.broadcasted_iota(jnp.int32, (rows, TOK), 0) + first
    okay = keys >= start
    return okay & (keys <= places) if diagonal else okay


def over_blocks(i, body, carry):
    per = TOK // KB if KB <= TOK else 1
    if i:
        carry = lax.fori_loop(0, i * per, lambda n, c: body(n * KB, c, False), carry)
    for n in range(per):
        carry = body(i * TOK + n * KB, carry, True)
    return carry


def key_rows(qkv, first, at):
    quarter = lax.div(first, TOK)
    here = pl.ds(pl.multiple_of(lax.rem(first, TOK), KB), KB)
    return qkv[quarter, here, at : at + WIDE]


def masked_heads(value_t, offset):
    rows = lax.div(lax.broadcasted_iota(jnp.int32, value_t.shape, 0), HEAD)
    return jnp.concatenate([jnp.where(rows == h + offset, value_t, 0.0) for h in range(PARTS)], 1).astype(BF16)


def magnitude_of(s):
    square = s * s + 1.0
    back = lax.rsqrt(square)
    return square * back, back


def attend_quarter(i, lens, qkv, vt, acc, o_ref, stats, signed):
    places, start, live = starts_of(lens, i)
    mine = masked_heads(qkv[i, :, 0:WIDE].astype(F32).T * 0.125, 0)
    acc[...] = jnp.zeros_like(acc)

    def block(first, carry, diagonal):
        keys = key_rows(qkv, first, 384)
        okay = masked_rows(first, KB, places, start, diagonal)
        here = pl.ds(pl.multiple_of(first, KB), KB)
        out, lows, shrinks = [], [], []
        scores = [dot(keys, mine[:, h * TOK : (h + 1) * TOK]) for h in range(PARTS)]
        for h in range(PARTS):
            old, total = carry[2 * h], carry[2 * h + 1]
            s = scores[h]
            value = jnp.where(okay, magnitude_of(s)[0] if signed else s, FAR)
            new = jnp.maximum(old, jnp.max(fold_rows(value, jnp.maximum), 0, keepdims=True))
            raised = jnp.exp(value - new)
            shrink = jnp.exp(old - new)
            lows.append((jnp.tanh(s) * raised if signed else raised).astype(BF16))
            shrinks.append(shrink)
            out += [new, total * shrink + jnp.sum(fold_rows(raised, jnp.add), 0, keepdims=True)]
        terms = [dot(vt[HEAD * (h + 1) : HEAD * (h + 2), here], lows[h]) for h in range(PARTS)]
        for h in range(PARTS):
            rows = slice(HEAD * h, HEAD * (h + 1))
            acc[rows, :] = acc[rows, :] * shrinks[h] + terms[h]
        return tuple(out)
    lowest = jnp.full((1, TOK), 0.0 if signed else -10000.0, F32)
    carry = over_blocks(i, block, (lowest, jnp.zeros((1, TOK), F32)) * PARTS)
    for h in range(PARTS):
        inverse = 1.0 / (carry[2 * h + 1] + (1.0 - live.astype(F32)))
        stats[i, h : h + 1, :] = carry[2 * h]
        stats[i, PARTS + h : PARTS + h + 1, :] = inverse
        acc[HEAD * h : HEAD * (h + 1), :] = acc[HEAD * h : HEAD * (h + 1), :] * inverse
    o_ref[i] = acc[...].astype(BF16)


def gelu_both(x):
    root = 0.7978845608028654
    square = x * x
    bend = jnp.tanh(root * (x + 0.044715 * x * square))
    half = 0.5 * (1.0 + bend)
    return x * half, half + 0.5 * x * (1.0 - bend * bend) * root * (1.0 + 3 * 0.044715 * square)


class Keep:
    def __init__(self, src, dst, sem):
        self.copy = pltpu.make_async_copy(src, dst, sem)
        self.copy.start()
        self.open = True

    def wait(self):
        if self.open:
            self.copy.wait()
        self.open = False


STASH = ("stream", "qkv", "middle", "nin_t", "att_t", "nmid_t", "pre", "act_t", "out", "stats")


def stash_shapes(d, ff):
    return [
        ((TOK, d), F32),
        ((4, TOK, GROUP), BF16),
        ((TOK, d), F32),
        ((d, 4 * TOK), BF16),
        ((d, TOK), BF16),
        ((d, TOK), BF16),
        ((TOK, ff), F32),
        ((ff, TOK), BF16),
        ((4, 192, TOK), F32),
        ((4, 8, TOK), F32),
    ]


def forward_kernel(*refs):
    refs = list(refs)
    take = lambda n: [refs.pop(0) for _ in range(n)]
    tok, cot, lengths = take(3)
    sources = take(4)
    gains, biases = take(2)
    result_o, cot_o, lens_o, norms_o = take(4)
    whole_o = take(2 * JOBS)
    stash_o = [take(10), take(10)]
    wholes = take(2 * JOBS)
    zbuf = [take((2, 1, 1, 1, 0, 0)[n % JOBS]) for n in range(2 * JOBS)]
    tok_v, lens_in, lens_v, stream, nin0, nin1, qkv, vt, outs, stats, o_ref, att0, att1, pre, act, act_t, nin_t, nt_mid, normed, middle, res = take(21)
    ssem, rsem, osem, stsem, ns, nr, os_, or_, ms, mr = take(10)
    spot = Spot()
    lens_in[...] = jnp.zeros_like(lens_in)
    lens_in[0:1, 0:4] = lengths[...]
    greet(spot.peers())
    jobs = []

    def grouped(layer):
        def pair(place):
            vectors = [ref[layer, which : which + 1, :].astype(F32) for which in (0, 1) for ref in (gains, biases)]
            own = vectors[0].shape[1]
            top = jnp.concatenate([jnp.concatenate(vectors, 0), jnp.zeros((4, 128 - own), F32)], 1)
            edge = jnp.concatenate([top, jnp.zeros((124, 128), F32)], 0).T[:own, :HEAD]
            parts = []
            for g in (place, place + 2):
                for at in (0, 2, 1):
                    parts.append(sources[0][layer, :, 768 * at + 192 * g : 768 * at + 192 * g + 192].astype(F32))
                parts.append(edge)
            return jnp.concatenate(parts, 1)
        return pair

    for layer in range(LAYERS):
        out_in, up_in, down_in = [source.at[layer] for source in sources[1:]]
        ff, d = up_in.shape[1] // 2, down_in.shape[1] // 2
        owns = [grouped(layer), out_in] + [up_in.at[:, h * ff : (h + 1) * ff] for h in (0, 1)] + [down_in.at[:, h * d : (h + 1) * d] for h in (0, 1)]
        for n, own in enumerate(owns):
            at = layer * JOBS + n
            jobs.append(Gather(own, wholes[at], zbuf[at], ssem, rsem, at * Gather.SEMS, n == 0))
    kept = {}

    def keep(name, src, dst, sem):
        kept[name] = Keep(src, dst, sem)

    def settle(name):
        if name in kept:
            kept[name].wait()

    def stash(layer, name, src):
        at = STASH.index(name)
        keep((layer, name), src, stash_o[layer][at], stsem.at[10 * layer + at])

    steps = {}

    def step(name):
        def note(run):
            steps[name] = run
        return note

    for n, job in enumerate(jobs):
        def first(job=job):
            job.prepare()
            job.send_z()

        def plane(job=job):
            job.wait_z()
            job.send_plane()

        def done(job=job, n=n):
            job.finish()
            src = wholes[n]
            if n % JOBS == 0:
                src = src.at[:, cols(spot.c, GROUP)]
            keep(("whole", n), src, whole_o[n], osem.at[n])
        steps.update({SEND + n: first, PLANE + n: plane, PASS + n: job.forward, LAST + n: job.forward_last, WHOLE + n: done})

    @step(TOKENS)
    def _():
        swap(spot, tok, tok_v, ms.at[0], mr.at[0])
        swap(spot, lens_in, lens_v, ms.at[1], mr.at[1])

    @step(COTANGENT)
    def _():
        swap(spot, cot, cot_o, ms.at[2], mr.at[2])

    @step(WIDEN)
    def _():
        swap_wait(spot, tok, tok_v, ms.at[0], mr.at[0])
        swap_wait(spot, lens_in, lens_v, ms.at[1], mr.at[1])
        lens_o[...] = lens_v[...]

        def widen(n):
            here = band(n * CHUNK, CHUNK)
            stream[here, :] = tok_v[here, :].astype(F32)
        loop(TOK // CHUNK, widen)
        stash(0, "stream", stream)

    def layer_steps(layer):
        base = layer * JOBS
        w_qkv, w_out, w_up0, w_up1, w_down0, w_down1 = wholes[base : base + JOBS]
        nin = (nin0, nin1)[layer]
        att = (att0, att1)[layer]
        signed = layer == 0

        def gathered(k):
            mate, member = spot.mate(k)
            return rcopy(nin.at[member], nin.at[member], ns.at[4 * layer + k], nr.at[4 * layer + k], mate)

        def give(k, member):
            mate = spot.mate(1 if k == 1 else 2)[0]
            return rcopy(nin.at[member], nin.at[member], ns.at[4 * layer + k], nr.at[4 * layer + k], mate)

        @step(NORM + layer)
        def _():
            edge = w_qkv[:, pl.ds(pl.multiple_of(spot.c * GROUP + 512, 128), 128)].astype(F32).T
            norms_o[layer] = edge[HEAD : HEAD + 8]

            def first_norm(n):
                here = band(n * CHUNK, CHUNK)
                value = centred(stream[here, :]) * norms_o[layer, 0:1, :] + norms_o[layer, 1:2, :]
                nin[spot.member, here, :] = value.astype(BF16)
            loop(TOK // CHUNK, first_norm)
            give(1, spot.member).start()
            give(2, spot.member).start()

        @step(SHARE + layer)
        def _():
            gathered(1).wait_recv()
            give(3, spot.mate(1)[1]).start()

        def project(k):
            def run():
                member = spot.member
                if k:
                    member = spot.mate(k)[1]
                    if k != 1:
                        gathered(k).wait_recv()
                group = dot(nin[member], w_qkv[:, cols(spot.c, GROUP)]).astype(BF16)
                if (layer, k) == (1, 0):
                    settle((0, "qkv"))
                    settle((0, "nin_t"))
                qkv[pl.ds(member, 1)] = group[None]
                at = pl.multiple_of(member * TOK, TOK)
                vt[:, pl.ds(at, TOK)] = group[:, 128:384].astype(F32).T.astype(BF16)
                nin_t[:, pl.ds(at, TOK)] = nin[member].astype(F32).T.astype(BF16)
                if k == 3:
                    stash(layer, "qkv", qkv)
                    stash(layer, "nin_t", nin_t)
            return run
        for k in range(4):
            steps[PROJECT + 10 * layer + k] = project(k)

        def returned(i):
            return rcopy(
                o_ref.at[layer, i], att.at[band(spot.member * 192, 192), :], os_.at[4 * layer + i], or_.at[4 * layer + spot.member], spot.device(i)
            )

        def attend(i):
            def run():
                attend_quarter(i, lens_v, qkv, vt, outs.at[layer, i], o_ref.at[layer], stats.at[layer], signed)

                @pl.when(spot.member != i)
                def _():
                    returned(i).start()

                @pl.when(spot.member == i)
                def _():
                    att[i * 192 : (i + 1) * 192, :] = o_ref[layer, i]
                if i == 3:
                    stash(layer, "out", outs.at[layer])
                    stash(layer, "stats", stats.at[layer])
            return run
        for i in range(4):
            steps[ATTEND + 10 * layer + i] = attend(i)

        @step(OUTPUT + layer)
        def _():
            for i in range(4):
                @pl.when(spot.member != i)
                def _():
                    ref = att.at[i * 192 : (i + 1) * 192, :]
                    rcopy(ref, ref, os_.at[4 * layer + i], or_.at[4 * layer + i], spot.device(i)).wait_recv()
            stash(layer, "att_t", att)
            settle((0, "middle"))
            middle[...] = stream[...] + dot_tn(att[...], w_out[...])
            stash(layer, "middle", middle)

            def second_norm(n):
                here = band(n * CHUNK, CHUNK)
                value = centred(middle[here, :]) * norms_o[layer, 2:3, :] + norms_o[layer, 3:4, :]
                normed[here, :] = value.astype(BF16)
            loop(TOK // CHUNK, second_norm)
            settle((0, "nmid_t"))
            nt_mid[...] = normed[...].astype(F32).T.astype(BF16)
            stash(layer, "nmid_t", nt_mid)
            settle((0, "pre"))
            settle((0, "act_t"))

        def up(h):
            w_up = (w_up0, w_up1)[h]
            tile = 512
            count = w_up.shape[1] // tile

            def run():
                def part(n):
                    value = dot(normed[...], w_up[:, cols(n, tile)])
                    here = cols(h * count + n, tile)
                    active, pre[:, here] = gelu_both(value)
                    act[:, here] = active.astype(BF16)
                    act_t[pl.ds(pl.multiple_of((h * count + n) * tile, tile), tile), :] = active.T.astype(BF16)
                loop(count, part)
                if h:
                    stash(layer, "pre", pre)
                    stash(layer, "act_t", act_t)
            return run

        def down(h):
            w_down = (w_down0, w_down1)[h]
            width = w_down.shape[1]

            def run():
                settle((layer, "stream"))

                def part(n):
                    here = cols(n + h * (width // 128), 128)
                    stream[:, here] = middle[:, here] + dot(act[...], w_down[:, cols(n, 128)])
                if width % 384 == 0:
                    here = slice(h * width, (h + 1) * width)
                    stream[:, here] = middle[:, here] + dot(act[...], w_down[...])
                else:
                    loop(width // 128, part)
                if h and layer == 0:
                    stash(1, "stream", stream)
            return run
        for h in (0, 1):
            steps[UP + 10 * layer + h] = up(h)
            steps[DOWN + 10 * layer + h] = down(h)

        def close():
            for k in (1, 2):
                give(k, spot.member).wait_send()
            give(3, spot.mate(1)[1]).wait_send()
            for i in range(4):
                @pl.when(spot.member != i)
                def _():
                    returned(i).wait_send()
        return close

    closes = [layer_steps(layer) for layer in range(LAYERS)]

    @step(RESULT)
    def _():
        def last(n):
            here = band(n * CHUNK, CHUNK)
            res[here, :] = (stream[here, :] * live_column(lens_v, spot, CHUNK, n * CHUNK)).astype(BF16)
        loop(TOK // CHUNK, last)
        keep("result", res, result_o, ms.at[3])

    for name in FORWARD_ORDER:
        steps.pop(name)()
    assert not steps
    for job in jobs:
        job.drain()
    for close in closes:
        close()
    for copy in kept.values():
        copy.wait()
    swap_wait(spot, cot, cot_o, ms.at[2], mr.at[2])


def forward_call(tok, cot, lengths, w_qkv, w_out, w_up, w_down, gains, biases):
    d, ff = tok.shape[1], w_up.shape[2]
    shapes = [(d, 2 * GROUP), (d, d), (d, ff // 2), (d, ff // 2), (ff, d // 2), (ff, d // 2)] * LAYERS
    zshapes = []
    for n, (rows, width) in enumerate(shapes):
        if n % JOBS < 4:
            zshapes.append(pltpu.VMEM((ZN, 16, width * 3 // 2), BF16))
        if n % JOBS == 0:
            zshapes.append(pltpu.VMEM((2, 16, width * 3 // 2), BF16))
    any_space = pl.BlockSpec(memory_space=pl.ANY)
    vmem = pl.BlockSpec(memory_space=pltpu.VMEM)
    stash = [jax.ShapeDtypeStruct(shape, kind) for shape, kind in stash_shapes(d, ff)]
    dma = lambda n: pltpu.SemaphoreType.DMA((n,))
    kept_shapes = [(rows, GROUP if n % JOBS == 0 else width) for n, (rows, width) in enumerate(shapes)]
    outs = pl.pallas_call(
        forward_kernel,
        out_shape=[
            jax.ShapeDtypeStruct((TOK, d), BF16),
            jax.ShapeDtypeStruct((TOK, d), BF16),
            jax.ShapeDtypeStruct((8, 128), jnp.int32),
            jax.ShapeDtypeStruct((LAYERS, 8, d), F32),
        ]
        + [jax.ShapeDtypeStruct(shape, BF16) for shape in kept_shapes]
        + stash
        + stash,
        in_specs=[any_space, any_space] + [vmem] * 7,
        out_specs=[any_space, any_space, vmem, vmem] + [any_space] * (2 * JOBS + 20),
        scratch_shapes=[pltpu.VMEM(shape, BF16) for shape in shapes]
        + zshapes
        + [
            pltpu.VMEM((TOK, d), BF16),
            pltpu.VMEM((8, 128), jnp.int32),
            pltpu.VMEM((8, 128), jnp.int32),
            pltpu.VMEM((TOK, d), F32),
            pltpu.VMEM((4, TOK, d), BF16),
            pltpu.VMEM((4, TOK, d), BF16),
            pltpu.VMEM((4, TOK, GROUP), BF16),
            pltpu.VMEM((WIDE, 4 * TOK), BF16),
            pltpu.VMEM((LAYERS, 4, 192, TOK), F32),
            pltpu.VMEM((LAYERS, 4, 8, TOK), F32),
            pltpu.VMEM((LAYERS, 4, 192, TOK), BF16),
            pltpu.VMEM((d, TOK), BF16),
            pltpu.VMEM((d, TOK), BF16),
            pltpu.VMEM((TOK, ff), F32),
            pltpu.VMEM((TOK, ff), BF16),
            pltpu.VMEM((ff, TOK), BF16),
            pltpu.VMEM((d, 4 * TOK), BF16),
            pltpu.VMEM((d, TOK), BF16),
            pltpu.VMEM((TOK, d), BF16),
            pltpu.VMEM((TOK, d), F32),
            pltpu.VMEM((TOK, d), BF16),
        ]
        + [dma(2 * JOBS * Gather.SEMS), dma(2 * JOBS * Gather.SEMS), dma(2 * JOBS), dma(20), dma(8), dma(8), dma(8), dma(8), dma(4), dma(4)],
        compiler_params=pltpu.CompilerParams(collective_id=0, has_side_effects=True, vmem_limit_bytes=62 * 2**20),
    )(tok, cot, lengths, w_qkv, w_out, w_up, w_down, gains, biases)
    at = 4 + 2 * JOBS
    return outs[:4], outs[4:at], (outs[at : at + 10], outs[at + 10 : at + 20])


class Reduce:
    SEMS = 10

    def __init__(self, send, bufs, out, ssem, rsem, base, paired=False):
        self.send = send
        self.got, self.half, self.near = bufs[:3]
        self.zs, self.zr = bufs[3:5]
        self.out = out
        self.ssem, self.rsem, self.base = ssem, rsem, base
        self.rows, self.width = self.got.shape[1], self.got.shape[2]
        self.split, self.paired = self.zs.shape[1] == 16, paired
        self.sent = []

    def _copy(self, src, dst, at, device):
        return rcopy(src, dst, self.ssem.at[self.base + at], self.rsem.at[self.base + at], device)

    def _send(self, src, dst, at, device):
        copy = self._copy(src, dst, at, device)
        copy.start()
        self.sent.append(copy)

    def _got(self, core):
        if self.paired:
            return self.got.at[:, :, cols(core, self.width // 2)]
        return self.got

    def send_core(self):
        r, z, rx, ry, rd, rc = places_of()
        self._send(self.send, self._got(lax.rem(r, 2)), 0, (rc, z))

    def wait_core(self):
        r, z, rx, ry, rd, rc = places_of()
        ref = self._got(lax.rem(rc, 2))
        self._copy(ref, ref, 0, (rc, z)).wait_recv()

    def _part(self, other, i):
        part = self.rows // 2
        return self.got.at[lax.div(other, 2), pl.ds(i * part, part)]

    def send_first(self):
        r, z, rx, ry, rd, rc = places_of()
        part = self.rows // 2
        self._send(self._part(rd, 0), self.half.at[0], 1, (ry, z))
        self._send(self._part(rd, 1), self.half.at[1], 2, (rx, z))

    def send_second(self):
        r, z, rx, ry, rd, rc = places_of()
        part = self.rows // 2
        self._send(self._part(rx, 1), self.near.at[0, pl.ds(part, part)], 3, (rx, z))
        self._send(self._part(ry, 0), self.near.at[1, pl.ds(0, part)], 4, (ry, z))

    def send_near(self):
        r, z, rx, ry, rd, rc = places_of()
        part = self.rows // 2
        for i, side, other in ((0, ry, rx), (1, rx, ry)):
            self._copy(self.half.at[i], self.half.at[i], 1 + i, (side, z)).wait_recv()
            block = self._part(other, i)
            add_rows(block, self.half.at[i], part)
            self._send(block, self.near.at[i, pl.ds(i * part, part)], 5 + i, (other, z))

    def send_z(self):
        r, z, rx, ry, rd, rc = places_of()
        part = self.rows // 2
        for at, i, h, side in ((3, 0, 1, rx), (4, 1, 0, ry), (5, 0, 0, rx), (6, 1, 1, ry)):
            ref = self.near.at[i, pl.ds(h * part, part)]
            self._copy(ref, ref, at, (side, z)).wait_recv()
        own = self.got.at[lax.div(r, 2)]
        near = self.near

        def total(rows, here):
            return own[rows, here].astype(F32) + near[0, rows, here].astype(F32) + near[1, rows, here].astype(F32)

        if self.split:
            half = self.width // 2
            step = col_step(half)

            def cut(i):
                at = pl.ds(pl.multiple_of(self.width + i * step, 128), step)
                sums = [
                    total(slice(None), pl.ds(pl.multiple_of(side * half + i * step, 128), step)) for side in (0, 1)
                ]
                for piece in range(ZN):
                    for side in (0, 1):
                        here = pl.ds(pl.multiple_of(side * half + i * step, 128), step)
                        self.zs[piece, :, here] = sums[side][24 * piece : 24 * piece + 16].astype(BF16)
                    self.zs[piece, :, at] = jnp.concatenate(
                        [sums[side][24 * piece + 16 : 24 * piece + 24] for side in (0, 1)], 0
                    ).astype(BF16)
            loop(half // step, cut)
        else:
            size = self.rows // ZN
            for piece in range(ZN):
                def cut_rows(i, piece=piece):
                    self.zs[piece, band(i * 16, 16), :] = total(band(piece * size + i * 16, 16), slice(None)).astype(BF16)
                loop(size // 16, cut_rows)
        for k in (1, 2, 3):
            self._send(self.zs.at[turn(z, k)], self.zr.at[k - 1], 6 + k, (r, turn(z, k)))

    def finish(self):
        r, z = places_of()[:2]
        for k in (1, 2, 3):
            ref = self.zr.at[k - 1]
            self._copy(ref, ref, 6 + k, (r, turn(z, ZN - k))).wait_recv()
        half, width = self.width // 2, self.width
        if self.paired:
            for place, value in (
                (lax.rem(z, 2), self.zs[z].astype(F32) + self.zr[1].astype(F32)),
                (lax.rem(z + 1, 2), self.zr[0].astype(F32) + self.zr[2].astype(F32)),
            ):
                for side in (0, 1):
                    here = cols(place + 2 * side, GROUP)
                    self.out[pl.ds(0, 16), here] = value[:, side * GROUP : (side + 1) * GROUP]
                    self.out[pl.ds(16, 8), here] = value[8 * side : 8 * side + 8, width:]
        elif self.split:
            value = self.zs[z].astype(F32)
            for k in range(3):
                value = value + self.zr[k].astype(F32)
            self.out[pl.ds(0, 16), :] = value[:, :width]
            self.out[pl.ds(16, 8), pl.ds(0, half)] = value[:8, width:]
            self.out[pl.ds(16, 8), pl.ds(half, half)] = value[8:, width:]
        else:
            def total(i):
                here = band(i * 16, 16)
                value = self.zs[z, here, :].astype(F32)
                for k in range(3):
                    value = value + self.zr[k, here, :].astype(F32)
                self.out[here, :] = value
            loop(self.out.shape[0] // 16, total)

    def drain(self):
        for copy in self.sent:
            copy.wait_send()
        self.sent = []


def left_rows(left, c):
    return jnp.concatenate([left[band((2 * b + c) * 96, 96), :] for b in range(4)], 0)


def norm_back(source, upstream, gain, add, out, low, sums):
    sums[...] = jnp.zeros_like(sums)

    def step(n):
        here = band(n * CHUNK, CHUNK)
        value = source[here, :]
        center = value - jnp.mean(value, -1, keepdims=True)
        scale = lax.rsqrt(jnp.mean(center * center, -1, keepdims=True) + EPSILON)
        normal = center * scale
        up = upstream(here)
        sums[0:8, :] += fold_rows(up * normal, jnp.add)
        sums[8:16, :] += fold_rows(up, jnp.add)
        up = up * gain
        inner = up - jnp.mean(up, -1, keepdims=True) - normal * jnp.mean(up * normal, -1, keepdims=True)
        total = add[here, :] + inner * scale
        out[here, :] = total
        low[here, :] = total.astype(BF16)
    loop(TOK // CHUNK, step)
    gain_grad = jnp.sum(sums[0:8, :], 0, keepdims=True)
    bias_grad = jnp.sum(sums[8:16, :], 0, keepdims=True)
    return gain_grad, bias_grad


def attend_quarter_back(i, lens, qkv, kt, datt, out, stats, scratch, signed):
    dk, dv, dq = scratch
    places, start, live = starts_of(lens, i)
    queries = qkv[i, :, 0:WIDE].astype(F32) * 0.125
    mine = masked_heads(queries.T, 0)
    mine_rows = jnp.concatenate(
        [jnp.where(head_lanes((TOK, WIDE), h, 0), queries, 0.0).astype(BF16) for h in range(PARTS)], 0
    )
    upstream = datt[i].astype(F32)
    grads_t = jnp.concatenate([jnp.zeros((HEAD, TOK), F32), upstream], 0)
    out_t = masked_heads(grads_t, 1)
    grads = grads_t.T
    out_rows = jnp.concatenate(
        [jnp.where(head_lanes((TOK, WIDE), h, 1), grads, 0.0).astype(BF16) for h in range(PARTS)], 0
    )
    product = upstream * out[i].astype(F32)
    inner = [
        jnp.sum(fold_rows(product[HEAD * h : HEAD * (h + 1)], jnp.add), 0, keepdims=True) for h in range(PARTS)
    ]
    top = [stats[i, h : h + 1, :] for h in range(PARTS)]
    inverse = [stats[i, PARTS + h : PARTS + h + 1, :] for h in range(PARTS)]
    dq[...] = jnp.zeros_like(dq)

    def block(first, carry, diagonal):
        keys = key_rows(qkv, first, 384)
        values = key_rows(qkv, first, 128)
        okay = masked_rows(first, KB, places, start, diagonal)
        here = pl.ds(pl.multiple_of(first, KB), KB)
        lows, slopes = [], []
        scores = [dot(keys, mine[:, h * TOK : (h + 1) * TOK]) for h in range(PARTS)]
        gains = [dot(values, out_t[:, h * TOK : (h + 1) * TOK]) for h in range(PARTS)]
        for h in range(PARTS):
            s, dp = scores[h], gains[h]
            if signed:
                size, back = magnitude_of(s)
                unsigned = jnp.exp(jnp.where(okay, size - top[h], FAR)) * inverse[h]
                bend = jnp.tanh(s)
                lows.append((unsigned * bend).astype(BF16))
                slope = unsigned * ((bend * dp - inner[h]) * (s * back) + dp * (1.0 - bend * bend))
            else:
                unsigned = jnp.exp(jnp.where(okay, s - top[h], FAR)) * inverse[h]
                lows.append(unsigned.astype(BF16))
                slope = unsigned * (dp - inner[h])
            slopes.append(slope.astype(BF16))
        value_terms = dot(jnp.concatenate(lows, 1), out_rows)
        key_terms = dot(jnp.concatenate(slopes, 1), mine_rows)
        query_terms = [dot(kt[HEAD * h : HEAD * (h + 1), here], slopes[h]) for h in range(PARTS)]
        dv[here, :] += value_terms
        dk[here, :] += key_terms
        for h in range(PARTS):
            dq[HEAD * h : HEAD * (h + 1), :] += query_terms[h]
        return carry
    over_blocks(i, block, 0)
    query_grad = jnp.concatenate([dq[...] * 0.125, jnp.zeros((HEAD, TOK), F32)], 0).T
    value_grad = dv[i * TOK : (i + 1) * TOK, :]
    key_grad = dk[i * TOK : (i + 1) * TOK, :]
    lanes = lax.broadcasted_iota(jnp.int32, (TOK, 128), 1)
    return jnp.concatenate(
        [
            query_grad[:, :128],
            jnp.where(lanes < HEAD, query_grad[:, 128:], value_grad[:, :128]),
            value_grad[:, 128:],
            key_grad,
        ],
        1,
    ).astype(BF16)


EDGE = 256


def reduce_shapes(d, ff):
    return [(96, 2 * GROUP), (96, d), (96, ff // 2), (96, ff // 2), (ff // 8, d // 2), (ff // 8, d // 2), (96, EDGE)]


def backward_kernel(*refs):
    refs = list(refs)
    take = lambda n: [refs.pop(0) for _ in range(n)]
    cot, result, lens, norms = take(4)
    wholes = take(2 * JOBS)
    stash = [take(10), take(10)]
    result_o, input_o = take(2)
    grads_o = take(4)
    (edge_o,) = take(1)
    weights = take(JOBS)
    homes = take(10)
    stream, qkv, middle, nin_t, att_t, nmid_t, pre, act_t, att_out, stats = homes
    w_qkv, w_out, w_up0, w_up1, w_down0, w_down1 = weights
    cot_v, grad, low, branch, dpre, dmid, sums, edges, datt_s, datt_r, kt, dk, dv, dq, dqkv, pn_s, pn_r, held = take(18)
    sends = take(JOBS + 1)
    buffers = [take(5) for n in range(JOBS + 1)]
    ssem, rsem, lsem, csem, as_, ar, ps, pr, ms, mr = take(10)
    spot = Spot()
    r, z, rx, ry, rd, rc = spot.r, spot.z, spot.rx, spot.ry, spot.rd, spot.rc
    loads = {}

    def load(layer, *names):
        for name in names:
            if name in STASH:
                at = STASH.index(name)
                src, dst = stash[layer][at], homes[at]
            else:
                src, dst = wholes[JOBS * layer + name], weights[name]
                at = 10 + name
            loads[(layer, name)] = Keep(src, dst, lsem.at[(10 + JOBS) * layer + at])

    def ready(layer, *names):
        for name in names:
            loads[(layer, name)].wait()

    def free(layer, *names):
        if layer:
            load(0, *names)

    start = Keep(cot, cot_v, lsem.at[2 * (10 + JOBS)])
    load(1, "act_t", 4, 5, "pre", "nmid_t", 2, 3, "middle", 1, "att_t", "qkv", "out", "stats", "nin_t", 0, "stream")
    greet(spot.peers())
    peers = comm_peers()
    jobs = []
    for layer in range(LAYERS):
        qkv_g, out_g, up_g, down_g = [ref.at[layer] for ref in grads_o]
        ff, d = up_g.shape[1] // 2, down_g.shape[1] // 2
        outs = [qkv_g, out_g] + [up_g.at[:, h * ff : (h + 1) * ff] for h in (0, 1)] + [down_g.at[:, h * d : (h + 1) * d] for h in (0, 1)]
        for n, out in enumerate(outs):
            jobs.append(Reduce(sends[n], buffers[n], out, ssem, rsem, (JOBS * layer + n) * Reduce.SEMS, n == 0))
    jobs.append(Reduce(sends[JOBS], buffers[JOBS], edge_o, ssem, rsem, 2 * JOBS * Reduce.SEMS))
    steps = {}

    def step(name):
        def note(run):
            steps[name] = run
        return note

    for at, job in enumerate(jobs):
        def close(job=job, at=at):
            job.finish()
            if JOBS <= at < 2 * JOBS:
                job.drain()
                for peer in peers:
                    pl.semaphore_signal(csem.at[at - JOBS], inc=1, device_id=peer, device_id_type=MESH)
        steps.update({SECOND + at: job.send_second, NEAR + at: job.send_near, OVER_Z + at: job.send_z, CLOSE + at: close})

    def credit(at):
        if at < JOBS:
            pl.semaphore_wait(csem.at[at], len(peers))

    @step(BEGIN)
    def _():
        def begin(n):
            here = band(n * CHUNK, CHUNK)
            value = cot_v[here, :].astype(F32) * live_column(lens, spot, CHUNK, n * CHUNK)
            grad[here, :] = value
            low[here, :] = value.astype(BF16)
        start.wait()
        loop(TOK // CHUNK, begin)

    def terms(job, left, tile, right, other):
        c = lax.rem(rc, 2) if other else spot.c
        rows = left_rows(left, c)
        width = job.width // 2 if job.paired else job.width

        def part(n):
            here = cols(n, tile)
            value = dot(rows, right(n))
            for b in range(4):
                piece = value[96 * b : 96 * b + 96]
                if other:
                    job.send[b, :, here] = piece.astype(BF16)
                elif job.paired:
                    job.got[b, :, cols(spot.c, GROUP)] = piece.astype(BF16)
                else:
                    job.got[b, :, here] = (job.got[b, :, here].astype(F32) + piece).astype(BF16)
        if width == tile:
            part(0)
        else:
            loop(width // tile, part)

    def down_terms(job, right, other):
        c = lax.rem(rc, 2) if other else spot.c

        def part(b):
            value = dot(act_t[band((2 * b + c) * 384, 384), :], right())
            if other:
                job.send[b] = value.astype(BF16)
            else:
                job.got[b] = (job.got[b].astype(F32) + value).astype(BF16)
        loop(4, part)

    late = {}

    def layer_steps(layer):
        base = JOBS * layer
        signed = layer == 0
        gains = norms.at[layer]

        def both(at, needs, compute, after=()):
            job = jobs[at]

            def theirs():
                ready(layer, *needs)
                credit(at)
                compute(job, True)
                job.send_core()

            def ours():
                job.wait_core()
                compute(job, False)
                free(layer, *after)
                job.send_first()
            steps[THEIRS + at] = theirs
            steps[OURS + at] = ours

        for h in (0, 1):
            half = w_down0.shape[1]
            both(
                base + 4 + h,
                ["act_t"],
                lambda job, other, h=h: down_terms(job, lambda: low[:, h * half : (h + 1) * half], other),
                ["act_t"] if h else [],
            )
            ff = w_up0.shape[1]
            both(
                base + 2 + h,
                ["nmid_t"],
                lambda job, other, h=h: terms(job, nmid_t, 512, lambda n: dpre[:, cols(n + h * (ff // 512), 512)], other),
                ["nmid_t"] if h else [],
            )
        both(base + 1, ["att_t"], lambda job, other: terms(job, att_t, 256, lambda n: branch[:, cols(n, 256)], other), ["att_t"])
        both(
            base,
            ["nin_t"],
            lambda job, other: terms(job, nin_t, GROUP, lambda n: dqkv[...].reshape(4 * TOK, GROUP), other),
            ["nin_t"],
        )

        def slope(h):
            def run():
                ready(layer, 4, 5, "pre")
                half = w_down0.shape[1]

                def part(n):
                    here = cols(n, 512)
                    rows = pl.ds(pl.multiple_of(n * 512, 512), 512)
                    value = dot_nt(low[:, :half], w_down0[rows, :]) + dot_nt(low[:, half:], w_down1[rows, :])
                    dpre[:, here] = (pre[:, here] * value).astype(BF16)
                lax.fori_loop(3 * h, 3 * h + 3, lambda n, carry: (part(n), carry)[1], 0)
                if h:
                    free(layer, 4, 5, "pre")
            return run
        steps[SLOPE + 10 * layer + 0] = slope(0)
        steps[SLOPE + 10 * layer + 1] = slope(1)

        def through(h):
            w_up = (w_up0, w_up1)[h]

            def run():
                ready(layer, 2 + h)
                if h == 0:
                    dmid[...] = jnp.zeros_like(dmid)
                count = w_up.shape[1] // 512

                def part(n):
                    dmid[...] += dot_nt(dpre[:, cols(n + h * count, 512)], w_up[:, cols(n, 512)])
                loop(count, part)
                free(layer, 2 + h)
            return run
        steps[THROUGH + 10 * layer + 0] = through(0)
        steps[THROUGH + 10 * layer + 1] = through(1)

        @step(NORM_BACK + layer)
        def _():
            ready(layer, "middle")
            late[layer] = norm_back(middle, lambda here: dmid[here, :], gains[2:3, :], grad, grad, branch, sums)
            free(layer, "middle")

        def asked(g, which=layer):
            return rcopy(
                datt_s.at[g], datt_r.at[spot.member], as_.at[4 * which + g], ar.at[4 * which + spot.member], spot.device(g)
            )

        @step(ASK + layer)
        def _():
            ready(layer, 1)
            for g in range(4):
                value = dot_nt(w_out[192 * g : 192 * g + 192, :], branch[...]).astype(BF16)
                if layer == 0:
                    @pl.when(spot.member != g)
                    def _():
                        asked(g, 1).wait_send()
                datt_s[g] = value

                @pl.when(spot.member != g)
                def _():
                    asked(g).start()

                @pl.when(spot.member == g)
                def _():
                    datt_r[g] = datt_s[g]
            free(layer, 1)

        @step(KEYS + layer)
        def _():
            ready(layer, "qkv", "out", "stats")

            def turn_keys(j):
                kt[:, cols(j, TOK)] = qkv[j, :, 384:640].astype(F32).T.astype(BF16)
            loop(4, turn_keys)
            dk[...] = jnp.zeros_like(dk)
            dv[...] = jnp.zeros_like(dv)

        @step(ASKED + layer)
        def _():
            for g in range(4):
                @pl.when(spot.member != g)
                def _():
                    rcopy(datt_r.at[g], datt_r.at[g], as_.at[4 * layer + g], ar.at[4 * layer + g], spot.device(g)).wait_recv()

        def back(i):
            def run():
                dqkv[i] = attend_quarter_back(i, lens, qkv, kt, datt_r, att_out, stats, (dk, dv, dq), signed)
                if i == 0:
                    free(layer, "qkv", "out", "stats")
            return run
        for i in range(4):
            steps[ATTEND_BACK + 10 * layer + i] = back(i)

        def given(which, k, i):
            mate = spot.mate(1 if k == 1 else 2)[0]
            return rcopy(pn_s.at[i], pn_r.at[k - 1], ps.at[4 * which + k], pr.at[4 * which + k], mate)

        def role(i, k):
            return spot.mate(k)[1] == i if k else spot.member == i

        def partial(i):
            def run():
                if i == 3:
                    ready(layer, 0)
                value = dot_nt(dqkv[i], w_qkv[...])

                @pl.when(role(i, 0))
                def _():
                    dmid[...] = value

                @pl.when(role(i, 1))
                def _():
                    held[...] = value
                for k in (2, 3):
                    @pl.when(role(i, k))
                    def _(k=k):
                        at = 3 if k == 2 else 2
                        if layer == 0:
                            given(1, at, i).wait_send()
                        pn_s[i] = value.astype(BF16)
                        given(layer, at, i).start()
                if i == 0:
                    free(layer, 0)
            return run

        def relay(i):
            def run():
                @pl.when(role(i, 1))
                def _():
                    if layer == 0:
                        given(1, 1, i).wait_send()
                    given(layer, 2, i).wait_recv()
                    pn_s[i] = (held[...] + pn_r[1].astype(F32)).astype(BF16)
                    given(layer, 1, i).start()
            return run
        for i in range(4):
            steps[PARTIAL + 10 * layer + i] = partial(i)
            steps[RELAY + 10 * layer + i] = relay(i)

        @step(FIRST_BACK + layer)
        def _():
            ready(layer, "stream")
            given(layer, 3, 0).wait_recv()
            given(layer, 1, 0).wait_recv()

            def upstream(here):
                return dmid[here, :] + pn_r[2, here, :].astype(F32) + pn_r[0, here, :].astype(F32)
            early = norm_back(stream, upstream, gains[0:1, :], grad, grad, low, sums)
            free(layer, "stream")
            for n, value in enumerate(early + late[layer]):
                edges[4 * layer + n : 4 * layer + n + 1, :] = value

    for layer in (1, 0):
        layer_steps(layer)

    @step(RESULT_BACK)
    def _():
        swap(spot, result, result_o, ms.at[1], mr.at[1])

    @step(SWAP_BACK)
    def _():
        swap(spot, low, input_o, ms.at[0], mr.at[0])

    last = 2 * JOBS

    def edge_rows(c):
        turned = jnp.concatenate([edges[...], jnp.zeros((128 - 8, edges.shape[1]), F32)], 0).T
        return [
            jnp.where(c == 0, turned[192 * b : 192 * b + 96], turned[192 * b + 96 : 192 * b + 192]) for b in range(4)
        ]

    @step(THEIRS + last)
    def _():
        job = jobs[last]
        for b, rows in enumerate(edge_rows(lax.rem(rc, 2))):
            job.send[b, :, 0:128] = rows.astype(BF16)
            job.send[b, :, 128:256] = jnp.zeros((96, 128), BF16)
        job.send_core()

    @step(OURS + last)
    def _():
        job = jobs[last]
        job.wait_core()
        for b, rows in enumerate(edge_rows(spot.c)):
            job.got[b, :, 0:128] = (job.got[b, :, 0:128].astype(F32) + rows).astype(BF16)
        job.send_first()

    for name in BACKWARD_ORDER:
        steps.pop(name)()
    assert not steps
    for job in jobs:
        job.drain()
    for g in range(4):
        @pl.when(spot.member != g)
        def _():
            rcopy(
                datt_s.at[g], datt_r.at[spot.member], as_.at[g], ar.at[spot.member], spot.device(g)
            ).wait_send()
    for k in (1, 2, 3):
        mate = spot.mate(1 if k == 1 else 2)[0]
        rcopy(pn_s.at[0], pn_r.at[k - 1], ps.at[k], pr.at[k], mate).wait_send()
    swap_wait(spot, low, input_o, ms.at[0], mr.at[0])
    swap_wait(spot, result, result_o, ms.at[1], mr.at[1])


def backward_call(cot, result, lens, norms, wholes, stash):
    d, ff = cot.shape[1], stash[0][6].shape[1]
    any_space = pl.BlockSpec(memory_space=pl.ANY)
    vmem = pl.BlockSpec(memory_space=pltpu.VMEM)
    dma = lambda n: pltpu.SemaphoreType.DMA((n,))
    shapes = reduce_shapes(d, ff)
    sends, buffers = [], []
    for n, (rows, width) in enumerate(shapes):
        sends.append(pltpu.VMEM((4, rows, width // 2 if n == 0 else width), BF16))
        cut = (rows // 4, width) if n in (4, 5) else (16, width * 3 // 2)
        buffers += [
            pltpu.VMEM((4, rows, width), BF16),
            pltpu.VMEM((2, rows // 2, width), BF16),
            pltpu.VMEM((2, rows, width), BF16),
        ]
        buffers += [pltpu.VMEM((4,) + cut, BF16), pltpu.VMEM((3,) + cut, BF16)]
    count = 2 * JOBS + 1
    outs = pl.pallas_call(
        backward_kernel,
        out_shape=[
            jax.ShapeDtypeStruct((TOK, d), BF16),
            jax.ShapeDtypeStruct((TOK, d), BF16),
            jax.ShapeDtypeStruct((LAYERS, 24, 4 * GROUP), F32),
            jax.ShapeDtypeStruct((LAYERS, 24, d), F32),
            jax.ShapeDtypeStruct((LAYERS, 24, ff), F32),
            jax.ShapeDtypeStruct((LAYERS, ff // 32, d), F32),
            jax.ShapeDtypeStruct((24, EDGE), F32),
        ],
        in_specs=[any_space, any_space, vmem, vmem] + [any_space] * (2 * JOBS + 20),
        out_specs=[any_space, any_space] + [vmem] * 5,
        scratch_shapes=[pltpu.VMEM(whole.shape, BF16) for whole in wholes[:JOBS]]
        + [pltpu.VMEM(shape, kind) for shape, kind in stash_shapes(d, ff)]
        + [
            pltpu.VMEM((TOK, d), BF16),
            pltpu.VMEM((TOK, d), F32),
            pltpu.VMEM((TOK, d), BF16),
            pltpu.VMEM((TOK, d), BF16),
            pltpu.VMEM((TOK, ff), BF16),
            pltpu.VMEM((TOK, d), F32),
            pltpu.VMEM((16, d), F32),
            pltpu.VMEM((8, d), F32),
            pltpu.VMEM((4, 192, TOK), BF16),
            pltpu.VMEM((4, 192, TOK), BF16),
            pltpu.VMEM((WIDE, 4 * TOK), BF16),
            pltpu.VMEM((4 * TOK, WIDE), F32),
            pltpu.VMEM((4 * TOK, WIDE), F32),
            pltpu.VMEM((192, TOK), F32),
            pltpu.VMEM((4, TOK, GROUP), BF16),
            pltpu.VMEM((4, TOK, d), BF16),
            pltpu.VMEM((3, TOK, d), BF16),
            pltpu.VMEM((TOK, d), F32),
        ]
        + sends
        + buffers
        + [
            dma(count * Reduce.SEMS),
            dma(count * Reduce.SEMS),
            dma(2 * (10 + JOBS) + 1),
            pltpu.SemaphoreType.REGULAR((JOBS,)),
            dma(8),
            dma(8),
            dma(8),
            dma(8),
            dma(2),
            dma(2),
        ],
        compiler_params=pltpu.CompilerParams(collective_id=1, has_side_effects=True, vmem_limit_bytes=62 * 2**20),
    )(cot, result, lens, norms, *wholes, *stash[0], *stash[1])
    return outs


def finish_kernel(result, grad_in, qkv, out, up, down, edge, result_o, input_o, qkv_o, out_o, up_o, down_o, gains_o, biases_o, mids_o):
    result_o[0] = result[...]
    input_o[0] = grad_in[...].astype(F32)
    out_o[...] = out[...]
    up_o[...] = up[...]
    down_o[...] = down[...]
    own = edge.shape[0]
    turned = jnp.concatenate([edge[:, 0:128], jnp.zeros((128 - own, 128), F32)], 0).T
    for layer in range(LAYERS):
        parts = [
            qkv[layer, :, GROUP * g + at : GROUP * g + at + 192] for at in (0, 384, 192) for g in range(4)
        ]
        qkv_o[layer] = jnp.concatenate(parts, 1)
        for n, ref in enumerate((gains_o.at[layer, 0:1], biases_o.at[layer : layer + 1], gains_o.at[layer, 1:2], mids_o.at[layer : layer + 1])):
            ref[...] = turned[4 * layer + n : 4 * layer + n + 1, 0:own]


def backward_part(result, cot, lens, norms, wholes, stash):
    grads = backward_call(cot, result, lens, norms, wholes, stash)
    d, own = cot.shape[1], grads[2].shape[1]
    shape = lambda *sizes: jax.ShapeDtypeStruct(sizes, F32)
    return pl.pallas_call(
        finish_kernel,
        out_shape=[
            jax.ShapeDtypeStruct((1, TOK, d), BF16),
            shape(1, TOK, d),
            shape(LAYERS, own, 3 * d),
            shape(*grads[3].shape),
            shape(*grads[4].shape),
            shape(*grads[5].shape),
            shape(LAYERS, 2, own),
            shape(LAYERS, own),
            shape(LAYERS, own),
        ],
        in_specs=[pl.BlockSpec(memory_space=pltpu.VMEM)] * 7,
        out_specs=[pl.BlockSpec(memory_space=pltpu.VMEM)] * 9,
        compiler_params=pltpu.CompilerParams(vmem_limit_bytes=62 * 2**20),
    )(*grads)


def local_fast(tokens, lengths, w_qkv, w_out, w_up, w_down, gains, biases, cotangent):
    (result, cot, lens, norms), wholes, stash = forward_call(
        tokens[0], cotangent[0], lengths, w_qkv, w_out, w_up, w_down, gains, biases
    )
    return tuple(backward_part(result, cot, lens, norms, wholes, stash))


def solution(mesh):
    in_specs = (
        P("rows", "kv", None),
        P("rows", None),
        P(None, ("rows", "kv"), None),
        P(None, ("rows", "kv"), None),
        P(None, ("rows", "kv"), None),
        P(None, ("rows", "kv"), None),
        P(None, None, ("rows", "kv")),
        P(None, None, ("rows", "kv")),
        P("rows", "kv", None),
    )
    out_specs = (
        P("rows", "kv", None),
        P("rows", "kv", None),
        P(None, ("rows", "kv"), None),
        P(None, ("rows", "kv"), None),
        P(None, ("rows", "kv"), None),
        P(None, ("rows", "kv"), None),
        P(None, None, ("rows", "kv")),
        P(None, ("rows", "kv")),
        P(None, ("rows", "kv")),
    )
    fast = dict(mesh.shape) == {"rows": 8, "kv": 4}
    return jax.shard_map(local_fast if fast else local_generic, mesh=mesh, in_specs=in_specs, out_specs=out_specs, check_vma=False)
```

```python
import math

import jax
import jax.numpy as jnp
from jax import lax
from jax.experimental import pallas as pl
from jax.experimental.pallas import tpu as pltpu
from jax.sharding import PartitionSpec as P

HEADS = 12
HEAD = 64
LAYERS = 2


EPSILON = 1e-05


def norm_rows(stream, gain, bias):
    center = stream - jnp.mean(stream, -1, keepdims=True)
    spread = jnp.mean(center * center, -1, keepdims=True)
    return center * lax.rsqrt(spread + EPSILON) * gain + bias


def normalise(scores, allowed, query_live, signed):
    if signed:
        magnitude = jnp.sqrt(scores * scores + 1.0)
        ceiling = jnp.max(jnp.where(allowed > 0, magnitude, 0.0), -1, keepdims=True)
        shifted = jnp.where(allowed > 0, magnitude - ceiling, -60.0)
    else:
        ceiling = jnp.max(jnp.where(allowed > 0, scores, -10000.0), -1, keepdims=True)
        shifted = jnp.where(allowed > 0, scores - ceiling, -60.0)
    raised = jnp.exp(shifted) * allowed
    normaliser = jnp.sum(raised, -1, keepdims=True) + (1.0 - query_live)[None, :, None]
    unsigned_w = raised / normaliser
    if signed:
        return (jnp.tanh(scores) * unsigned_w, unsigned_w)
    return (unsigned_w, unsigned_w)


def make_mask(query_places, query_docs, query_live, key_places, key_docs, key_live):
    allowed = (
        (query_docs[:, None] == key_docs[None, :]) & (key_places[None, :] <= query_places[:, None])
    ).astype(jnp.float32)
    return allowed * query_live[:, None] * key_live[None, :]


def split_heads(query, keys_vals):
    model_width = query.shape[-1]
    slot_count = keys_vals.shape[0]
    query_heads = query.reshape(-1, HEADS, HEAD)
    key_heads = keys_vals[:, :model_width].reshape(slot_count, HEADS, HEAD)
    value_heads = keys_vals[:, model_width:].reshape(slot_count, HEADS, HEAD)
    return (query_heads, key_heads, value_heads)


def score_grads(scores, unsigned_w, weight_grad, inner_sum, signed):
    if signed:
        tanh_s = jnp.tanh(scores)
        magnitude = jnp.sqrt(scores * scores + 1.0)
        return unsigned_w * (
            (tanh_s * weight_grad - inner_sum) * scores / magnitude
            + weight_grad * (1.0 - tanh_s * tanh_s)
        )
    return unsigned_w * (weight_grad - inner_sum)


def attend_row(query, keys_vals, allowed, query_live, signed, scaling):
    query_heads, key_heads, value_heads = split_heads(query, keys_vals)
    scores = (
        jnp.einsum("qhd,khd->hqk", query_heads, key_heads, preferred_element_type=jnp.float32)
        * scaling
    )
    weights, unsigned_w = normalise(scores, allowed, query_live, signed)
    outcome = jnp.einsum(
        "hqk,khd->qhd",
        weights.astype(jnp.bfloat16),
        value_heads,
        preferred_element_type=jnp.float32,
    )
    return outcome.reshape(query.shape[0], query.shape[1]).astype(jnp.bfloat16)


def attend_back(query, keys_vals, grad_att, allowed, query_live, signed, scaling):
    query_heads, key_heads, value_heads = split_heads(query, keys_vals)
    slot_count = keys_vals.shape[0]
    model_width = query.shape[-1]
    scores = (
        jnp.einsum("qhd,khd->hqk", query_heads, key_heads, preferred_element_type=jnp.float32)
        * scaling
    )
    weights, unsigned_w = normalise(scores, allowed, query_live, signed)
    weights_low = weights.astype(jnp.bfloat16)
    grad_heads = grad_att.reshape(-1, HEADS, HEAD)
    weight_grad = jnp.einsum(
        "qhd,khd->hqk", grad_heads, value_heads, preferred_element_type=jnp.float32
    )
    inner_sum = jnp.sum(weight_grad * weights, -1, keepdims=True)
    score_low = score_grads(scores, unsigned_w, weight_grad, inner_sum, signed).astype(jnp.bfloat16)
    query_grad = (
        jnp.einsum("hqk,khd->qhd", score_low, key_heads, preferred_element_type=jnp.float32)
        * scaling
    )
    key_grad = (
        jnp.einsum("hqk,qhd->khd", score_low, query_heads, preferred_element_type=jnp.float32)
        * scaling
    )
    value_grad = jnp.einsum(
        "hqk,qhd->khd", weights_low, grad_heads, preferred_element_type=jnp.float32
    )
    kv_grad = jnp.concatenate(
        [key_grad.reshape(slot_count, model_width), value_grad.reshape(slot_count, model_width)], -1
    )
    return (query_grad.reshape(query.shape[0], model_width), kv_grad)


def reduce_grads(pairs, g_gain, g_bias):
    n_rows = lax.axis_size("rows")
    n_kv = lax.axis_size("kv")
    lefts = []
    rights = []
    for left_side, right_side in pairs:
        tok_count = left_side.shape[0] * left_side.shape[1]
        in_width = left_side.shape[-1]
        lefts.append(left_side.reshape(tok_count, n_rows, n_kv, in_width // (n_rows * n_kv)))
        rights.append(right_side.reshape(tok_count, right_side.shape[-1]))
    moved = (
        lax.all_to_all(lefts[0], "kv", split_axis=2, concat_axis=0, tiled=True),
        lax.all_to_all(lefts[1], "kv", split_axis=2, concat_axis=0, tiled=True),
        lax.all_to_all(lefts[2], "kv", split_axis=2, concat_axis=0, tiled=True),
        lax.all_to_all(lefts[3], "kv", split_axis=2, concat_axis=0, tiled=True),
    )
    whole = (
        lax.all_gather(rights[0], "kv", axis=0, tiled=True),
        lax.all_gather(rights[1], "kv", axis=0, tiled=True),
        lax.all_gather(rights[2], "kv", axis=0, tiled=True),
        lax.all_gather(rights[3], "kv", axis=0, tiled=True),
    )
    partial_sums = []
    for number in range(4):
        left_block = moved[number].reshape(moved[number].shape[0], -1)
        product = jnp.einsum(
            "ti,to->io", left_block, whole[number], preferred_element_type=jnp.float32
        )
        partial_sums.append(product.reshape(n_rows, -1, product.shape[-1]))
    reduced = (
        lax.psum_scatter(
            partial_sums[0].astype(jnp.bfloat16), "rows", scatter_dimension=0, tiled=True
        ).astype(jnp.float32),
        lax.psum_scatter(
            partial_sums[1].astype(jnp.bfloat16), "rows", scatter_dimension=0, tiled=True
        ).astype(jnp.float32),
        lax.psum_scatter(
            partial_sums[2].astype(jnp.bfloat16), "rows", scatter_dimension=0, tiled=True
        ).astype(jnp.float32),
        lax.psum_scatter(
            partial_sums[3].astype(jnp.bfloat16), "rows", scatter_dimension=0, tiled=True
        ).astype(jnp.float32),
    )
    norm_parts = (
        lax.psum_scatter(g_gain, ("rows", "kv"), scatter_dimension=1, tiled=True),
        lax.psum_scatter(g_bias, ("rows", "kv"), scatter_dimension=1, tiled=True),
    )
    results = tuple((piece.reshape(piece.shape[1], piece.shape[2]) for piece in reduced))
    return results + (norm_parts[0], norm_parts[1])


def local_generic(tokens, lengths, w_qkv, w_out, w_up, w_down, gains, biases, cotangent):
    rows_here, slot_dev, model_width = tokens.shape
    slot_count = slot_dev * lax.axis_size("kv")
    first_slot = lax.axis_index("kv") * slot_dev
    scaling = 1.0 / math.sqrt(HEAD)
    doc_ends = jnp.cumsum(lengths, -1)
    places = jnp.arange(slot_count, dtype=jnp.int32)
    docs_all = jnp.sum((doc_ends[:, None, :] <= places[None, :, None]).astype(jnp.int32), -1)
    live_all = (places[None, :] < doc_ends[:, -1:]).astype(jnp.float32)
    docs_here = lax.dynamic_slice_in_dim(docs_all, first_slot, slot_dev, 1)
    live_here = lax.dynamic_slice_in_dim(live_all, first_slot, slot_dev, 1)
    local_places = first_slot + jnp.arange(slot_dev, dtype=jnp.int32)
    masks = make_mask(local_places, docs_here[0], live_here[0], places, docs_all[0], live_all[0])
    stream = tokens.astype(jnp.float32)
    stored = []
    for number in range(LAYERS):
        signed = number == 0
        pieces = (
            lax.all_gather(w_qkv[number], ("rows", "kv"), axis=0, tiled=True),
            lax.all_gather(w_out[number], ("rows", "kv"), axis=0, tiled=True),
            lax.all_gather(w_up[number], ("rows", "kv"), axis=0, tiled=True),
            lax.all_gather(w_down[number], ("rows", "kv"), axis=0, tiled=True),
            lax.all_gather(gains[number], ("rows", "kv"), axis=1, tiled=True),
            lax.all_gather(biases[number], ("rows", "kv"), axis=1, tiled=True),
        )
        full_qkv, full_out, full_up, full_down, gain_pair, bias_pair = pieces
        gain_pair = gain_pair.astype(jnp.float32)
        bias_pair = bias_pair.astype(jnp.float32)
        normed_in = norm_rows(stream, gain_pair[0], bias_pair[0]).astype(jnp.bfloat16)
        projected = jnp.dot(normed_in, full_qkv, preferred_element_type=jnp.float32).astype(
            jnp.bfloat16
        )
        kv_all = lax.all_gather(projected[:, :, model_width:], "kv", axis=1, tiled=True)
        attended = jnp.stack(
            [
                attend_row(
                    projected[0, :, :model_width], kv_all[0], masks, live_here[0], signed, scaling
                )
            ]
        )
        shared = kv_all
        middle = stream + jnp.dot(attended, full_out, preferred_element_type=jnp.float32)
        normed_mid = norm_rows(middle, gain_pair[1], bias_pair[1]).astype(jnp.bfloat16)
        pre_act = jnp.dot(normed_mid, full_up, preferred_element_type=jnp.float32)
        activated = jax.nn.gelu(pre_act).astype(jnp.bfloat16)
        stored.append(
            (
                stream,
                normed_in,
                projected,
                shared,
                attended,
                middle,
                normed_mid,
                pre_act,
                activated,
                pieces,
            )
        )
        stream = middle + jnp.dot(activated, full_down, preferred_element_type=jnp.float32)
    result = (stream * live_here[..., None]).astype(jnp.bfloat16)
    residual_grad = cotangent.astype(jnp.float32) * live_here[..., None]
    collected = [None] * LAYERS
    for number in reversed(range(LAYERS)):
        signed = number == 0
        (
            stream_in,
            normed_in,
            projected,
            shared,
            attended,
            middle,
            normed_mid,
            pre_act,
            activated,
            kept,
        ) = stored[number]
        pieces = (
            lax.all_gather(w_qkv[number], ("rows", "kv"), axis=0, tiled=True),
            lax.all_gather(w_out[number], ("rows", "kv"), axis=0, tiled=True),
            lax.all_gather(w_up[number], ("rows", "kv"), axis=0, tiled=True),
            lax.all_gather(w_down[number], ("rows", "kv"), axis=0, tiled=True),
            lax.all_gather(gains[number], ("rows", "kv"), axis=1, tiled=True),
            lax.all_gather(biases[number], ("rows", "kv"), axis=1, tiled=True),
        )
        full_qkv, full_out, full_up, full_down, gain_pair, bias_pair = pieces
        gain_pair = gain_pair.astype(jnp.float32)
        bias_pair = bias_pair.astype(jnp.float32)
        down_in = residual_grad.astype(jnp.bfloat16)
        act_grad = jnp.einsum("rtd,fd->rtf", down_in, full_down, preferred_element_type=jnp.float32)
        unused, gelu_pull = jax.vjp(jax.nn.gelu, pre_act)
        pre_grad = gelu_pull(act_grad)[0].astype(jnp.bfloat16)
        mid_normed_grad = jnp.einsum(
            "rtf,df->rtd", pre_grad, full_up, preferred_element_type=jnp.float32
        )
        unused, norm_pull = jax.vjp(norm_rows, middle, gain_pair[1], bias_pair[1])
        middle_part, gain_late, bias_late = norm_pull(mid_normed_grad)
        middle_grad = residual_grad + middle_part
        branch_grad = middle_grad.astype(jnp.bfloat16)
        att_grad = jnp.einsum(
            "rte,de->rtd", branch_grad, full_out, preferred_element_type=jnp.float32
        ).astype(jnp.bfloat16)
        kv_all = shared
        query_grad, kv_grad = attend_back(
            projected[0, :, :model_width],
            kv_all[0],
            att_grad[0],
            masks,
            live_here[0],
            signed,
            scaling,
        )
        query_grads = [query_grad]
        kv_grads = [kv_grad]
        kv_here = lax.psum_scatter(
            jnp.stack(kv_grads).astype(jnp.bfloat16), "kv", scatter_dimension=1, tiled=True
        ).astype(jnp.float32)
        qkv_grad = jnp.concatenate([jnp.stack(query_grads), kv_here], -1).astype(jnp.bfloat16)
        in_normed_grad = jnp.einsum(
            "rte,de->rtd", qkv_grad, full_qkv, preferred_element_type=jnp.float32
        )
        unused, first_pull = jax.vjp(norm_rows, stream_in, gain_pair[0], bias_pair[0])
        stream_part, gain_early, bias_early = first_pull(in_normed_grad)
        residual_grad = middle_grad + stream_part
        g_gain = jnp.stack([gain_early, gain_late])
        g_bias = jnp.stack([bias_early, bias_late])
        pairs = [
            (normed_in, qkv_grad),
            (attended, branch_grad),
            (normed_mid, pre_grad),
            (activated, down_in),
        ]
        collected[number] = reduce_grads(pairs, g_gain, g_bias)
    grad_qkv = jnp.stack([collected[number][0] for number in range(LAYERS)])
    grad_out = jnp.stack([collected[number][1] for number in range(LAYERS)])
    grad_up = jnp.stack([collected[number][2] for number in range(LAYERS)])
    grad_down = jnp.stack([collected[number][3] for number in range(LAYERS)])
    grad_gains = jnp.stack([collected[number][4] for number in range(LAYERS)])
    grad_biases = jnp.stack([collected[number][5][0] for number in range(LAYERS)])
    grad_mid_biases = jnp.stack([collected[number][5][1] for number in range(LAYERS)])
    return (
        result,
        residual_grad,
        grad_qkv,
        grad_out,
        grad_up,
        grad_down,
        grad_gains,
        grad_biases,
        grad_mid_biases,
    )


F32 = jnp.float32
BF16 = jnp.bfloat16
MESH = pl.DeviceIdType.MESH
ZN = 4


def flip(value, unit):
    bit = lax.rem(lax.div(value, unit), 2)
    return value + unit - 2 * unit * bit


def places_of():
    r = lax.axis_index("rows")
    z = lax.axis_index("kv")
    return r, z, flip(r, 2), flip(r, 4), flip(flip(r, 2), 4), flip(r, 1)


def turn(z, k):
    return lax.rem(z + k, ZN)


def rcopy(src, dst, ssem, rsem, device):
    return pltpu.make_async_remote_copy(
        src_ref=src, dst_ref=dst, send_sem=ssem, recv_sem=rsem, device_id=device, device_id_type=MESH
    )


def band(start, size):
    return pl.ds(pl.multiple_of(start, 16), size)


def greet(peers):
    barrier = pltpu.get_barrier_semaphore()
    for peer in peers:
        pl.semaphore_signal(barrier, inc=1, device_id=peer, device_id_type=MESH)
    pl.semaphore_wait(barrier, len(peers))


def comm_peers():
    r, z, rx, ry, rd, rc = places_of()
    return [(r, turn(z, 1)), (r, turn(z, 2)), (r, turn(z, 3)), (rx, z), (ry, z), (rc, z)]


def col_step(width):
    return 256 if width % 256 == 0 else 128


def add_rows(dst, src, rows):
    def step(i, carry):
        here = band(i * 16, 16)
        dst[here, :] = (dst[here, :].astype(F32) + src[here, :].astype(F32)).astype(BF16)
        return carry
    lax.fori_loop(0, rows // 16, step, 0)


SEND = 0
PLANE = 100
PASS = 200
LAST = 300
WHOLE = 400
NORM = 600
SHARE = 700
PROJECT = 800
ATTEND = 900
OUTPUT = 1000
UP = 1100
DOWN = 1200
EARLY_THEIRS = 1400
EARLY_OURS = 1500
EARLY_SECOND = 1600
TOKENS = 500
COTANGENT = 510
WIDEN = 520
RESULT = 530
COTANGENT_LOW = 540
SECOND = 0
NEAR = 100
OVER_Z = 200
CLOSE = 300
THEIRS = 400
OURS = 500
SLOPE = 600
THROUGH = 700
NORM_BACK = 800
ASK = 900
KEYS = 1000
ASKED = 1100
ATTEND_BACK = 1200
PARTIAL = 1300
FIRST_BACK = 1400
RELAY = 1600
BEGIN = 1500
SWAP_BACK = 1510
RESULT_BACK = 1520

FORWARD_ORDER = [
    0, 1, 2, 101, 3, 100, 201, 500, 102, 301, 4, 103, 401, 200, 520, 5, 202, 300, 104, 400, 6, 600, 800, 203,
    802, 105, 106, 7, 8, 303, 403, 302, 9, 700, 801, 204, 402, 803, 900, 901, 107, 10, 205, 902, 903, 206,
    304, 11, 108, 305, 404, 1000, 405, 306, 109, 1100, 207, 1101, 1200, 1201, 110, 406, 601, 208, 810, 307,
    812, 407, 111, 701, 510, 811, 209, 308, 813, 910, 911, 912, 408, 913, 210, 309, 211, 1001, 1110, 409, 310,
    1111, 311, 410, 411,
]
BACKWARD_ORDER = [
    1500, 410, 610, 611, 411, 710, 510, 10, 711, 801, 901, 408, 1001, 511, 11, 1520, 409, 1101, 1213, 508,
    1313, 1212, 1312, 8, 1613, 110, 1211, 1311, 1612, 1210, 1310, 509, 108, 1611, 406, 407, 1610, 210, 506, 6,
    111, 507, 7, 208, 1401, 600, 700, 601, 701, 800, 900, 107, 310, 404, 106, 109, 1000, 211, 207, 308, 9,
    402, 1100, 504, 1203, 206, 4, 1202, 104, 307, 209, 502, 401, 1303, 2, 1302, 1201, 306, 204, 1603, 1602,
    501, 1, 1301, 1200, 102, 1300, 400, 309, 311, 403, 405, 101, 1601, 1600, 500, 0, 202, 201, 304, 505, 5,
    100, 1400, 1510, 503, 412, 301, 512, 12, 105, 200, 112, 103, 302, 212, 205, 3, 312, 203, 305, 300, 303,
]


GROUP = 640
TOK = 256
WIDE = 256
PARTS = HEADS // 4
CHUNK = 64
FAR = -1e30
KB = 256
JOBS = 6


def dot(a, b):
    return jnp.dot(a, b, preferred_element_type=F32)


def dot_nt(a, b):
    return lax.dot_general(a, b, (((1,), (1,)), ((), ())), preferred_element_type=F32)


def dot_tn(a, b):
    return lax.dot_general(a, b, (((0,), (0,)), ((), ())), preferred_element_type=F32)


def loop(count, body):
    def step(i, carry):
        body(i)
        return carry
    lax.fori_loop(0, count, step, 0)


def cols(i, size):
    return pl.ds(pl.multiple_of(i * size, 128), size)


class Spot:
    def __init__(self):
        self.r, self.z, self.rx, self.ry, self.rd, self.rc = places_of()
        self.c = lax.rem(self.r, 2)
        self.parity = lax.rem(self.z, 2)
        self.member = 2 * self.c + self.parity
        self.swaps = (self.c + lax.div(self.z, 2)) == 1
        self.partner = (self.rc, flip(self.z, 2))

    def mate(self, k):
        r = self.rc if k >= 2 else self.r
        z = flip(self.z, 1) if k % 2 else self.z
        return (r, z), 2 * lax.rem(r, 2) + lax.rem(z, 2)

    def device(self, member):
        return (self.r - self.c + lax.div(member, 2), self.z - self.parity + lax.rem(member, 2))

    def peers(self):
        return comm_peers() + [(self.rc, flip(self.z, 1)), self.partner]


class Gather:
    SEMS = 11

    def __init__(self, own, whole, bufs, ssem, rsem, base, paired=False):
        self.own, self.whole, self.bufs = own, whole, bufs
        self.ssem, self.rsem, self.base = ssem, rsem, base
        self.split, self.paired = len(bufs) > 0, paired
        self.rows, self.width = whole.shape[0] // 8, whole.shape[1]
        self.sent = []

    def _copy(self, src, dst, at, device):
        return rcopy(src, dst, self.ssem.at[self.base + at], self.rsem.at[self.base + at], device)

    def _block(self, r, half=None):
        if half is None:
            return self.whole.at[band(r * self.rows, self.rows), :]
        part = self.rows // 2
        return self.whole.at[band(r * self.rows + half * part, part), :]

    def _cored(self, r, column):
        if not self.paired:
            return self._block(r)
        return self.whole.at[band(r * self.rows, self.rows), cols(column, self.width // 2)]

    def _send(self, src, dst, at, device):
        copy = self._copy(src, dst, at, device)
        copy.start()
        self.sent.append(copy)

    def prepare(self):
        r, z = places_of()[:2]
        if self.split:
            zbuf = self.bufs[0]
            half = self.width // 2
            values = [self.own(place) for place in (0, 1)] if self.paired else [self.own[...].astype(F32)]
            for place, own in enumerate(values):
                packed = jnp.concatenate(
                    [own[:16], jnp.concatenate([own[16:, :half], own[16:, half:]], 0)], 1
                ).astype(BF16)
                if self.paired:
                    self.bufs[1][place] = packed
                else:
                    zbuf[pl.ds(z, 1)] = packed[None]
            if self.paired:
                zbuf[pl.ds(z, 1)] = self.bufs[1][pl.ds(lax.rem(z, 2), 1)]
        else:
            part = self.rows // ZN
            self.whole[band(r * self.rows + z * part, part), :] = self.own[...]

    def _zref(self, z):
        if self.split:
            return self.bufs[0].at[z]
        part = self.rows // ZN
        return self.whole.at[band(places_of()[0] * self.rows + z * part, part), :]

    def send_z(self):
        r, z = places_of()[:2]
        for k in (1, 2, 3):
            there = turn(z, k)
            src = self.bufs[1].at[lax.rem(there, 2)] if self.paired else self._zref(z)
            self._send(src, self._zref(z), k - 1, (r, there))

    def wait_z(self):
        r, z = places_of()[:2]
        for k in (1, 2, 3):
            ref = self._zref(turn(z, ZN - k))
            self._copy(ref, ref, k - 1, (r, turn(z, ZN - k))).wait_recv()
        if self.split:
            zbuf = self.bufs[0]
            half = self.width // 2
            step = col_step(half)
            for side in (0, 1):
                def assemble(i, side=side):
                    at = pl.multiple_of(self.width + i * step, 128)
                    here = pl.ds(pl.multiple_of(side * half + i * step, 128), step)
                    parts = []
                    for piece in range(ZN):
                        parts.append(zbuf[piece, :, here].astype(F32))
                        parts.append(zbuf[piece, :, pl.ds(at, step)].astype(F32)[8 * side : 8 * side + 8])
                    self.whole[band(r * self.rows, self.rows), here] = jnp.concatenate(parts, 0).astype(BF16)
                loop(half // step, assemble)

    def send_plane(self):
        r, z, rx, ry, rd, rc = places_of()
        own = self._block(r)
        self._send(own, own, 3, (rx, z))
        self._send(own, own, 4, (ry, z))
        self._core(r, 7)

    def _core(self, block, at):
        r, z, rx, ry, rd, rc = places_of()
        ref = self._cored(block, lax.rem(rc, 2))
        self._send(ref, ref, at, (rc, z))

    def forward(self):
        r, z, rx, ry, rd, rc = places_of()
        first, second = self._block(rx), self._block(ry)
        self._copy(first, first, 3, (rx, z)).wait_recv()
        part = self._block(rx, 0)
        self._send(part, part, 5, (ry, z))
        self._copy(second, second, 4, (ry, z)).wait_recv()
        part = self._block(ry, 1)
        self._send(part, part, 6, (rx, z))
        self._core(rx, 8)
        self._core(ry, 9)

    def forward_last(self):
        r, z, rx, ry, rd, rc = places_of()
        part = self._block(rd, 0)
        self._copy(part, part, 5, (ry, z)).wait_recv()
        part = self._block(rd, 1)
        self._copy(part, part, 6, (rx, z)).wait_recv()
        self._core(rd, 10)

    def finish(self):
        r, z, rx, ry, rd, rc = places_of()
        for at, block in ((7, r), (8, rx), (9, ry), (10, rd)):
            ref = self._cored(flip(block, 1), lax.rem(r, 2))
            self._copy(ref, ref, at, (rc, z)).wait_recv()

    def drain(self):
        for copy in self.sent:
            copy.wait_send()


def swap(spot, src, dst, ssem, rsem):
    @pl.when(spot.swaps)
    def _():
        rcopy(src, dst, ssem, rsem, spot.partner).start()

    @pl.when(jnp.logical_not(spot.swaps))
    def _():
        pltpu.make_async_copy(src, dst, rsem).start()


def swap_wait(spot, src, dst, ssem, rsem):
    @pl.when(spot.swaps)
    def _():
        rcopy(src, dst, ssem, rsem, spot.partner).wait()

    @pl.when(jnp.logical_not(spot.swaps))
    def _():
        pltpu.make_async_copy(src, dst, rsem).wait()


def starts_of(lens, i):
    places = lax.broadcasted_iota(jnp.int32, (1, TOK), 1) + i * TOK
    end = jnp.zeros((1, 1), jnp.int32)
    start = jnp.zeros((1, TOK), jnp.int32)
    for n in range(4):
        end = end + lens[0:1, n : n + 1]
        start = jnp.maximum(start, jnp.where(end <= places, end, 0))
    live = places < end
    return places, jnp.where(live, start, 1 << 20), live


def live_column(lens, spot, rows, first):
    places = lax.broadcasted_iota(jnp.int32, (rows, 1), 0) + spot.member * TOK + first
    end = lens[0:1, 0:1] + lens[0:1, 1:2] + lens[0:1, 2:3] + lens[0:1, 3:4]
    return (places < end).astype(F32)


def centred(value):
    center = value - jnp.mean(value, -1, keepdims=True)
    spread = jnp.mean(center * center, -1, keepdims=True)
    return center * lax.rsqrt(spread + EPSILON)


def fold_rows(value, op):
    rows = value.shape[0]
    parts = [value[8 * n : 8 * n + 8] for n in range(rows // 8)]
    while len(parts) > 1:
        parts = [op(parts[n], parts[n + 1]) if n + 1 < len(parts) else parts[n] for n in range(0, len(parts), 2)]
    return parts[0]


def head_lanes(shape, h, offset):
    lanes = lax.broadcasted_iota(jnp.int32, shape, 1)
    return lax.div(lanes, HEAD) == h + offset


def masked_rows(first, rows, places, start, diagonal):
    keys = lax.broadcasted_iota(jnp.int32, (rows, TOK), 0) + first
    okay = keys >= start
    return okay & (keys <= places) if diagonal else okay


def over_blocks(i, body, carry):
    per = TOK // KB if KB <= TOK else 1
    if i:
        carry = lax.fori_loop(0, i * per, lambda n, c: body(n * KB, c, False), carry)
    for n in range(per):
        carry = body(i * TOK + n * KB, carry, True)
    return carry


def key_rows(qkv, first, at):
    quarter = lax.div(first, TOK)
    here = pl.ds(pl.multiple_of(lax.rem(first, TOK), KB), KB)
    return qkv[quarter, here, at : at + WIDE]


def masked_heads(value_t, offset):
    rows = lax.div(lax.broadcasted_iota(jnp.int32, value_t.shape, 0), HEAD)
    return jnp.concatenate([jnp.where(rows == h + offset, value_t, 0.0) for h in range(PARTS)], 1).astype(BF16)


def magnitude_of(s):
    square = s * s + 1.0
    back = lax.rsqrt(square)
    return square * back, back


def attend_quarter(i, lens, qkv, vt, acc, o_ref, stats, signed):
    places, start, live = starts_of(lens, i)
    mine = masked_heads(qkv[i, :, 0:WIDE].astype(F32).T * 0.125, 0)
    acc[...] = jnp.zeros_like(acc)

    def block(first, carry, diagonal):
        keys = key_rows(qkv, first, 384)
        okay = masked_rows(first, KB, places, start, diagonal)
        here = pl.ds(pl.multiple_of(first, KB), KB)
        out, lows, shrinks = [], [], []
        scores = [dot(keys, mine[:, h * TOK : (h + 1) * TOK]) for h in range(PARTS)]
        for h in range(PARTS):
            old, total = carry[2 * h], carry[2 * h + 1]
            s = scores[h]
            value = jnp.where(okay, magnitude_of(s)[0] if signed else s, FAR)
            new = jnp.maximum(old, jnp.max(fold_rows(value, jnp.maximum), 0, keepdims=True))
            raised = jnp.exp(value - new)
            shrink = jnp.exp(old - new)
            lows.append((jnp.tanh(s) * raised if signed else raised).astype(BF16))
            shrinks.append(shrink)
            out += [new, total * shrink + jnp.sum(fold_rows(raised, jnp.add), 0, keepdims=True)]
        terms = [dot(vt[HEAD * (h + 1) : HEAD * (h + 2), here], lows[h]) for h in range(PARTS)]
        for h in range(PARTS):
            rows = slice(HEAD * h, HEAD * (h + 1))
            acc[rows, :] = acc[rows, :] * shrinks[h] + terms[h]
        return tuple(out)
    lowest = jnp.full((1, TOK), 0.0 if signed else -10000.0, F32)
    carry = over_blocks(i, block, (lowest, jnp.zeros((1, TOK), F32)) * PARTS)
    for h in range(PARTS):
        inverse = 1.0 / (carry[2 * h + 1] + (1.0 - live.astype(F32)))
        stats[i, h : h + 1, :] = carry[2 * h]
        stats[i, PARTS + h : PARTS + h + 1, :] = inverse
        acc[HEAD * h : HEAD * (h + 1), :] = acc[HEAD * h : HEAD * (h + 1), :] * inverse
    o_ref[i] = acc[...].astype(BF16)


def gelu_both(x):
    root = 0.7978845608028654
    square = x * x
    bend = jnp.tanh(root * (x + 0.044715 * x * square))
    half = 0.5 * (1.0 + bend)
    return x * half, half + 0.5 * x * (1.0 - bend * bend) * root * (1.0 + 3 * 0.044715 * square)


class Keep:
    def __init__(self, src, dst, sem):
        self.copy = pltpu.make_async_copy(src, dst, sem)
        self.copy.start()
        self.open = True

    def wait(self):
        if self.open:
            self.copy.wait()
        self.open = False


STASH = ("stream", "qkv", "middle", "nin_t", "att_t", "nmid_t", "pre", "act_t", "out", "stats")


def stash_shapes(d, ff):
    return [
        ((TOK, d), F32),
        ((4, TOK, GROUP), BF16),
        ((TOK, d), F32),
        ((d, 4 * TOK), BF16),
        ((d, TOK), BF16),
        ((d, TOK), BF16),
        ((TOK, ff), F32),
        ((ff, TOK), BF16),
        ((4, 192, TOK), F32),
        ((4, 8, TOK), F32),
    ]


def forward_kernel(*refs):
    refs = list(refs)
    take = lambda n: [refs.pop(0) for _ in range(n)]
    tok, cot, lengths = take(3)
    sources = take(4)
    gains, biases = take(2)
    cot_o, lens_o, norms_o = take(3)
    whole_o = take(2 * JOBS)
    stash_o = [take(10), take(10)]
    wholes = take(2 * JOBS)
    zbuf = [take((2, 1, 1, 1, 0, 0)[n % JOBS]) for n in range(2 * JOBS)]
    tok_v, lens_in, lens_v, stream, nin0, nin1, qkv, vt, outs, stats, o_ref, att0, att1, pre, act, act_t, nin_t, nt_mid, normed, middle = take(20)
    ssem, rsem, osem, stsem, ns, nr, os_, or_, ms, mr = take(10)
    spot = Spot()
    lens_in[...] = jnp.zeros_like(lens_in)
    lens_in[0:1, 0:4] = lengths[...]
    greet(spot.peers())
    jobs = []

    def grouped(layer):
        def pair(place):
            vectors = [ref[layer, which : which + 1, :].astype(F32) for which in (0, 1) for ref in (gains, biases)]
            own = vectors[0].shape[1]
            top = jnp.concatenate([jnp.concatenate(vectors, 0), jnp.zeros((4, 128 - own), F32)], 1)
            edge = jnp.concatenate([top, jnp.zeros((124, 128), F32)], 0).T[:own, :HEAD]
            parts = []
            for g in (place, place + 2):
                for at in (0, 2, 1):
                    parts.append(sources[0][layer, :, 768 * at + 192 * g : 768 * at + 192 * g + 192].astype(F32))
                parts.append(edge)
            return jnp.concatenate(parts, 1)
        return pair

    for layer in range(LAYERS):
        out_in, up_in, down_in = [source.at[layer] for source in sources[1:]]
        ff, d = up_in.shape[1] // 2, down_in.shape[1] // 2
        owns = [grouped(layer), out_in] + [up_in.at[:, h * ff : (h + 1) * ff] for h in (0, 1)] + [down_in.at[:, h * d : (h + 1) * d] for h in (0, 1)]
        for n, own in enumerate(owns):
            at = layer * JOBS + n
            jobs.append(Gather(own, wholes[at], zbuf[at], ssem, rsem, at * Gather.SEMS, n == 0))
    kept = {}

    def keep(name, src, dst, sem):
        kept[name] = Keep(src, dst, sem)

    def settle(name):
        if name in kept:
            kept[name].wait()

    def stash(layer, name, src):
        at = STASH.index(name)
        keep((layer, name), src, stash_o[layer][at], stsem.at[10 * layer + at])

    steps = {}

    def step(name):
        def note(run):
            steps[name] = run
        return note

    for n, job in enumerate(jobs):
        def first(job=job):
            job.prepare()
            job.send_z()

        def plane(job=job):
            job.wait_z()
            job.send_plane()

        def done(job=job, n=n):
            job.finish()
            src = wholes[n]
            if n % JOBS == 0:
                src = src.at[:, cols(spot.c, GROUP)]
            keep(("whole", n), src, whole_o[n], osem.at[n])
        steps.update({SEND + n: first, PLANE + n: plane, PASS + n: job.forward, LAST + n: job.forward_last, WHOLE + n: done})

    @step(TOKENS)
    def _():
        swap(spot, tok, tok_v, ms.at[0], mr.at[0])
        swap(spot, lens_in, lens_v, ms.at[1], mr.at[1])

    @step(COTANGENT)
    def _():
        swap(spot, cot, cot_o, ms.at[2], mr.at[2])

    @step(WIDEN)
    def _():
        swap_wait(spot, tok, tok_v, ms.at[0], mr.at[0])
        swap_wait(spot, lens_in, lens_v, ms.at[1], mr.at[1])
        lens_o[...] = lens_v[...]

        def widen(n):
            here = band(n * CHUNK, CHUNK)
            stream[here, :] = tok_v[here, :].astype(F32)
        loop(TOK // CHUNK, widen)
        stash(0, "stream", stream)

    def layer_steps(layer):
        base = layer * JOBS
        w_qkv, w_out, w_up0, w_up1, w_down0, w_down1 = wholes[base : base + JOBS]
        nin = (nin0, nin1)[layer]
        att = (att0, att1)[layer]
        signed = layer == 0

        def gathered(k):
            mate, member = spot.mate(k)
            return rcopy(nin.at[member], nin.at[member], ns.at[4 * layer + k], nr.at[4 * layer + k], mate)

        def give(k, member):
            mate = spot.mate(1 if k == 1 else 2)[0]
            return rcopy(nin.at[member], nin.at[member], ns.at[4 * layer + k], nr.at[4 * layer + k], mate)

        @step(NORM + layer)
        def _():
            edge = w_qkv[:, pl.ds(pl.multiple_of(spot.c * GROUP + 512, 128), 128)].astype(F32).T
            norms_o[layer] = edge[HEAD : HEAD + 8]

            def first_norm(n):
                here = band(n * CHUNK, CHUNK)
                value = centred(stream[here, :]) * norms_o[layer, 0:1, :] + norms_o[layer, 1:2, :]
                nin[spot.member, here, :] = value.astype(BF16)
            loop(TOK // CHUNK, first_norm)
            give(1, spot.member).start()
            give(2, spot.member).start()

        @step(SHARE + layer)
        def _():
            gathered(1).wait_recv()
            give(3, spot.mate(1)[1]).start()

        def project(k):
            def run():
                member = spot.member
                if k:
                    member = spot.mate(k)[1]
                    if k != 1:
                        gathered(k).wait_recv()
                group = dot(nin[member], w_qkv[:, cols(spot.c, GROUP)]).astype(BF16)
                if (layer, k) == (1, 0):
                    settle((0, "qkv"))
                    settle((0, "nin_t"))
                qkv[pl.ds(member, 1)] = group[None]
                at = pl.multiple_of(member * TOK, TOK)
                vt[:, pl.ds(at, TOK)] = group[:, 128:384].astype(F32).T.astype(BF16)
                nin_t[:, pl.ds(at, TOK)] = nin[member].astype(F32).T.astype(BF16)
                if k == 3:
                    stash(layer, "qkv", qkv)
                    stash(layer, "nin_t", nin_t)
            return run
        for k in range(4):
            steps[PROJECT + 10 * layer + k] = project(k)

        def returned(i):
            return rcopy(
                o_ref.at[layer, i], att.at[band(spot.member * 192, 192), :], os_.at[4 * layer + i], or_.at[4 * layer + spot.member], spot.device(i)
            )

        def attend(i):
            def run():
                attend_quarter(i, lens_v, qkv, vt, outs.at[layer, i], o_ref.at[layer], stats.at[layer], signed)

                @pl.when(spot.member != i)
                def _():
                    returned(i).start()

                @pl.when(spot.member == i)
                def _():
                    att[i * 192 : (i + 1) * 192, :] = o_ref[layer, i]
                if i == 3:
                    stash(layer, "out", outs.at[layer])
                    stash(layer, "stats", stats.at[layer])
            return run
        for i in range(4):
            steps[ATTEND + 10 * layer + i] = attend(i)

        @step(OUTPUT + layer)
        def _():
            for i in range(4):
                @pl.when(spot.member != i)
                def _():
                    ref = att.at[i * 192 : (i + 1) * 192, :]
                    rcopy(ref, ref, os_.at[4 * layer + i], or_.at[4 * layer + i], spot.device(i)).wait_recv()
            stash(layer, "att_t", att)
            settle((0, "middle"))
            middle[...] = stream[...] + dot_tn(att[...], w_out[...])
            stash(layer, "middle", middle)

            def second_norm(n):
                here = band(n * CHUNK, CHUNK)
                value = centred(middle[here, :]) * norms_o[layer, 2:3, :] + norms_o[layer, 3:4, :]
                normed[here, :] = value.astype(BF16)
            loop(TOK // CHUNK, second_norm)
            settle((0, "nmid_t"))
            nt_mid[...] = normed[...].astype(F32).T.astype(BF16)
            stash(layer, "nmid_t", nt_mid)
            settle((0, "pre"))
            settle((0, "act_t"))

        def up(h):
            w_up = (w_up0, w_up1)[h]
            tile = 512
            count = w_up.shape[1] // tile

            def run():
                def part(n):
                    value = dot(normed[...], w_up[:, cols(n, tile)])
                    here = cols(h * count + n, tile)
                    active, pre[:, here] = gelu_both(value)
                    act[:, here] = active.astype(BF16)
                    act_t[pl.ds(pl.multiple_of((h * count + n) * tile, tile), tile), :] = active.T.astype(BF16)
                loop(count, part)
                if h:
                    stash(layer, "pre", pre)
                    stash(layer, "act_t", act_t)
            return run

        def down(h):
            w_down = (w_down0, w_down1)[h]
            width = w_down.shape[1]

            def run():
                settle((layer, "stream"))

                def part(n):
                    here = cols(n + h * (width // 128), 128)
                    stream[:, here] = middle[:, here] + dot(act[...], w_down[:, cols(n, 128)])
                if width % 384 == 0:
                    here = slice(h * width, (h + 1) * width)
                    stream[:, here] = middle[:, here] + dot(act[...], w_down[...])
                else:
                    loop(width // 128, part)
                if h and layer == 0:
                    stash(1, "stream", stream)
            return run
        for h in (0, 1):
            steps[UP + 10 * layer + h] = up(h)
            if layer == 0:
                steps[DOWN + 10 * layer + h] = down(h)

        def close():
            for k in (1, 2):
                give(k, spot.member).wait_send()
            give(3, spot.mate(1)[1]).wait_send()
            for i in range(4):
                @pl.when(spot.member != i)
                def _():
                    returned(i).wait_send()
        return close

    closes = [layer_steps(layer) for layer in range(LAYERS)]

    for name in FORWARD_ORDER:
        steps.pop(name)()
    assert not steps
    for job in jobs:
        job.drain()
    for close in closes:
        close()
    for copy in kept.values():
        copy.wait()
    swap_wait(spot, cot, cot_o, ms.at[2], mr.at[2])


def forward_call(tok, cot, lengths, w_qkv, w_out, w_up, w_down, gains, biases):
    d, ff = tok.shape[1], w_up.shape[2]
    shapes = [(d, 2 * GROUP), (d, d), (d, ff // 2), (d, ff // 2), (ff, d // 2), (ff, d // 2)] * LAYERS
    zshapes = []
    for n, (rows, width) in enumerate(shapes):
        if n % JOBS < 4:
            zshapes.append(pltpu.VMEM((ZN, 16, width * 3 // 2), BF16))
        if n % JOBS == 0:
            zshapes.append(pltpu.VMEM((2, 16, width * 3 // 2), BF16))
    any_space = pl.BlockSpec(memory_space=pl.ANY)
    vmem = pl.BlockSpec(memory_space=pltpu.VMEM)
    stash = [jax.ShapeDtypeStruct(shape, kind) for shape, kind in stash_shapes(d, ff)]
    dma = lambda n: pltpu.SemaphoreType.DMA((n,))
    kept_shapes = [(rows, GROUP if n % JOBS == 0 else width) for n, (rows, width) in enumerate(shapes)]
    outs = pl.pallas_call(
        forward_kernel,
        out_shape=[
            jax.ShapeDtypeStruct((TOK, d), BF16),
            jax.ShapeDtypeStruct((8, 128), jnp.int32),
            jax.ShapeDtypeStruct((LAYERS, 8, d), F32),
        ]
        + [jax.ShapeDtypeStruct(shape, BF16) for shape in kept_shapes]
        + stash
        + stash,
        in_specs=[any_space, any_space] + [vmem] * 7,
        out_specs=[any_space, vmem, vmem] + [any_space] * (2 * JOBS + 20),
        scratch_shapes=[pltpu.VMEM(shape, BF16) for shape in shapes]
        + zshapes
        + [
            pltpu.VMEM((TOK, d), BF16),
            pltpu.VMEM((8, 128), jnp.int32),
            pltpu.VMEM((8, 128), jnp.int32),
            pltpu.VMEM((TOK, d), F32),
            pltpu.VMEM((4, TOK, d), BF16),
            pltpu.VMEM((4, TOK, d), BF16),
            pltpu.VMEM((4, TOK, GROUP), BF16),
            pltpu.VMEM((WIDE, 4 * TOK), BF16),
            pltpu.VMEM((LAYERS, 4, 192, TOK), F32),
            pltpu.VMEM((LAYERS, 4, 8, TOK), F32),
            pltpu.VMEM((LAYERS, 4, 192, TOK), BF16),
            pltpu.VMEM((d, TOK), BF16),
            pltpu.VMEM((d, TOK), BF16),
            pltpu.VMEM((TOK, ff), F32),
            pltpu.VMEM((TOK, ff), BF16),
            pltpu.VMEM((ff, TOK), BF16),
            pltpu.VMEM((d, 4 * TOK), BF16),
            pltpu.VMEM((d, TOK), BF16),
            pltpu.VMEM((TOK, d), BF16),
            pltpu.VMEM((TOK, d), F32),
        ]
        + [dma(2 * JOBS * Gather.SEMS), dma(2 * JOBS * Gather.SEMS), dma(2 * JOBS), dma(20), dma(8), dma(8), dma(8), dma(8), dma(4), dma(4)],
        compiler_params=pltpu.CompilerParams(collective_id=0, has_side_effects=True, vmem_limit_bytes=62 * 2**20),
    )(tok, cot, lengths, w_qkv, w_out, w_up, w_down, gains, biases)
    at = 3 + 2 * JOBS
    return outs[:3], outs[3:at], (outs[at : at + 10], outs[at + 10 : at + 20])


class Reduce:
    SEMS = 10

    def __init__(self, send, bufs, out, ssem, rsem, base, paired=False):
        self.send = send
        self.got, self.half, self.near = bufs[:3]
        self.zs, self.zr = bufs[3:5]
        self.out = out
        self.ssem, self.rsem, self.base = ssem, rsem, base
        self.rows, self.width = self.got.shape[1], self.got.shape[2]
        self.split, self.paired = self.zs.shape[1] == 16, paired
        self.sent = []

    def _copy(self, src, dst, at, device):
        return rcopy(src, dst, self.ssem.at[self.base + at], self.rsem.at[self.base + at], device)

    def _send(self, src, dst, at, device):
        copy = self._copy(src, dst, at, device)
        copy.start()
        self.sent.append(copy)

    def _got(self, core):
        if self.paired:
            return self.got.at[:, :, cols(core, self.width // 2)]
        return self.got

    def send_core(self):
        r, z, rx, ry, rd, rc = places_of()
        self._send(self.send, self._got(lax.rem(r, 2)), 0, (rc, z))

    def wait_core(self):
        r, z, rx, ry, rd, rc = places_of()
        ref = self._got(lax.rem(rc, 2))
        self._copy(ref, ref, 0, (rc, z)).wait_recv()

    def _part(self, other, i):
        part = self.rows // 2
        return self.got.at[lax.div(other, 2), pl.ds(i * part, part)]

    def send_first(self):
        r, z, rx, ry, rd, rc = places_of()
        part = self.rows // 2
        self._send(self._part(rd, 0), self.half.at[0], 1, (ry, z))
        self._send(self._part(rd, 1), self.half.at[1], 2, (rx, z))

    def send_second(self):
        r, z, rx, ry, rd, rc = places_of()
        part = self.rows // 2
        self._send(self._part(rx, 1), self.near.at[0, pl.ds(part, part)], 3, (rx, z))
        self._send(self._part(ry, 0), self.near.at[1, pl.ds(0, part)], 4, (ry, z))

    def send_near(self):
        r, z, rx, ry, rd, rc = places_of()
        part = self.rows // 2
        for i, side, other in ((0, ry, rx), (1, rx, ry)):
            self._copy(self.half.at[i], self.half.at[i], 1 + i, (side, z)).wait_recv()
            block = self._part(other, i)
            add_rows(block, self.half.at[i], part)
            self._send(block, self.near.at[i, pl.ds(i * part, part)], 5 + i, (other, z))

    def send_z(self):
        r, z, rx, ry, rd, rc = places_of()
        part = self.rows // 2
        for at, i, h, side in ((3, 0, 1, rx), (4, 1, 0, ry), (5, 0, 0, rx), (6, 1, 1, ry)):
            ref = self.near.at[i, pl.ds(h * part, part)]
            self._copy(ref, ref, at, (side, z)).wait_recv()
        own = self.got.at[lax.div(r, 2)]
        near = self.near

        def total(rows, here):
            return own[rows, here].astype(F32) + near[0, rows, here].astype(F32) + near[1, rows, here].astype(F32)

        if self.split:
            half = self.width // 2
            step = col_step(half)

            def cut(i):
                at = pl.ds(pl.multiple_of(self.width + i * step, 128), step)
                sums = [
                    total(slice(None), pl.ds(pl.multiple_of(side * half + i * step, 128), step)) for side in (0, 1)
                ]
                for piece in range(ZN):
                    for side in (0, 1):
                        here = pl.ds(pl.multiple_of(side * half + i * step, 128), step)
                        self.zs[piece, :, here] = sums[side][24 * piece : 24 * piece + 16].astype(BF16)
                    self.zs[piece, :, at] = jnp.concatenate(
                        [sums[side][24 * piece + 16 : 24 * piece + 24] for side in (0, 1)], 0
                    ).astype(BF16)
            loop(half // step, cut)
        else:
            size = self.rows // ZN
            for piece in range(ZN):
                def cut_rows(i, piece=piece):
                    self.zs[piece, band(i * 16, 16), :] = total(band(piece * size + i * 16, 16), slice(None)).astype(BF16)
                loop(size // 16, cut_rows)
        for k in (1, 2, 3):
            self._send(self.zs.at[turn(z, k)], self.zr.at[k - 1], 6 + k, (r, turn(z, k)))

    def finish(self):
        r, z = places_of()[:2]
        for k in (1, 2, 3):
            ref = self.zr.at[k - 1]
            self._copy(ref, ref, 6 + k, (r, turn(z, ZN - k))).wait_recv()
        half, width = self.width // 2, self.width
        if self.paired:
            for place, value in (
                (lax.rem(z, 2), self.zs[z].astype(F32) + self.zr[1].astype(F32)),
                (lax.rem(z + 1, 2), self.zr[0].astype(F32) + self.zr[2].astype(F32)),
            ):
                for side in (0, 1):
                    here = cols(place + 2 * side, GROUP)
                    self.out[pl.ds(0, 16), here] = value[:, side * GROUP : (side + 1) * GROUP]
                    self.out[pl.ds(16, 8), here] = value[8 * side : 8 * side + 8, width:]
        elif self.split:
            value = self.zs[z].astype(F32)
            for k in range(3):
                value = value + self.zr[k].astype(F32)
            self.out[pl.ds(0, 16), :] = value[:, :width]
            self.out[pl.ds(16, 8), pl.ds(0, half)] = value[:8, width:]
            self.out[pl.ds(16, 8), pl.ds(half, half)] = value[8:, width:]
        else:
            def total(i):
                here = band(i * 16, 16)
                value = self.zs[z, here, :].astype(F32)
                for k in range(3):
                    value = value + self.zr[k, here, :].astype(F32)
                self.out[here, :] = value
            loop(self.out.shape[0] // 16, total)

    def drain(self):
        for copy in self.sent:
            copy.wait_send()
        self.sent = []


def left_rows(left, c):
    return jnp.concatenate([left[band((2 * b + c) * 96, 96), :] for b in range(4)], 0)


def norm_back(source, upstream, gain, add, out, low, sums):
    sums[...] = jnp.zeros_like(sums)

    def step(n):
        here = band(n * CHUNK, CHUNK)
        value = source[here, :]
        center = value - jnp.mean(value, -1, keepdims=True)
        scale = lax.rsqrt(jnp.mean(center * center, -1, keepdims=True) + EPSILON)
        normal = center * scale
        up = upstream(here)
        sums[0:8, :] += fold_rows(up * normal, jnp.add)
        sums[8:16, :] += fold_rows(up, jnp.add)
        up = up * gain
        inner = up - jnp.mean(up, -1, keepdims=True) - normal * jnp.mean(up * normal, -1, keepdims=True)
        total = add[here, :] + inner * scale
        out[here, :] = total
        low[here, :] = total.astype(BF16)
    loop(TOK // CHUNK, step)
    gain_grad = jnp.sum(sums[0:8, :], 0, keepdims=True)
    bias_grad = jnp.sum(sums[8:16, :], 0, keepdims=True)
    return gain_grad, bias_grad


def attend_quarter_back(i, lens, qkv, kt, datt, out, stats, scratch, signed):
    dk, dv, dq = scratch
    places, start, live = starts_of(lens, i)
    queries = qkv[i, :, 0:WIDE].astype(F32) * 0.125
    mine = masked_heads(queries.T, 0)
    mine_rows = jnp.concatenate(
        [jnp.where(head_lanes((TOK, WIDE), h, 0), queries, 0.0).astype(BF16) for h in range(PARTS)], 0
    )
    upstream = datt[i].astype(F32)
    grads_t = jnp.concatenate([jnp.zeros((HEAD, TOK), F32), upstream], 0)
    out_t = masked_heads(grads_t, 1)
    grads = grads_t.T
    out_rows = jnp.concatenate(
        [jnp.where(head_lanes((TOK, WIDE), h, 1), grads, 0.0).astype(BF16) for h in range(PARTS)], 0
    )
    product = upstream * out[i].astype(F32)
    inner = [
        jnp.sum(fold_rows(product[HEAD * h : HEAD * (h + 1)], jnp.add), 0, keepdims=True) for h in range(PARTS)
    ]
    top = [stats[i, h : h + 1, :] for h in range(PARTS)]
    inverse = [stats[i, PARTS + h : PARTS + h + 1, :] for h in range(PARTS)]
    dq[...] = jnp.zeros_like(dq)

    def block(first, carry, diagonal):
        keys = key_rows(qkv, first, 384)
        values = key_rows(qkv, first, 128)
        okay = masked_rows(first, KB, places, start, diagonal)
        here = pl.ds(pl.multiple_of(first, KB), KB)
        lows, slopes = [], []
        scores = [dot(keys, mine[:, h * TOK : (h + 1) * TOK]) for h in range(PARTS)]
        gains = [dot(values, out_t[:, h * TOK : (h + 1) * TOK]) for h in range(PARTS)]
        for h in range(PARTS):
            s, dp = scores[h], gains[h]
            if signed:
                size, back = magnitude_of(s)
                unsigned = jnp.exp(jnp.where(okay, size - top[h], FAR)) * inverse[h]
                bend = jnp.tanh(s)
                lows.append((unsigned * bend).astype(BF16))
                slope = unsigned * ((bend * dp - inner[h]) * (s * back) + dp * (1.0 - bend * bend))
            else:
                unsigned = jnp.exp(jnp.where(okay, s - top[h], FAR)) * inverse[h]
                lows.append(unsigned.astype(BF16))
                slope = unsigned * (dp - inner[h])
            slopes.append(slope.astype(BF16))
        value_terms = dot(jnp.concatenate(lows, 1), out_rows)
        key_terms = dot(jnp.concatenate(slopes, 1), mine_rows)
        query_terms = [dot(kt[HEAD * h : HEAD * (h + 1), here], slopes[h]) for h in range(PARTS)]
        dv[here, :] += value_terms
        dk[here, :] += key_terms
        for h in range(PARTS):
            dq[HEAD * h : HEAD * (h + 1), :] += query_terms[h]
        return carry
    over_blocks(i, block, 0)
    query_grad = jnp.concatenate([dq[...] * 0.125, jnp.zeros((HEAD, TOK), F32)], 0).T
    value_grad = dv[i * TOK : (i + 1) * TOK, :]
    key_grad = dk[i * TOK : (i + 1) * TOK, :]
    lanes = lax.broadcasted_iota(jnp.int32, (TOK, 128), 1)
    return jnp.concatenate(
        [
            query_grad[:, :128],
            jnp.where(lanes < HEAD, query_grad[:, 128:], value_grad[:, :128]),
            value_grad[:, 128:],
            key_grad,
        ],
        1,
    ).astype(BF16)


EDGE = 256


def reduce_shapes(d, ff):
    return [(96, 2 * GROUP), (96, d), (96, ff // 2), (96, ff // 2), (ff // 8, d // 2), (ff // 8, d // 2), (96, EDGE)]


def backward_kernel(*refs):
    refs = list(refs)
    take = lambda n: [refs.pop(0) for _ in range(n)]
    cot, lens, norms = take(3)
    wholes = take(2 * JOBS)
    stash = [take(10), take(10)]
    result_o, input_o = take(2)
    grads_o = take(4)
    (edge_o,) = take(1)
    weights = take(JOBS)
    homes = take(10)
    stream, qkv, middle, nin_t, att_t, nmid_t, pre, act_t, att_out, stats = homes
    w_qkv, w_out, w_up0, w_up1, w_down0, w_down1 = weights
    cot_v, grad, low, branch, dpre, dmid, sums, edges, datt_s, datt_r, kt, dk, dv, dq, dqkv, pn_s, pn_r, held, res = take(19)
    sends = take(JOBS + 1)
    buffers = [take(5) for n in range(JOBS + 1)]
    ssem, rsem, lsem, csem, as_, ar, ps, pr, ms, mr = take(10)
    spot = Spot()
    r, z, rx, ry, rd, rc = spot.r, spot.z, spot.rx, spot.ry, spot.rd, spot.rc
    loads = {}

    def load(layer, *names):
        for name in names:
            if name in STASH:
                at = STASH.index(name)
                src, dst = stash[layer][at], homes[at]
            else:
                src, dst = wholes[JOBS * layer + name], weights[name]
                at = 10 + name
            loads[(layer, name)] = Keep(src, dst, lsem.at[(10 + JOBS) * layer + at])

    def ready(layer, *names):
        for name in names:
            loads[(layer, name)].wait()

    def free(layer, *names):
        if layer:
            load(0, *names)

    start = Keep(cot, cot_v, lsem.at[2 * (10 + JOBS)])
    load(1, "act_t", 4, 5, "pre", "nmid_t", 2, 3, "middle", 1, "att_t", "qkv", "out", "stats", "nin_t", 0, "stream")
    greet(spot.peers())
    peers = comm_peers()
    jobs = []
    for layer in range(LAYERS):
        qkv_g, out_g, up_g, down_g = [ref.at[layer] for ref in grads_o]
        ff, d = up_g.shape[1] // 2, down_g.shape[1] // 2
        outs = [qkv_g, out_g] + [up_g.at[:, h * ff : (h + 1) * ff] for h in (0, 1)] + [down_g.at[:, h * d : (h + 1) * d] for h in (0, 1)]
        for n, out in enumerate(outs):
            jobs.append(Reduce(sends[n], buffers[n], out, ssem, rsem, (JOBS * layer + n) * Reduce.SEMS, n == 0))
    jobs.append(Reduce(sends[JOBS], buffers[JOBS], edge_o, ssem, rsem, 2 * JOBS * Reduce.SEMS))
    steps = {}

    def step(name):
        def note(run):
            steps[name] = run
        return note

    for at, job in enumerate(jobs):
        def close(job=job, at=at):
            job.finish()
            if JOBS <= at < 2 * JOBS:
                job.drain()
                for peer in peers:
                    pl.semaphore_signal(csem.at[at - JOBS], inc=1, device_id=peer, device_id_type=MESH)
        steps.update({SECOND + at: job.send_second, NEAR + at: job.send_near, OVER_Z + at: job.send_z, CLOSE + at: close})

    def credit(at):
        if at < JOBS:
            pl.semaphore_wait(csem.at[at], len(peers))

    @step(BEGIN)
    def _():
        def begin(n):
            here = band(n * CHUNK, CHUNK)
            value = cot_v[here, :].astype(F32) * live_column(lens, spot, CHUNK, n * CHUNK)
            grad[here, :] = value
            low[here, :] = value.astype(BF16)
        start.wait()
        loop(TOK // CHUNK, begin)

    def terms(job, left, tile, right, other):
        c = lax.rem(rc, 2) if other else spot.c
        rows = left_rows(left, c)
        width = job.width // 2 if job.paired else job.width

        def part(n):
            here = cols(n, tile)
            value = dot(rows, right(n))
            for b in range(4):
                piece = value[96 * b : 96 * b + 96]
                if other:
                    job.send[b, :, here] = piece.astype(BF16)
                elif job.paired:
                    job.got[b, :, cols(spot.c, GROUP)] = piece.astype(BF16)
                else:
                    job.got[b, :, here] = (job.got[b, :, here].astype(F32) + piece).astype(BF16)
        if width == tile:
            part(0)
        else:
            loop(width // tile, part)

    def down_terms(job, right, other):
        c = lax.rem(rc, 2) if other else spot.c

        def part(b):
            value = dot(act_t[band((2 * b + c) * 384, 384), :], right())
            if other:
                job.send[b] = value.astype(BF16)
            else:
                job.got[b] = (job.got[b].astype(F32) + value).astype(BF16)
        loop(4, part)

    late = {}

    def layer_steps(layer):
        base = JOBS * layer
        signed = layer == 0
        gains = norms.at[layer]

        def both(at, needs, compute, after=()):
            job = jobs[at]

            def theirs():
                ready(layer, *needs)
                credit(at)
                compute(job, True)
                job.send_core()

            def ours():
                job.wait_core()
                compute(job, False)
                free(layer, *after)
                job.send_first()
            steps[THEIRS + at] = theirs
            steps[OURS + at] = ours

        for h in (0, 1):
            half = w_down0.shape[1]
            both(
                base + 4 + h,
                ["act_t"],
                lambda job, other, h=h: down_terms(job, lambda: low[:, h * half : (h + 1) * half], other),
                [],
            )
            ff = w_up0.shape[1]
            both(
                base + 2 + h,
                ["nmid_t"],
                lambda job, other, h=h: terms(job, nmid_t, 512, lambda n: dpre[:, cols(n + h * (ff // 512), 512)], other),
                ["nmid_t"] if h else [],
            )
        both(base + 1, ["att_t"], lambda job, other: terms(job, att_t, 256, lambda n: branch[:, cols(n, 256)], other), ["att_t"])
        both(
            base,
            ["nin_t"],
            lambda job, other: terms(job, nin_t, GROUP, lambda n: dqkv[...].reshape(4 * TOK, GROUP), other),
            ["nin_t"],
        )

        def slope(h):
            def run():
                ready(layer, 4, 5, "pre")
                half = w_down0.shape[1]

                def part(n):
                    here = cols(n, 512)
                    rows = pl.ds(pl.multiple_of(n * 512, 512), 512)
                    value = dot_nt(low[:, :half], w_down0[rows, :]) + dot_nt(low[:, half:], w_down1[rows, :])
                    dpre[:, here] = (pre[:, here] * value).astype(BF16)
                lax.fori_loop(3 * h, 3 * h + 3, lambda n, carry: (part(n), carry)[1], 0)
                if h:
                    free(layer, "pre")
            return run
        steps[SLOPE + 10 * layer + 0] = slope(0)
        steps[SLOPE + 10 * layer + 1] = slope(1)

        def through(h):
            w_up = (w_up0, w_up1)[h]

            def run():
                ready(layer, 2 + h)
                if h == 0:
                    dmid[...] = jnp.zeros_like(dmid)
                count = w_up.shape[1] // 512

                def part(n):
                    dmid[...] += dot_nt(dpre[:, cols(n + h * count, 512)], w_up[:, cols(n, 512)])
                loop(count, part)
                free(layer, 2 + h)
            return run
        steps[THROUGH + 10 * layer + 0] = through(0)
        steps[THROUGH + 10 * layer + 1] = through(1)

        @step(NORM_BACK + layer)
        def _():
            ready(layer, "middle")
            late[layer] = norm_back(middle, lambda here: dmid[here, :], gains[2:3, :], grad, grad, branch, sums)

        def asked(g, which=layer):
            return rcopy(
                datt_s.at[g], datt_r.at[spot.member], as_.at[4 * which + g], ar.at[4 * which + spot.member], spot.device(g)
            )

        @step(ASK + layer)
        def _():
            ready(layer, 1)
            for g in range(4):
                value = dot_nt(w_out[192 * g : 192 * g + 192, :], branch[...]).astype(BF16)
                if layer == 0:
                    @pl.when(spot.member != g)
                    def _():
                        asked(g, 1).wait_send()
                datt_s[g] = value

                @pl.when(spot.member != g)
                def _():
                    asked(g).start()

                @pl.when(spot.member == g)
                def _():
                    datt_r[g] = datt_s[g]
            free(layer, 1)

        @step(KEYS + layer)
        def _():
            ready(layer, "qkv", "out", "stats")

            def turn_keys(j):
                kt[:, cols(j, TOK)] = qkv[j, :, 384:640].astype(F32).T.astype(BF16)
            loop(4, turn_keys)
            dk[...] = jnp.zeros_like(dk)
            dv[...] = jnp.zeros_like(dv)

        @step(ASKED + layer)
        def _():
            for g in range(4):
                @pl.when(spot.member != g)
                def _():
                    rcopy(datt_r.at[g], datt_r.at[g], as_.at[4 * layer + g], ar.at[4 * layer + g], spot.device(g)).wait_recv()

        def back(i):
            def run():
                dqkv[i] = attend_quarter_back(i, lens, qkv, kt, datt_r, att_out, stats, (dk, dv, dq), signed)
                if i == 0:
                    free(layer, "qkv", "out", "stats")
            return run
        for i in range(4):
            steps[ATTEND_BACK + 10 * layer + i] = back(i)

        def given(which, k, i):
            mate = spot.mate(1 if k == 1 else 2)[0]
            return rcopy(pn_s.at[i], pn_r.at[k - 1], ps.at[4 * which + k], pr.at[4 * which + k], mate)

        def role(i, k):
            return spot.mate(k)[1] == i if k else spot.member == i

        def partial(i):
            def run():
                if i == 3:
                    ready(layer, 0)
                value = dot_nt(dqkv[i], w_qkv[...])

                @pl.when(role(i, 0))
                def _():
                    dmid[...] = value

                @pl.when(role(i, 1))
                def _():
                    held[...] = value
                for k in (2, 3):
                    @pl.when(role(i, k))
                    def _(k=k):
                        at = 3 if k == 2 else 2
                        if layer == 0:
                            given(1, at, i).wait_send()
                        pn_s[i] = value.astype(BF16)
                        given(layer, at, i).start()
                if i == 0:
                    free(layer, 0)
            return run

        def relay(i):
            def run():
                @pl.when(role(i, 1))
                def _():
                    if layer == 0:
                        given(1, 1, i).wait_send()
                    given(layer, 2, i).wait_recv()
                    pn_s[i] = (held[...] + pn_r[1].astype(F32)).astype(BF16)
                    given(layer, 1, i).start()
            return run
        for i in range(4):
            steps[PARTIAL + 10 * layer + i] = partial(i)
            steps[RELAY + 10 * layer + i] = relay(i)

        @step(FIRST_BACK + layer)
        def _():
            ready(layer, "stream")
            given(layer, 3, 0).wait_recv()
            given(layer, 1, 0).wait_recv()

            def upstream(here):
                return dmid[here, :] + pn_r[2, here, :].astype(F32) + pn_r[0, here, :].astype(F32)
            early = norm_back(stream, upstream, gains[0:1, :], grad, grad, low, sums)
            free(layer, "stream")
            for n, value in enumerate(early + late[layer]):
                edges[4 * layer + n : 4 * layer + n + 1, :] = value

    for layer in (1, 0):
        layer_steps(layer)

    @step(RESULT_BACK)
    def _():
        ready(1, "middle", "act_t", 4, 5)
        half = w_down0.shape[1]
        for h, w_down in ((0, w_down0), (1, w_down1)):
            here = slice(h * half, (h + 1) * half)
            value = middle[:, here] + dot_tn(act_t[...], w_down[...])
            res[:, here] = (value * live_column(lens, spot, TOK, 0)).astype(BF16)
        swap(spot, res, result_o, ms.at[1], mr.at[1])
        free(1, "middle", "act_t", 4, 5)

    @step(SWAP_BACK)
    def _():
        swap(spot, low, input_o, ms.at[0], mr.at[0])

    last = 2 * JOBS

    def edge_rows(c):
        turned = jnp.concatenate([edges[...], jnp.zeros((128 - 8, edges.shape[1]), F32)], 0).T
        return [
            jnp.where(c == 0, turned[192 * b : 192 * b + 96], turned[192 * b + 96 : 192 * b + 192]) for b in range(4)
        ]

    @step(THEIRS + last)
    def _():
        job = jobs[last]
        for b, rows in enumerate(edge_rows(lax.rem(rc, 2))):
            job.send[b, :, 0:128] = rows.astype(BF16)
            job.send[b, :, 128:256] = jnp.zeros((96, 128), BF16)
        job.send_core()

    @step(OURS + last)
    def _():
        job = jobs[last]
        job.wait_core()
        for b, rows in enumerate(edge_rows(spot.c)):
            job.got[b, :, 0:128] = (job.got[b, :, 0:128].astype(F32) + rows).astype(BF16)
        job.send_first()

    for name in BACKWARD_ORDER:
        steps.pop(name)()
    assert not steps
    for job in jobs:
        job.drain()
    for g in range(4):
        @pl.when(spot.member != g)
        def _():
            rcopy(
                datt_s.at[g], datt_r.at[spot.member], as_.at[g], ar.at[spot.member], spot.device(g)
            ).wait_send()
    for k in (1, 2, 3):
        mate = spot.mate(1 if k == 1 else 2)[0]
        rcopy(pn_s.at[0], pn_r.at[k - 1], ps.at[k], pr.at[k], mate).wait_send()
    swap_wait(spot, low, input_o, ms.at[0], mr.at[0])
    swap_wait(spot, res, result_o, ms.at[1], mr.at[1])


def backward_call(cot, lens, norms, wholes, stash):
    d, ff = cot.shape[1], stash[0][6].shape[1]
    any_space = pl.BlockSpec(memory_space=pl.ANY)
    vmem = pl.BlockSpec(memory_space=pltpu.VMEM)
    dma = lambda n: pltpu.SemaphoreType.DMA((n,))
    shapes = reduce_shapes(d, ff)
    sends, buffers = [], []
    for n, (rows, width) in enumerate(shapes):
        sends.append(pltpu.VMEM((4, rows, width // 2 if n == 0 else width), BF16))
        cut = (rows // 4, width) if n in (4, 5) else (16, width * 3 // 2)
        buffers += [
            pltpu.VMEM((4, rows, width), BF16),
            pltpu.VMEM((2, rows // 2, width), BF16),
            pltpu.VMEM((2, rows, width), BF16),
        ]
        buffers += [pltpu.VMEM((4,) + cut, BF16), pltpu.VMEM((3,) + cut, BF16)]
    count = 2 * JOBS + 1
    outs = pl.pallas_call(
        backward_kernel,
        out_shape=[
            jax.ShapeDtypeStruct((TOK, d), BF16),
            jax.ShapeDtypeStruct((TOK, d), BF16),
            jax.ShapeDtypeStruct((LAYERS, 24, 4 * GROUP), F32),
            jax.ShapeDtypeStruct((LAYERS, 24, d), F32),
            jax.ShapeDtypeStruct((LAYERS, 24, ff), F32),
            jax.ShapeDtypeStruct((LAYERS, ff // 32, d), F32),
            jax.ShapeDtypeStruct((24, EDGE), F32),
        ],
        in_specs=[any_space, vmem, vmem] + [any_space] * (2 * JOBS + 20),
        out_specs=[any_space, any_space] + [vmem] * 5,
        scratch_shapes=[pltpu.VMEM(whole.shape, BF16) for whole in wholes[:JOBS]]
        + [pltpu.VMEM(shape, kind) for shape, kind in stash_shapes(d, ff)]
        + [
            pltpu.VMEM((TOK, d), BF16),
            pltpu.VMEM((TOK, d), F32),
            pltpu.VMEM((TOK, d), BF16),
            pltpu.VMEM((TOK, d), BF16),
            pltpu.VMEM((TOK, ff), BF16),
            pltpu.VMEM((TOK, d), F32),
            pltpu.VMEM((16, d), F32),
            pltpu.VMEM((8, d), F32),
            pltpu.VMEM((4, 192, TOK), BF16),
            pltpu.VMEM((4, 192, TOK), BF16),
            pltpu.VMEM((WIDE, 4 * TOK), BF16),
            pltpu.VMEM((4 * TOK, WIDE), F32),
            pltpu.VMEM((4 * TOK, WIDE), F32),
            pltpu.VMEM((192, TOK), F32),
            pltpu.VMEM((4, TOK, GROUP), BF16),
            pltpu.VMEM((4, TOK, d), BF16),
            pltpu.VMEM((3, TOK, d), BF16),
            pltpu.VMEM((TOK, d), F32),
            pltpu.VMEM((TOK, d), BF16),
        ]
        + sends
        + buffers
        + [
            dma(count * Reduce.SEMS),
            dma(count * Reduce.SEMS),
            dma(2 * (10 + JOBS) + 1),
            pltpu.SemaphoreType.REGULAR((JOBS,)),
            dma(8),
            dma(8),
            dma(8),
            dma(8),
            dma(2),
            dma(2),
        ],
        compiler_params=pltpu.CompilerParams(collective_id=1, has_side_effects=True, vmem_limit_bytes=62 * 2**20),
    )(cot, lens, norms, *wholes, *stash[0], *stash[1])
    return outs


def finish_kernel(result, grad_in, qkv, out, up, down, edge, result_o, input_o, qkv_o, out_o, up_o, down_o, gains_o, biases_o, mids_o):
    result_o[0] = result[...]
    input_o[0] = grad_in[...].astype(F32)
    out_o[...] = out[...]
    up_o[...] = up[...]
    down_o[...] = down[...]
    own = edge.shape[0]
    turned = jnp.concatenate([edge[:, 0:128], jnp.zeros((128 - own, 128), F32)], 0).T
    for layer in range(LAYERS):
        parts = [
            qkv[layer, :, GROUP * g + at : GROUP * g + at + 192] for at in (0, 384, 192) for g in range(4)
        ]
        qkv_o[layer] = jnp.concatenate(parts, 1)
        for n, ref in enumerate((gains_o.at[layer, 0:1], biases_o.at[layer : layer + 1], gains_o.at[layer, 1:2], mids_o.at[layer : layer + 1])):
            ref[...] = turned[4 * layer + n : 4 * layer + n + 1, 0:own]


def backward_part(cot, lens, norms, wholes, stash):
    grads = backward_call(cot, lens, norms, wholes, stash)
    d, own = cot.shape[1], grads[2].shape[1]
    shape = lambda *sizes: jax.ShapeDtypeStruct(sizes, F32)
    return pl.pallas_call(
        finish_kernel,
        out_shape=[
            jax.ShapeDtypeStruct((1, TOK, d), BF16),
            shape(1, TOK, d),
            shape(LAYERS, own, 3 * d),
            shape(*grads[3].shape),
            shape(*grads[4].shape),
            shape(*grads[5].shape),
            shape(LAYERS, 2, own),
            shape(LAYERS, own),
            shape(LAYERS, own),
        ],
        in_specs=[pl.BlockSpec(memory_space=pltpu.VMEM)] * 7,
        out_specs=[pl.BlockSpec(memory_space=pltpu.VMEM)] * 9,
        compiler_params=pltpu.CompilerParams(vmem_limit_bytes=62 * 2**20),
    )(*grads)


def local_fast(tokens, lengths, w_qkv, w_out, w_up, w_down, gains, biases, cotangent):
    (cot, lens, norms), wholes, stash = forward_call(
        tokens[0], cotangent[0], lengths, w_qkv, w_out, w_up, w_down, gains, biases
    )
    return tuple(backward_part(cot, lens, norms, wholes, stash))


def solution(mesh):
    in_specs = (
        P("rows", "kv", None),
        P("rows", None),
        P(None, ("rows", "kv"), None),
        P(None, ("rows", "kv"), None),
        P(None, ("rows", "kv"), None),
        P(None, ("rows", "kv"), None),
        P(None, None, ("rows", "kv")),
        P(None, None, ("rows", "kv")),
        P("rows", "kv", None),
    )
    out_specs = (
        P("rows", "kv", None),
        P("rows", "kv", None),
        P(None, ("rows", "kv"), None),
        P(None, ("rows", "kv"), None),
        P(None, ("rows", "kv"), None),
        P(None, ("rows", "kv"), None),
        P(None, None, ("rows", "kv")),
        P(None, ("rows", "kv")),
        P(None, ("rows", "kv")),
    )
    fast = dict(mesh.shape) == {"rows": 8, "kv": 4}
    return jax.shard_map(local_fast if fast else local_generic, mesh=mesh, in_specs=in_specs, out_specs=out_specs, check_vma=False)
```

```python
import math

import jax
import jax.numpy as jnp
from jax import lax
from jax.experimental import pallas as pl
from jax.experimental.pallas import tpu as pltpu
from jax.sharding import PartitionSpec as P

HEADS = 12
HEAD = 64
LAYERS = 2


EPSILON = 1e-05


def norm_rows(stream, gain, bias):
    center = stream - jnp.mean(stream, -1, keepdims=True)
    spread = jnp.mean(center * center, -1, keepdims=True)
    return center * lax.rsqrt(spread + EPSILON) * gain + bias


def normalise(scores, allowed, query_live, signed):
    if signed:
        magnitude = jnp.sqrt(scores * scores + 1.0)
        ceiling = jnp.max(jnp.where(allowed > 0, magnitude, 0.0), -1, keepdims=True)
        shifted = jnp.where(allowed > 0, magnitude - ceiling, -60.0)
    else:
        ceiling = jnp.max(jnp.where(allowed > 0, scores, -10000.0), -1, keepdims=True)
        shifted = jnp.where(allowed > 0, scores - ceiling, -60.0)
    raised = jnp.exp(shifted) * allowed
    normaliser = jnp.sum(raised, -1, keepdims=True) + (1.0 - query_live)[None, :, None]
    unsigned_w = raised / normaliser
    if signed:
        return (jnp.tanh(scores) * unsigned_w, unsigned_w)
    return (unsigned_w, unsigned_w)


def make_mask(query_places, query_docs, query_live, key_places, key_docs, key_live):
    allowed = (
        (query_docs[:, None] == key_docs[None, :]) & (key_places[None, :] <= query_places[:, None])
    ).astype(jnp.float32)
    return allowed * query_live[:, None] * key_live[None, :]


def split_heads(query, keys_vals):
    model_width = query.shape[-1]
    slot_count = keys_vals.shape[0]
    query_heads = query.reshape(-1, HEADS, HEAD)
    key_heads = keys_vals[:, :model_width].reshape(slot_count, HEADS, HEAD)
    value_heads = keys_vals[:, model_width:].reshape(slot_count, HEADS, HEAD)
    return (query_heads, key_heads, value_heads)


def score_grads(scores, unsigned_w, weight_grad, inner_sum, signed):
    if signed:
        tanh_s = jnp.tanh(scores)
        magnitude = jnp.sqrt(scores * scores + 1.0)
        return unsigned_w * (
            (tanh_s * weight_grad - inner_sum) * scores / magnitude
            + weight_grad * (1.0 - tanh_s * tanh_s)
        )
    return unsigned_w * (weight_grad - inner_sum)


def attend_row(query, keys_vals, allowed, query_live, signed, scaling):
    query_heads, key_heads, value_heads = split_heads(query, keys_vals)
    scores = (
        jnp.einsum("qhd,khd->hqk", query_heads, key_heads, preferred_element_type=jnp.float32)
        * scaling
    )
    weights, unsigned_w = normalise(scores, allowed, query_live, signed)
    outcome = jnp.einsum(
        "hqk,khd->qhd",
        weights.astype(jnp.bfloat16),
        value_heads,
        preferred_element_type=jnp.float32,
    )
    return outcome.reshape(query.shape[0], query.shape[1]).astype(jnp.bfloat16)


def attend_back(query, keys_vals, grad_att, allowed, query_live, signed, scaling):
    query_heads, key_heads, value_heads = split_heads(query, keys_vals)
    slot_count = keys_vals.shape[0]
    model_width = query.shape[-1]
    scores = (
        jnp.einsum("qhd,khd->hqk", query_heads, key_heads, preferred_element_type=jnp.float32)
        * scaling
    )
    weights, unsigned_w = normalise(scores, allowed, query_live, signed)
    weights_low = weights.astype(jnp.bfloat16)
    grad_heads = grad_att.reshape(-1, HEADS, HEAD)
    weight_grad = jnp.einsum(
        "qhd,khd->hqk", grad_heads, value_heads, preferred_element_type=jnp.float32
    )
    inner_sum = jnp.sum(weight_grad * weights, -1, keepdims=True)
    score_low = score_grads(scores, unsigned_w, weight_grad, inner_sum, signed).astype(jnp.bfloat16)
    query_grad = (
        jnp.einsum("hqk,khd->qhd", score_low, key_heads, preferred_element_type=jnp.float32)
        * scaling
    )
    key_grad = (
        jnp.einsum("hqk,qhd->khd", score_low, query_heads, preferred_element_type=jnp.float32)
        * scaling
    )
    value_grad = jnp.einsum(
        "hqk,qhd->khd", weights_low, grad_heads, preferred_element_type=jnp.float32
    )
    kv_grad = jnp.concatenate(
        [key_grad.reshape(slot_count, model_width), value_grad.reshape(slot_count, model_width)], -1
    )
    return (query_grad.reshape(query.shape[0], model_width), kv_grad)


def reduce_grads(pairs, g_gain, g_bias):
    n_rows = lax.axis_size("rows")
    n_kv = lax.axis_size("kv")
    lefts = []
    rights = []
    for left_side, right_side in pairs:
        tok_count = left_side.shape[0] * left_side.shape[1]
        in_width = left_side.shape[-1]
        lefts.append(left_side.reshape(tok_count, n_rows, n_kv, in_width // (n_rows * n_kv)))
        rights.append(right_side.reshape(tok_count, right_side.shape[-1]))
    moved = (
        lax.all_to_all(lefts[0], "kv", split_axis=2, concat_axis=0, tiled=True),
        lax.all_to_all(lefts[1], "kv", split_axis=2, concat_axis=0, tiled=True),
        lax.all_to_all(lefts[2], "kv", split_axis=2, concat_axis=0, tiled=True),
        lax.all_to_all(lefts[3], "kv", split_axis=2, concat_axis=0, tiled=True),
    )
    whole = (
        lax.all_gather(rights[0], "kv", axis=0, tiled=True),
        lax.all_gather(rights[1], "kv", axis=0, tiled=True),
        lax.all_gather(rights[2], "kv", axis=0, tiled=True),
        lax.all_gather(rights[3], "kv", axis=0, tiled=True),
    )
    partial_sums = []
    for number in range(4):
        left_block = moved[number].reshape(moved[number].shape[0], -1)
        product = jnp.einsum(
            "ti,to->io", left_block, whole[number], preferred_element_type=jnp.float32
        )
        partial_sums.append(product.reshape(n_rows, -1, product.shape[-1]))
    reduced = (
        lax.psum_scatter(
            partial_sums[0].astype(jnp.bfloat16), "rows", scatter_dimension=0, tiled=True
        ).astype(jnp.float32),
        lax.psum_scatter(
            partial_sums[1].astype(jnp.bfloat16), "rows", scatter_dimension=0, tiled=True
        ).astype(jnp.float32),
        lax.psum_scatter(
            partial_sums[2].astype(jnp.bfloat16), "rows", scatter_dimension=0, tiled=True
        ).astype(jnp.float32),
        lax.psum_scatter(
            partial_sums[3].astype(jnp.bfloat16), "rows", scatter_dimension=0, tiled=True
        ).astype(jnp.float32),
    )
    norm_parts = (
        lax.psum_scatter(g_gain, ("rows", "kv"), scatter_dimension=1, tiled=True),
        lax.psum_scatter(g_bias, ("rows", "kv"), scatter_dimension=1, tiled=True),
    )
    results = tuple((piece.reshape(piece.shape[1], piece.shape[2]) for piece in reduced))
    return results + (norm_parts[0], norm_parts[1])


def local_generic(tokens, lengths, w_qkv, w_out, w_up, w_down, gains, biases, cotangent):
    rows_here, slot_dev, model_width = tokens.shape
    slot_count = slot_dev * lax.axis_size("kv")
    first_slot = lax.axis_index("kv") * slot_dev
    scaling = 1.0 / math.sqrt(HEAD)
    doc_ends = jnp.cumsum(lengths, -1)
    places = jnp.arange(slot_count, dtype=jnp.int32)
    docs_all = jnp.sum((doc_ends[:, None, :] <= places[None, :, None]).astype(jnp.int32), -1)
    live_all = (places[None, :] < doc_ends[:, -1:]).astype(jnp.float32)
    docs_here = lax.dynamic_slice_in_dim(docs_all, first_slot, slot_dev, 1)
    live_here = lax.dynamic_slice_in_dim(live_all, first_slot, slot_dev, 1)
    local_places = first_slot + jnp.arange(slot_dev, dtype=jnp.int32)
    masks = make_mask(local_places, docs_here[0], live_here[0], places, docs_all[0], live_all[0])
    stream = tokens.astype(jnp.float32)
    stored = []
    for number in range(LAYERS):
        signed = number == 0
        pieces = (
            lax.all_gather(w_qkv[number], ("rows", "kv"), axis=0, tiled=True),
            lax.all_gather(w_out[number], ("rows", "kv"), axis=0, tiled=True),
            lax.all_gather(w_up[number], ("rows", "kv"), axis=0, tiled=True),
            lax.all_gather(w_down[number], ("rows", "kv"), axis=0, tiled=True),
            lax.all_gather(gains[number], ("rows", "kv"), axis=1, tiled=True),
            lax.all_gather(biases[number], ("rows", "kv"), axis=1, tiled=True),
        )
        full_qkv, full_out, full_up, full_down, gain_pair, bias_pair = pieces
        gain_pair = gain_pair.astype(jnp.float32)
        bias_pair = bias_pair.astype(jnp.float32)
        normed_in = norm_rows(stream, gain_pair[0], bias_pair[0]).astype(jnp.bfloat16)
        projected = jnp.dot(normed_in, full_qkv, preferred_element_type=jnp.float32).astype(
            jnp.bfloat16
        )
        kv_all = lax.all_gather(projected[:, :, model_width:], "kv", axis=1, tiled=True)
        attended = jnp.stack(
            [
                attend_row(
                    projected[0, :, :model_width], kv_all[0], masks, live_here[0], signed, scaling
                )
            ]
        )
        shared = kv_all
        middle = stream + jnp.dot(attended, full_out, preferred_element_type=jnp.float32)
        normed_mid = norm_rows(middle, gain_pair[1], bias_pair[1]).astype(jnp.bfloat16)
        pre_act = jnp.dot(normed_mid, full_up, preferred_element_type=jnp.float32)
        activated = jax.nn.gelu(pre_act).astype(jnp.bfloat16)
        stored.append(
            (
                stream,
                normed_in,
                projected,
                shared,
                attended,
                middle,
                normed_mid,
                pre_act,
                activated,
                pieces,
            )
        )
        stream = middle + jnp.dot(activated, full_down, preferred_element_type=jnp.float32)
    result = (stream * live_here[..., None]).astype(jnp.bfloat16)
    residual_grad = cotangent.astype(jnp.float32) * live_here[..., None]
    collected = [None] * LAYERS
    for number in reversed(range(LAYERS)):
        signed = number == 0
        (
            stream_in,
            normed_in,
            projected,
            shared,
            attended,
            middle,
            normed_mid,
            pre_act,
            activated,
            kept,
        ) = stored[number]
        pieces = (
            lax.all_gather(w_qkv[number], ("rows", "kv"), axis=0, tiled=True),
            lax.all_gather(w_out[number], ("rows", "kv"), axis=0, tiled=True),
            lax.all_gather(w_up[number], ("rows", "kv"), axis=0, tiled=True),
            lax.all_gather(w_down[number], ("rows", "kv"), axis=0, tiled=True),
            lax.all_gather(gains[number], ("rows", "kv"), axis=1, tiled=True),
            lax.all_gather(biases[number], ("rows", "kv"), axis=1, tiled=True),
        )
        full_qkv, full_out, full_up, full_down, gain_pair, bias_pair = pieces
        gain_pair = gain_pair.astype(jnp.float32)
        bias_pair = bias_pair.astype(jnp.float32)
        down_in = residual_grad.astype(jnp.bfloat16)
        act_grad = jnp.einsum("rtd,fd->rtf", down_in, full_down, preferred_element_type=jnp.float32)
        unused, gelu_pull = jax.vjp(jax.nn.gelu, pre_act)
        pre_grad = gelu_pull(act_grad)[0].astype(jnp.bfloat16)
        mid_normed_grad = jnp.einsum(
            "rtf,df->rtd", pre_grad, full_up, preferred_element_type=jnp.float32
        )
        unused, norm_pull = jax.vjp(norm_rows, middle, gain_pair[1], bias_pair[1])
        middle_part, gain_late, bias_late = norm_pull(mid_normed_grad)
        middle_grad = residual_grad + middle_part
        branch_grad = middle_grad.astype(jnp.bfloat16)
        att_grad = jnp.einsum(
            "rte,de->rtd", branch_grad, full_out, preferred_element_type=jnp.float32
        ).astype(jnp.bfloat16)
        kv_all = shared
        query_grad, kv_grad = attend_back(
            projected[0, :, :model_width],
            kv_all[0],
            att_grad[0],
            masks,
            live_here[0],
            signed,
            scaling,
        )
        query_grads = [query_grad]
        kv_grads = [kv_grad]
        kv_here = lax.psum_scatter(
            jnp.stack(kv_grads).astype(jnp.bfloat16), "kv", scatter_dimension=1, tiled=True
        ).astype(jnp.float32)
        qkv_grad = jnp.concatenate([jnp.stack(query_grads), kv_here], -1).astype(jnp.bfloat16)
        in_normed_grad = jnp.einsum(
            "rte,de->rtd", qkv_grad, full_qkv, preferred_element_type=jnp.float32
        )
        unused, first_pull = jax.vjp(norm_rows, stream_in, gain_pair[0], bias_pair[0])
        stream_part, gain_early, bias_early = first_pull(in_normed_grad)
        residual_grad = middle_grad + stream_part
        g_gain = jnp.stack([gain_early, gain_late])
        g_bias = jnp.stack([bias_early, bias_late])
        pairs = [
            (normed_in, qkv_grad),
            (attended, branch_grad),
            (normed_mid, pre_grad),
            (activated, down_in),
        ]
        collected[number] = reduce_grads(pairs, g_gain, g_bias)
    grad_qkv = jnp.stack([collected[number][0] for number in range(LAYERS)])
    grad_out = jnp.stack([collected[number][1] for number in range(LAYERS)])
    grad_up = jnp.stack([collected[number][2] for number in range(LAYERS)])
    grad_down = jnp.stack([collected[number][3] for number in range(LAYERS)])
    grad_gains = jnp.stack([collected[number][4] for number in range(LAYERS)])
    grad_biases = jnp.stack([collected[number][5][0] for number in range(LAYERS)])
    grad_mid_biases = jnp.stack([collected[number][5][1] for number in range(LAYERS)])
    return (
        result,
        residual_grad,
        grad_qkv,
        grad_out,
        grad_up,
        grad_down,
        grad_gains,
        grad_biases,
        grad_mid_biases,
    )


F32 = jnp.float32
BF16 = jnp.bfloat16
MESH = pl.DeviceIdType.MESH
ZN = 4


def flip(value, unit):
    bit = lax.rem(lax.div(value, unit), 2)
    return value + unit - 2 * unit * bit


def places_of():
    r = lax.axis_index("rows")
    z = lax.axis_index("kv")
    return r, z, flip(r, 2), flip(r, 4), flip(flip(r, 2), 4), flip(r, 1)


def turn(z, k):
    return lax.rem(z + k, ZN)


def rcopy(src, dst, ssem, rsem, device):
    return pltpu.make_async_remote_copy(
        src_ref=src, dst_ref=dst, send_sem=ssem, recv_sem=rsem, device_id=device, device_id_type=MESH
    )


def band(start, size):
    return pl.ds(pl.multiple_of(start, 16), size)


def greet(peers):
    barrier = pltpu.get_barrier_semaphore()
    for peer in peers:
        pl.semaphore_signal(barrier, inc=1, device_id=peer, device_id_type=MESH)
    pl.semaphore_wait(barrier, len(peers))


def comm_peers():
    r, z, rx, ry, rd, rc = places_of()
    return [(r, turn(z, 1)), (r, turn(z, 2)), (r, turn(z, 3)), (rx, z), (ry, z), (rc, z)]


def col_step(width):
    return 256 if width % 256 == 0 else 128


def add_rows(dst, src, rows):
    def step(i, carry):
        here = band(i * 16, 16)
        dst[here, :] = (dst[here, :].astype(F32) + src[here, :].astype(F32)).astype(BF16)
        return carry
    lax.fori_loop(0, rows // 16, step, 0)


SEND = 0
PLANE = 100
PASS = 200
LAST = 300
WHOLE = 400
NORM = 600
SHARE = 700
PROJECT = 800
ATTEND = 900
OUTPUT = 1000
UP = 1100
DOWN = 1200
EARLY_THEIRS = 1400
EARLY_OURS = 1500
EARLY_SECOND = 1600
TOKENS = 500
COTANGENT = 510
WIDEN = 520
RESULT = 530
COTANGENT_LOW = 540
SECOND = 0
NEAR = 100
OVER_Z = 200
CLOSE = 300
THEIRS = 400
OURS = 500
SLOPE = 600
THROUGH = 700
NORM_BACK = 800
ASK = 900
KEYS = 1000
ASKED = 1100
ATTEND_BACK = 1200
PARTIAL = 1300
FIRST_BACK = 1400
RELAY = 1600
BEGIN = 1500
SWAP_BACK = 1510
RESULT_BACK = 1520

FORWARD_ORDER = [
    1, 2, 101, 0, 102, 201, 3, 100, 4, 202, 301, 500, 103, 401, 200, 302, 104, 5, 402, 300, 520, 400, 6, 600,
    800, 203, 802, 204, 105, 303, 403, 106, 7, 8, 304, 700, 801, 803, 9, 900, 205, 901, 206, 902, 107, 903,
    404, 108, 305, 306, 10, 406, 1000, 11, 109, 405, 1100, 207, 1101, 1200, 1201, 208, 601, 307, 110, 810,
    407, 111, 812, 308, 701, 811, 510, 408, 209, 813, 910, 911, 912, 210, 913, 211, 309, 1001, 310, 1110, 311,
    409, 1111, 410, 411,
]
BACKWARD_ORDER = [
    1500, 410, 610, 611, 411, 710, 510, 10, 711, 801, 901, 408, 1001, 511, 11, 1520, 409, 1101, 1213, 508,
    1313, 1212, 1312, 8, 1613, 110, 1211, 1311, 1612, 1210, 1310, 509, 108, 1611, 406, 407, 1610, 210, 506, 6,
    111, 507, 7, 208, 1401, 600, 700, 601, 701, 800, 900, 107, 310, 404, 106, 109, 1000, 211, 207, 308, 9,
    402, 1100, 504, 1203, 206, 4, 1202, 104, 307, 209, 502, 401, 1303, 2, 1302, 1201, 306, 204, 1603, 1602,
    501, 1, 1301, 1200, 102, 1300, 400, 309, 311, 403, 405, 101, 1601, 1600, 500, 0, 202, 201, 304, 505, 5,
    100, 1400, 1510, 503, 412, 301, 512, 12, 105, 200, 112, 103, 302, 212, 205, 3, 312, 203, 305, 300, 303,
]


GROUP = 640
TOK = 256
WIDE = 256
PARTS = HEADS // 4
CHUNK = 64
FAR = -1e30
KB = 256
JOBS = 6


def dot(a, b):
    return jnp.dot(a, b, preferred_element_type=F32)


def dot_nt(a, b):
    return lax.dot_general(a, b, (((1,), (1,)), ((), ())), preferred_element_type=F32)


def dot_tn(a, b):
    return lax.dot_general(a, b, (((0,), (0,)), ((), ())), preferred_element_type=F32)


def loop(count, body):
    def step(i, carry):
        body(i)
        return carry
    lax.fori_loop(0, count, step, 0)


def cols(i, size):
    return pl.ds(pl.multiple_of(i * size, 128), size)


class Spot:
    def __init__(self):
        self.r, self.z, self.rx, self.ry, self.rd, self.rc = places_of()
        self.c = lax.rem(self.r, 2)
        self.parity = lax.rem(self.z, 2)
        self.member = 2 * self.c + self.parity
        self.swaps = (self.c + lax.div(self.z, 2)) == 1
        self.partner = (self.rc, flip(self.z, 2))

    def mate(self, k):
        r = self.rc if k >= 2 else self.r
        z = flip(self.z, 1) if k % 2 else self.z
        return (r, z), 2 * lax.rem(r, 2) + lax.rem(z, 2)

    def device(self, member):
        return (self.r - self.c + lax.div(member, 2), self.z - self.parity + lax.rem(member, 2))

    def peers(self):
        return comm_peers() + [(self.rc, flip(self.z, 1)), self.partner]


class Gather:
    SEMS = 11

    def __init__(self, own, whole, bufs, ssem, rsem, base, paired=False):
        self.own, self.whole, self.bufs = own, whole, bufs
        self.ssem, self.rsem, self.base = ssem, rsem, base
        self.split, self.paired = len(bufs) > 0, paired
        self.rows, self.width = whole.shape[0] // 8, whole.shape[1]
        self.sent = []

    def _copy(self, src, dst, at, device):
        return rcopy(src, dst, self.ssem.at[self.base + at], self.rsem.at[self.base + at], device)

    def _block(self, r, half=None):
        if half is None:
            return self.whole.at[band(r * self.rows, self.rows), :]
        part = self.rows // 2
        return self.whole.at[band(r * self.rows + half * part, part), :]

    def _cored(self, r, column):
        if not self.paired:
            return self._block(r)
        return self.whole.at[band(r * self.rows, self.rows), cols(column, self.width // 2)]

    def _send(self, src, dst, at, device):
        copy = self._copy(src, dst, at, device)
        copy.start()
        self.sent.append(copy)

    def prepare(self):
        r, z = places_of()[:2]
        if self.split:
            zbuf = self.bufs[0]
            half = self.width // 2
            values = [self.own(place) for place in (0, 1)] if self.paired else [self.own[...].astype(F32)]
            for place, own in enumerate(values):
                packed = jnp.concatenate(
                    [own[:16], jnp.concatenate([own[16:, :half], own[16:, half:]], 0)], 1
                ).astype(BF16)
                if self.paired:
                    self.bufs[1][place] = packed
                else:
                    zbuf[pl.ds(z, 1)] = packed[None]
            if self.paired:
                zbuf[pl.ds(z, 1)] = self.bufs[1][pl.ds(lax.rem(z, 2), 1)]
        else:
            part = self.rows // ZN
            self.whole[band(r * self.rows + z * part, part), :] = self.own[...]

    def _zref(self, z):
        if self.split:
            return self.bufs[0].at[z]
        part = self.rows // ZN
        return self.whole.at[band(places_of()[0] * self.rows + z * part, part), :]

    def send_z(self):
        r, z = places_of()[:2]
        for k in (1, 2, 3):
            there = turn(z, k)
            src = self.bufs[1].at[lax.rem(there, 2)] if self.paired else self._zref(z)
            self._send(src, self._zref(z), k - 1, (r, there))

    def wait_z(self):
        r, z = places_of()[:2]
        for k in (1, 2, 3):
            ref = self._zref(turn(z, ZN - k))
            self._copy(ref, ref, k - 1, (r, turn(z, ZN - k))).wait_recv()
        if self.split:
            zbuf = self.bufs[0]
            half = self.width // 2
            step = col_step(half)
            for side in (0, 1):
                def assemble(i, side=side):
                    at = pl.multiple_of(self.width + i * step, 128)
                    here = pl.ds(pl.multiple_of(side * half + i * step, 128), step)
                    parts = []
                    for piece in range(ZN):
                        parts.append(zbuf[piece, :, here].astype(F32))
                        parts.append(zbuf[piece, :, pl.ds(at, step)].astype(F32)[8 * side : 8 * side + 8])
                    self.whole[band(r * self.rows, self.rows), here] = jnp.concatenate(parts, 0).astype(BF16)
                loop(half // step, assemble)

    def send_plane(self):
        r, z, rx, ry, rd, rc = places_of()
        own = self._block(r)
        self._send(own, own, 3, (rx, z))
        self._send(own, own, 4, (ry, z))
        self._core(r, 7)

    def _core(self, block, at):
        r, z, rx, ry, rd, rc = places_of()
        ref = self._cored(block, lax.rem(rc, 2))
        self._send(ref, ref, at, (rc, z))

    def forward(self):
        r, z, rx, ry, rd, rc = places_of()
        first, second = self._block(rx), self._block(ry)
        self._copy(first, first, 3, (rx, z)).wait_recv()
        part = self._block(rx, 0)
        self._send(part, part, 5, (ry, z))
        self._copy(second, second, 4, (ry, z)).wait_recv()
        part = self._block(ry, 1)
        self._send(part, part, 6, (rx, z))
        self._core(rx, 8)
        self._core(ry, 9)

    def forward_last(self):
        r, z, rx, ry, rd, rc = places_of()
        part = self._block(rd, 0)
        self._copy(part, part, 5, (ry, z)).wait_recv()
        part = self._block(rd, 1)
        self._copy(part, part, 6, (rx, z)).wait_recv()
        self._core(rd, 10)

    def finish(self):
        r, z, rx, ry, rd, rc = places_of()
        for at, block in ((7, r), (8, rx), (9, ry), (10, rd)):
            ref = self._cored(flip(block, 1), lax.rem(r, 2))
            self._copy(ref, ref, at, (rc, z)).wait_recv()

    def drain(self):
        for copy in self.sent:
            copy.wait_send()


def swap(spot, src, dst, ssem, rsem):
    @pl.when(spot.swaps)
    def _():
        rcopy(src, dst, ssem, rsem, spot.partner).start()

    @pl.when(jnp.logical_not(spot.swaps))
    def _():
        pltpu.make_async_copy(src, dst, rsem).start()


def swap_wait(spot, src, dst, ssem, rsem):
    @pl.when(spot.swaps)
    def _():
        rcopy(src, dst, ssem, rsem, spot.partner).wait()

    @pl.when(jnp.logical_not(spot.swaps))
    def _():
        pltpu.make_async_copy(src, dst, rsem).wait()


def starts_of(lens, i):
    places = lax.broadcasted_iota(jnp.int32, (1, TOK), 1) + i * TOK
    end = jnp.zeros((1, 1), jnp.int32)
    start = jnp.zeros((1, TOK), jnp.int32)
    for n in range(4):
        end = end + lens[0:1, n : n + 1]
        start = jnp.maximum(start, jnp.where(end <= places, end, 0))
    live = places < end
    return places, jnp.where(live, start, 1 << 20), live


def live_column(lens, spot, rows, first):
    places = lax.broadcasted_iota(jnp.int32, (rows, 1), 0) + spot.member * TOK + first
    end = lens[0:1, 0:1] + lens[0:1, 1:2] + lens[0:1, 2:3] + lens[0:1, 3:4]
    return (places < end).astype(F32)


def centred(value):
    center = value - jnp.mean(value, -1, keepdims=True)
    spread = jnp.mean(center * center, -1, keepdims=True)
    return center * lax.rsqrt(spread + EPSILON)


def fold_rows(value, op):
    rows = value.shape[0]
    parts = [value[8 * n : 8 * n + 8] for n in range(rows // 8)]
    while len(parts) > 1:
        parts = [op(parts[n], parts[n + 1]) if n + 1 < len(parts) else parts[n] for n in range(0, len(parts), 2)]
    return parts[0]


def head_lanes(shape, h, offset):
    lanes = lax.broadcasted_iota(jnp.int32, shape, 1)
    return lax.div(lanes, HEAD) == h + offset


def masked_rows(first, rows, places, start, diagonal):
    keys = lax.broadcasted_iota(jnp.int32, (rows, TOK), 0) + first
    okay = keys >= start
    return okay & (keys <= places) if diagonal else okay


def over_blocks(i, body, carry):
    per = TOK // KB if KB <= TOK else 1
    if i:
        carry = lax.fori_loop(0, i * per, lambda n, c: body(n * KB, c, False), carry)
    for n in range(per):
        carry = body(i * TOK + n * KB, carry, True)
    return carry


def key_rows(qkv, first, at):
    quarter = lax.div(first, TOK)
    here = pl.ds(pl.multiple_of(lax.rem(first, TOK), KB), KB)
    return qkv[quarter, here, at : at + WIDE]


def masked_heads(value_t, offset):
    rows = lax.div(lax.broadcasted_iota(jnp.int32, value_t.shape, 0), HEAD)
    return jnp.concatenate([jnp.where(rows == h + offset, value_t, 0.0) for h in range(PARTS)], 1).astype(BF16)


def magnitude_of(s):
    square = s * s + 1.0
    back = lax.rsqrt(square)
    return square * back, back


def attend_quarter(i, lens, qkv, vt, acc, o_ref, stats, signed):
    places, start, live = starts_of(lens, i)
    mine = masked_heads(qkv[i, :, 0:WIDE].astype(F32).T * 0.125, 0)
    acc[...] = jnp.zeros_like(acc)

    def block(first, carry, diagonal):
        keys = key_rows(qkv, first, 384)
        okay = masked_rows(first, KB, places, start, diagonal)
        here = pl.ds(pl.multiple_of(first, KB), KB)
        out, lows, shrinks = [], [], []
        scores = [dot(keys, mine[:, h * TOK : (h + 1) * TOK]) for h in range(PARTS)]
        for h in range(PARTS):
            old, total = carry[2 * h], carry[2 * h + 1]
            s = scores[h]
            value = jnp.where(okay, magnitude_of(s)[0] if signed else s, FAR)
            new = jnp.maximum(old, jnp.max(fold_rows(value, jnp.maximum), 0, keepdims=True))
            raised = jnp.exp(value - new)
            shrink = jnp.exp(old - new)
            lows.append((jnp.tanh(s) * raised if signed else raised).astype(BF16))
            shrinks.append(shrink)
            out += [new, total * shrink + jnp.sum(fold_rows(raised, jnp.add), 0, keepdims=True)]
        terms = [dot(vt[HEAD * (h + 1) : HEAD * (h + 2), here], lows[h]) for h in range(PARTS)]
        for h in range(PARTS):
            rows = slice(HEAD * h, HEAD * (h + 1))
            acc[rows, :] = acc[rows, :] * shrinks[h] + terms[h]
        return tuple(out)
    lowest = jnp.full((1, TOK), 0.0 if signed else -10000.0, F32)
    carry = over_blocks(i, block, (lowest, jnp.zeros((1, TOK), F32)) * PARTS)
    for h in range(PARTS):
        inverse = 1.0 / (carry[2 * h + 1] + (1.0 - live.astype(F32)))
        stats[i, h : h + 1, :] = carry[2 * h]
        stats[i, PARTS + h : PARTS + h + 1, :] = inverse
        acc[HEAD * h : HEAD * (h + 1), :] = acc[HEAD * h : HEAD * (h + 1), :] * inverse
    o_ref[i] = acc[...].astype(BF16)


def gelu_both(x):
    root = 0.7978845608028654
    square = x * x
    bend = jnp.tanh(root * (x + 0.044715 * x * square))
    half = 0.5 * (1.0 + bend)
    return x * half, half + 0.5 * x * (1.0 - bend * bend) * root * (1.0 + 3 * 0.044715 * square)


class Keep:
    def __init__(self, src, dst, sem):
        self.copy = pltpu.make_async_copy(src, dst, sem)
        self.copy.start()
        self.open = True

    def wait(self):
        if self.open:
            self.copy.wait()
        self.open = False


STASH = ("stream", "qkv", "middle", "nin_t", "att_t", "nmid_t", "pre", "act_t", "out", "stats")


def stash_shapes(d, ff):
    return [
        ((TOK, d), F32),
        ((4, TOK, GROUP), BF16),
        ((TOK, d), F32),
        ((d, 4 * TOK), BF16),
        ((d, TOK), BF16),
        ((d, TOK), BF16),
        ((TOK, ff), F32),
        ((ff, TOK), BF16),
        ((4, 192, TOK), F32),
        ((4, 8, TOK), F32),
    ]


def forward_kernel(*refs):
    refs = list(refs)
    take = lambda n: [refs.pop(0) for _ in range(n)]
    tok, cot, lengths = take(3)
    sources = take(4)
    gains, biases = take(2)
    cot_o, lens_o, norms_o = take(3)
    whole_o = take(2 * JOBS)
    stash_o = [take(10), take(10)]
    wholes = take(2 * JOBS)
    zbuf = [take((2, 1, 1, 1, 0, 0)[n % JOBS]) for n in range(2 * JOBS)]
    tok_v, lens_in, lens_v, stream, nin0, nin1, qkv, vt, outs, stats, o_ref, att0, att1, pre, act, act_t, nin_t, nt_mid, normed, middle = take(20)
    ssem, rsem, osem, stsem, ns, nr, os_, or_, ms, mr = take(10)
    spot = Spot()
    lens_in[...] = jnp.zeros_like(lens_in)
    lens_in[0:1, 0:4] = lengths[...]
    greet(spot.peers())
    jobs = []

    def grouped(layer):
        def pair(place):
            vectors = [ref[layer, which : which + 1, :].astype(F32) for which in (0, 1) for ref in (gains, biases)]
            own = vectors[0].shape[1]
            top = jnp.concatenate([jnp.concatenate(vectors, 0), jnp.zeros((4, 128 - own), F32)], 1)
            edge = jnp.concatenate([top, jnp.zeros((124, 128), F32)], 0).T[:own, :HEAD]
            parts = []
            for g in (place, place + 2):
                for at in (0, 2, 1):
                    parts.append(sources[0][layer, :, 768 * at + 192 * g : 768 * at + 192 * g + 192].astype(F32))
                parts.append(edge)
            return jnp.concatenate(parts, 1)
        return pair

    for layer in range(LAYERS):
        out_in, up_in, down_in = [source.at[layer] for source in sources[1:]]
        ff, d = up_in.shape[1] // 2, down_in.shape[1] // 2
        owns = [grouped(layer), out_in] + [up_in.at[:, h * ff : (h + 1) * ff] for h in (0, 1)] + [down_in.at[:, h * d : (h + 1) * d] for h in (0, 1)]
        for n, own in enumerate(owns):
            at = layer * JOBS + n
            jobs.append(Gather(own, wholes[at], zbuf[at], ssem, rsem, at * Gather.SEMS, n == 0))
    kept = {}

    def keep(name, src, dst, sem):
        kept[name] = Keep(src, dst, sem)

    def settle(name):
        if name in kept:
            kept[name].wait()

    def stash(layer, name, src):
        at = STASH.index(name)
        keep((layer, name), src, stash_o[layer][at], stsem.at[10 * layer + at])

    steps = {}

    def step(name):
        def note(run):
            steps[name] = run
        return note

    for n, job in enumerate(jobs):
        def first(job=job):
            job.prepare()
            job.send_z()

        def plane(job=job):
            job.wait_z()
            job.send_plane()

        def done(job=job, n=n):
            job.finish()
            src = wholes[n]
            if n % JOBS == 0:
                src = src.at[:, cols(spot.c, GROUP)]
            keep(("whole", n), src, whole_o[n], osem.at[n])
        steps.update({SEND + n: first, PLANE + n: plane, PASS + n: job.forward, LAST + n: job.forward_last, WHOLE + n: done})

    @step(TOKENS)
    def _():
        swap(spot, tok, tok_v, ms.at[0], mr.at[0])
        swap(spot, lens_in, lens_v, ms.at[1], mr.at[1])

    @step(COTANGENT)
    def _():
        swap(spot, cot, cot_o, ms.at[2], mr.at[2])

    @step(WIDEN)
    def _():
        swap_wait(spot, tok, tok_v, ms.at[0], mr.at[0])
        swap_wait(spot, lens_in, lens_v, ms.at[1], mr.at[1])
        lens_o[...] = lens_v[...]

        def widen(n):
            here = band(n * CHUNK, CHUNK)
            stream[here, :] = tok_v[here, :].astype(F32)
        loop(TOK // CHUNK, widen)
        stash(0, "stream", stream)

    def layer_steps(layer):
        base = layer * JOBS
        w_qkv, w_out, w_up0, w_up1, w_down0, w_down1 = wholes[base : base + JOBS]
        nin = (nin0, nin1)[layer]
        att = (att0, att1)[layer]
        signed = layer == 0

        def gathered(k):
            mate, member = spot.mate(k)
            return rcopy(nin.at[member], nin.at[member], ns.at[4 * layer + k], nr.at[4 * layer + k], mate)

        def give(k, member):
            mate = spot.mate(1 if k == 1 else 2)[0]
            return rcopy(nin.at[member], nin.at[member], ns.at[4 * layer + k], nr.at[4 * layer + k], mate)

        @step(NORM + layer)
        def _():
            edge = w_qkv[:, pl.ds(pl.multiple_of(spot.c * GROUP + 512, 128), 128)].astype(F32).T
            norms_o[layer] = edge[HEAD : HEAD + 8]

            def first_norm(n):
                here = band(n * CHUNK, CHUNK)
                value = centred(stream[here, :]) * norms_o[layer, 0:1, :] + norms_o[layer, 1:2, :]
                nin[spot.member, here, :] = value.astype(BF16)
            loop(TOK // CHUNK, first_norm)
            give(1, spot.member).start()
            give(2, spot.member).start()

        @step(SHARE + layer)
        def _():
            gathered(1).wait_recv()
            give(3, spot.mate(1)[1]).start()

        def project(k):
            def run():
                member = spot.member
                if k:
                    member = spot.mate(k)[1]
                    if k != 1:
                        gathered(k).wait_recv()
                group = dot(nin[member], w_qkv[:, cols(spot.c, GROUP)]).astype(BF16)
                if (layer, k) == (1, 0):
                    settle((0, "qkv"))
                    settle((0, "nin_t"))
                qkv[pl.ds(member, 1)] = group[None]
                at = pl.multiple_of(member * TOK, TOK)
                vt[:, pl.ds(at, TOK)] = group[:, 128:384].astype(F32).T.astype(BF16)
                nin_t[:, pl.ds(at, TOK)] = nin[member].astype(F32).T.astype(BF16)
                if k == 3:
                    stash(layer, "qkv", qkv)
                    stash(layer, "nin_t", nin_t)
            return run
        for k in range(4):
            steps[PROJECT + 10 * layer + k] = project(k)

        def returned(i):
            return rcopy(
                o_ref.at[layer, i], att.at[band(spot.member * 192, 192), :], os_.at[4 * layer + i], or_.at[4 * layer + spot.member], spot.device(i)
            )

        def attend(i):
            def run():
                attend_quarter(i, lens_v, qkv, vt, outs.at[layer, i], o_ref.at[layer], stats.at[layer], signed)

                @pl.when(spot.member != i)
                def _():
                    returned(i).start()

                @pl.when(spot.member == i)
                def _():
                    att[i * 192 : (i + 1) * 192, :] = o_ref[layer, i]
                if i == 3:
                    stash(layer, "out", outs.at[layer])
                    stash(layer, "stats", stats.at[layer])
            return run
        for i in range(4):
            steps[ATTEND + 10 * layer + i] = attend(i)

        @step(OUTPUT + layer)
        def _():
            for i in range(4):
                @pl.when(spot.member != i)
                def _():
                    ref = att.at[i * 192 : (i + 1) * 192, :]
                    rcopy(ref, ref, os_.at[4 * layer + i], or_.at[4 * layer + i], spot.device(i)).wait_recv()
            stash(layer, "att_t", att)
            settle((0, "middle"))
            middle[...] = stream[...] + dot_tn(att[...], w_out[...])
            stash(layer, "middle", middle)

            def second_norm(n):
                here = band(n * CHUNK, CHUNK)
                value = centred(middle[here, :]) * norms_o[layer, 2:3, :] + norms_o[layer, 3:4, :]
                normed[here, :] = value.astype(BF16)
            loop(TOK // CHUNK, second_norm)
            settle((0, "nmid_t"))
            nt_mid[...] = normed[...].astype(F32).T.astype(BF16)
            stash(layer, "nmid_t", nt_mid)
            settle((0, "pre"))
            settle((0, "act_t"))

        def up(h):
            w_up = (w_up0, w_up1)[h]
            tile = 512
            count = w_up.shape[1] // tile

            def run():
                def part(n):
                    value = dot(normed[...], w_up[:, cols(n, tile)])
                    here = cols(h * count + n, tile)
                    active, pre[:, here] = gelu_both(value)
                    act[:, here] = active.astype(BF16)
                    act_t[pl.ds(pl.multiple_of((h * count + n) * tile, tile), tile), :] = active.T.astype(BF16)
                loop(count, part)
                if h:
                    stash(layer, "pre", pre)
                    stash(layer, "act_t", act_t)
            return run

        def down(h):
            w_down = (w_down0, w_down1)[h]
            width = w_down.shape[1]

            def run():
                settle((layer, "stream"))

                def part(n):
                    here = cols(n + h * (width // 128), 128)
                    stream[:, here] = middle[:, here] + dot(act[...], w_down[:, cols(n, 128)])
                if width % 384 == 0:
                    here = slice(h * width, (h + 1) * width)
                    stream[:, here] = middle[:, here] + dot(act[...], w_down[...])
                else:
                    loop(width // 128, part)
                if h and layer == 0:
                    stash(1, "stream", stream)
            return run
        for h in (0, 1):
            steps[UP + 10 * layer + h] = up(h)
            if layer == 0:
                steps[DOWN + 10 * layer + h] = down(h)

        def close():
            for k in (1, 2):
                give(k, spot.member).wait_send()
            give(3, spot.mate(1)[1]).wait_send()
            for i in range(4):
                @pl.when(spot.member != i)
                def _():
                    returned(i).wait_send()
        return close

    closes = [layer_steps(layer) for layer in range(LAYERS)]

    for name in FORWARD_ORDER:
        steps.pop(name)()
    assert not steps
    for job in jobs:
        job.drain()
    for close in closes:
        close()
    for copy in kept.values():
        copy.wait()
    swap_wait(spot, cot, cot_o, ms.at[2], mr.at[2])


def forward_call(tok, cot, lengths, w_qkv, w_out, w_up, w_down, gains, biases):
    d, ff = tok.shape[1], w_up.shape[2]
    shapes = [(d, 2 * GROUP), (d, d), (d, ff // 2), (d, ff // 2), (ff, d // 2), (ff, d // 2)] * LAYERS
    zshapes = []
    for n, (rows, width) in enumerate(shapes):
        if n % JOBS < 4:
            zshapes.append(pltpu.VMEM((ZN, 16, width * 3 // 2), BF16))
        if n % JOBS == 0:
            zshapes.append(pltpu.VMEM((2, 16, width * 3 // 2), BF16))
    any_space = pl.BlockSpec(memory_space=pl.ANY)
    vmem = pl.BlockSpec(memory_space=pltpu.VMEM)
    stash = [jax.ShapeDtypeStruct(shape, kind) for shape, kind in stash_shapes(d, ff)]
    dma = lambda n: pltpu.SemaphoreType.DMA((n,))
    kept_shapes = [(rows, GROUP if n % JOBS == 0 else width) for n, (rows, width) in enumerate(shapes)]
    outs = pl.pallas_call(
        forward_kernel,
        out_shape=[
            jax.ShapeDtypeStruct((TOK, d), BF16),
            jax.ShapeDtypeStruct((8, 128), jnp.int32),
            jax.ShapeDtypeStruct((LAYERS, 8, d), F32),
        ]
        + [jax.ShapeDtypeStruct(shape, BF16) for shape in kept_shapes]
        + stash
        + stash,
        in_specs=[any_space, any_space] + [vmem] * 7,
        out_specs=[any_space, vmem, vmem] + [any_space] * (2 * JOBS + 20),
        scratch_shapes=[pltpu.VMEM(shape, BF16) for shape in shapes]
        + zshapes
        + [
            pltpu.VMEM((TOK, d), BF16),
            pltpu.VMEM((8, 128), jnp.int32),
            pltpu.VMEM((8, 128), jnp.int32),
            pltpu.VMEM((TOK, d), F32),
            pltpu.VMEM((4, TOK, d), BF16),
            pltpu.VMEM((4, TOK, d), BF16),
            pltpu.VMEM((4, TOK, GROUP), BF16),
            pltpu.VMEM((WIDE, 4 * TOK), BF16),
            pltpu.VMEM((LAYERS, 4, 192, TOK), F32),
            pltpu.VMEM((LAYERS, 4, 8, TOK), F32),
            pltpu.VMEM((LAYERS, 4, 192, TOK), BF16),
            pltpu.VMEM((d, TOK), BF16),
            pltpu.VMEM((d, TOK), BF16),
            pltpu.VMEM((TOK, ff), F32),
            pltpu.VMEM((TOK, ff), BF16),
            pltpu.VMEM((ff, TOK), BF16),
            pltpu.VMEM((d, 4 * TOK), BF16),
            pltpu.VMEM((d, TOK), BF16),
            pltpu.VMEM((TOK, d), BF16),
            pltpu.VMEM((TOK, d), F32),
        ]
        + [dma(2 * JOBS * Gather.SEMS), dma(2 * JOBS * Gather.SEMS), dma(2 * JOBS), dma(20), dma(8), dma(8), dma(8), dma(8), dma(4), dma(4)],
        compiler_params=pltpu.CompilerParams(collective_id=0, has_side_effects=True, vmem_limit_bytes=62 * 2**20),
    )(tok, cot, lengths, w_qkv, w_out, w_up, w_down, gains, biases)
    at = 3 + 2 * JOBS
    return outs[:3], outs[3:at], (outs[at : at + 10], outs[at + 10 : at + 20])


class Reduce:
    SEMS = 10

    def __init__(self, send, bufs, out, ssem, rsem, base, paired=False):
        self.send = send
        self.got, self.half, self.near = bufs[:3]
        self.zs, self.zr = bufs[3:5]
        self.out = out
        self.ssem, self.rsem, self.base = ssem, rsem, base
        self.rows, self.width = self.got.shape[1], self.got.shape[2]
        self.split, self.paired = self.zs.shape[1] == 16, paired
        self.sent = []

    def _copy(self, src, dst, at, device):
        return rcopy(src, dst, self.ssem.at[self.base + at], self.rsem.at[self.base + at], device)

    def _send(self, src, dst, at, device):
        copy = self._copy(src, dst, at, device)
        copy.start()
        self.sent.append(copy)

    def _got(self, core):
        if self.paired:
            return self.got.at[:, :, cols(core, self.width // 2)]
        return self.got

    def send_core(self):
        r, z, rx, ry, rd, rc = places_of()
        self._send(self.send, self._got(lax.rem(r, 2)), 0, (rc, z))

    def wait_core(self):
        r, z, rx, ry, rd, rc = places_of()
        ref = self._got(lax.rem(rc, 2))
        self._copy(ref, ref, 0, (rc, z)).wait_recv()

    def _part(self, other, i):
        part = self.rows // 2
        return self.got.at[lax.div(other, 2), pl.ds(i * part, part)]

    def send_first(self):
        r, z, rx, ry, rd, rc = places_of()
        part = self.rows // 2
        self._send(self._part(rd, 0), self.half.at[0], 1, (ry, z))
        self._send(self._part(rd, 1), self.half.at[1], 2, (rx, z))

    def send_second(self):
        r, z, rx, ry, rd, rc = places_of()
        part = self.rows // 2
        self._send(self._part(rx, 1), self.near.at[0, pl.ds(part, part)], 3, (rx, z))
        self._send(self._part(ry, 0), self.near.at[1, pl.ds(0, part)], 4, (ry, z))

    def send_near(self):
        r, z, rx, ry, rd, rc = places_of()
        part = self.rows // 2
        for i, side, other in ((0, ry, rx), (1, rx, ry)):
            self._copy(self.half.at[i], self.half.at[i], 1 + i, (side, z)).wait_recv()
            block = self._part(other, i)
            add_rows(block, self.half.at[i], part)
            self._send(block, self.near.at[i, pl.ds(i * part, part)], 5 + i, (other, z))

    def send_z(self):
        r, z, rx, ry, rd, rc = places_of()
        part = self.rows // 2
        for at, i, h, side in ((3, 0, 1, rx), (4, 1, 0, ry), (5, 0, 0, rx), (6, 1, 1, ry)):
            ref = self.near.at[i, pl.ds(h * part, part)]
            self._copy(ref, ref, at, (side, z)).wait_recv()
        own = self.got.at[lax.div(r, 2)]
        near = self.near

        def total(rows, here):
            return own[rows, here].astype(F32) + near[0, rows, here].astype(F32) + near[1, rows, here].astype(F32)

        if self.split:
            half = self.width // 2
            step = col_step(half)

            def cut(i):
                at = pl.ds(pl.multiple_of(self.width + i * step, 128), step)
                sums = [
                    total(slice(None), pl.ds(pl.multiple_of(side * half + i * step, 128), step)) for side in (0, 1)
                ]
                for piece in range(ZN):
                    for side in (0, 1):
                        here = pl.ds(pl.multiple_of(side * half + i * step, 128), step)
                        self.zs[piece, :, here] = sums[side][24 * piece : 24 * piece + 16].astype(BF16)
                    self.zs[piece, :, at] = jnp.concatenate(
                        [sums[side][24 * piece + 16 : 24 * piece + 24] for side in (0, 1)], 0
                    ).astype(BF16)
            loop(half // step, cut)
        else:
            size = self.rows // ZN
            for piece in range(ZN):
                def cut_rows(i, piece=piece):
                    self.zs[piece, band(i * 16, 16), :] = total(band(piece * size + i * 16, 16), slice(None)).astype(BF16)
                loop(size // 16, cut_rows)
        for k in (1, 2, 3):
            self._send(self.zs.at[turn(z, k)], self.zr.at[k - 1], 6 + k, (r, turn(z, k)))

    def finish(self):
        r, z = places_of()[:2]
        for k in (1, 2, 3):
            ref = self.zr.at[k - 1]
            self._copy(ref, ref, 6 + k, (r, turn(z, ZN - k))).wait_recv()
        half, width = self.width // 2, self.width
        if self.paired:
            for place, value in (
                (lax.rem(z, 2), self.zs[z].astype(F32) + self.zr[1].astype(F32)),
                (lax.rem(z + 1, 2), self.zr[0].astype(F32) + self.zr[2].astype(F32)),
            ):
                for side in (0, 1):
                    here = cols(place + 2 * side, GROUP)
                    self.out[pl.ds(0, 16), here] = value[:, side * GROUP : (side + 1) * GROUP]
                    self.out[pl.ds(16, 8), here] = value[8 * side : 8 * side + 8, width:]
        elif self.split:
            value = self.zs[z].astype(F32)
            for k in range(3):
                value = value + self.zr[k].astype(F32)
            self.out[pl.ds(0, 16), :] = value[:, :width]
            self.out[pl.ds(16, 8), pl.ds(0, half)] = value[:8, width:]
            self.out[pl.ds(16, 8), pl.ds(half, half)] = value[8:, width:]
        else:
            def total(i):
                here = band(i * 16, 16)
                value = self.zs[z, here, :].astype(F32)
                for k in range(3):
                    value = value + self.zr[k, here, :].astype(F32)
                self.out[here, :] = value
            loop(self.out.shape[0] // 16, total)

    def drain(self):
        for copy in self.sent:
            copy.wait_send()
        self.sent = []


def left_rows(left, c):
    return jnp.concatenate([left[band((2 * b + c) * 96, 96), :] for b in range(4)], 0)


def norm_back(source, upstream, gain, add, out, low, sums):
    sums[...] = jnp.zeros_like(sums)

    def step(n):
        here = band(n * CHUNK, CHUNK)
        value = source[here, :]
        center = value - jnp.mean(value, -1, keepdims=True)
        scale = lax.rsqrt(jnp.mean(center * center, -1, keepdims=True) + EPSILON)
        normal = center * scale
        up = upstream(here)
        sums[0:8, :] += fold_rows(up * normal, jnp.add)
        sums[8:16, :] += fold_rows(up, jnp.add)
        up = up * gain
        inner = up - jnp.mean(up, -1, keepdims=True) - normal * jnp.mean(up * normal, -1, keepdims=True)
        total = add[here, :] + inner * scale
        out[here, :] = total
        low[here, :] = total.astype(BF16)
    loop(TOK // CHUNK, step)
    gain_grad = jnp.sum(sums[0:8, :], 0, keepdims=True)
    bias_grad = jnp.sum(sums[8:16, :], 0, keepdims=True)
    return gain_grad, bias_grad


def attend_quarter_back(i, lens, qkv, kt, datt, out, stats, scratch, signed):
    dk, dv, dq = scratch
    places, start, live = starts_of(lens, i)
    queries = qkv[i, :, 0:WIDE].astype(F32) * 0.125
    mine = masked_heads(queries.T, 0)
    mine_rows = jnp.concatenate(
        [jnp.where(head_lanes((TOK, WIDE), h, 0), queries, 0.0).astype(BF16) for h in range(PARTS)], 0
    )
    upstream = datt[i].astype(F32)
    grads_t = jnp.concatenate([jnp.zeros((HEAD, TOK), F32), upstream], 0)
    out_t = masked_heads(grads_t, 1)
    grads = grads_t.T
    out_rows = jnp.concatenate(
        [jnp.where(head_lanes((TOK, WIDE), h, 1), grads, 0.0).astype(BF16) for h in range(PARTS)], 0
    )
    product = upstream * out[i].astype(F32)
    inner = [
        jnp.sum(fold_rows(product[HEAD * h : HEAD * (h + 1)], jnp.add), 0, keepdims=True) for h in range(PARTS)
    ]
    top = [stats[i, h : h + 1, :] for h in range(PARTS)]
    inverse = [stats[i, PARTS + h : PARTS + h + 1, :] for h in range(PARTS)]
    dq[...] = jnp.zeros_like(dq)

    def block(first, carry, diagonal):
        keys = key_rows(qkv, first, 384)
        values = key_rows(qkv, first, 128)
        okay = masked_rows(first, KB, places, start, diagonal)
        here = pl.ds(pl.multiple_of(first, KB), KB)
        lows, slopes = [], []
        scores = [dot(keys, mine[:, h * TOK : (h + 1) * TOK]) for h in range(PARTS)]
        gains = [dot(values, out_t[:, h * TOK : (h + 1) * TOK]) for h in range(PARTS)]
        for h in range(PARTS):
            s, dp = scores[h], gains[h]
            if signed:
                size, back = magnitude_of(s)
                unsigned = jnp.exp(jnp.where(okay, size - top[h], FAR)) * inverse[h]
                bend = jnp.tanh(s)
                lows.append((unsigned * bend).astype(BF16))
                slope = unsigned * ((bend * dp - inner[h]) * (s * back) + dp * (1.0 - bend * bend))
            else:
                unsigned = jnp.exp(jnp.where(okay, s - top[h], FAR)) * inverse[h]
                lows.append(unsigned.astype(BF16))
                slope = unsigned * (dp - inner[h])
            slopes.append(slope.astype(BF16))
        value_terms = dot(jnp.concatenate(lows, 1), out_rows)
        key_terms = dot(jnp.concatenate(slopes, 1), mine_rows)
        query_terms = [dot(kt[HEAD * h : HEAD * (h + 1), here], slopes[h]) for h in range(PARTS)]
        dv[here, :] += value_terms
        dk[here, :] += key_terms
        for h in range(PARTS):
            dq[HEAD * h : HEAD * (h + 1), :] += query_terms[h]
        return carry
    over_blocks(i, block, 0)
    query_grad = jnp.concatenate([dq[...] * 0.125, jnp.zeros((HEAD, TOK), F32)], 0).T
    value_grad = dv[i * TOK : (i + 1) * TOK, :]
    key_grad = dk[i * TOK : (i + 1) * TOK, :]
    lanes = lax.broadcasted_iota(jnp.int32, (TOK, 128), 1)
    return jnp.concatenate(
        [
            query_grad[:, :128],
            jnp.where(lanes < HEAD, query_grad[:, 128:], value_grad[:, :128]),
            value_grad[:, 128:],
            key_grad,
        ],
        1,
    ).astype(BF16)


EDGE = 256


def reduce_shapes(d, ff):
    return [(96, 2 * GROUP), (96, d), (96, ff // 2), (96, ff // 2), (ff // 8, d // 2), (ff // 8, d // 2), (96, EDGE)]


def backward_kernel(*refs):
    refs = list(refs)
    take = lambda n: [refs.pop(0) for _ in range(n)]
    cot, lens, norms = take(3)
    wholes = take(2 * JOBS)
    stash = [take(10), take(10)]
    result_o, input_o = take(2)
    grads_o = take(4)
    (edge_o,) = take(1)
    weights = take(JOBS)
    homes = take(10)
    stream, qkv, middle, nin_t, att_t, nmid_t, pre, act_t, att_out, stats = homes
    w_qkv, w_out, w_up0, w_up1, w_down0, w_down1 = weights
    cot_v, grad, low, branch, dpre, dmid, sums, edges, datt_s, datt_r, kt, dk, dv, dq, dqkv, pn_s, pn_r, held, res = take(19)
    sends = take(JOBS + 1)
    buffers = [take(5) for n in range(JOBS + 1)]
    ssem, rsem, lsem, csem, as_, ar, ps, pr, ms, mr = take(10)
    spot = Spot()
    r, z, rx, ry, rd, rc = spot.r, spot.z, spot.rx, spot.ry, spot.rd, spot.rc
    loads = {}

    def load(layer, *names):
        for name in names:
            if name in STASH:
                at = STASH.index(name)
                src, dst = stash[layer][at], homes[at]
            else:
                src, dst = wholes[JOBS * layer + name], weights[name]
                at = 10 + name
            loads[(layer, name)] = Keep(src, dst, lsem.at[(10 + JOBS) * layer + at])

    def ready(layer, *names):
        for name in names:
            loads[(layer, name)].wait()

    def free(layer, *names):
        if layer:
            load(0, *names)

    start = Keep(cot, cot_v, lsem.at[2 * (10 + JOBS)])
    load(1, "act_t", 4, 5, "pre", "nmid_t", 2, 3, "middle", 1, "att_t", "qkv", "out", "stats", "nin_t", 0, "stream")
    greet(spot.peers())
    peers = comm_peers()
    jobs = []
    for layer in range(LAYERS):
        qkv_g, out_g, up_g, down_g = [ref.at[layer] for ref in grads_o]
        ff, d = up_g.shape[1] // 2, down_g.shape[1] // 2
        outs = [qkv_g, out_g] + [up_g.at[:, h * ff : (h + 1) * ff] for h in (0, 1)] + [down_g.at[:, h * d : (h + 1) * d] for h in (0, 1)]
        for n, out in enumerate(outs):
            jobs.append(Reduce(sends[n], buffers[n], out, ssem, rsem, (JOBS * layer + n) * Reduce.SEMS, n == 0))
    jobs.append(Reduce(sends[JOBS], buffers[JOBS], edge_o, ssem, rsem, 2 * JOBS * Reduce.SEMS))
    steps = {}

    def step(name):
        def note(run):
            steps[name] = run
        return note

    for at, job in enumerate(jobs):
        def close(job=job, at=at):
            job.finish()
            if JOBS <= at < 2 * JOBS:
                job.drain()
                for peer in peers:
                    pl.semaphore_signal(csem.at[at - JOBS], inc=1, device_id=peer, device_id_type=MESH)
        steps.update({SECOND + at: job.send_second, NEAR + at: job.send_near, OVER_Z + at: job.send_z, CLOSE + at: close})

    def credit(at):
        if at < JOBS:
            pl.semaphore_wait(csem.at[at], len(peers))

    @step(BEGIN)
    def _():
        def begin(n):
            here = band(n * CHUNK, CHUNK)
            value = cot_v[here, :].astype(F32) * live_column(lens, spot, CHUNK, n * CHUNK)
            grad[here, :] = value
            low[here, :] = value.astype(BF16)
        start.wait()
        loop(TOK // CHUNK, begin)

    def terms(job, left, tile, right, other):
        c = lax.rem(rc, 2) if other else spot.c
        rows = left_rows(left, c)
        width = job.width // 2 if job.paired else job.width

        def part(n):
            here = cols(n, tile)
            value = dot(rows, right(n))
            for b in range(4):
                piece = value[96 * b : 96 * b + 96]
                if other:
                    job.send[b, :, here] = piece.astype(BF16)
                elif job.paired:
                    job.got[b, :, cols(spot.c, GROUP)] = piece.astype(BF16)
                else:
                    job.got[b, :, here] = (job.got[b, :, here].astype(F32) + piece).astype(BF16)
        if width == tile:
            part(0)
        else:
            loop(width // tile, part)

    def down_terms(job, right, other):
        c = lax.rem(rc, 2) if other else spot.c

        def part(b):
            value = dot(act_t[band((2 * b + c) * 384, 384), :], right())
            if other:
                job.send[b] = value.astype(BF16)
            else:
                job.got[b] = (job.got[b].astype(F32) + value).astype(BF16)
        loop(4, part)

    late = {}

    def layer_steps(layer):
        base = JOBS * layer
        signed = layer == 0
        gains = norms.at[layer]

        def both(at, needs, compute, after=()):
            job = jobs[at]

            def theirs():
                ready(layer, *needs)
                credit(at)
                compute(job, True)
                job.send_core()

            def ours():
                job.wait_core()
                compute(job, False)
                free(layer, *after)
                job.send_first()
            steps[THEIRS + at] = theirs
            steps[OURS + at] = ours

        for h in (0, 1):
            half = w_down0.shape[1]
            both(
                base + 4 + h,
                ["act_t"],
                lambda job, other, h=h: down_terms(job, lambda: low[:, h * half : (h + 1) * half], other),
                [],
            )
            ff = w_up0.shape[1]
            both(
                base + 2 + h,
                ["nmid_t"],
                lambda job, other, h=h: terms(job, nmid_t, 512, lambda n: dpre[:, cols(n + h * (ff // 512), 512)], other),
                ["nmid_t"] if h else [],
            )
        both(base + 1, ["att_t"], lambda job, other: terms(job, att_t, 256, lambda n: branch[:, cols(n, 256)], other), ["att_t"])
        both(
            base,
            ["nin_t"],
            lambda job, other: terms(job, nin_t, GROUP, lambda n: dqkv[...].reshape(4 * TOK, GROUP), other),
            ["nin_t"],
        )

        def slope(h):
            def run():
                ready(layer, 4, 5, "pre")
                half = w_down0.shape[1]

                def part(n):
                    here = cols(n, 512)
                    rows = pl.ds(pl.multiple_of(n * 512, 512), 512)
                    value = dot_nt(low[:, :half], w_down0[rows, :]) + dot_nt(low[:, half:], w_down1[rows, :])
                    dpre[:, here] = (pre[:, here] * value).astype(BF16)
                lax.fori_loop(3 * h, 3 * h + 3, lambda n, carry: (part(n), carry)[1], 0)
                if h:
                    free(layer, "pre")
            return run
        steps[SLOPE + 10 * layer + 0] = slope(0)
        steps[SLOPE + 10 * layer + 1] = slope(1)

        def through(h):
            w_up = (w_up0, w_up1)[h]

            def run():
                ready(layer, 2 + h)
                if h == 0:
                    dmid[...] = jnp.zeros_like(dmid)
                count = w_up.shape[1] // 512

                def part(n):
                    dmid[...] += dot_nt(dpre[:, cols(n + h * count, 512)], w_up[:, cols(n, 512)])
                loop(count, part)
                free(layer, 2 + h)
            return run
        steps[THROUGH + 10 * layer + 0] = through(0)
        steps[THROUGH + 10 * layer + 1] = through(1)

        @step(NORM_BACK + layer)
        def _():
            ready(layer, "middle")
            late[layer] = norm_back(middle, lambda here: dmid[here, :], gains[2:3, :], grad, grad, branch, sums)

        def asked(g, which=layer):
            return rcopy(
                datt_s.at[g], datt_r.at[spot.member], as_.at[4 * which + g], ar.at[4 * which + spot.member], spot.device(g)
            )

        @step(ASK + layer)
        def _():
            ready(layer, 1)
            for g in range(4):
                value = dot_nt(w_out[192 * g : 192 * g + 192, :], branch[...]).astype(BF16)
                if layer == 0:
                    @pl.when(spot.member != g)
                    def _():
                        asked(g, 1).wait_send()
                datt_s[g] = value

                @pl.when(spot.member != g)
                def _():
                    asked(g).start()

                @pl.when(spot.member == g)
                def _():
                    datt_r[g] = datt_s[g]
            free(layer, 1)

        @step(KEYS + layer)
        def _():
            ready(layer, "qkv", "out", "stats")

            def turn_keys(j):
                kt[:, cols(j, TOK)] = qkv[j, :, 384:640].astype(F32).T.astype(BF16)
            loop(4, turn_keys)
            dk[...] = jnp.zeros_like(dk)
            dv[...] = jnp.zeros_like(dv)

        @step(ASKED + layer)
        def _():
            for g in range(4):
                @pl.when(spot.member != g)
                def _():
                    rcopy(datt_r.at[g], datt_r.at[g], as_.at[4 * layer + g], ar.at[4 * layer + g], spot.device(g)).wait_recv()

        def back(i):
            def run():
                dqkv[i] = attend_quarter_back(i, lens, qkv, kt, datt_r, att_out, stats, (dk, dv, dq), signed)
                if i == 0:
                    free(layer, "qkv", "out", "stats")
            return run
        for i in range(4):
            steps[ATTEND_BACK + 10 * layer + i] = back(i)

        def given(which, k, i):
            mate = spot.mate(1 if k == 1 else 2)[0]
            return rcopy(pn_s.at[i], pn_r.at[k - 1], ps.at[4 * which + k], pr.at[4 * which + k], mate)

        def role(i, k):
            return spot.mate(k)[1] == i if k else spot.member == i

        def partial(i):
            def run():
                if i == 3:
                    ready(layer, 0)
                value = dot_nt(dqkv[i], w_qkv[...])

                @pl.when(role(i, 0))
                def _():
                    dmid[...] = value

                @pl.when(role(i, 1))
                def _():
                    held[...] = value
                for k in (2, 3):
                    @pl.when(role(i, k))
                    def _(k=k):
                        at = 3 if k == 2 else 2
                        if layer == 0:
                            given(1, at, i).wait_send()
                        pn_s[i] = value.astype(BF16)
                        given(layer, at, i).start()
                if i == 0:
                    free(layer, 0)
            return run

        def relay(i):
            def run():
                @pl.when(role(i, 1))
                def _():
                    if layer == 0:
                        given(1, 1, i).wait_send()
                    given(layer, 2, i).wait_recv()
                    pn_s[i] = (held[...] + pn_r[1].astype(F32)).astype(BF16)
                    given(layer, 1, i).start()
            return run
        for i in range(4):
            steps[PARTIAL + 10 * layer + i] = partial(i)
            steps[RELAY + 10 * layer + i] = relay(i)

        @step(FIRST_BACK + layer)
        def _():
            ready(layer, "stream")
            given(layer, 3, 0).wait_recv()
            given(layer, 1, 0).wait_recv()

            def upstream(here):
                return dmid[here, :] + pn_r[2, here, :].astype(F32) + pn_r[0, here, :].astype(F32)
            early = norm_back(stream, upstream, gains[0:1, :], grad, grad, low, sums)
            free(layer, "stream")
            for n, value in enumerate(early + late[layer]):
                edges[4 * layer + n : 4 * layer + n + 1, :] = value

    for layer in (1, 0):
        layer_steps(layer)

    @step(RESULT_BACK)
    def _():
        ready(1, "middle", "act_t", 4, 5)
        half = w_down0.shape[1]
        act = act_t[...].T
        for h, w_down in ((0, w_down0), (1, w_down1)):
            here = slice(h * half, (h + 1) * half)
            value = middle[:, here] + dot(act, w_down[...])
            res[:, here] = (value * live_column(lens, spot, TOK, 0)).astype(BF16)
        swap(spot, res, result_o, ms.at[1], mr.at[1])
        free(1, "middle", "act_t", 4, 5)

    @step(SWAP_BACK)
    def _():
        swap(spot, low, input_o, ms.at[0], mr.at[0])

    last = 2 * JOBS

    def edge_rows(c):
        turned = jnp.concatenate([edges[...], jnp.zeros((128 - 8, edges.shape[1]), F32)], 0).T
        return [
            jnp.where(c == 0, turned[192 * b : 192 * b + 96], turned[192 * b + 96 : 192 * b + 192]) for b in range(4)
        ]

    @step(THEIRS + last)
    def _():
        job = jobs[last]
        for b, rows in enumerate(edge_rows(lax.rem(rc, 2))):
            job.send[b, :, 0:128] = rows.astype(BF16)
            job.send[b, :, 128:256] = jnp.zeros((96, 128), BF16)
        job.send_core()

    @step(OURS + last)
    def _():
        job = jobs[last]
        job.wait_core()
        for b, rows in enumerate(edge_rows(spot.c)):
            job.got[b, :, 0:128] = (job.got[b, :, 0:128].astype(F32) + rows).astype(BF16)
        job.send_first()

    for name in BACKWARD_ORDER:
        steps.pop(name)()
    assert not steps
    for job in jobs:
        job.drain()
    for g in range(4):
        @pl.when(spot.member != g)
        def _():
            rcopy(
                datt_s.at[g], datt_r.at[spot.member], as_.at[g], ar.at[spot.member], spot.device(g)
            ).wait_send()
    for k in (1, 2, 3):
        mate = spot.mate(1 if k == 1 else 2)[0]
        rcopy(pn_s.at[0], pn_r.at[k - 1], ps.at[k], pr.at[k], mate).wait_send()
    swap_wait(spot, low, input_o, ms.at[0], mr.at[0])
    swap_wait(spot, res, result_o, ms.at[1], mr.at[1])


def backward_call(cot, lens, norms, wholes, stash):
    d, ff = cot.shape[1], stash[0][6].shape[1]
    any_space = pl.BlockSpec(memory_space=pl.ANY)
    vmem = pl.BlockSpec(memory_space=pltpu.VMEM)
    dma = lambda n: pltpu.SemaphoreType.DMA((n,))
    shapes = reduce_shapes(d, ff)
    sends, buffers = [], []
    for n, (rows, width) in enumerate(shapes):
        sends.append(pltpu.VMEM((4, rows, width // 2 if n == 0 else width), BF16))
        cut = (rows // 4, width) if n in (4, 5) else (16, width * 3 // 2)
        buffers += [
            pltpu.VMEM((4, rows, width), BF16),
            pltpu.VMEM((2, rows // 2, width), BF16),
            pltpu.VMEM((2, rows, width), BF16),
        ]
        buffers += [pltpu.VMEM((4,) + cut, BF16), pltpu.VMEM((3,) + cut, BF16)]
    count = 2 * JOBS + 1
    outs = pl.pallas_call(
        backward_kernel,
        out_shape=[
            jax.ShapeDtypeStruct((TOK, d), BF16),
            jax.ShapeDtypeStruct((TOK, d), BF16),
            jax.ShapeDtypeStruct((LAYERS, 24, 4 * GROUP), F32),
            jax.ShapeDtypeStruct((LAYERS, 24, d), F32),
            jax.ShapeDtypeStruct((LAYERS, 24, ff), F32),
            jax.ShapeDtypeStruct((LAYERS, ff // 32, d), F32),
            jax.ShapeDtypeStruct((24, EDGE), F32),
        ],
        in_specs=[any_space, vmem, vmem] + [any_space] * (2 * JOBS + 20),
        out_specs=[any_space, any_space] + [vmem] * 5,
        scratch_shapes=[pltpu.VMEM(whole.shape, BF16) for whole in wholes[:JOBS]]
        + [pltpu.VMEM(shape, kind) for shape, kind in stash_shapes(d, ff)]
        + [
            pltpu.VMEM((TOK, d), BF16),
            pltpu.VMEM((TOK, d), F32),
            pltpu.VMEM((TOK, d), BF16),
            pltpu.VMEM((TOK, d), BF16),
            pltpu.VMEM((TOK, ff), BF16),
            pltpu.VMEM((TOK, d), F32),
            pltpu.VMEM((16, d), F32),
            pltpu.VMEM((8, d), F32),
            pltpu.VMEM((4, 192, TOK), BF16),
            pltpu.VMEM((4, 192, TOK), BF16),
            pltpu.VMEM((WIDE, 4 * TOK), BF16),
            pltpu.VMEM((4 * TOK, WIDE), F32),
            pltpu.VMEM((4 * TOK, WIDE), F32),
            pltpu.VMEM((192, TOK), F32),
            pltpu.VMEM((4, TOK, GROUP), BF16),
            pltpu.VMEM((4, TOK, d), BF16),
            pltpu.VMEM((3, TOK, d), BF16),
            pltpu.VMEM((TOK, d), F32),
            pltpu.VMEM((TOK, d), BF16),
        ]
        + sends
        + buffers
        + [
            dma(count * Reduce.SEMS),
            dma(count * Reduce.SEMS),
            dma(2 * (10 + JOBS) + 1),
            pltpu.SemaphoreType.REGULAR((JOBS,)),
            dma(8),
            dma(8),
            dma(8),
            dma(8),
            dma(2),
            dma(2),
        ],
        compiler_params=pltpu.CompilerParams(collective_id=1, has_side_effects=True, vmem_limit_bytes=62 * 2**20),
    )(cot, lens, norms, *wholes, *stash[0], *stash[1])
    return outs


def finish_kernel(result, grad_in, qkv, out, up, down, edge, result_o, input_o, qkv_o, out_o, up_o, down_o, gains_o, biases_o, mids_o):
    result_o[0] = result[...]
    input_o[0] = grad_in[...].astype(F32)
    out_o[...] = out[...]
    up_o[...] = up[...]
    down_o[...] = down[...]
    own = edge.shape[0]
    turned = jnp.concatenate([edge[:, 0:128], jnp.zeros((128 - own, 128), F32)], 0).T
    layer = pl.program_id(0)
    parts = [qkv[0, :, GROUP * g + at : GROUP * g + at + 192] for at in (0, 384, 192) for g in range(4)]
    qkv_o[0] = jnp.concatenate(parts, 1)
    rows = jnp.where(layer == 0, turned[0:4, 0:own], turned[4:8, 0:own])
    gains_o[0, 0:1, :] = rows[0:1]
    gains_o[0, 1:2, :] = rows[2:3]
    biases_o[pl.ds(layer, 1), :] = rows[1:2]
    mids_o[pl.ds(layer, 1), :] = rows[3:4]


def backward_part(cot, lens, norms, wholes, stash):
    grads = backward_call(cot, lens, norms, wholes, stash)
    d, own = cot.shape[1], grads[2].shape[1]
    shape = lambda *sizes: jax.ShapeDtypeStruct(sizes, F32)
    return pl.pallas_call(
        finish_kernel,
        out_shape=[
            jax.ShapeDtypeStruct((1, TOK, d), BF16),
            shape(1, TOK, d),
            shape(LAYERS, own, 3 * d),
            shape(*grads[3].shape),
            shape(*grads[4].shape),
            shape(*grads[5].shape),
            shape(LAYERS, 2, own),
            shape(LAYERS, own),
            shape(LAYERS, own),
        ],
        grid=(LAYERS,),
        in_specs=[pl.BlockSpec((TOK // LAYERS, d), lambda i: (i, 0))] * 2
        + [pl.BlockSpec((1,) + grad.shape[1:], lambda i: (i, 0, 0)) for grad in grads[2:6]]
        + [pl.BlockSpec(grads[6].shape, lambda i: (0, 0))],
        out_specs=[pl.BlockSpec((1, TOK // LAYERS, d), lambda i: (0, i, 0))] * 2
        + [pl.BlockSpec((1, own, 3 * d), lambda i: (i, 0, 0))]
        + [pl.BlockSpec((1,) + grad.shape[1:], lambda i: (i, 0, 0)) for grad in grads[3:6]]
        + [pl.BlockSpec((1, 2, own), lambda i: (i, 0, 0))]
        + [pl.BlockSpec((LAYERS, own), lambda i: (0, 0))] * 2,
        compiler_params=pltpu.CompilerParams(vmem_limit_bytes=62 * 2**20),
    )(*grads)


def local_fast(tokens, lengths, w_qkv, w_out, w_up, w_down, gains, biases, cotangent):
    (cot, lens, norms), wholes, stash = forward_call(
        tokens[0], cotangent[0], lengths, w_qkv, w_out, w_up, w_down, gains, biases
    )
    return tuple(backward_part(cot, lens, norms, wholes, stash))


def solution(mesh):
    in_specs = (
        P("rows", "kv", None),
        P("rows", None),
        P(None, ("rows", "kv"), None),
        P(None, ("rows", "kv"), None),
        P(None, ("rows", "kv"), None),
        P(None, ("rows", "kv"), None),
        P(None, None, ("rows", "kv")),
        P(None, None, ("rows", "kv")),
        P("rows", "kv", None),
    )
    out_specs = (
        P("rows", "kv", None),
        P("rows", "kv", None),
        P(None, ("rows", "kv"), None),
        P(None, ("rows", "kv"), None),
        P(None, ("rows", "kv"), None),
        P(None, ("rows", "kv"), None),
        P(None, None, ("rows", "kv")),
        P(None, ("rows", "kv")),
        P(None, ("rows", "kv")),
    )
    fast = dict(mesh.shape) == {"rows": 8, "kv": 4}
    return jax.shard_map(local_fast if fast else local_generic, mesh=mesh, in_specs=in_specs, out_specs=out_specs, check_vma=False)
```
